512 devices in a mesh: seq: 128 (over z_lo, y, x, core), pair: 4 (over z_hi).
Axes of the slice: x: 4, y: 8, z: 8 (z_hi: 4, z_lo: 2; z = z_hi * 2 + z_lo), core: 2. Of those that a mesh axis runs over, the one named last changes fastest.
Arguments:
- tokens: int32 [262144], P('seq'), may hold values from 0 to 3
- w_stem: bfloat16 [60, 768], replicated, may hold values from -1.5 to 1.5
- w_conv: bfloat16 [3840, 1536], P('seq', 'pair'), may hold values from -0.09375 to 0.09375
- w_query: bfloat16 [1536, 512], P(None, 'pair')
- w_key: bfloat16 [1536, 512], P(None, 'pair'), may hold values from -0.15625 to 0.15625
- w_value: bfloat16 [1536, 768], P(None, 'pair'), may hold values from -0.15625 to 0.15625
- w_out: bfloat16 [768, 1536], P('pair'), may hold values from -0.21875 to 0.21875
- w_pair: bfloat16 [2, 1536, 128], P(None, None, 'pair'), may hold values from -0.15625 to 0.15625
- pair_bias: bfloat16 [18, 128], P(None, 'pair'), may hold values from -6 to 6
- pair_in: bfloat16 [128, 128, 128], P('seq', None, 'pair'), may hold values from -6 to 6
Outputs:
- seq_out: bfloat16 [2048, 1536], P('seq', 'pair')
- pair_out: bfloat16 [128, 128, 128], P('seq', None, 'pair')
The draws below stay inside these ranges and needn't reach their ends.
All inputs are finite; a program needn't handle non-finite values.
Results may differ from the reference program's by a relative error of at most 0.02.
Values may be sent and summed in bfloat16 or wider, within the bound.
No kernel may reach another device: no remote copies, remote signals or barrier semaphores. Data moves between devices by JAX's collectives and lax.ppermute only.
A program may use at most 64 MiB of HBM per device.

```python
import math
import jax
import jax.numpy as jnp
from jax import lax

C_IN = 768
C_OUT = 1536
HEADS = 4
HQK = 128
HV = 192
PAIR_CH = 128
KS_STEM = 15
KS_CONV = 5
STEM_POOL = 64
CONV_POOL = 2
PAIR_POOL = 16
NBINS = 18
BASES = 262144
PAIR = 128


def draw_w_query(key, part):
    key = jax.random.fold_in(key, 11)
    values = jax.random.normal(key, (C_OUT, HEADS * HQK), jnp.float32) / math.sqrt(C_OUT)
    return values.astype(jnp.bfloat16)


def draw_tokens(key, part):
    key = jax.random.fold_in(key, 23)
    stretch = STEM_POOL * CONV_POOL * PAIR_POOL
    regions = BASES // stretch
    key_main, key_strength, key_pick, key_other = jax.random.split(key, 4)
    dominant = jax.random.randint(key_main, (regions,), 0, 4, jnp.int32)
    strength = jax.random.randint(key_strength, (regions,), 0, 12, jnp.int32)
    pick = jax.random.randint(key_pick, (regions, stretch), 0, 12, jnp.int32)
    other = jax.random.randint(key_other, (regions, stretch), 0, 4, jnp.int32)
    bases = jnp.where(pick < strength[:, None], dominant[:, None], other)
    return bases.reshape(BASES).astype(jnp.int32)


def block_scale(stream_key, shape, cuts, low, top_value):
    gain, own = 1.0, jax.random.fold_in(stream_key, 6)
    for axis_at, blocks in cuts:
        heights = jnp.exp(jax.random.uniform(jax.random.fold_in(own, axis_at), (blocks,), jnp.float32, low / len(cuts), top_value / len(cuts)))
        gain = gain * jnp.repeat(heights, shape[axis_at] // blocks).reshape([-1 if axis == axis_at else 1 for axis in range(len(shape))])
    return gain


def scatter_about(rng, extent, scale, reach, pieces=(), kind=jnp.bfloat16):
    entries = scale * jax.random.normal(rng, extent, jnp.float32)
    if pieces:
        entries = entries * block_scale(rng, extent, pieces, -0.22, 0.18)
    return jnp.clip(entries, -reach, reach).astype(kind)


def setup_inputs(seed: int = 0) -> dict:
    splits = jax.random.split(jax.random.key(seed), 11)
    tokens = draw_tokens(jax.random.fold_in(splits[10], 71), 0)
    w_stem = scatter_about(splits[1], (KS_STEM * 4, C_IN), KS_STEM ** -0.5, 1.5)
    w_conv = scatter_about(splits[2], (KS_CONV * C_IN, C_OUT), (KS_CONV * C_IN) ** -0.5, 0.09375, ((0, 128), (1, 4)))
    w_query = draw_w_query(jax.random.fold_in(splits[10], 71), 0)
    w_key = scatter_about(splits[4], (C_OUT, HEADS * HQK), C_OUT ** -0.5, 0.15625, ((1, 4),))
    w_value = scatter_about(splits[5], (C_OUT, HEADS * HV), C_OUT ** -0.5, 0.15625, ((1, 4),))
    w_out = scatter_about(splits[6], (HEADS * HV, C_OUT), (HEADS * HV) ** -0.5, 0.21875, ((0, 4),))
    w_pair = scatter_about(splits[7], (2, C_OUT, PAIR_CH), C_OUT ** -0.5, 0.15625, ((2, 4),))
    pair_bias = scatter_about(splits[8], (NBINS, PAIR_CH), 1.0, 6.0, ((1, 4),))
    pair_in = scatter_about(splits[9], (PAIR, PAIR, PAIR_CH), 1.0, 6.0, ((0, 128), (2, 4)))
    return {"tokens": tokens, "w_stem": w_stem, "w_conv": w_conv, "w_query": w_query, "w_key": w_key, "w_value": w_value, "w_out": w_out, "w_pair": w_pair, "pair_bias": pair_bias, "pair_in": pair_in}


EDGES = (1, 2, 3, 4, 6, 8, 12, 16, 24, 32, 48, 64, 96, 128, 192, 256, 384)

def distance_bins(delta):
    total = jnp.zeros(delta.shape, jnp.int32)
    for edge in EDGES:
        total = total + (delta >= edge).astype(jnp.int32)
    return total

def stem_section(tokens, w_stem):
    count_bases = tokens.shape[0]
    half = KS_STEM // 2
    rim = jnp.full((half,), -1, jnp.int32)
    padded = jnp.concatenate([rim, tokens.astype(jnp.int32), rim])
    block = min(1024, count_bases)
    levels = jnp.arange(4, dtype=jnp.int32)

    def one_block(index):
        window = lax.dynamic_slice_in_dim(padded, (index * block).astype(jnp.int32), block + 2 * half)
        columns = [window[k:k + block, None] == levels[None, :] for k in range(KS_STEM)]
        onehot = jnp.concatenate(columns, axis=1).astype(jnp.bfloat16)
        hidden = jax.nn.gelu(jnp.dot(onehot, w_stem, preferred_element_type=jnp.float32))
        return lax.optimization_barrier(jnp.max(hidden.reshape(block // STEM_POOL, STEM_POOL, hidden.shape[1]), axis=1))
    pooled = lax.map(one_block, jnp.arange(count_bases // block, dtype=jnp.int32))
    return pooled.reshape(count_bases // STEM_POOL, -1).astype(jnp.bfloat16)

def conv_section(section, w_conv):
    half = KS_CONV // 2
    rows = section.shape[0]
    padded = jnp.pad(section, ((half, half), (0, 0)))
    unfold = jnp.concatenate([padded[k:k + rows] for k in range(KS_CONV)], axis=1)
    conv = jnp.dot(unfold, w_conv, preferred_element_type=jnp.float32)
    active = jax.nn.gelu(conv)
    return lax.optimization_barrier(jnp.max(active.reshape(rows // CONV_POOL, CONV_POOL, active.shape[1]), axis=1)).astype(jnp.bfloat16)

def attention(trunk, w_query, w_key, w_value):
    count = trunk.shape[0]
    queries = jnp.dot(trunk, w_query, preferred_element_type=jnp.float32).astype(jnp.bfloat16)
    keys = jnp.dot(trunk, w_key, preferred_element_type=jnp.float32).astype(jnp.bfloat16)
    values = jnp.dot(trunk, w_value, preferred_element_type=jnp.float32).astype(jnp.bfloat16)
    queries = queries.reshape(count, HEADS, HQK)
    keys = keys.reshape(count, HEADS, HQK).astype(jnp.float32)
    values = values.reshape(count, HEADS, HV).astype(jnp.float32)
    block = min(512, count)
    scale = 1.0 / math.sqrt(HQK)

    def one_block(query_block):
        scores = jnp.einsum('qhd,khd->hqk', query_block.astype(jnp.float32), keys) * scale
        top = lax.optimization_barrier(jnp.max(scores, axis=2, keepdims=True))
        expo = jnp.exp(scores - top)
        total = lax.optimization_barrier(jnp.sum(expo, axis=2))
        weights = expo.astype(jnp.bfloat16).astype(jnp.float32)
        mixed = jnp.einsum('hqk,khd->qhd', weights, values) / jnp.transpose(total)[:, :, None]
        return mixed.astype(jnp.bfloat16)
    mixed = lax.map(one_block, queries.reshape(count // block, block, HEADS, HQK))
    return mixed.reshape(count, HEADS * HV)

def reference(tokens, w_stem, w_conv, w_query, w_key, w_value, w_out, w_pair, pair_bias, pair_in):
    section = stem_section(tokens, w_stem)
    trunk = conv_section(section, w_conv)
    mixed = attention(trunk, w_query, w_key, w_value)
    summed = trunk.astype(jnp.float32) + jnp.dot(mixed, w_out, preferred_element_type=jnp.float32)
    seq_out = summed.astype(jnp.bfloat16)
    count = summed.shape[0]
    pooled = lax.optimization_barrier(jnp.mean(summed.reshape(count // PAIR_POOL, PAIR_POOL, summed.shape[1]), axis=1)).astype(jnp.bfloat16)
    row_a = jnp.dot(pooled, w_pair[0], preferred_element_type=jnp.float32)
    row_b = jnp.dot(pooled, w_pair[1], preferred_element_type=jnp.float32)
    index = jnp.arange(pooled.shape[0], dtype=jnp.int32)
    bins = distance_bins(jnp.abs(index[:, None] - index[None, :]))
    bias = pair_bias.astype(jnp.float32)[bins]
    direct = pair_in.astype(jnp.float32) + row_a[:, None, :] * row_b[None, :, :] + bias
    pair_out = (0.5 * (direct + jnp.transpose(direct, (1, 0, 2)))).astype(jnp.bfloat16)
    return (seq_out, pair_out)
```

```python
import math

import jax
import jax.numpy as jnp
from jax import lax
from jax.experimental import pallas as pl
from jax.experimental.pallas import tpu as pltpu
from jax.sharding import Mesh
from jax.sharding import PartitionSpec as P

HQK = 128
HV = 192
KS_STEM = 15
KS_CONV = 5
STEM_POOL = 64
PAIR_POOL = 16
EDGES = (1, 2, 3, 4, 6, 8, 12, 16, 24, 32, 48, 64, 96, 128, 192, 256, 384)

SEQ = ("zl", "y", "x", "core")
SHARE = ("zl", "core")
SIZES = {"zl": 2, "y": 8, "x": 4, "core": 2, "pair": 4}
N_SEQ = 128
N_SHARE = 4
N_PAIR = 4

SIDE = 256
ROWS = 32
EXT = ROWS + 4
EXT_PAD = 40
VMEM = 48 * 1024 * 1024


def params(**kw):
    return pltpu.CompilerParams(vmem_limit_bytes=VMEM, **kw)


def whole(count):
    return [pl.BlockSpec(memory_space=pltpu.VMEM) for _ in range(count)]


def gelu(x):
    return 0.5 * x * (1.0 + jnp.tanh(math.sqrt(2.0 / math.pi) * (x + 0.044715 * (x * x * x))))


def stem_kernel(place_ref, codes_ref, weight_ref, out_ref):
    length = codes_ref.shape[1]
    codes = jnp.broadcast_to(codes_ref[...], (16, length))
    first = SIDE - 2 * STEM_POOL + KS_STEM // 2
    shifted = pltpu.roll(codes, length - first, 1, stride=1, stride_axis=0)
    shifted = shifted[:, : EXT * STEM_POOL]
    onehot = jnp.concatenate(
        [(shifted == base + 1).astype(jnp.float32) for base in range(4)], axis=0
    ).astype(jnp.bfloat16)
    weight = weight_ref[...]
    step = 6
    for at in range(0, EXT, step):
        part = onehot[:, at * STEM_POOL : (at + step) * STEM_POOL]
        hidden = lax.dot_general(
            part, weight, (((0,), (0,)), ((), ())), preferred_element_type=jnp.float32
        ).reshape(step, STEM_POOL, weight.shape[1])
        high = gelu(jnp.max(hidden, axis=1))
        low = gelu(jnp.min(hidden, axis=1))
        rows = jnp.maximum(high, low)
        index = place_ref[0] * ROWS - 2 + at + lax.broadcasted_iota(jnp.int32, rows.shape, 0)
        inside = (index >= 0) & (index < N_SEQ * ROWS)
        out_ref[at : at + step, :] = jnp.where(inside, rows, 0.0)
    out_ref[EXT:EXT_PAD, :] = jnp.zeros((EXT_PAD - EXT, weight.shape[1]), jnp.float32)


def stem(place, codes, weight):
    return pl.pallas_call(
        stem_kernel,
        out_shape=jax.ShapeDtypeStruct((EXT_PAD, weight.shape[1]), jnp.float32),
        in_specs=[pl.BlockSpec(memory_space=pltpu.SMEM)] + whole(2),
        out_specs=whole(1)[0],
        compiler_params=params(),
        cost_estimate=pl.CostEstimate(flops=2 * 2304 * 64 * 768, bytes_accessed=200000, transcendentals=0),
    )(place, codes, weight)


def conv_kernel(section_ref, weight_ref, out_ref, wide, act):
    windows, _, channels = section_ref.shape
    wide[...] = section_ref[...].astype(jnp.float32)
    total = None
    for tap in range(KS_CONV):
        rows = wide[:, tap : tap + ROWS, :].astype(jnp.bfloat16).reshape(windows * ROWS, channels)
        term = jnp.dot(
            rows,
            weight_ref[tap * channels : (tap + 1) * channels, :],
            preferred_element_type=jnp.float32,
        )
        total = term if total is None else total + term
    act[...] = gelu(total)
    half = windows * ROWS // 2
    best = jnp.maximum(act[pl.ds(0, half, stride=2), :], act[pl.ds(1, half, stride=2), :])
    out_ref[...] = best.astype(jnp.bfloat16).reshape(out_ref.shape)


def conv(section, weight):
    windows, _, channels = section.shape
    columns = weight.shape[1]
    return pl.pallas_call(
        conv_kernel,
        out_shape=jax.ShapeDtypeStruct((windows, ROWS // 2, columns), jnp.bfloat16),
        in_specs=whole(2),
        out_specs=whole(1)[0],
        scratch_shapes=[
            pltpu.VMEM((windows, EXT_PAD, channels), jnp.float32),
            pltpu.VMEM((windows * ROWS, columns), jnp.float32),
        ],
        compiler_params=params(),
    )(section, weight)


def attention_kernel(query_ref, kv_ref, w_out_ref, out_ref):
    scale = 1.0 / math.sqrt(HQK)
    scores = (
        lax.dot_general(
            query_ref[...],
            kv_ref[:, :HQK],
            (((1,), (1,)), ((), ())),
            preferred_element_type=jnp.float32,
        )
        * scale
    )
    top = jnp.max(scores, axis=1, keepdims=True)
    expo = jnp.exp(scores - top)
    total = jnp.sum(expo, axis=1, keepdims=True)
    mixed = jnp.dot(
        expo.astype(jnp.bfloat16), kv_ref[:, HQK : HQK + HV], preferred_element_type=jnp.float32
    )
    mixed = (mixed / total).astype(jnp.bfloat16)
    term = jnp.dot(mixed, w_out_ref[...], preferred_element_type=jnp.float32)
    mean = jnp.sum(term, axis=0, keepdims=True) * (1.0 / PAIR_POOL)
    width = term.shape[1] // N_PAIR
    count = term.shape[0]
    tail = jnp.concatenate(
        [mean[:, c * width : (c + 1) * width] for c in range(N_PAIR)]
        + [jnp.zeros((4, width), jnp.float32)],
        axis=0,
    )
    for c in range(N_PAIR):
        out_ref[c, :count, :] = term[:, c * width : (c + 1) * width]
        out_ref[c, count : count + 8, :] = tail


def attention(query, kv, w_out):
    count = query.shape[0]
    width = w_out.shape[1] // N_PAIR
    return pl.pallas_call(
        attention_kernel,
        out_shape=jax.ShapeDtypeStruct((N_PAIR, count + 8, width), jnp.float32),
        in_specs=whole(3),
        out_specs=whole(1)[0],
        compiler_params=params(),
    )(query, kv, w_out)


def close_kernel(terms_ref, own_ref, trunk_ref, w_pair_ref, seq_ref, rows_ref):
    count, width = own_ref.shape
    total = terms_ref[0] + terms_ref[1] + terms_ref[2] + terms_ref[3]
    seq_ref[...] = (own_ref[...].astype(jnp.float32) + total[:count, :]).astype(jnp.bfloat16)
    trunk_mean = jnp.sum(trunk_ref[...].astype(jnp.float32), axis=0, keepdims=True) * (1.0 / PAIR_POOL)
    rows = None
    for c in range(N_PAIR):
        pooled = trunk_mean[:, c * width : (c + 1) * width] + total[count + c : count + c + 1, :]
        term = jnp.dot(
            jnp.broadcast_to(pooled, (8, width)).astype(jnp.bfloat16),
            w_pair_ref[c * width : (c + 1) * width, :],
            preferred_element_type=jnp.float32,
        )
        rows = term if rows is None else rows + term
    rows_ref[...] = rows


def close(terms, own, trunk, w_pair):
    return pl.pallas_call(
        close_kernel,
        out_shape=(
            jax.ShapeDtypeStruct(own.shape, jnp.bfloat16),
            jax.ShapeDtypeStruct((8, w_pair.shape[1]), jnp.float32),
        ),
        in_specs=whole(4),
        out_specs=tuple(whole(2)),
        compiler_params=params(),
    )(terms, own, trunk, w_pair)


def distance_bias(row, cols, pair_bias):
    delta = jnp.abs(row - cols)
    bins = jnp.zeros(delta.shape, jnp.int32)
    for edge in EDGES:
        bins = bins + (delta >= edge).astype(jnp.int32)
    labels = jnp.arange(pair_bias.shape[0], dtype=jnp.int32)
    onehot = (bins[:, None] == labels[None, :]).astype(jnp.bfloat16)
    return jnp.dot(onehot, pair_bias, preferred_element_type=jnp.float32)


def on_device(tokens, w_stem, w_conv, w_query, w_key, w_value, w_out, w_pair, pair_bias, pair_in):
    place = lax.axis_index(SEQ)
    pair_place = lax.axis_index("pair")

    taps, width = w_conv.shape
    share = width // N_SHARE
    blocks = w_conv.reshape(taps, N_SHARE, share).transpose(1, 0, 2)
    blocks = blocks.reshape(2, 1, 1, 2, taps, share)
    blocks = jnp.broadcast_to(blocks, (2, 8, 4, 2, taps, share)).reshape(N_SEQ, taps, share)
    channels = pair_in.shape[2]
    mirror = jnp.pad(pair_in.reshape(N_SEQ, 1, channels), ((0, 0), (0, 0), (0, share - channels)))
    sent = jnp.concatenate([blocks, mirror], axis=1)
    held = lax.all_to_all(sent, SEQ, split_axis=0, concat_axis=0, tiled=True)
    conv_weight = held[:, :taps, :].reshape(N_SEQ * taps, share)
    mirror = held[:, taps, :channels]

    codes = tokens + 1
    ends = N_SEQ - 1
    left = lax.ppermute(codes[-SIDE:], SEQ, [(i, i + 1) for i in range(ends)])
    right = lax.ppermute(codes[:SIDE], SEQ, [(i + 1, i) for i in range(ends)])
    codes = jnp.concatenate([left, codes, right])[None, :]
    stem_weight = w_stem.reshape(KS_STEM, 4, -1)[::-1].transpose(1, 0, 2)
    stem_weight = jnp.pad(stem_weight, ((0, 0), (0, 1), (0, 0))).reshape(64, -1)
    section = stem(place.astype(jnp.int32)[None], codes, stem_weight).astype(jnp.bfloat16)
    sections = lax.all_gather(section, SHARE, axis=0, tiled=False)

    parts = conv(sections, conv_weight)
    count = parts.shape[1]
    parts = jnp.broadcast_to(parts[:, None], (N_SHARE, N_PAIR, count, share))
    parts = lax.all_to_all(
        parts.reshape(N_SHARE * N_PAIR, count, share),
        SHARE + ("pair",),
        split_axis=0,
        concat_axis=0,
        tiled=True,
    )
    trunk = parts.reshape(N_SHARE, N_PAIR, count, share).transpose(2, 1, 0, 3)
    trunk = trunk.reshape(count, N_PAIR * width)

    w_qkv = jnp.concatenate([w_query, w_key, w_value], axis=1)
    qkv = jnp.dot(trunk, w_qkv, preferred_element_type=jnp.float32).astype(jnp.bfloat16)
    kv = jnp.broadcast_to(qkv[None, :, HQK:], (N_SEQ, count, HQK + HV))
    kv = lax.all_to_all(kv, SEQ, split_axis=0, concat_axis=0, tiled=True)
    terms = attention(qkv[:, :HQK], kv.reshape(N_SEQ * count, HQK + HV), w_out)
    terms = lax.all_to_all(terms, "pair", split_axis=0, concat_axis=0, tiled=True)

    own = lax.dynamic_slice_in_dim(trunk, pair_place * width, width, 1)
    factors = jnp.concatenate([w_pair[0], w_pair[1]], axis=1)
    seq_out, rows = close(terms, own, trunk, factors)
    rows = rows[:1]
    every = lax.all_to_all(
        jnp.broadcast_to(rows[None], (N_SEQ, 1, 2 * channels)),
        SEQ,
        split_axis=0,
        concat_axis=0,
        tiled=True,
    ).reshape(N_SEQ, 2 * channels)

    cols = jnp.arange(N_SEQ, dtype=jnp.int32)
    bias = distance_bias(place.astype(jnp.int32), cols, pair_bias)
    base = 0.5 * (pair_in[0].astype(jnp.float32) + mirror.astype(jnp.float32)) + bias
    cross = rows[:, :channels] * every[:, channels:] + every[:, :channels] * rows[:, channels:]
    pair_out = (base + 0.5 * cross).astype(jnp.bfloat16)[None]
    return (seq_out, pair_out)


def solution(mesh):
    names = SEQ + ("pair",)
    fine = Mesh(mesh.devices.reshape([SIZES[name] for name in names]), names)
    placed = (
        P(SEQ),
        P(),
        P(SEQ, "pair"),
        P(None, "pair"),
        P(None, "pair"),
        P(None, "pair"),
        P("pair", None),
        P(None, None, "pair"),
        P(None, "pair"),
        P(SEQ, None, "pair"),
    )
    return jax.shard_map(
        on_device,
        mesh=fine,
        in_specs=placed,
        out_specs=(P(SEQ, "pair"), P(SEQ, None, "pair")),
        check_vma=False,
    )
```

```python
import math

import jax
import jax.numpy as jnp
from jax import lax
from jax.experimental import pallas as pl
from jax.experimental.pallas import tpu as pltpu
from jax.sharding import Mesh
from jax.sharding import PartitionSpec as P

HQK = 128
HV = 192
KS_STEM = 15
KS_CONV = 5
STEM_POOL = 64
PAIR_POOL = 16
EDGES = (1, 2, 3, 4, 6, 8, 12, 16, 24, 32, 48, 64, 96, 128, 192, 256, 384)

SIZES = {"zl": 2, "y": 8, "xh": 2, "xl": 2, "core": 2, "pair": 4}
SEQ = ("zl", "y", "xh", "xl", "core")
SHARE = ("zl", "core")
N_SEQ = math.prod(SIZES[name] for name in SEQ)
N_SHARE = math.prod(SIZES[name] for name in SHARE)
N_PAIR = SIZES["pair"]

SIDE = 256
ROWS = 32
EXT = ROWS + 4
EXT_PAD = 40
VMEM = 48 * 1024 * 1024


def params(**kw):
    return pltpu.CompilerParams(vmem_limit_bytes=VMEM, **kw)


def whole(count):
    return [pl.BlockSpec(memory_space=pltpu.VMEM) for _ in range(count)]


def gelu(x):
    return 0.5 * x * (1.0 + jnp.tanh(math.sqrt(2.0 / math.pi) * (x + 0.044715 * (x * x * x))))


def stem_kernel(place_ref, codes_ref, weight_ref, out_ref):
    length = codes_ref.shape[1]
    codes = jnp.broadcast_to(codes_ref[...], (16, length))
    first = SIDE - 2 * STEM_POOL + KS_STEM // 2
    shifted = pltpu.roll(codes, length - first, 1, stride=1, stride_axis=0)
    shifted = shifted[:, : EXT * STEM_POOL]
    onehot = jnp.concatenate(
        [(shifted == base + 1).astype(jnp.float32) for base in range(4)], axis=0
    ).astype(jnp.bfloat16)
    weight = weight_ref[...]
    step = 6
    for at in range(0, EXT, step):
        part = onehot[:, at * STEM_POOL : (at + step) * STEM_POOL]
        hidden = lax.dot_general(
            part, weight, (((0,), (0,)), ((), ())), preferred_element_type=jnp.float32
        ).reshape(step, STEM_POOL, weight.shape[1])
        high = gelu(jnp.max(hidden, axis=1))
        low = gelu(jnp.min(hidden, axis=1))
        rows = jnp.maximum(high, low)
        index = place_ref[0] * ROWS - 2 + at + lax.broadcasted_iota(jnp.int32, rows.shape, 0)
        inside = (index >= 0) & (index < N_SEQ * ROWS)
        out_ref[at : at + step, :] = jnp.where(inside, rows, 0.0)
    out_ref[EXT:EXT_PAD, :] = jnp.zeros((EXT_PAD - EXT, weight.shape[1]), jnp.float32)


def stem(place, codes, weight):
    return pl.pallas_call(
        stem_kernel,
        out_shape=jax.ShapeDtypeStruct((EXT_PAD, weight.shape[1]), jnp.float32),
        in_specs=[pl.BlockSpec(memory_space=pltpu.SMEM)] + whole(2),
        out_specs=whole(1)[0],
        compiler_params=params(),
        cost_estimate=pl.CostEstimate(flops=2 * 2304 * 64 * 768, bytes_accessed=200000, transcendentals=0),
    )(place, codes, weight)


def conv_kernel(section_ref, weight_ref, out_ref, wide, act):
    windows, _, channels = section_ref.shape
    wide[...] = section_ref[...].astype(jnp.float32)
    total = None
    for tap in range(KS_CONV):
        rows = wide[:, tap : tap + ROWS, :].astype(jnp.bfloat16).reshape(windows * ROWS, channels)
        term = jnp.dot(
            rows,
            weight_ref[tap * channels : (tap + 1) * channels, :],
            preferred_element_type=jnp.float32,
        )
        total = term if total is None else total + term
    act[...] = gelu(total)
    half = windows * ROWS // 2
    best = jnp.maximum(act[pl.ds(0, half, stride=2), :], act[pl.ds(1, half, stride=2), :])
    out_ref[...] = best.astype(jnp.bfloat16).reshape(out_ref.shape)


def conv(section, weight):
    windows, _, channels = section.shape
    columns = weight.shape[1]
    return pl.pallas_call(
        conv_kernel,
        out_shape=jax.ShapeDtypeStruct((windows, ROWS // 2, columns), jnp.bfloat16),
        in_specs=whole(2),
        out_specs=whole(1)[0],
        scratch_shapes=[
            pltpu.VMEM((windows, EXT_PAD, channels), jnp.float32),
            pltpu.VMEM((windows * ROWS, columns), jnp.float32),
        ],
        compiler_params=params(),
    )(section, weight)


def attention_kernel(query_ref, kv_ref, w_out_ref, out_ref):
    scale = 1.0 / math.sqrt(HQK)
    scores = (
        lax.dot_general(
            query_ref[...],
            kv_ref[:, :HQK],
            (((1,), (1,)), ((), ())),
            preferred_element_type=jnp.float32,
        )
        * scale
    )
    top = jnp.max(scores, axis=1, keepdims=True)
    expo = jnp.exp(scores - top)
    total = jnp.sum(expo, axis=1, keepdims=True)
    mixed = jnp.dot(
        expo.astype(jnp.bfloat16), kv_ref[:, HQK : HQK + HV], preferred_element_type=jnp.float32
    )
    mixed = (mixed / total).astype(jnp.bfloat16)
    term = jnp.dot(mixed, w_out_ref[...], preferred_element_type=jnp.float32)
    mean = jnp.sum(term, axis=0, keepdims=True) * (1.0 / PAIR_POOL)
    width = term.shape[1] // N_PAIR
    count = term.shape[0]
    tail = jnp.concatenate(
        [mean[:, c * width : (c + 1) * width] for c in range(N_PAIR)]
        + [jnp.zeros((4, width), jnp.float32)],
        axis=0,
    )
    for c in range(N_PAIR):
        out_ref[c, :count, :] = term[:, c * width : (c + 1) * width]
        out_ref[c, count : count + 8, :] = tail


def attention(query, kv, w_out):
    count = query.shape[0]
    width = w_out.shape[1] // N_PAIR
    return pl.pallas_call(
        attention_kernel,
        out_shape=jax.ShapeDtypeStruct((N_PAIR, count + 8, width), jnp.float32),
        in_specs=whole(3),
        out_specs=whole(1)[0],
        compiler_params=params(),
    )(query, kv, w_out)


def close_kernel(terms_ref, own_ref, trunk_ref, w_pair_ref, seq_ref, rows_ref):
    count, width = own_ref.shape
    total = terms_ref[0] + terms_ref[1] + terms_ref[2] + terms_ref[3]
    seq_ref[...] = (own_ref[...].astype(jnp.float32) + total[:count, :]).astype(jnp.bfloat16)
    trunk_mean = jnp.sum(trunk_ref[...].astype(jnp.float32), axis=0, keepdims=True) * (1.0 / PAIR_POOL)
    rows = None
    for c in range(N_PAIR):
        pooled = trunk_mean[:, c * width : (c + 1) * width] + total[count + c : count + c + 1, :]
        term = jnp.dot(
            jnp.broadcast_to(pooled, (8, width)).astype(jnp.bfloat16),
            w_pair_ref[c * width : (c + 1) * width, :],
            preferred_element_type=jnp.float32,
        )
        rows = term if rows is None else rows + term
    rows_ref[...] = rows


def close(terms, own, trunk, w_pair):
    return pl.pallas_call(
        close_kernel,
        out_shape=(
            jax.ShapeDtypeStruct(own.shape, jnp.bfloat16),
            jax.ShapeDtypeStruct((8, w_pair.shape[1]), jnp.float32),
        ),
        in_specs=whole(4),
        out_specs=tuple(whole(2)),
        compiler_params=params(),
    )(terms, own, trunk, w_pair)


def distance_bias(row, cols, pair_bias):
    delta = jnp.abs(row - cols)
    bins = jnp.zeros(delta.shape, jnp.int32)
    for edge in EDGES:
        bins = bins + (delta >= edge).astype(jnp.int32)
    labels = jnp.arange(pair_bias.shape[0], dtype=jnp.int32)
    onehot = (bins[:, None] == labels[None, :]).astype(jnp.bfloat16)
    return jnp.dot(onehot, pair_bias, preferred_element_type=jnp.float32)


def exchange(blocks, axes):
    return lax.all_to_all(blocks, axes, split_axis=0, concat_axis=0, tiled=True)


def gather(rows, axes):
    count = math.prod(SIZES[name] for name in axes)
    blocks = jnp.broadcast_to(rows[None], (count,) + rows.shape)
    return exchange(blocks, axes).reshape(count * rows.shape[0], *rows.shape[1:])


def on_device(tokens, w_stem, w_conv, w_query, w_key, w_value, w_out, w_pair, pair_bias, pair_in):
    place = lax.axis_index(SEQ)
    pair_place = lax.axis_index("pair")

    taps, width = w_conv.shape
    share = width // N_SHARE
    blocks = w_conv.reshape(taps, N_SHARE, share).transpose(1, 0, 2)
    blocks = blocks.reshape([SIZES[name] if name in SHARE else 1 for name in SEQ] + [taps, share])
    blocks = jnp.broadcast_to(blocks, [SIZES[name] for name in SEQ] + [taps, share])
    conv_weight = exchange(blocks.reshape(N_SEQ, taps, share), SEQ).reshape(N_SEQ * taps, share)

    codes = tokens + 1
    ends = N_SEQ - 1
    left = lax.ppermute(codes[-SIDE:], SEQ, [(i, i + 1) for i in range(ends)])
    right = lax.ppermute(codes[:SIDE], SEQ, [(i + 1, i) for i in range(ends)])
    codes = jnp.concatenate([left, codes, right])[None, :]
    stem_weight = w_stem.reshape(KS_STEM, 4, -1)[::-1].transpose(1, 0, 2)
    stem_weight = jnp.pad(stem_weight, ((0, 0), (0, 1), (0, 0))).reshape(64, -1)
    section = stem(place.astype(jnp.int32)[None], codes, stem_weight).astype(jnp.bfloat16)
    sections = lax.all_gather(section, SHARE, axis=0, tiled=False)

    parts = conv(sections, conv_weight)
    count = parts.shape[1]
    parts = jnp.broadcast_to(parts[:, None], (N_SHARE, N_PAIR, count, share))
    parts = exchange(parts.reshape(N_SHARE * N_PAIR, count, share), SHARE + ("pair",))
    trunk = parts.reshape(N_SHARE, N_PAIR, count, share).transpose(2, 1, 0, 3)
    trunk = trunk.reshape(count, N_PAIR * width)

    w_qkv = jnp.concatenate([w_query, w_key, w_value], axis=1)
    qkv = jnp.dot(trunk, w_qkv, preferred_element_type=jnp.float32).astype(jnp.bfloat16)
    kv = gather(gather(qkv[:, HQK:], ("zl", "y")), ("xh", "xl"))
    kv = lax.all_gather(kv, "core", axis=0, tiled=True)
    terms = exchange(attention(qkv[:, :HQK], kv, w_out), ("pair",))

    own = lax.dynamic_slice_in_dim(trunk, pair_place * width, width, 1)
    factors = jnp.concatenate([w_pair[0], w_pair[1]], axis=1)
    seq_out, rows = close(terms, own, trunk, factors)
    channels = pair_in.shape[2]
    mine = pair_in[0].astype(jnp.float32)
    rows = rows[:1]
    every = jnp.concatenate([jnp.broadcast_to(rows, (N_SEQ, 2 * channels)), mine], axis=1)
    every = exchange(every[:, None], SEQ)[:, 0]
    mirror = every[:, 2 * channels :]

    cols = jnp.arange(N_SEQ, dtype=jnp.int32)
    bias = distance_bias(place.astype(jnp.int32), cols, pair_bias)
    cross = rows[:, :channels] * every[:, channels : 2 * channels]
    cross = cross + every[:, :channels] * rows[:, channels:]
    pair_out = (0.5 * (mine + mirror + cross) + bias).astype(jnp.bfloat16)[None]
    return (seq_out, pair_out)


def solution(mesh):
    names = SEQ + ("pair",)
    fine = Mesh(mesh.devices.reshape([SIZES[name] for name in names]), names)
    placed = (
        P(SEQ),
        P(),
        P(SEQ, "pair"),
        P(None, "pair"),
        P(None, "pair"),
        P(None, "pair"),
        P("pair", None),
        P(None, None, "pair"),
        P(None, "pair"),
        P(SEQ, None, "pair"),
    )
    return jax.shard_map(
        on_device,
        mesh=fine,
        in_specs=placed,
        out_specs=(P(SEQ, "pair"), P(SEQ, None, "pair")),
        check_vma=False,
    )
```

```python
import math

import jax
import jax.numpy as jnp
from jax import lax
from jax.experimental import pallas as pl
from jax.experimental.pallas import tpu as pltpu
from jax.sharding import Mesh
from jax.sharding import PartitionSpec as P

HQK = 128
HV = 192
KS_STEM = 15
KS_CONV = 5
STEM_POOL = 64
PAIR_POOL = 16
EDGES = (1, 2, 3, 4, 6, 8, 12, 16, 24, 32, 48, 64, 96, 128, 192, 256, 384)

SIZES = {"zl": 2, "y": 8, "xh": 2, "xl": 2, "core": 2, "pair": 4}
SEQ = ("zl", "y", "xh", "xl", "core")
SHARE = ("zl", "xl", "core")
N_SEQ = math.prod(SIZES[name] for name in SEQ)
N_SHARE = math.prod(SIZES[name] for name in SHARE)
N_PAIR = SIZES["pair"]

SIDE = 256
ROWS = 32
EXT = ROWS + 4
EXT_PAD = 40
VMEM = 48 * 1024 * 1024


def params(**kw):
    return pltpu.CompilerParams(vmem_limit_bytes=VMEM, **kw)


def whole(count):
    return [pl.BlockSpec(memory_space=pltpu.VMEM) for _ in range(count)]


def gelu(x):
    return 0.5 * x * (1.0 + jnp.tanh(math.sqrt(2.0 / math.pi) * (x + 0.044715 * (x * x * x))))


def stem_kernel(place_ref, codes_ref, weight_ref, out_ref):
    length = codes_ref.shape[1]
    codes = jnp.broadcast_to(codes_ref[...], (16, length))
    first = SIDE - 2 * STEM_POOL + KS_STEM // 2
    shifted = pltpu.roll(codes, length - first, 1, stride=1, stride_axis=0)
    shifted = shifted[:, : EXT * STEM_POOL]
    onehot = jnp.concatenate(
        [(shifted == base + 1).astype(jnp.float32) for base in range(4)], axis=0
    ).astype(jnp.bfloat16)
    weight = weight_ref[...]
    step = 6
    for at in range(0, EXT, step):
        part = onehot[:, at * STEM_POOL : (at + step) * STEM_POOL]
        hidden = lax.dot_general(
            part, weight, (((0,), (0,)), ((), ())), preferred_element_type=jnp.float32
        ).reshape(step, STEM_POOL, weight.shape[1])
        high = gelu(jnp.max(hidden, axis=1))
        low = gelu(jnp.min(hidden, axis=1))
        rows = jnp.maximum(high, low)
        index = place_ref[0] * ROWS - 2 + at + lax.broadcasted_iota(jnp.int32, rows.shape, 0)
        inside = (index >= 0) & (index < N_SEQ * ROWS)
        out_ref[at : at + step, :] = jnp.where(inside, rows, 0.0)
    out_ref[EXT:EXT_PAD, :] = jnp.zeros((EXT_PAD - EXT, weight.shape[1]), jnp.float32)


def stem(place, codes, weight):
    return pl.pallas_call(
        stem_kernel,
        out_shape=jax.ShapeDtypeStruct((EXT_PAD, weight.shape[1]), jnp.float32),
        in_specs=[pl.BlockSpec(memory_space=pltpu.SMEM)] + whole(2),
        out_specs=whole(1)[0],
        compiler_params=params(),
        cost_estimate=pl.CostEstimate(flops=40_000_000_000, bytes_accessed=200000, transcendentals=0),
    )(place, codes, weight)


def conv_kernel(section_ref, weight_ref, out_ref, wide, act):
    windows, _, channels = section_ref.shape
    half = channels // 2
    columns = out_ref.shape[2]
    wide[...] = section_ref[...].astype(jnp.float32)
    even, odd = None, None
    for tap in range(KS_CONV):
        rows = wide[:, tap : tap + ROWS, :].astype(jnp.bfloat16).reshape(windows * ROWS, channels)
        weight = weight_ref[tap * half : (tap + 1) * half, :]
        term = jnp.dot(rows[:, :half], weight, preferred_element_type=jnp.float32)
        even = term if even is None else even + term
        term = jnp.dot(rows[:, half:], weight, preferred_element_type=jnp.float32)
        odd = term if odd is None else odd + term
    act[...] = gelu(even[:, :columns] + odd[:, columns:])
    count = windows * ROWS // 2
    best = jnp.maximum(act[pl.ds(0, count, stride=2), :], act[pl.ds(1, count, stride=2), :])
    out_ref[...] = best.astype(jnp.bfloat16).reshape(out_ref.shape)


def conv(section, weight):
    windows, _, channels = section.shape
    columns = weight.shape[1] // 2
    return pl.pallas_call(
        conv_kernel,
        out_shape=jax.ShapeDtypeStruct((windows, ROWS // 2, columns), jnp.bfloat16),
        in_specs=whole(2),
        out_specs=whole(1)[0],
        scratch_shapes=[
            pltpu.VMEM((windows, EXT_PAD, channels), jnp.float32),
            pltpu.VMEM((windows * ROWS, columns), jnp.float32),
        ],
        compiler_params=params(),
    )(section, weight)


def attention_kernel(query_ref, near_ref, far_ref, w_out_ref, out_ref):
    scale = 1.0 / math.sqrt(HQK)
    scores = [
        lax.dot_general(
            query_ref[...],
            ref[:, :HQK],
            (((1,), (1,)), ((), ())),
            preferred_element_type=jnp.float32,
        )
        * scale
        for ref in (near_ref, far_ref)
    ]
    top = jnp.maximum(*[jnp.max(part, axis=1, keepdims=True) for part in scores])
    total, mixed = 0.0, 0.0
    for part, ref in zip(scores, (near_ref, far_ref)):
        expo = jnp.exp(part - top)
        total = total + jnp.sum(expo, axis=1, keepdims=True)
        mixed = mixed + jnp.dot(
            expo.astype(jnp.bfloat16), ref[:, HQK : HQK + HV], preferred_element_type=jnp.float32
        )
    mixed = (mixed / total).astype(jnp.bfloat16)
    term = jnp.dot(mixed, w_out_ref[...], preferred_element_type=jnp.float32)
    mean = jnp.sum(term, axis=0, keepdims=True) * (1.0 / PAIR_POOL)
    width = term.shape[1] // N_PAIR
    count = term.shape[0]
    tail = jnp.concatenate(
        [mean[:, c * width : (c + 1) * width] for c in range(N_PAIR)]
        + [jnp.zeros((4, width), jnp.float32)],
        axis=0,
    )
    for c in range(N_PAIR):
        out_ref[c, :count, :] = term[:, c * width : (c + 1) * width]
        out_ref[c, count : count + 8, :] = tail


def attention(query, near, far, w_out):
    count = query.shape[0]
    width = w_out.shape[1] // N_PAIR
    return pl.pallas_call(
        attention_kernel,
        out_shape=jax.ShapeDtypeStruct((N_PAIR, count + 8, width), jnp.float32),
        in_specs=whole(4),
        out_specs=whole(1)[0],
        compiler_params=params(),
    )(query, near, far, w_out)


def close_kernel(terms_ref, own_ref, trunk_ref, w_pair_ref, seq_ref, rows_ref):
    count, width = own_ref.shape
    total = terms_ref[0] + terms_ref[1] + terms_ref[2] + terms_ref[3]
    seq_ref[...] = (own_ref[...].astype(jnp.float32) + total[:count, :]).astype(jnp.bfloat16)
    trunk_mean = jnp.sum(trunk_ref[...].astype(jnp.float32), axis=0, keepdims=True) * (1.0 / PAIR_POOL)
    rows = None
    for c in range(N_PAIR):
        pooled = trunk_mean[:, c * width : (c + 1) * width] + total[count + c : count + c + 1, :]
        term = jnp.dot(
            jnp.broadcast_to(pooled, (8, width)).astype(jnp.bfloat16),
            w_pair_ref[c * width : (c + 1) * width, :],
            preferred_element_type=jnp.float32,
        )
        rows = term if rows is None else rows + term
    rows_ref[...] = rows


def close(terms, own, trunk, w_pair):
    return pl.pallas_call(
        close_kernel,
        out_shape=(
            jax.ShapeDtypeStruct(own.shape, jnp.bfloat16),
            jax.ShapeDtypeStruct((8, w_pair.shape[1]), jnp.float32),
        ),
        in_specs=whole(4),
        out_specs=tuple(whole(2)),
        compiler_params=params(),
    )(terms, own, trunk, w_pair)


def distance_bias(row, cols, pair_bias):
    delta = jnp.abs(row - cols)
    bins = jnp.zeros(delta.shape, jnp.int32)
    for edge in EDGES:
        bins = bins + (delta >= edge).astype(jnp.int32)
    labels = jnp.arange(pair_bias.shape[0], dtype=jnp.int32)
    onehot = (bins[:, None] == labels[None, :]).astype(jnp.bfloat16)
    return jnp.dot(onehot, pair_bias, preferred_element_type=jnp.float32)


def exchange(blocks, axes):
    return lax.all_to_all(blocks, axes, split_axis=0, concat_axis=0, tiled=True)


def gather(rows, axes):
    count = math.prod(SIZES[name] for name in axes)
    blocks = jnp.broadcast_to(rows[None], (count,) + rows.shape)
    return exchange(blocks, axes).reshape(count * rows.shape[0], *rows.shape[1:])


def on_device(tokens, w_stem, w_conv, w_query, w_key, w_value, w_out, w_pair, pair_bias, pair_in):
    place = lax.axis_index(SEQ)
    pair_place = lax.axis_index("pair")

    taps, width = w_conv.shape
    share = width // N_SHARE
    block = [taps // 2, 2 * share]
    blocks = w_conv.reshape(taps // 2, 2, N_SHARE, share).transpose(2, 0, 1, 3)
    blocks = blocks.reshape([SIZES[name] if name in SHARE else 1 for name in SEQ] + block)
    blocks = jnp.broadcast_to(blocks, [SIZES[name] for name in SEQ] + block)
    conv_weight = exchange(blocks.reshape([N_SEQ] + block), SEQ).reshape(N_SEQ * block[0], block[1])

    codes = tokens + 1
    ends = N_SEQ - 1
    left = lax.ppermute(codes[-SIDE:], SEQ, [(i, i + 1) for i in range(ends)])
    right = lax.ppermute(codes[:SIDE], SEQ, [(i + 1, i) for i in range(ends)])
    codes = jnp.concatenate([left, codes, right])[None, :]
    source = jnp.arange(w_stem.shape[1]).reshape(2, -1)
    source = (2 * (source % source.shape[1]) + jnp.arange(2)[:, None]).reshape(-1)
    order = (jnp.arange(w_stem.shape[1])[:, None] == source[None, :]).astype(jnp.bfloat16)
    stem_weight = jnp.dot(w_stem, order, preferred_element_type=jnp.float32).astype(jnp.bfloat16)
    stem_weight = stem_weight.reshape(KS_STEM, 4, -1)[::-1].transpose(1, 0, 2)
    stem_weight = jnp.pad(stem_weight, ((0, 0), (0, 1), (0, 0))).reshape(64, -1)
    section = stem(place.astype(jnp.int32)[None], codes, stem_weight).astype(jnp.bfloat16)
    sections = lax.all_gather(section, SHARE, axis=0, tiled=False)

    parts = conv(sections, conv_weight)
    count = parts.shape[1]
    parts = jnp.broadcast_to(parts[:, None], (N_SHARE, N_PAIR, count, share))
    parts = exchange(parts.reshape(N_SHARE * N_PAIR, count, share), SHARE + ("pair",))
    trunk = parts.reshape(N_SHARE, N_PAIR, count, share).transpose(2, 1, 0, 3)
    trunk = trunk.reshape(count, N_PAIR * width)

    w_qkv = jnp.concatenate([w_query, w_key, w_value], axis=1)
    w_qkv = jnp.pad(w_qkv, ((0, 0), (0, 4 * HQK - w_qkv.shape[1])))
    qkv = jnp.dot(trunk, w_qkv, preferred_element_type=jnp.float32).astype(jnp.bfloat16)
    kv = gather(gather(qkv[:, HQK:], ("zl", "y")), ("xh", "xl"))
    other = lax.ppermute(kv, "core", [(0, 1), (1, 0)])
    terms = exchange(attention(qkv[:, :HQK], kv, other, w_out), ("pair",))

    own = lax.dynamic_slice_in_dim(trunk, pair_place * width, width, 1)
    factors = jnp.concatenate([w_pair[0], w_pair[1]], axis=1)
    seq_out, rows = close(terms, own, trunk, factors)
    channels = pair_in.shape[2]
    mine = pair_in[0].astype(jnp.float32)
    rows = rows[:1]
    every = jnp.concatenate([jnp.broadcast_to(rows, (N_SEQ, 2 * channels)), mine], axis=1)
    every = exchange(every[:, None], SEQ)[:, 0]
    mirror = every[:, 2 * channels :]

    cols = jnp.arange(N_SEQ, dtype=jnp.int32)
    bias = distance_bias(place.astype(jnp.int32), cols, pair_bias)
    cross = rows[:, :channels] * every[:, channels : 2 * channels]
    cross = cross + every[:, :channels] * rows[:, channels:]
    pair_out = (0.5 * (mine + mirror + cross) + bias).astype(jnp.bfloat16)[None]
    return (seq_out, pair_out)


def solution(mesh):
    names = SEQ + ("pair",)
    fine = Mesh(mesh.devices.reshape([SIZES[name] for name in names]), names)
    placed = (
        P(SEQ),
        P(),
        P(SEQ, "pair"),
        P(None, "pair"),
        P(None, "pair"),
        P(None, "pair"),
        P("pair", None),
        P(None, None, "pair"),
        P(None, "pair"),
        P(SEQ, None, "pair"),
    )
    return jax.shard_map(
        on_device,
        mesh=fine,
        in_specs=placed,
        out_specs=(P(SEQ, "pair"), P(SEQ, None, "pair")),
        check_vma=False,
    )
```

```python
import math

import jax
import jax.numpy as jnp
from jax import lax
from jax.experimental import pallas as pl
from jax.experimental.pallas import tpu as pltpu
from jax.sharding import Mesh
from jax.sharding import PartitionSpec as P

HQK = 128
HV = 192
KS_STEM = 15
KS_CONV = 5
STEM_POOL = 64
PAIR_POOL = 16
EDGES = (1, 2, 3, 4, 6, 8, 12, 16, 24, 32, 48, 64, 96, 128, 192, 256, 384)

SIZES = {"zl": 2, "y": 8, "xh": 2, "xl": 2, "core": 2, "pair": 4}
SEQ = ("zl", "y", "xh", "xl", "core")
SHARE = ("zl", "xl", "core")
SPREAD = ("xh", "xl", "core")
LINE = ("zl", "y")
N_SEQ = math.prod(SIZES[name] for name in SEQ)
N_SHARE = math.prod(SIZES[name] for name in SHARE)
N_PAIR = SIZES["pair"]

SIDE = 256
ROWS = 32
EXT = ROWS + 4
EXT_PAD = 40
VMEM = 48 * 1024 * 1024


def params(**kw):
    return pltpu.CompilerParams(vmem_limit_bytes=VMEM, **kw)


def whole(count):
    return [pl.BlockSpec(memory_space=pltpu.VMEM) for _ in range(count)]


def gelu(x):
    return 0.5 * x * (1.0 + jnp.tanh(math.sqrt(2.0 / math.pi) * (x + 0.044715 * (x * x * x))))


def stem_kernel(place_ref, codes_ref, weight_ref, out_ref):
    length = codes_ref.shape[1]
    codes = jnp.broadcast_to(codes_ref[...], (16, length))
    first = SIDE - 2 * STEM_POOL + KS_STEM // 2
    shifted = pltpu.roll(codes, length - first, 1, stride=1, stride_axis=0)
    shifted = shifted[:, : EXT * STEM_POOL]
    onehot = jnp.concatenate(
        [(shifted == base + 1).astype(jnp.float32) for base in range(4)], axis=0
    ).astype(jnp.bfloat16)
    weight = weight_ref[...]
    step = 6
    for at in range(0, EXT, step):
        part = onehot[:, at * STEM_POOL : (at + step) * STEM_POOL]
        hidden = lax.dot_general(
            part, weight, (((0,), (0,)), ((), ())), preferred_element_type=jnp.float32
        ).reshape(step, STEM_POOL, weight.shape[1])
        high = gelu(jnp.max(hidden, axis=1))
        low = gelu(jnp.min(hidden, axis=1))
        rows = jnp.maximum(high, low)
        index = place_ref[0] * ROWS - 2 + at + lax.broadcasted_iota(jnp.int32, rows.shape, 0)
        inside = (index >= 0) & (index < N_SEQ * ROWS)
        out_ref[at : at + step, :] = jnp.where(inside, rows, 0.0)
    out_ref[EXT:EXT_PAD, :] = jnp.zeros((EXT_PAD - EXT, weight.shape[1]), jnp.float32)


def stem(place, codes, weight):
    return pl.pallas_call(
        stem_kernel,
        out_shape=jax.ShapeDtypeStruct((EXT_PAD, weight.shape[1]), jnp.float32),
        in_specs=[pl.BlockSpec(memory_space=pltpu.SMEM)] + whole(2),
        out_specs=whole(1)[0],
        compiler_params=params(),
        cost_estimate=pl.CostEstimate(flops=40_000_000_000, bytes_accessed=200000, transcendentals=0),
    )(place, codes, weight)


def pack_kernel(weight_ref, out_ref, wide):
    taps, width = weight_ref.shape
    share = width // N_SHARE
    half = taps // 2
    even, odd = [], []
    for part in range(wide.shape[0]):
        lanes = weight_ref[:, part * HQK : (part + 1) * HQK]
        wide[part, :taps, :] = lanes.astype(jnp.float32)
        wide[part, taps:, :] = jnp.zeros((wide.shape[1] - taps, HQK), jnp.float32)
        even.append(wide[part, pl.ds(0, half + 1, stride=2), :])
        odd.append(wide[part, pl.ds(1, half + 1, stride=2), :])
    even, odd = jnp.concatenate(even, axis=1), jnp.concatenate(odd, axis=1)
    lane = lax.broadcasted_iota(jnp.int32, (half + 1, HQK), 1)
    blocks = []
    for index in range(N_SHARE):
        low = pltpu.roll(even, (width - index * share) % width, 1)[:, :HQK]
        high = pltpu.roll(odd, (width - index * share + share) % width, 1)[:, :HQK]
        block = jnp.where(lane < share, low, high).astype(jnp.bfloat16)
        blocks.append(block[:half, : 2 * share])
    for place in range(N_SEQ):
        at, index, base = place, 0, 1
        for name in reversed(SEQ):
            if name in SHARE:
                index, base = index + base * (at % SIZES[name]), base * SIZES[name]
            at = at // SIZES[name]
        out_ref[place] = blocks[index]


def pack(weight):
    taps, width = weight.shape
    return pl.pallas_call(
        pack_kernel,
        out_shape=jax.ShapeDtypeStruct((N_SEQ, taps // 2, 2 * width // N_SHARE), jnp.bfloat16),
        in_specs=whole(1),
        out_specs=whole(1)[0],
        scratch_shapes=[pltpu.VMEM((width // HQK, taps + 2, HQK), jnp.float32)],
        compiler_params=params(),
    )(weight)


def conv_kernel(section_ref, weight_ref, out_ref, wide, act):
    windows, _, channels = section_ref.shape
    half = channels // 2
    columns = out_ref.shape[2]
    wide[...] = section_ref[...].astype(jnp.float32)
    even, odd = None, None
    for tap in range(KS_CONV):
        rows = wide[:, tap : tap + ROWS, :].astype(jnp.bfloat16).reshape(windows * ROWS, channels)
        weight = weight_ref[tap * half : (tap + 1) * half, :]
        term = jnp.dot(rows[:, :half], weight, preferred_element_type=jnp.float32)
        even = term if even is None else even + term
        term = jnp.dot(rows[:, half:], weight, preferred_element_type=jnp.float32)
        odd = term if odd is None else odd + term
    act[...] = gelu(even[:, :columns] + odd[:, columns:])
    count = windows * ROWS // 2
    best = jnp.maximum(act[pl.ds(0, count, stride=2), :], act[pl.ds(1, count, stride=2), :])
    out_ref[...] = best.astype(jnp.bfloat16).reshape(out_ref.shape)


def conv(section, weight):
    windows, _, channels = section.shape
    columns = weight.shape[1] // 2
    return pl.pallas_call(
        conv_kernel,
        out_shape=jax.ShapeDtypeStruct((windows, ROWS // 2, columns), jnp.bfloat16),
        in_specs=whole(2),
        out_specs=whole(1)[0],
        scratch_shapes=[
            pltpu.VMEM((windows, EXT_PAD, channels), jnp.float32),
            pltpu.VMEM((windows * ROWS, columns), jnp.float32),
        ],
        compiler_params=params(),
    )(section, weight)


def attention_kernel(query_ref, kv_ref, out_ref):
    scale = 1.0 / math.sqrt(HQK)
    scores = (
        lax.dot_general(
            query_ref[...],
            kv_ref[:, :HQK],
            (((1,), (1,)), ((), ())),
            preferred_element_type=jnp.float32,
        )
        * scale
    )
    top = jnp.max(scores, axis=1, keepdims=True)
    expo = jnp.exp(scores - top)
    total = jnp.sum(expo, axis=1, keepdims=True)
    mixed = jnp.dot(expo.astype(jnp.bfloat16), kv_ref[:, HQK:], preferred_element_type=jnp.float32)
    lane = lax.broadcasted_iota(jnp.int32, mixed.shape, 1)
    mixed = jnp.where(lane == HV, top, jnp.where(lane == HV + 1, total, mixed))
    out_ref[...] = mixed.reshape(out_ref.shape)


def attention(query, kv, groups):
    count, width = query.shape[0] // groups, kv.shape[1] - HQK
    return pl.pallas_call(
        attention_kernel,
        out_shape=jax.ShapeDtypeStruct((groups, count, width), jnp.float32),
        in_specs=whole(2),
        out_specs=whole(1)[0],
        compiler_params=params(),
    )(query, kv)


def combine_kernel(parts_ref, w_out_ref, out_ref):
    parts = parts_ref[...]
    top = parts[:, :, HV : HV + 1]
    gain = jnp.exp(top - jnp.max(top, axis=0, keepdims=True))
    total = jnp.sum(gain * parts[:, :, HV + 1 : HV + 2], axis=0)
    mixed = (jnp.sum(gain * parts, axis=0) / total)[:, :HV].astype(jnp.bfloat16)
    term = jnp.dot(mixed, w_out_ref[...], preferred_element_type=jnp.float32)
    mean = jnp.sum(term, axis=0, keepdims=True) * (1.0 / PAIR_POOL)
    width = term.shape[1] // N_PAIR
    count = term.shape[0]
    tail = jnp.concatenate(
        [mean[:, c * width : (c + 1) * width] for c in range(N_PAIR)]
        + [jnp.zeros((4, width), jnp.float32)],
        axis=0,
    )
    for c in range(N_PAIR):
        out_ref[c, :count, :] = term[:, c * width : (c + 1) * width]
        out_ref[c, count : count + 8, :] = tail


def combine(parts, w_out):
    count = parts.shape[1]
    width = w_out.shape[1] // N_PAIR
    return pl.pallas_call(
        combine_kernel,
        out_shape=jax.ShapeDtypeStruct((N_PAIR, count + 8, width), jnp.float32),
        in_specs=whole(2),
        out_specs=whole(1)[0],
        compiler_params=params(),
    )(parts, w_out)


def close_kernel(terms_ref, own_ref, trunk_ref, w_pair_ref, pair_ref, seq_ref, rows_ref, every_ref):
    count, width = own_ref.shape
    total = terms_ref[0] + terms_ref[1] + terms_ref[2] + terms_ref[3]
    seq_ref[...] = (own_ref[...].astype(jnp.float32) + total[:count, :]).astype(jnp.bfloat16)
    trunk_mean = jnp.sum(trunk_ref[...].astype(jnp.float32), axis=0, keepdims=True) * (1.0 / PAIR_POOL)
    rows = None
    for c in range(N_PAIR):
        pooled = trunk_mean[:, c * width : (c + 1) * width] + total[count + c : count + c + 1, :]
        term = jnp.dot(
            jnp.broadcast_to(pooled, (8, width)).astype(jnp.bfloat16),
            w_pair_ref[c * width : (c + 1) * width, :],
            preferred_element_type=jnp.float32,
        )
        rows = term if rows is None else rows + term
    rows_ref[...] = rows
    mine = pair_ref[0].astype(jnp.float32)
    factors = jnp.broadcast_to(rows[:1], (mine.shape[0], rows.shape[1]))
    every_ref[...] = jnp.concatenate([factors, mine], axis=1)


def close(terms, own, trunk, w_pair, pair_in):
    return pl.pallas_call(
        close_kernel,
        out_shape=(
            jax.ShapeDtypeStruct(own.shape, jnp.bfloat16),
            jax.ShapeDtypeStruct((8, w_pair.shape[1]), jnp.float32),
            jax.ShapeDtypeStruct((pair_in.shape[1], w_pair.shape[1] + pair_in.shape[2]), jnp.float32),
        ),
        in_specs=whole(5),
        out_specs=tuple(whole(3)),
        compiler_params=params(),
    )(terms, own, trunk, w_pair, pair_in)


def distance_bias(row, cols, pair_bias):
    delta = jnp.abs(row - cols)
    bins = jnp.zeros(delta.shape, jnp.int32)
    for edge in EDGES:
        bins = bins + (delta >= edge).astype(jnp.int32)
    labels = jnp.arange(pair_bias.shape[0], dtype=jnp.int32)
    onehot = (bins[:, None] == labels[None, :]).astype(jnp.bfloat16)
    return jnp.dot(onehot, pair_bias, preferred_element_type=jnp.float32)


def exchange(blocks, axes):
    return lax.all_to_all(blocks, axes, split_axis=0, concat_axis=0, tiled=True)


def gather(rows, axes):
    count = math.prod(SIZES[name] for name in axes)
    blocks = jnp.broadcast_to(rows[None], (count,) + rows.shape)
    return exchange(blocks, axes).reshape(count * rows.shape[0], *rows.shape[1:])


def on_device(tokens, w_stem, w_conv, w_query, w_key, w_value, w_out, w_pair, pair_bias, pair_in):
    place = lax.axis_index(SEQ)
    pair_place = lax.axis_index("pair")

    taps, width = w_conv.shape
    share = width // N_SHARE
    blocks = exchange(pack(w_conv), SEQ)
    conv_weight = blocks.reshape(N_SEQ * blocks.shape[1], blocks.shape[2])

    codes = tokens + 1
    ends = N_SEQ - 1
    left = lax.ppermute(codes[-SIDE:], SEQ, [(i, i + 1) for i in range(ends)])
    right = lax.ppermute(codes[:SIDE], SEQ, [(i + 1, i) for i in range(ends)])
    codes = jnp.concatenate([left, codes, right])[None, :]
    source = jnp.arange(w_stem.shape[1]).reshape(2, -1)
    source = (2 * (source % source.shape[1]) + jnp.arange(2)[:, None]).reshape(-1)
    order = (jnp.arange(w_stem.shape[1])[:, None] == source[None, :]).astype(jnp.bfloat16)
    stem_weight = jnp.dot(w_stem, order, preferred_element_type=jnp.float32).astype(jnp.bfloat16)
    stem_weight = stem_weight.reshape(KS_STEM, 4, -1)[::-1].transpose(1, 0, 2)
    stem_weight = jnp.pad(stem_weight, ((0, 0), (0, 1), (0, 0))).reshape(64, -1)
    section = stem(place.astype(jnp.int32)[None], codes, stem_weight).astype(jnp.bfloat16)
    sections = lax.all_gather(section, SHARE, axis=0, tiled=False)

    parts = conv(sections, conv_weight)
    count = parts.shape[1]
    parts = jnp.broadcast_to(parts[:, None], (N_SHARE, N_PAIR, count, share))
    parts = exchange(parts.reshape(N_SHARE * N_PAIR, count, share), SHARE + ("pair",))
    trunk = parts.reshape(N_SHARE, N_PAIR, count, share).transpose(2, 1, 0, 3)
    trunk = trunk.reshape(count, N_PAIR * width)

    w_qkv = jnp.concatenate([w_query, w_key, w_value], axis=1)
    w_qkv = jnp.pad(w_qkv, ((0, 0), (0, 4 * HQK - w_qkv.shape[1])))
    qkv = jnp.dot(trunk, w_qkv, preferred_element_type=jnp.float32).astype(jnp.bfloat16)
    query = gather(qkv[:, :HQK], SPREAD)
    kv = gather(qkv[:, HQK:], LINE)
    parts = exchange(attention(query, kv, query.shape[0] // count), SPREAD)
    terms = exchange(combine(parts, w_out), ("pair",))

    own = lax.dynamic_slice_in_dim(trunk, pair_place * width, width, 1)
    factors = jnp.concatenate([w_pair[0], w_pair[1]], axis=1)
    seq_out, rows, every = close(terms, own, trunk, factors, pair_in)
    channels = pair_in.shape[2]
    mine = pair_in[0].astype(jnp.float32)
    rows = rows[:1]
    every = exchange(every[:, None], SEQ)[:, 0]
    mirror = every[:, 2 * channels :]

    cols = jnp.arange(N_SEQ, dtype=jnp.int32)
    bias = distance_bias(place.astype(jnp.int32), cols, pair_bias)
    cross = rows[:, :channels] * every[:, channels : 2 * channels]
    cross = cross + every[:, :channels] * rows[:, channels:]
    pair_out = (0.5 * (mine + mirror + cross) + bias).astype(jnp.bfloat16)[None]
    return (seq_out, pair_out)


def solution(mesh):
    names = SEQ + ("pair",)
    fine = Mesh(mesh.devices.reshape([SIZES[name] for name in names]), names)
    placed = (
        P(SEQ),
        P(),
        P(SEQ, "pair"),
        P(None, "pair"),
        P(None, "pair"),
        P(None, "pair"),
        P("pair", None),
        P(None, None, "pair"),
        P(None, "pair"),
        P(SEQ, None, "pair"),
    )
    return jax.shard_map(
        on_device,
        mesh=fine,
        in_specs=placed,
        out_specs=(P(SEQ, "pair"), P(SEQ, None, "pair")),
        check_vma=False,
    )
```

```python
import math

import jax
import jax.numpy as jnp
from jax import lax
from jax.experimental import pallas as pl
from jax.experimental.pallas import tpu as pltpu
from jax.sharding import Mesh
from jax.sharding import PartitionSpec as P

HQK = 128
HV = 192
KS_STEM = 15
KS_CONV = 5
STEM_POOL = 64
PAIR_POOL = 16
EDGES = (1, 2, 3, 4, 6, 8, 12, 16, 24, 32, 48, 64, 96, 128, 192, 256, 384)

SIZES = {"zl": 2, "y": 8, "xh": 2, "xl": 2, "core": 2, "pair": 4}
SEQ = ("zl", "y", "xh", "xl", "core")
SHARE = ("zl", "xl", "core")
SPREAD = ("zl", "xl", "core")
LINE = ("y", "xh")
N_SEQ = math.prod(SIZES[name] for name in SEQ)
N_SHARE = math.prod(SIZES[name] for name in SHARE)
N_PAIR = SIZES["pair"]
N_SPREAD = math.prod(SIZES[name] for name in SPREAD)
N_LINE = math.prod(SIZES[name] for name in LINE)

SIDE = 256
ROWS = 32
EXT = ROWS + 4
EXT_PAD = 40
VMEM = 48 * 1024 * 1024


def params(**kw):
    return pltpu.CompilerParams(vmem_limit_bytes=VMEM, **kw)


def whole(count):
    return [pl.BlockSpec(memory_space=pltpu.VMEM) for _ in range(count)]


def gelu(x):
    return 0.5 * x * (1.0 + jnp.tanh(math.sqrt(2.0 / math.pi) * (x + 0.044715 * (x * x * x))))


def stem_kernel(place_ref, codes_ref, weight_ref, out_ref):
    length = codes_ref.shape[1]
    codes = jnp.broadcast_to(codes_ref[...], (16, length))
    first = SIDE - 2 * STEM_POOL + KS_STEM // 2
    shifted = pltpu.roll(codes, length - first, 1, stride=1, stride_axis=0)
    shifted = shifted[:, : EXT * STEM_POOL]
    onehot = jnp.concatenate(
        [(shifted == base + 1).astype(jnp.float32) for base in range(4)], axis=0
    ).astype(jnp.bfloat16)
    weight = weight_ref[...]
    step = 6
    for at in range(0, EXT, step):
        part = onehot[:, at * STEM_POOL : (at + step) * STEM_POOL]
        hidden = lax.dot_general(
            part, weight, (((0,), (0,)), ((), ())), preferred_element_type=jnp.float32
        ).reshape(step, STEM_POOL, weight.shape[1])
        high = gelu(jnp.max(hidden, axis=1))
        low = gelu(jnp.min(hidden, axis=1))
        rows = jnp.maximum(high, low)
        index = place_ref[0] * ROWS - 2 + at + lax.broadcasted_iota(jnp.int32, rows.shape, 0)
        inside = (index >= 0) & (index < N_SEQ * ROWS)
        out_ref[at : at + step, :] = jnp.where(inside, rows, 0.0)
    out_ref[EXT:EXT_PAD, :] = jnp.zeros((EXT_PAD - EXT, weight.shape[1]), jnp.float32)


def stem(place, codes, weight):
    return pl.pallas_call(
        stem_kernel,
        out_shape=jax.ShapeDtypeStruct((EXT_PAD, weight.shape[1]), jnp.float32),
        in_specs=[pl.BlockSpec(memory_space=pltpu.SMEM)] + whole(2),
        out_specs=whole(1)[0],
        compiler_params=params(),
        cost_estimate=pl.CostEstimate(flops=40_000_000_000, bytes_accessed=200000, transcendentals=0),
    )(place, codes, weight)


def pack_kernel(weight_ref, out_ref, wide):
    taps, width = weight_ref.shape
    share = width // N_SHARE
    half = taps // 2
    even, odd = [], []
    for part in range(wide.shape[0]):
        lanes = weight_ref[:, part * HQK : (part + 1) * HQK]
        wide[part, :taps, :] = lanes.astype(jnp.float32)
        wide[part, taps:, :] = jnp.zeros((wide.shape[1] - taps, HQK), jnp.float32)
        even.append(wide[part, pl.ds(0, half + 1, stride=2), :])
        odd.append(wide[part, pl.ds(1, half + 1, stride=2), :])
    even, odd = jnp.concatenate(even, axis=1), jnp.concatenate(odd, axis=1)
    lane = lax.broadcasted_iota(jnp.int32, (half + 1, HQK), 1)
    blocks = []
    for index in range(N_SHARE):
        low = pltpu.roll(even, (width - index * share) % width, 1)[:, :HQK]
        high = pltpu.roll(odd, (width - index * share + share) % width, 1)[:, :HQK]
        block = jnp.where(lane < share, low, high).astype(jnp.bfloat16)
        blocks.append(block[:half, : 2 * share])
    for place in range(N_SEQ):
        at, index, base = place, 0, 1
        for name in reversed(SEQ):
            if name in SHARE:
                index, base = index + base * (at % SIZES[name]), base * SIZES[name]
            at = at // SIZES[name]
        out_ref[place] = blocks[index]


def pack(weight):
    taps, width = weight.shape
    return pl.pallas_call(
        pack_kernel,
        out_shape=jax.ShapeDtypeStruct((N_SEQ, taps // 2, 2 * width // N_SHARE), jnp.bfloat16),
        in_specs=whole(1),
        out_specs=whole(1)[0],
        scratch_shapes=[pltpu.VMEM((width // HQK, taps + 2, HQK), jnp.float32)],
        compiler_params=params(),
    )(weight)


def conv_kernel(section_ref, weight_ref, out_ref, wide, act, best):
    windows, _, channels = section_ref.shape
    half = channels // 2
    columns = out_ref.shape[2] // 8
    wide[...] = section_ref[...].astype(jnp.float32)
    even, odd = None, None
    for tap in range(KS_CONV):
        rows = wide[:, tap : tap + ROWS, :].astype(jnp.bfloat16).reshape(windows * ROWS, channels)
        weight = weight_ref[tap * half : (tap + 1) * half, :]
        term = jnp.dot(rows[:, :half], weight, preferred_element_type=jnp.float32)
        even = term if even is None else even + term
        term = jnp.dot(rows[:, half:], weight, preferred_element_type=jnp.float32)
        odd = term if odd is None else odd + term
    act[...] = jnp.zeros(act.shape, jnp.float32)
    act[:, :columns] = gelu(even[:, :columns] + odd[:, columns:])
    count = windows * ROWS // 2
    best[...] = jnp.maximum(act[pl.ds(0, count, stride=2), :], act[pl.ds(1, count, stride=2), :])
    flat = None
    for index in range(8):
        part = best[pl.ds(index, count // 8, stride=8), :]
        part = jnp.pad(part, ((0, 0), (0, 8 * columns - part.shape[1])))
        part = pltpu.roll(part, index * columns, 1)
        flat = part if flat is None else flat + part
    for window in range(windows):
        block = flat[2 * window : 2 * window + 2, :].astype(jnp.bfloat16)
        for index in range(N_PAIR):
            out_ref[window * N_PAIR + index] = block


def conv(section, weight):
    windows, _, channels = section.shape
    columns = weight.shape[1] // 2
    return pl.pallas_call(
        conv_kernel,
        out_shape=jax.ShapeDtypeStruct((windows * N_PAIR, 2, 8 * columns), jnp.bfloat16),
        in_specs=whole(2),
        out_specs=whole(1)[0],
        scratch_shapes=[
            pltpu.VMEM((windows, EXT_PAD, channels), jnp.float32),
            pltpu.VMEM((windows * ROWS, HQK), jnp.float32),
            pltpu.VMEM((windows * ROWS // 2, HQK), jnp.float32),
        ],
        compiler_params=params(),
    )(section, weight)


def project_kernel(trunk_ref, w_query_ref, w_key_ref, w_value_ref, query_ref, kv_ref):
    trunk = trunk_ref[...]
    query, key, value = [
        jnp.dot(trunk, ref[...], preferred_element_type=jnp.float32).astype(jnp.bfloat16)
        for ref in (w_query_ref, w_key_ref, w_value_ref)
    ]
    for index in range(N_SPREAD):
        query_ref[index] = query
    rest = jnp.zeros((trunk.shape[0], kv_ref.shape[2] - HQK - HV), jnp.bfloat16)
    for index in range(N_LINE):
        kv_ref[index, :, :HQK] = key
        kv_ref[index, :, HQK : HQK + HV] = value
        kv_ref[index, :, HQK + HV :] = rest


def project(trunk, w_query, w_key, w_value):
    count = trunk.shape[0]
    return pl.pallas_call(
        project_kernel,
        out_shape=(
            jax.ShapeDtypeStruct((N_SPREAD, count, HQK), jnp.bfloat16),
            jax.ShapeDtypeStruct((N_LINE, count, 3 * HQK), jnp.bfloat16),
        ),
        in_specs=whole(4),
        out_specs=tuple(whole(2)),
        compiler_params=params(),
    )(trunk, w_query, w_key, w_value)


def attention_kernel(query_ref, kv_ref, out_ref):
    scale = 1.0 / math.sqrt(HQK)
    scores = (
        lax.dot_general(
            query_ref[...],
            kv_ref[:, :HQK],
            (((1,), (1,)), ((), ())),
            preferred_element_type=jnp.float32,
        )
        * scale
    )
    top = jnp.max(scores, axis=1, keepdims=True)
    expo = jnp.exp(scores - top)
    total = jnp.sum(expo, axis=1, keepdims=True)
    mixed = jnp.dot(expo.astype(jnp.bfloat16), kv_ref[:, HQK:], preferred_element_type=jnp.float32)
    lane = lax.broadcasted_iota(jnp.int32, mixed.shape, 1)
    mixed = jnp.where(lane == HV, top, jnp.where(lane == HV + 1, total, mixed))
    out_ref[...] = mixed.reshape(out_ref.shape)


def attention(query, kv, groups):
    count, width = query.shape[0] // groups, kv.shape[1] - HQK
    return pl.pallas_call(
        attention_kernel,
        out_shape=jax.ShapeDtypeStruct((groups, count, width), jnp.float32),
        in_specs=whole(2),
        out_specs=whole(1)[0],
        compiler_params=params(),
    )(query, kv)


def combine_kernel(parts_ref, w_out_ref, out_ref):
    parts = parts_ref[...]
    top = parts[:, :, HV : HV + 1]
    gain = jnp.exp(top - jnp.max(top, axis=0, keepdims=True))
    total = jnp.sum(gain * parts[:, :, HV + 1 : HV + 2], axis=0)
    mixed = (jnp.sum(gain * parts, axis=0) / total)[:, :HV].astype(jnp.bfloat16)
    term = jnp.dot(mixed, w_out_ref[...], preferred_element_type=jnp.float32)
    mean = jnp.sum(term, axis=0, keepdims=True) * (1.0 / PAIR_POOL)
    width = term.shape[1] // N_PAIR
    count = term.shape[0]
    tail = jnp.concatenate(
        [mean[:, c * width : (c + 1) * width] for c in range(N_PAIR)]
        + [jnp.zeros((count - N_PAIR, width), jnp.float32)],
        axis=0,
    ).astype(jnp.bfloat16)
    for c in range(N_PAIR):
        out_ref[c, :count, :] = term[:, c * width : (c + 1) * width].astype(jnp.bfloat16)
        out_ref[c, count:, :] = tail


def combine(parts, w_out):
    count = parts.shape[1]
    width = w_out.shape[1] // N_PAIR
    return pl.pallas_call(
        combine_kernel,
        out_shape=jax.ShapeDtypeStruct((N_PAIR, 2 * count, width), jnp.bfloat16),
        in_specs=whole(2),
        out_specs=whole(1)[0],
        compiler_params=params(),
    )(parts, w_out)


def close_kernel(terms_ref, own_ref, trunk_ref, w_pair_ref, pair_ref, seq_ref, rows_ref, every_ref):
    count, width = own_ref.shape
    total = jnp.sum(terms_ref[...].astype(jnp.float32), axis=0)
    seq_ref[...] = (own_ref[...].astype(jnp.float32) + total[:count, :]).astype(jnp.bfloat16)
    trunk_mean = jnp.sum(trunk_ref[...].astype(jnp.float32), axis=0, keepdims=True) * (1.0 / PAIR_POOL)
    rows = None
    for c in range(N_PAIR):
        pooled = trunk_mean[:, c * width : (c + 1) * width] + total[count + c : count + c + 1, :]
        term = jnp.dot(
            jnp.broadcast_to(pooled, (8, width)).astype(jnp.bfloat16),
            w_pair_ref[c * width : (c + 1) * width, :],
            preferred_element_type=jnp.float32,
        )
        rows = term if rows is None else rows + term
    rows_ref[...] = rows
    mine = pair_ref[0].astype(jnp.float32)
    factors = jnp.broadcast_to(rows[:1], (mine.shape[0], rows.shape[1]))
    every_ref[...] = jnp.concatenate([factors, mine], axis=1)


def close(terms, own, trunk, w_pair, pair_in):
    return pl.pallas_call(
        close_kernel,
        out_shape=(
            jax.ShapeDtypeStruct(own.shape, jnp.bfloat16),
            jax.ShapeDtypeStruct((8, w_pair.shape[1]), jnp.float32),
            jax.ShapeDtypeStruct((pair_in.shape[1], w_pair.shape[1] + pair_in.shape[2]), jnp.float32),
        ),
        in_specs=whole(5),
        out_specs=tuple(whole(3)),
        compiler_params=params(),
    )(terms, own, trunk, w_pair, pair_in)


def distance_bias(row, cols, pair_bias):
    delta = jnp.abs(row - cols)
    bins = jnp.zeros(delta.shape, jnp.int32)
    for edge in EDGES:
        bins = bins + (delta >= edge).astype(jnp.int32)
    labels = jnp.arange(pair_bias.shape[0], dtype=jnp.int32)
    onehot = (bins[:, None] == labels[None, :]).astype(jnp.bfloat16)
    return jnp.dot(onehot, pair_bias, preferred_element_type=jnp.float32)


def exchange(blocks, axes):
    return lax.all_to_all(blocks, axes, split_axis=0, concat_axis=0, tiled=True)


def on_device(tokens, w_stem, w_conv, w_query, w_key, w_value, w_out, w_pair, pair_bias, pair_in):
    place = lax.axis_index(SEQ)
    pair_place = lax.axis_index("pair")

    taps, width = w_conv.shape
    share = width // N_SHARE
    blocks = exchange(pack(w_conv), SEQ)
    conv_weight = blocks.reshape(N_SEQ * blocks.shape[1], blocks.shape[2])

    codes = tokens + 1
    ends = N_SEQ - 1
    left = lax.ppermute(codes[-SIDE:], SEQ, [(i, i + 1) for i in range(ends)])
    right = lax.ppermute(codes[:SIDE], SEQ, [(i + 1, i) for i in range(ends)])
    codes = jnp.concatenate([left, codes, right])[None, :]
    source = jnp.arange(w_stem.shape[1]).reshape(2, -1)
    source = (2 * (source % source.shape[1]) + jnp.arange(2)[:, None]).reshape(-1)
    order = (jnp.arange(w_stem.shape[1])[:, None] == source[None, :]).astype(jnp.bfloat16)
    stem_weight = jnp.dot(w_stem, order, preferred_element_type=jnp.float32).astype(jnp.bfloat16)
    stem_weight = stem_weight.reshape(KS_STEM, 4, -1)[::-1].transpose(1, 0, 2)
    stem_weight = jnp.pad(stem_weight, ((0, 0), (0, 1), (0, 0))).reshape(64, -1)
    section = stem(place.astype(jnp.int32)[None], codes, stem_weight).astype(jnp.bfloat16)
    sections = lax.all_gather(section, SHARE, axis=0, tiled=False)

    parts = exchange(conv(sections, conv_weight), SHARE + ("pair",))
    count = ROWS // 2
    trunk = parts.reshape(N_SHARE, N_PAIR, count, share).transpose(2, 1, 0, 3)
    trunk = trunk.reshape(count, N_PAIR * width)

    query, kv = project(trunk, w_query, w_key, w_value)
    query = exchange(query, SPREAD).reshape(N_SPREAD * count, HQK)
    kv = exchange(kv, LINE).reshape(N_LINE * count, kv.shape[2])
    parts = exchange(attention(query, kv, N_SPREAD), SPREAD)
    terms = exchange(combine(parts, w_out), ("pair",))

    own = lax.dynamic_slice_in_dim(trunk, pair_place * width, width, 1)
    factors = jnp.concatenate([w_pair[0], w_pair[1]], axis=1)
    seq_out, rows, every = close(terms, own, trunk, factors, pair_in)
    channels = pair_in.shape[2]
    mine = pair_in[0].astype(jnp.float32)
    rows = rows[:1]
    every = exchange(every[:, None], SEQ)[:, 0]
    mirror = every[:, 2 * channels :]

    cols = jnp.arange(N_SEQ, dtype=jnp.int32)
    bias = distance_bias(place.astype(jnp.int32), cols, pair_bias)
    cross = rows[:, :channels] * every[:, channels : 2 * channels]
    cross = cross + every[:, :channels] * rows[:, channels:]
    pair_out = (0.5 * (mine + mirror + cross) + bias).astype(jnp.bfloat16)[None]
    return (seq_out, pair_out)


def solution(mesh):
    names = SEQ + ("pair",)
    fine = Mesh(mesh.devices.reshape([SIZES[name] for name in names]), names)
    placed = (
        P(SEQ),
        P(),
        P(SEQ, "pair"),
        P(None, "pair"),
        P(None, "pair"),
        P(None, "pair"),
        P("pair", None),
        P(None, None, "pair"),
        P(None, "pair"),
        P(SEQ, None, "pair"),
    )
    return jax.shard_map(
        on_device,
        mesh=fine,
        in_specs=placed,
        out_specs=(P(SEQ, "pair"), P(SEQ, None, "pair")),
        check_vma=False,
    )
```

```python
import math

import jax
import jax.numpy as jnp
import numpy as np
from jax import lax
from jax.experimental import pallas as pl
from jax.experimental.pallas import tpu as pltpu
from jax.sharding import Mesh
from jax.sharding import PartitionSpec as P

HQK = 128
HV = 192
KS_STEM = 15
KS_CONV = 5
STEM_POOL = 64
PAIR_POOL = 16
EDGES = (1, 2, 3, 4, 6, 8, 12, 16, 24, 32, 48, 64, 96, 128, 192, 256, 384)

SIZES = {"zl": 2, "y": 8, "xh": 2, "xl": 2, "core": 2, "pair": 4}
SEQ = ("zl", "y", "xh", "xl", "core")
SHARE = ("zl", "xl", "core")
SPREAD = ("xh", "xl", "core")
LINE = ("zl", "y")
N_SEQ = math.prod(SIZES[name] for name in SEQ)
N_SHARE = math.prod(SIZES[name] for name in SHARE)
N_PAIR = SIZES["pair"]
N_SPREAD = math.prod(SIZES[name] for name in SPREAD)
N_LINE = math.prod(SIZES[name] for name in LINE)

SIDE = 256
ROWS = 32
EXT = ROWS + 4
EXT_PAD = 40
VMEM = 48 * 1024 * 1024


def params(**kw):
    return pltpu.CompilerParams(vmem_limit_bytes=VMEM, **kw)


def whole(count):
    return [pl.BlockSpec(memory_space=pltpu.VMEM) for _ in range(count)]


def gelu(x):
    return 0.5 * x * (1.0 + jnp.tanh(math.sqrt(2.0 / math.pi) * (x + 0.044715 * (x * x * x))))


def stem_kernel(place_ref, codes_ref, weight_ref, order_ref, out_ref):
    length = codes_ref.shape[1]
    codes = jnp.broadcast_to(codes_ref[...], (16, length))
    first = SIDE - 2 * STEM_POOL + KS_STEM // 2
    shifted = pltpu.roll(codes, length - first, 1, stride=1, stride_axis=0)
    shifted = shifted[:, : EXT * STEM_POOL]
    onehot = jnp.concatenate(
        [(shifted == base + 1).astype(jnp.float32) for base in range(4)], axis=0
    ).astype(jnp.bfloat16)
    taps = weight_ref.shape[0]
    row = lax.broadcasted_iota(jnp.int32, (64, taps), 0)
    column = lax.broadcasted_iota(jnp.int32, (64, taps), 1)
    picked = (column == (KS_STEM - 1 - row % 16) * 4 + row // 16) & (row % 16 < KS_STEM)
    picked = picked.astype(jnp.float32).astype(jnp.bfloat16)
    weight = jnp.dot(picked, weight_ref[...], preferred_element_type=jnp.float32)
    weight = jnp.dot(weight.astype(jnp.bfloat16), order_ref[...], preferred_element_type=jnp.float32)
    weight = weight.astype(jnp.bfloat16)
    step = 6
    for at in range(0, EXT, step):
        part = onehot[:, at * STEM_POOL : (at + step) * STEM_POOL]
        hidden = lax.dot_general(
            part, weight, (((0,), (0,)), ((), ())), preferred_element_type=jnp.float32
        ).reshape(step, STEM_POOL, weight.shape[1])
        high = gelu(jnp.max(hidden, axis=1))
        low = gelu(jnp.min(hidden, axis=1))
        rows = jnp.maximum(high, low)
        index = place_ref[0] * ROWS - 2 + at + lax.broadcasted_iota(jnp.int32, rows.shape, 0)
        inside = (index >= 0) & (index < N_SEQ * ROWS)
        out_ref[at : at + step, :] = jnp.where(inside, rows, 0.0)
    out_ref[EXT:EXT_PAD, :] = jnp.zeros((EXT_PAD - EXT, weight.shape[1]), jnp.float32)


def stem(place, codes, weight, order):
    return pl.pallas_call(
        stem_kernel,
        out_shape=jax.ShapeDtypeStruct((EXT_PAD, weight.shape[1]), jnp.float32),
        in_specs=[pl.BlockSpec(memory_space=pltpu.SMEM)] + whole(3),
        out_specs=whole(1)[0],
        compiler_params=params(),
        cost_estimate=pl.CostEstimate(flops=40_000_000_000, bytes_accessed=200000, transcendentals=0),
    )(place, codes, weight, order)


def start_kernel(weight_ref, tokens_ref, out_ref, codes_ref, head_ref, tail_ref, wide):
    codes = tokens_ref[...] + 1
    codes_ref[...] = codes
    head_ref[...] = codes[: head_ref.shape[0]]
    tail_ref[...] = codes[codes.shape[0] - tail_ref.shape[0] :]
    taps, width = weight_ref.shape
    share = width // N_SHARE
    half = taps // 2
    even, odd = [], []
    for part in range(wide.shape[0]):
        lanes = weight_ref[:, part * HQK : (part + 1) * HQK]
        wide[part, :taps, :] = lanes.astype(jnp.float32)
        wide[part, taps:, :] = jnp.zeros((wide.shape[1] - taps, HQK), jnp.float32)
        even.append(wide[part, pl.ds(0, half + 1, stride=2), :])
        odd.append(wide[part, pl.ds(1, half + 1, stride=2), :])
    even, odd = jnp.concatenate(even, axis=1), jnp.concatenate(odd, axis=1)
    lane = lax.broadcasted_iota(jnp.int32, (half + 1, HQK), 1)
    blocks = []
    for index in range(N_SHARE):
        low = pltpu.roll(even, (width - index * share) % width, 1)[:, :HQK]
        high = pltpu.roll(odd, (width - index * share + share) % width, 1)[:, :HQK]
        block = jnp.where(lane < share, low, high).astype(jnp.bfloat16)
        blocks.append(block[:half, : 2 * share])
    for place in range(N_SEQ):
        at, index, base = place, 0, 1
        for name in reversed(SEQ):
            if name in SHARE:
                index, base = index + base * (at % SIZES[name]), base * SIZES[name]
            at = at // SIZES[name]
        out_ref[place] = blocks[index]


def start(weight, tokens):
    taps, width = weight.shape
    ends = jax.ShapeDtypeStruct((SIDE // HQK, HQK), jnp.int32)
    return pl.pallas_call(
        start_kernel,
        out_shape=(
            jax.ShapeDtypeStruct((N_SEQ, taps // 2, 2 * width // N_SHARE), jnp.bfloat16),
            jax.ShapeDtypeStruct(tokens.shape, jnp.int32),
            ends,
            ends,
        ),
        in_specs=whole(2),
        out_specs=tuple(whole(4)),
        scratch_shapes=[pltpu.VMEM((width // HQK, taps + 2, HQK), jnp.float32)],
        compiler_params=params(),
    )(weight, tokens)


def conv_kernel(section_ref, weight_ref, out_ref, wide, act, best):
    windows, _, channels = section_ref.shape
    half = channels // 2
    columns = out_ref.shape[2] // 8
    wide[...] = section_ref[...].astype(jnp.float32)
    even, odd = None, None
    for tap in range(KS_CONV):
        rows = wide[:, tap : tap + ROWS, :].astype(jnp.bfloat16).reshape(windows * ROWS, channels)
        weight = weight_ref[tap * half : (tap + 1) * half, :]
        term = jnp.dot(rows[:, :half], weight, preferred_element_type=jnp.float32)
        even = term if even is None else even + term
        term = jnp.dot(rows[:, half:], weight, preferred_element_type=jnp.float32)
        odd = term if odd is None else odd + term
    act[...] = jnp.zeros(act.shape, jnp.float32)
    act[:, :columns] = gelu(even[:, :columns] + odd[:, columns:])
    count = windows * ROWS // 2
    best[...] = jnp.maximum(act[pl.ds(0, count, stride=2), :], act[pl.ds(1, count, stride=2), :])
    flat = None
    for index in range(8):
        part = best[pl.ds(index, count // 8, stride=8), :]
        part = jnp.pad(part, ((0, 0), (0, 8 * columns - part.shape[1])))
        part = pltpu.roll(part, index * columns, 1)
        flat = part if flat is None else flat + part
    for window in range(windows):
        block = flat[2 * window : 2 * window + 2, :].astype(jnp.bfloat16)
        for index in range(N_PAIR):
            out_ref[window * N_PAIR + index] = block


def conv(section, weight):
    windows, _, channels = section.shape
    columns = weight.shape[1] // 2
    return pl.pallas_call(
        conv_kernel,
        out_shape=jax.ShapeDtypeStruct((windows * N_PAIR, 2, 8 * columns), jnp.bfloat16),
        in_specs=whole(2),
        out_specs=whole(1)[0],
        scratch_shapes=[
            pltpu.VMEM((windows, EXT_PAD, channels), jnp.float32),
            pltpu.VMEM((windows * ROWS, HQK), jnp.float32),
            pltpu.VMEM((windows * ROWS // 2, HQK), jnp.float32),
        ],
        compiler_params=params(),
    )(section, weight)


def project_kernel(trunk_ref, w_query_ref, w_key_ref, w_value_ref, query_ref, kv_ref):
    trunk = trunk_ref[...]
    query, key, value = [
        jnp.dot(trunk, ref[...], preferred_element_type=jnp.float32).astype(jnp.bfloat16)
        for ref in (w_query_ref, w_key_ref, w_value_ref)
    ]
    query_ref[...] = query
    rest = jnp.zeros((trunk.shape[0], kv_ref.shape[2] - HQK - HV), jnp.bfloat16)
    for index in range(N_LINE):
        kv_ref[index, :, :HQK] = key
        kv_ref[index, :, HQK : HQK + HV] = value
        kv_ref[index, :, HQK + HV :] = rest


def project(trunk, w_query, w_key, w_value):
    count = trunk.shape[0]
    return pl.pallas_call(
        project_kernel,
        out_shape=(
            jax.ShapeDtypeStruct((count, HQK), jnp.bfloat16),
            jax.ShapeDtypeStruct((N_LINE, count, 3 * HQK), jnp.bfloat16),
        ),
        in_specs=whole(4),
        out_specs=tuple(whole(2)),
        compiler_params=params(),
    )(trunk, w_query, w_key, w_value)


def attention_kernel(place_ref, query_ref, kv_ref, out_ref):
    scale = 1.0 / math.sqrt(HQK)
    scores = (
        lax.dot_general(
            query_ref[...],
            kv_ref[:, :HQK],
            (((1,), (1,)), ((), ())),
            preferred_element_type=jnp.float32,
        )
        * scale
    )
    top = jnp.max(scores, axis=1, keepdims=True)
    expo = jnp.exp(scores - top)
    total = jnp.sum(expo, axis=1, keepdims=True)
    mixed = jnp.dot(expo.astype(jnp.bfloat16), kv_ref[:, HQK:], preferred_element_type=jnp.float32)
    lane = lax.broadcasted_iota(jnp.int32, mixed.shape, 1)
    mixed = jnp.where(lane == HV, top, jnp.where(lane == HV + 1, total, mixed))
    groups, count, _ = out_ref.shape
    for index in range(groups):
        out_ref[place_ref[0] ^ index] = mixed[index * count : (index + 1) * count, :]


def attention(place, query, kv):
    groups = N_SPREAD
    count, width = query.shape[0] // groups, kv.shape[1] - HQK
    return pl.pallas_call(
        attention_kernel,
        out_shape=jax.ShapeDtypeStruct((groups, count, width), jnp.float32),
        in_specs=[pl.BlockSpec(memory_space=pltpu.SMEM)] + whole(2),
        out_specs=whole(1)[0],
        compiler_params=params(),
    )(place, query, kv)


def combine_kernel(parts_ref, w_out_ref, out_ref):
    parts = parts_ref[...]
    top = parts[:, :, HV : HV + 1]
    gain = jnp.exp(top - jnp.max(top, axis=0, keepdims=True))
    total = jnp.sum(gain * parts[:, :, HV + 1 : HV + 2], axis=0)
    mixed = (jnp.sum(gain * parts, axis=0) / total)[:, :HV].astype(jnp.bfloat16)
    term = jnp.dot(mixed, w_out_ref[...], preferred_element_type=jnp.float32)
    mean = jnp.sum(term, axis=0, keepdims=True) * (1.0 / PAIR_POOL)
    width = term.shape[1] // N_PAIR
    count = term.shape[0]
    tail = jnp.concatenate(
        [mean[:, c * width : (c + 1) * width] for c in range(N_PAIR)]
        + [jnp.zeros((8 - N_PAIR, width), jnp.float32)],
        axis=0,
    )
    for c in range(N_PAIR):
        out_ref[c, :count, :] = term[:, c * width : (c + 1) * width]
        out_ref[c, count:, :] = tail


def combine(parts, w_out):
    count = parts.shape[1]
    width = w_out.shape[1] // N_PAIR
    return pl.pallas_call(
        combine_kernel,
        out_shape=jax.ShapeDtypeStruct((N_PAIR, count + 8, width), jnp.float32),
        in_specs=whole(2),
        out_specs=whole(1)[0],
        compiler_params=params(),
    )(parts, w_out)


def close_kernel(terms_ref, own_ref, trunk_ref, w_pair_ref, pair_ref, seq_ref, rows_ref, every_ref):
    count, width = own_ref.shape
    total = jnp.sum(terms_ref[...], axis=0)
    seq_ref[...] = (own_ref[...].astype(jnp.float32) + total[:count, :]).astype(jnp.bfloat16)
    trunk_mean = jnp.sum(trunk_ref[...].astype(jnp.float32), axis=0, keepdims=True) * (1.0 / PAIR_POOL)
    rows = None
    for c in range(N_PAIR):
        pooled = trunk_mean[:, c * width : (c + 1) * width] + total[count + c : count + c + 1, :]
        term = jnp.dot(
            jnp.broadcast_to(pooled, (8, width)).astype(jnp.bfloat16),
            w_pair_ref[c * width : (c + 1) * width, :],
            preferred_element_type=jnp.float32,
        )
        rows = term if rows is None else rows + term
    rows_ref[...] = rows
    mine = pair_ref[0].astype(jnp.float32)
    factors = jnp.broadcast_to(rows[:1], (mine.shape[0], rows.shape[1]))
    every_ref[...] = jnp.concatenate([factors, mine], axis=1)


def close(terms, own, trunk, w_pair, pair_in):
    return pl.pallas_call(
        close_kernel,
        out_shape=(
            jax.ShapeDtypeStruct(own.shape, jnp.bfloat16),
            jax.ShapeDtypeStruct((8, w_pair.shape[1]), jnp.float32),
            jax.ShapeDtypeStruct((pair_in.shape[1], w_pair.shape[1] + pair_in.shape[2]), jnp.float32),
        ),
        in_specs=whole(5),
        out_specs=tuple(whole(3)),
        compiler_params=params(),
    )(terms, own, trunk, w_pair, pair_in)


def distance_bias(row, cols, pair_bias):
    delta = jnp.abs(row - cols)
    bins = jnp.zeros(delta.shape, jnp.int32)
    for edge in EDGES:
        bins = bins + (delta >= edge).astype(jnp.int32)
    labels = jnp.arange(pair_bias.shape[0], dtype=jnp.int32)
    onehot = (bins[:, None] == labels[None, :]).astype(jnp.bfloat16)
    return jnp.dot(onehot, pair_bias, preferred_element_type=jnp.float32)


def exchange(blocks, axes):
    return lax.all_to_all(blocks, axes, split_axis=0, concat_axis=0, tiled=True)


def on_device(tokens, w_stem, w_conv, w_query, w_key, w_value, w_out, w_pair, pair_bias, pair_in):
    place = lax.axis_index(SEQ)
    pair_place = lax.axis_index("pair")

    taps, width = w_conv.shape
    share = width // N_SHARE
    blocks, codes, head, tail = start(w_conv, tokens.reshape(-1, HQK))
    blocks = exchange(blocks, SEQ)
    conv_weight = blocks.reshape(N_SEQ * blocks.shape[1], blocks.shape[2])

    ends = N_SEQ - 1
    left = lax.ppermute(tail, SEQ, [(i, i + 1) for i in range(ends)])
    right = lax.ppermute(head, SEQ, [(i + 1, i) for i in range(ends)])
    codes = jnp.concatenate([left, codes, right]).reshape(1, -1)
    half = w_stem.shape[1] // 2
    order = np.zeros((2 * half, 2 * half), np.float32)
    order[2 * np.arange(half), np.arange(half)] = 1
    order[2 * np.arange(half) + 1, half + np.arange(half)] = 1
    order = jnp.asarray(order, jnp.bfloat16)
    section = stem(place.astype(jnp.int32)[None], codes, w_stem, order).astype(jnp.bfloat16)
    sections = lax.all_gather(section, SHARE, axis=0, tiled=False)

    parts = exchange(conv(sections, conv_weight), SHARE + ("pair",))
    count = ROWS // 2
    trunk = parts.reshape(N_SHARE, N_PAIR, count, share).transpose(2, 1, 0, 3)
    trunk = trunk.reshape(count, N_PAIR * width)

    query, kv = project(trunk, w_query, w_key, w_value)
    for name in reversed(SPREAD):
        other = lax.ppermute(query, name, [(0, 1), (1, 0)])
        query = jnp.concatenate([query, other], axis=0)
    kv = exchange(kv, LINE).reshape(N_LINE * count, kv.shape[2])
    spread = lax.axis_index(SPREAD).astype(jnp.int32)[None]
    parts = exchange(attention(spread, query, kv), SPREAD)
    terms = exchange(combine(parts, w_out), ("pair",))

    own = lax.dynamic_slice_in_dim(trunk, pair_place * width, width, 1)
    factors = jnp.concatenate([w_pair[0], w_pair[1]], axis=1)
    seq_out, rows, every = close(terms, own, trunk, factors, pair_in)
    channels = pair_in.shape[2]
    mine = pair_in[0].astype(jnp.float32)
    rows = rows[:1]
    every = exchange(every[:, None], SEQ)[:, 0]
    mirror = every[:, 2 * channels :]

    cols = jnp.arange(N_SEQ, dtype=jnp.int32)
    bias = distance_bias(place.astype(jnp.int32), cols, pair_bias)
    cross = rows[:, :channels] * every[:, channels : 2 * channels]
    cross = cross + every[:, :channels] * rows[:, channels:]
    pair_out = (0.5 * (mine + mirror + cross) + bias).astype(jnp.bfloat16)[None]
    return (seq_out, pair_out)


def solution(mesh):
    names = SEQ + ("pair",)
    fine = Mesh(mesh.devices.reshape([SIZES[name] for name in names]), names)
    placed = (
        P(SEQ),
        P(),
        P(SEQ, "pair"),
        P(None, "pair"),
        P(None, "pair"),
        P(None, "pair"),
        P("pair", None),
        P(None, None, "pair"),
        P(None, "pair"),
        P(SEQ, None, "pair"),
    )
    return jax.shard_map(
        on_device,
        mesh=fine,
        in_specs=placed,
        out_specs=(P(SEQ, "pair"), P(SEQ, None, "pair")),
        check_vma=False,
    )
```

```python
import math

import jax
import jax.numpy as jnp
from jax import lax
from jax.experimental import pallas as pl
from jax.experimental.pallas import tpu as pltpu
from jax.sharding import Mesh
from jax.sharding import PartitionSpec as P

HQK = 128
HV = 192
KS_STEM = 15
KS_CONV = 5
STEM_POOL = 64
PAIR_POOL = 16
EDGES = (1, 2, 3, 4, 6, 8, 12, 16, 24, 32, 48, 64, 96, 128, 192, 256, 384)

SIZES = {"zl": 2, "y": 8, "xh": 2, "xl": 2, "core": 2, "pair": 4}
SEQ = ("zl", "y", "xh", "xl", "core")
SHARE = ("zl", "xl", "core")
SPREAD = ("xh", "xl", "core")
LINE = ("zl", "y")
N_SEQ = math.prod(SIZES[name] for name in SEQ)
N_SHARE = math.prod(SIZES[name] for name in SHARE)
N_PAIR = SIZES["pair"]
N_SPREAD = math.prod(SIZES[name] for name in SPREAD)
N_LINE = math.prod(SIZES[name] for name in LINE)

SIDE = 256
ROWS = 32
EXT = ROWS + 4
EXT_PAD = 40
VMEM = 48 * 1024 * 1024


def params(**kw):
    return pltpu.CompilerParams(vmem_limit_bytes=VMEM, **kw)


def whole(count):
    return [pl.BlockSpec(memory_space=pltpu.VMEM) for _ in range(count)]


def gelu(x):
    return 0.5 * x * (1.0 + jnp.tanh(math.sqrt(2.0 / math.pi) * (x + 0.044715 * (x * x * x))))


def stem_kernel(place_ref, codes_ref, weight_ref, out_ref):
    length = codes_ref.shape[1]
    codes = jnp.broadcast_to(codes_ref[...], (16, length))
    first = SIDE - 2 * STEM_POOL + KS_STEM // 2
    shifted = pltpu.roll(codes, length - first, 1, stride=1, stride_axis=0)
    shifted = shifted[:, : EXT * STEM_POOL]
    onehot = jnp.concatenate(
        [(shifted == base + 1).astype(jnp.float32) for base in range(4)], axis=0
    ).astype(jnp.bfloat16)
    weight = weight_ref[...]
    step = 6
    for at in range(0, EXT, step):
        part = onehot[:, at * STEM_POOL : (at + step) * STEM_POOL]
        hidden = lax.dot_general(
            part, weight, (((0,), (0,)), ((), ())), preferred_element_type=jnp.float32
        ).reshape(step, STEM_POOL, weight.shape[1])
        high = gelu(jnp.max(hidden, axis=1))
        low = gelu(jnp.min(hidden, axis=1))
        rows = jnp.maximum(high, low)
        index = place_ref[0] * ROWS - 2 + at + lax.broadcasted_iota(jnp.int32, rows.shape, 0)
        inside = (index >= 0) & (index < N_SEQ * ROWS)
        out_ref[at : at + step, :] = jnp.where(inside, rows, 0.0)
    out_ref[EXT:EXT_PAD, :] = jnp.zeros((EXT_PAD - EXT, weight.shape[1]), jnp.float32)


def stem(place, codes, weight):
    return pl.pallas_call(
        stem_kernel,
        out_shape=jax.ShapeDtypeStruct((EXT_PAD, weight.shape[1]), jnp.float32),
        in_specs=[pl.BlockSpec(memory_space=pltpu.SMEM)] + whole(2),
        out_specs=whole(1)[0],
        compiler_params=params(),
        cost_estimate=pl.CostEstimate(flops=40_000_000_000, bytes_accessed=200000, transcendentals=0),
    )(place, codes, weight)


def pack_kernel(weight_ref, out_ref, wide):
    taps, width = weight_ref.shape
    share = width // N_SHARE
    half = taps // 2
    even, odd = [], []
    for part in range(wide.shape[0]):
        lanes = weight_ref[:, part * HQK : (part + 1) * HQK]
        wide[part, :taps, :] = lanes.astype(jnp.float32)
        wide[part, taps:, :] = jnp.zeros((wide.shape[1] - taps, HQK), jnp.float32)
        even.append(wide[part, pl.ds(0, half + 1, stride=2), :])
        odd.append(wide[part, pl.ds(1, half + 1, stride=2), :])
    even, odd = jnp.concatenate(even, axis=1), jnp.concatenate(odd, axis=1)
    lane = lax.broadcasted_iota(jnp.int32, (half + 1, HQK), 1)
    blocks = []
    for index in range(N_SHARE):
        low = pltpu.roll(even, (width - index * share) % width, 1)[:, :HQK]
        high = pltpu.roll(odd, (width - index * share + share) % width, 1)[:, :HQK]
        block = jnp.where(lane < share, low, high).astype(jnp.bfloat16)
        blocks.append(block[:half, : 2 * share])
    for place in range(N_SEQ):
        at, index, base = place, 0, 1
        for name in reversed(SEQ):
            if name in SHARE:
                index, base = index + base * (at % SIZES[name]), base * SIZES[name]
            at = at // SIZES[name]
        out_ref[place] = blocks[index]


def pack(weight):
    taps, width = weight.shape
    return pl.pallas_call(
        pack_kernel,
        out_shape=jax.ShapeDtypeStruct((N_SEQ, taps // 2, 2 * width // N_SHARE), jnp.bfloat16),
        in_specs=whole(1),
        out_specs=whole(1)[0],
        scratch_shapes=[pltpu.VMEM((width // HQK, taps + 2, HQK), jnp.float32)],
        compiler_params=params(),
    )(weight)


def conv_kernel(section_ref, weight_ref, out_ref, wide, act, best):
    windows, _, channels = section_ref.shape
    half = channels // 2
    columns = out_ref.shape[2] // 8
    wide[...] = section_ref[...].astype(jnp.float32)
    even, odd = None, None
    for tap in range(KS_CONV):
        rows = wide[:, tap : tap + ROWS, :].astype(jnp.bfloat16).reshape(windows * ROWS, channels)
        weight = weight_ref[tap * half : (tap + 1) * half, :]
        term = jnp.dot(rows[:, :half], weight, preferred_element_type=jnp.float32)
        even = term if even is None else even + term
        term = jnp.dot(rows[:, half:], weight, preferred_element_type=jnp.float32)
        odd = term if odd is None else odd + term
    act[...] = jnp.zeros(act.shape, jnp.float32)
    act[:, :columns] = gelu(even[:, :columns] + odd[:, columns:])
    count = windows * ROWS // 2
    best[...] = jnp.maximum(act[pl.ds(0, count, stride=2), :], act[pl.ds(1, count, stride=2), :])
    flat = None
    for index in range(8):
        part = best[pl.ds(index, count // 8, stride=8), :]
        part = jnp.pad(part, ((0, 0), (0, 8 * columns - part.shape[1])))
        part = pltpu.roll(part, index * columns, 1)
        flat = part if flat is None else flat + part
    for window in range(windows):
        block = flat[2 * window : 2 * window + 2, :].astype(jnp.bfloat16)
        for index in range(N_PAIR):
            out_ref[window * N_PAIR + index] = block


def conv(section, weight):
    windows, _, channels = section.shape
    columns = weight.shape[1] // 2
    return pl.pallas_call(
        conv_kernel,
        out_shape=jax.ShapeDtypeStruct((windows * N_PAIR, 2, 8 * columns), jnp.bfloat16),
        in_specs=whole(2),
        out_specs=whole(1)[0],
        scratch_shapes=[
            pltpu.VMEM((windows, EXT_PAD, channels), jnp.float32),
            pltpu.VMEM((windows * ROWS, HQK), jnp.float32),
            pltpu.VMEM((windows * ROWS // 2, HQK), jnp.float32),
        ],
        compiler_params=params(),
    )(section, weight)


def project_kernel(trunk_ref, w_query_ref, w_key_ref, w_value_ref, query_ref, kv_ref):
    trunk = trunk_ref[...]
    query, key, value = [
        jnp.dot(trunk, ref[...], preferred_element_type=jnp.float32).astype(jnp.bfloat16)
        for ref in (w_query_ref, w_key_ref, w_value_ref)
    ]
    query_ref[...] = query
    rest = jnp.zeros((trunk.shape[0], kv_ref.shape[2] - HQK - HV), jnp.bfloat16)
    for index in range(N_LINE):
        kv_ref[index, :, :HQK] = key
        kv_ref[index, :, HQK : HQK + HV] = value
        kv_ref[index, :, HQK + HV :] = rest


def project(trunk, w_query, w_key, w_value):
    count = trunk.shape[0]
    return pl.pallas_call(
        project_kernel,
        out_shape=(
            jax.ShapeDtypeStruct((count, HQK), jnp.bfloat16),
            jax.ShapeDtypeStruct((N_LINE, count, 3 * HQK), jnp.bfloat16),
        ),
        in_specs=whole(4),
        out_specs=tuple(whole(2)),
        compiler_params=params(),
    )(trunk, w_query, w_key, w_value)


def attention_kernel(place_ref, query_ref, kv_ref, out_ref):
    scale = 1.0 / math.sqrt(HQK)
    scores = (
        lax.dot_general(
            query_ref[...],
            kv_ref[:, :HQK],
            (((1,), (1,)), ((), ())),
            preferred_element_type=jnp.float32,
        )
        * scale
    )
    top = jnp.max(scores, axis=1, keepdims=True)
    expo = jnp.exp(scores - top)
    total = jnp.sum(expo, axis=1, keepdims=True)
    mixed = jnp.dot(expo.astype(jnp.bfloat16), kv_ref[:, HQK:], preferred_element_type=jnp.float32)
    lane = lax.broadcasted_iota(jnp.int32, mixed.shape, 1)
    mixed = jnp.where(lane == HV, top, jnp.where(lane == HV + 1, total, mixed))
    groups, count, _ = out_ref.shape
    for index in range(groups):
        out_ref[place_ref[0] ^ index] = mixed[index * count : (index + 1) * count, :]


def attention(place, query, kv):
    groups = N_SPREAD
    count, width = query.shape[0] // groups, kv.shape[1] - HQK
    return pl.pallas_call(
        attention_kernel,
        out_shape=jax.ShapeDtypeStruct((groups, count, width), jnp.float32),
        in_specs=[pl.BlockSpec(memory_space=pltpu.SMEM)] + whole(2),
        out_specs=whole(1)[0],
        compiler_params=params(),
    )(place, query, kv)


def combine_kernel(parts_ref, w_out_ref, out_ref):
    parts = parts_ref[...]
    top = parts[:, :, HV : HV + 1]
    gain = jnp.exp(top - jnp.max(top, axis=0, keepdims=True))
    total = jnp.sum(gain * parts[:, :, HV + 1 : HV + 2], axis=0)
    mixed = (jnp.sum(gain * parts, axis=0) / total)[:, :HV].astype(jnp.bfloat16)
    term = jnp.dot(mixed, w_out_ref[...], preferred_element_type=jnp.float32)
    mean = jnp.sum(term, axis=0, keepdims=True) * (1.0 / PAIR_POOL)
    width = term.shape[1] // N_PAIR
    count = term.shape[0]
    tail = jnp.concatenate(
        [mean[:, c * width : (c + 1) * width] for c in range(N_PAIR)]
        + [jnp.zeros((8 - N_PAIR, width), jnp.float32)],
        axis=0,
    )
    for c in range(N_PAIR):
        out_ref[c, :count, :] = term[:, c * width : (c + 1) * width]
        out_ref[c, count:, :] = tail


def combine(parts, w_out):
    count = parts.shape[1]
    width = w_out.shape[1] // N_PAIR
    return pl.pallas_call(
        combine_kernel,
        out_shape=jax.ShapeDtypeStruct((N_PAIR, count + 8, width), jnp.float32),
        in_specs=whole(2),
        out_specs=whole(1)[0],
        compiler_params=params(),
    )(parts, w_out)


def close_kernel(terms_ref, own_ref, trunk_ref, w_pair_ref, pair_ref, seq_ref, rows_ref, every_ref):
    count, width = own_ref.shape
    total = jnp.sum(terms_ref[...], axis=0)
    seq_ref[...] = (own_ref[...].astype(jnp.float32) + total[:count, :]).astype(jnp.bfloat16)
    trunk_mean = jnp.sum(trunk_ref[...].astype(jnp.float32), axis=0, keepdims=True) * (1.0 / PAIR_POOL)
    rows = None
    for c in range(N_PAIR):
        pooled = trunk_mean[:, c * width : (c + 1) * width] + total[count + c : count + c + 1, :]
        term = jnp.dot(
            jnp.broadcast_to(pooled, (8, width)).astype(jnp.bfloat16),
            w_pair_ref[c * width : (c + 1) * width, :],
            preferred_element_type=jnp.float32,
        )
        rows = term if rows is None else rows + term
    rows_ref[...] = rows
    mine = pair_ref[0].astype(jnp.float32)
    factors = jnp.broadcast_to(rows[:1], (mine.shape[0], rows.shape[1]))
    every_ref[...] = jnp.concatenate([factors, mine], axis=1)


def close(terms, own, trunk, w_pair, pair_in):
    return pl.pallas_call(
        close_kernel,
        out_shape=(
            jax.ShapeDtypeStruct(own.shape, jnp.bfloat16),
            jax.ShapeDtypeStruct((8, w_pair.shape[1]), jnp.float32),
            jax.ShapeDtypeStruct((pair_in.shape[1], w_pair.shape[1] + pair_in.shape[2]), jnp.float32),
        ),
        in_specs=whole(5),
        out_specs=tuple(whole(3)),
        compiler_params=params(),
    )(terms, own, trunk, w_pair, pair_in)


def distance_bias(row, cols, pair_bias):
    delta = jnp.abs(row - cols)
    bins = jnp.zeros(delta.shape, jnp.int32)
    for edge in EDGES:
        bins = bins + (delta >= edge).astype(jnp.int32)
    labels = jnp.arange(pair_bias.shape[0], dtype=jnp.int32)
    onehot = (bins[:, None] == labels[None, :]).astype(jnp.bfloat16)
    return jnp.dot(onehot, pair_bias, preferred_element_type=jnp.float32)


def exchange(blocks, axes):
    return lax.all_to_all(blocks, axes, split_axis=0, concat_axis=0, tiled=True)


def on_device(tokens, w_stem, w_conv, w_query, w_key, w_value, w_out, w_pair, pair_bias, pair_in):
    place = lax.axis_index(SEQ)
    pair_place = lax.axis_index("pair")

    taps, width = w_conv.shape
    share = width // N_SHARE
    blocks = exchange(pack(w_conv), SEQ)
    conv_weight = blocks.reshape(N_SEQ * blocks.shape[1], blocks.shape[2])

    codes = tokens + 1
    ends = N_SEQ - 1
    left = lax.ppermute(codes[-SIDE:], SEQ, [(i, i + 1) for i in range(ends)])
    right = lax.ppermute(codes[:SIDE], SEQ, [(i + 1, i) for i in range(ends)])
    codes = jnp.concatenate([left, codes, right])[None, :]
    source = jnp.arange(w_stem.shape[1]).reshape(2, -1)
    source = (2 * (source % source.shape[1]) + jnp.arange(2)[:, None]).reshape(-1)
    order = (jnp.arange(w_stem.shape[1])[:, None] == source[None, :]).astype(jnp.bfloat16)
    stem_weight = jnp.dot(w_stem, order, preferred_element_type=jnp.float32).astype(jnp.bfloat16)
    stem_weight = stem_weight.reshape(KS_STEM, 4, -1)[::-1].transpose(1, 0, 2)
    stem_weight = jnp.pad(stem_weight, ((0, 0), (0, 1), (0, 0))).reshape(64, -1)
    section = stem(place.astype(jnp.int32)[None], codes, stem_weight).astype(jnp.bfloat16)
    sections = lax.all_gather(section, SHARE, axis=0, tiled=False)

    parts = exchange(conv(sections, conv_weight), SHARE + ("pair",))
    count = ROWS // 2
    trunk = parts.reshape(N_SHARE, N_PAIR, count, share).transpose(2, 1, 0, 3)
    trunk = trunk.reshape(count, N_PAIR * width)

    query, kv = project(trunk, w_query, w_key, w_value)
    for name in reversed(SPREAD):
        other = lax.ppermute(query, name, [(0, 1), (1, 0)])
        query = jnp.concatenate([query, other], axis=0)
    kv = exchange(kv, LINE).reshape(N_LINE * count, kv.shape[2])
    spread = lax.axis_index(SPREAD).astype(jnp.int32)[None]
    parts = exchange(attention(spread, query, kv), SPREAD)
    terms = exchange(combine(parts, w_out), ("pair",))

    own = lax.dynamic_slice_in_dim(trunk, pair_place * width, width, 1)
    factors = jnp.concatenate([w_pair[0], w_pair[1]], axis=1)
    seq_out, rows, every = close(terms, own, trunk, factors, pair_in)
    channels = pair_in.shape[2]
    mine = pair_in[0].astype(jnp.float32)
    rows = rows[:1]
    every = exchange(every[:, None], SEQ)[:, 0]
    mirror = every[:, 2 * channels :]

    cols = jnp.arange(N_SEQ, dtype=jnp.int32)
    bias = distance_bias(place.astype(jnp.int32), cols, pair_bias)
    cross = rows[:, :channels] * every[:, channels : 2 * channels]
    cross = cross + every[:, :channels] * rows[:, channels:]
    pair_out = (0.5 * (mine + mirror + cross) + bias).astype(jnp.bfloat16)[None]
    return (seq_out, pair_out)


def solution(mesh):
    names = SEQ + ("pair",)
    fine = Mesh(mesh.devices.reshape([SIZES[name] for name in names]), names)
    placed = (
        P(SEQ),
        P(),
        P(SEQ, "pair"),
        P(None, "pair"),
        P(None, "pair"),
        P(None, "pair"),
        P("pair", None),
        P(None, None, "pair"),
        P(None, "pair"),
        P(SEQ, None, "pair"),
    )
    return jax.shard_map(
        on_device,
        mesh=fine,
        in_specs=placed,
        out_specs=(P(SEQ, "pair"), P(SEQ, None, "pair")),
        check_vma=False,
    )
```

```python
import math

import jax
import jax.numpy as jnp
from jax import lax
from jax.experimental import pallas as pl
from jax.experimental.pallas import tpu as pltpu
from jax.sharding import Mesh
from jax.sharding import PartitionSpec as P

HQK = 128
HV = 192
KS_STEM = 15
KS_CONV = 5
STEM_POOL = 64
PAIR_POOL = 16
EDGES = (1, 2, 3, 4, 6, 8, 12, 16, 24, 32, 48, 64, 96, 128, 192, 256, 384)

SIZES = {"zl": 2, "y": 8, "xh": 2, "xl": 2, "core": 2, "pair": 4}
SEQ = ("zl", "y", "xh", "xl", "core")
SHARE = ("zl", "xl", "core")
SPREAD = ("xh", "xl", "core")
LINE = ("zl", "y")
N_SEQ = math.prod(SIZES[name] for name in SEQ)
N_SHARE = math.prod(SIZES[name] for name in SHARE)
N_PAIR = SIZES["pair"]
N_SPREAD = math.prod(SIZES[name] for name in SPREAD)
N_LINE = math.prod(SIZES[name] for name in LINE)

SIDE = 256
ROWS = 32
EXT = ROWS + 4
EXT_PAD = 40
VMEM = 48 * 1024 * 1024


def params(**kw):
    return pltpu.CompilerParams(vmem_limit_bytes=VMEM, **kw)


def whole(count):
    return [pl.BlockSpec(memory_space=pltpu.VMEM) for _ in range(count)]


def gelu(x):
    return 0.5 * x * (1.0 + jnp.tanh(math.sqrt(2.0 / math.pi) * (x + 0.044715 * (x * x * x))))


def stem_kernel(place_ref, codes_ref, weight_ref, out_ref):
    length = codes_ref.shape[1]
    codes = jnp.broadcast_to(codes_ref[...], (16, length))
    first = SIDE - 2 * STEM_POOL + KS_STEM // 2
    shifted = pltpu.roll(codes, length - first, 1, stride=1, stride_axis=0)
    shifted = shifted[:, : EXT * STEM_POOL]
    onehot = jnp.concatenate(
        [(shifted == base + 1).astype(jnp.float32) for base in range(4)], axis=0
    ).astype(jnp.bfloat16)
    weight = weight_ref[...]
    step = 6
    for at in range(0, EXT, step):
        part = onehot[:, at * STEM_POOL : (at + step) * STEM_POOL]
        hidden = lax.dot_general(
            part, weight, (((0,), (0,)), ((), ())), preferred_element_type=jnp.float32
        ).reshape(step, STEM_POOL, weight.shape[1])
        high = gelu(jnp.max(hidden, axis=1))
        low = gelu(jnp.min(hidden, axis=1))
        rows = jnp.maximum(high, low)
        index = place_ref[0] * ROWS - 2 + at + lax.broadcasted_iota(jnp.int32, rows.shape, 0)
        inside = (index >= 0) & (index < N_SEQ * ROWS)
        out_ref[at : at + step, :] = jnp.where(inside, rows, 0.0)
    out_ref[EXT:EXT_PAD, :] = jnp.zeros((EXT_PAD - EXT, weight.shape[1]), jnp.float32)


def stem(place, codes, weight):
    return pl.pallas_call(
        stem_kernel,
        out_shape=jax.ShapeDtypeStruct((EXT_PAD, weight.shape[1]), jnp.float32),
        in_specs=[pl.BlockSpec(memory_space=pltpu.SMEM)] + whole(2),
        out_specs=whole(1)[0],
        compiler_params=params(),
        cost_estimate=pl.CostEstimate(flops=40_000_000_000, bytes_accessed=200000, transcendentals=0),
    )(place, codes, weight)


def pack_kernel(weight_ref, out_ref, wide):
    taps, width = weight_ref.shape
    share = width // N_SHARE
    half = taps // 2
    even, odd = [], []
    for part in range(wide.shape[0]):
        lanes = weight_ref[:, part * HQK : (part + 1) * HQK]
        wide[part, :taps, :] = lanes.astype(jnp.float32)
        wide[part, taps:, :] = jnp.zeros((wide.shape[1] - taps, HQK), jnp.float32)
        even.append(wide[part, pl.ds(0, half + 1, stride=2), :])
        odd.append(wide[part, pl.ds(1, half + 1, stride=2), :])
    even, odd = jnp.concatenate(even, axis=1), jnp.concatenate(odd, axis=1)
    lane = lax.broadcasted_iota(jnp.int32, (half + 1, HQK), 1)
    blocks = []
    for index in range(N_SHARE):
        low = pltpu.roll(even, (width - index * share) % width, 1)[:, :HQK]
        high = pltpu.roll(odd, (width - index * share + share) % width, 1)[:, :HQK]
        block = jnp.where(lane < share, low, high).astype(jnp.bfloat16)
        blocks.append(block[:half, : 2 * share])
    for place in range(N_SEQ):
        at, index, base = place, 0, 1
        for name in reversed(SEQ):
            if name in SHARE:
                index, base = index + base * (at % SIZES[name]), base * SIZES[name]
            at = at // SIZES[name]
        out_ref[place] = blocks[index]


def pack(weight):
    taps, width = weight.shape
    return pl.pallas_call(
        pack_kernel,
        out_shape=jax.ShapeDtypeStruct((N_SEQ, taps // 2, 2 * width // N_SHARE), jnp.bfloat16),
        in_specs=whole(1),
        out_specs=whole(1)[0],
        scratch_shapes=[pltpu.VMEM((width // HQK, taps + 2, HQK), jnp.float32)],
        compiler_params=params(),
    )(weight)


def conv_kernel(core_ref, near_ref, far_ref, weight_ref, out_ref, wide, act, best):
    windows, _, channels = wide.shape
    half = channels // 2
    columns = out_ref.shape[2] // 8
    wide[: windows // 2] = near_ref[...].astype(jnp.float32)
    wide[windows // 2 :] = far_ref[...].astype(jnp.float32)
    even, odd = None, None
    for tap in range(KS_CONV):
        rows = wide[:, tap : tap + ROWS, :].astype(jnp.bfloat16).reshape(windows * ROWS, channels)
        weight = weight_ref[tap * half : (tap + 1) * half, :]
        term = jnp.dot(rows[:, :half], weight, preferred_element_type=jnp.float32)
        even = term if even is None else even + term
        term = jnp.dot(rows[:, half:], weight, preferred_element_type=jnp.float32)
        odd = term if odd is None else odd + term
    act[...] = jnp.zeros(act.shape, jnp.float32)
    act[:, :columns] = gelu(even[:, :columns] + odd[:, columns:])
    count = windows * ROWS // 2
    best[...] = jnp.maximum(act[pl.ds(0, count, stride=2), :], act[pl.ds(1, count, stride=2), :])
    flat = None
    for index in range(8):
        part = best[pl.ds(index, count // 8, stride=8), :]
        part = jnp.pad(part, ((0, 0), (0, 8 * columns - part.shape[1])))
        part = pltpu.roll(part, index * columns, 1)
        flat = part if flat is None else flat + part
    for window in range(windows):
        block = flat[2 * window : 2 * window + 2, :].astype(jnp.bfloat16)
        far = window * 2 // windows
        place = window % (windows // 2) * 2 + (core_ref[0] ^ far)
        for index in range(N_PAIR):
            out_ref[place * N_PAIR + index] = block


def conv(core, near, far, weight):
    windows, _, channels = near.shape
    windows = 2 * windows
    columns = weight.shape[1] // 2
    return pl.pallas_call(
        conv_kernel,
        out_shape=jax.ShapeDtypeStruct((windows * N_PAIR, 2, 8 * columns), jnp.bfloat16),
        in_specs=[pl.BlockSpec(memory_space=pltpu.SMEM)] + whole(3),
        out_specs=whole(1)[0],
        scratch_shapes=[
            pltpu.VMEM((windows, EXT_PAD, channels), jnp.float32),
            pltpu.VMEM((windows * ROWS, HQK), jnp.float32),
            pltpu.VMEM((windows * ROWS // 2, HQK), jnp.float32),
        ],
        compiler_params=params(),
    )(core, near, far, weight)


def project_kernel(trunk_ref, w_query_ref, w_key_ref, w_value_ref, query_ref, kv_ref):
    trunk = trunk_ref[...]
    query, key, value = [
        jnp.dot(trunk, ref[...], preferred_element_type=jnp.float32).astype(jnp.bfloat16)
        for ref in (w_query_ref, w_key_ref, w_value_ref)
    ]
    query_ref[...] = query
    rest = jnp.zeros((trunk.shape[0], kv_ref.shape[2] - HQK - HV), jnp.bfloat16)
    for index in range(N_LINE):
        kv_ref[index, :, :HQK] = key
        kv_ref[index, :, HQK : HQK + HV] = value
        kv_ref[index, :, HQK + HV :] = rest


def project(trunk, w_query, w_key, w_value):
    count = trunk.shape[0]
    return pl.pallas_call(
        project_kernel,
        out_shape=(
            jax.ShapeDtypeStruct((count, HQK), jnp.bfloat16),
            jax.ShapeDtypeStruct((N_LINE, count, 3 * HQK), jnp.bfloat16),
        ),
        in_specs=whole(4),
        out_specs=tuple(whole(2)),
        compiler_params=params(),
    )(trunk, w_query, w_key, w_value)


def attention_kernel(place_ref, query_ref, kv_ref, out_ref):
    scale = 1.0 / math.sqrt(HQK)
    scores = (
        lax.dot_general(
            query_ref[...],
            kv_ref[:, :HQK],
            (((1,), (1,)), ((), ())),
            preferred_element_type=jnp.float32,
        )
        * scale
    )
    top = jnp.max(scores, axis=1, keepdims=True)
    expo = jnp.exp(scores - top)
    total = jnp.sum(expo, axis=1, keepdims=True)
    mixed = jnp.dot(expo.astype(jnp.bfloat16), kv_ref[:, HQK:], preferred_element_type=jnp.float32)
    lane = lax.broadcasted_iota(jnp.int32, mixed.shape, 1)
    mixed = jnp.where(lane == HV, top, jnp.where(lane == HV + 1, total, mixed))
    groups, count, _ = out_ref.shape
    for index in range(groups):
        out_ref[place_ref[0] ^ index] = mixed[index * count : (index + 1) * count, :]


def attention(place, query, kv):
    groups = N_SPREAD
    count, width = query.shape[0] // groups, kv.shape[1] - HQK
    return pl.pallas_call(
        attention_kernel,
        out_shape=jax.ShapeDtypeStruct((groups, count, width), jnp.float32),
        in_specs=[pl.BlockSpec(memory_space=pltpu.SMEM)] + whole(2),
        out_specs=whole(1)[0],
        compiler_params=params(),
    )(place, query, kv)


def combine_kernel(place_ref, parts_ref, w_out_ref, means_ref, *refs):
    terms_refs, blocks = refs[:-1], refs[-1]
    parts = parts_ref[...]
    top = parts[:, :, HV : HV + 1]
    gain = jnp.exp(top - jnp.max(top, axis=0, keepdims=True))
    total = jnp.sum(gain * parts[:, :, HV + 1 : HV + 2], axis=0)
    mixed = (jnp.sum(gain * parts, axis=0) / total)[:, :HV].astype(jnp.bfloat16)
    term = jnp.dot(mixed, w_out_ref[...], preferred_element_type=jnp.float32)
    mean = jnp.sum(term, axis=0, keepdims=True) * (1.0 / PAIR_POOL)
    width = term.shape[1] // N_PAIR
    tail = jnp.concatenate(
        [mean[:, c * width : (c + 1) * width] for c in range(N_PAIR)]
        + [jnp.zeros((8 - N_PAIR, width), jnp.float32)],
        axis=0,
    )
    for c in range(N_PAIR):
        means_ref[c] = tail
        blocks[c] = term[:, c * width : (c + 1) * width]
    for shift, ref in enumerate(terms_refs):
        ref[...] = blocks[(place_ref[0] + shift) % N_PAIR]


def combine(place, parts, w_out):
    count = parts.shape[1]
    width = w_out.shape[1] // N_PAIR
    block = jax.ShapeDtypeStruct((count, width), jnp.float32)
    return pl.pallas_call(
        combine_kernel,
        out_shape=(jax.ShapeDtypeStruct((N_PAIR, 8, width), jnp.float32),) + (block,) * N_PAIR,
        in_specs=[pl.BlockSpec(memory_space=pltpu.SMEM)] + whole(2),
        out_specs=tuple(whole(1 + N_PAIR)),
        scratch_shapes=[pltpu.VMEM((N_PAIR, count, width), jnp.float32)],
        compiler_params=params(),
    )(place, parts, w_out)


def close_kernel(means_ref, trunk_ref, w_pair_ref, pair_ref, *refs):
    terms_refs, (rows_ref, every_ref), sent_refs = refs[:3], refs[3:5], refs[5:]
    total = jnp.sum(means_ref[...], axis=0)
    width = total.shape[1]
    trunk_mean = jnp.sum(trunk_ref[...].astype(jnp.float32), axis=0, keepdims=True) * (1.0 / PAIR_POOL)
    rows = None
    for c in range(N_PAIR):
        pooled = trunk_mean[:, c * width : (c + 1) * width] + total[c : c + 1, :]
        term = jnp.dot(
            jnp.broadcast_to(pooled, (8, width)).astype(jnp.bfloat16),
            w_pair_ref[c * width : (c + 1) * width, :],
            preferred_element_type=jnp.float32,
        )
        rows = term if rows is None else rows + term
    rows_ref[...] = rows
    mine = pair_ref[0].astype(jnp.float32)
    factors = jnp.broadcast_to(rows[:1], (mine.shape[0], rows.shape[1]))
    every_ref[...] = jnp.concatenate([factors, mine], axis=1)
    for term_ref, sent_ref in zip(terms_refs, sent_refs):
        sent_ref[...] = term_ref[...]


def close(means, trunk, w_pair, pair_in, terms):
    factors = w_pair.shape[1]
    return pl.pallas_call(
        close_kernel,
        out_shape=(
            jax.ShapeDtypeStruct((8, factors), jnp.float32),
            jax.ShapeDtypeStruct((pair_in.shape[1], factors + pair_in.shape[2]), jnp.float32),
        )
        + tuple(jax.ShapeDtypeStruct(term.shape, jnp.float32) for term in terms),
        in_specs=whole(4 + len(terms)),
        out_specs=tuple(whole(2 + len(terms))),
        compiler_params=params(),
    )(means, trunk, w_pair, pair_in, *terms)


def distance_bias(row, cols, pair_bias):
    delta = jnp.abs(row - cols)
    bins = jnp.zeros(delta.shape, jnp.int32)
    for edge in EDGES:
        bins = bins + (delta >= edge).astype(jnp.int32)
    labels = jnp.arange(pair_bias.shape[0], dtype=jnp.int32)
    onehot = (bins[:, None] == labels[None, :]).astype(jnp.bfloat16)
    return jnp.dot(onehot, pair_bias, preferred_element_type=jnp.float32)


def exchange(blocks, axes):
    return lax.all_to_all(blocks, axes, split_axis=0, concat_axis=0, tiled=True)


def on_device(tokens, w_stem, w_conv, w_query, w_key, w_value, w_out, w_pair, pair_bias, pair_in):
    place = lax.axis_index(SEQ)
    pair_place = lax.axis_index("pair")
    core = lax.axis_index("core").astype(jnp.int32)[None]

    taps, width = w_conv.shape
    share = width // N_SHARE
    blocks = exchange(pack(w_conv), SEQ)
    conv_weight = blocks.reshape(N_SEQ * blocks.shape[1], blocks.shape[2])

    codes = tokens + 1
    ends = N_SEQ - 1
    left = lax.ppermute(codes[-SIDE:], SEQ, [(i, i + 1) for i in range(ends)])
    right = lax.ppermute(codes[:SIDE], SEQ, [(i + 1, i) for i in range(ends)])
    codes = jnp.concatenate([left, codes, right])[None, :]
    source = jnp.arange(w_stem.shape[1]).reshape(2, -1)
    source = (2 * (source % source.shape[1]) + jnp.arange(2)[:, None]).reshape(-1)
    order = (jnp.arange(w_stem.shape[1])[:, None] == source[None, :]).astype(jnp.bfloat16)
    stem_weight = jnp.dot(w_stem, order, preferred_element_type=jnp.float32).astype(jnp.bfloat16)
    stem_weight = stem_weight.reshape(KS_STEM, 4, -1)[::-1].transpose(1, 0, 2)
    stem_weight = jnp.pad(stem_weight, ((0, 0), (0, 1), (0, 0))).reshape(64, -1)
    section = stem(place.astype(jnp.int32)[None], codes, stem_weight).astype(jnp.bfloat16)
    near = lax.all_gather(section, SHARE[:-1], axis=0, tiled=False)
    far = lax.ppermute(near, "core", [(0, 1), (1, 0)])

    parts = exchange(conv(core, near, far, conv_weight), SHARE + ("pair",))
    count = ROWS // 2
    trunk = parts.reshape(N_SHARE, N_PAIR, count, share).transpose(2, 1, 0, 3)
    trunk = trunk.reshape(count, N_PAIR * width)

    query, kv = project(trunk, w_query, w_key, w_value)
    for name in reversed(SPREAD):
        other = lax.ppermute(query, name, [(0, 1), (1, 0)])
        query = jnp.concatenate([query, other], axis=0)
    kv = exchange(kv, LINE).reshape(N_LINE * count, kv.shape[2])
    spread = lax.axis_index(SPREAD).astype(jnp.int32)[None]
    parts = exchange(attention(spread, query, kv), SPREAD)
    means, term, *terms = combine(pair_place.astype(jnp.int32)[None], parts, w_out)
    means = exchange(means, ("pair",))

    factors = jnp.concatenate([w_pair[0], w_pair[1]], axis=1)
    rows, every, *terms = close(means, trunk, factors, pair_in, terms)
    channels = pair_in.shape[2]
    mine = pair_in[0].astype(jnp.float32)
    rows = rows[:1]
    every = exchange(every[:, None], SEQ)[:, 0]
    mirror = every[:, 2 * channels :]
    summed = lax.dynamic_slice_in_dim(trunk, pair_place * width, width, 1).astype(jnp.float32) + term
    for shift, block in enumerate(terms, 1):
        summed = summed + lax.ppermute(block, "pair", [(i, (i + shift) % N_PAIR) for i in range(N_PAIR)])
    seq_out = summed.astype(jnp.bfloat16)

    cols = jnp.arange(N_SEQ, dtype=jnp.int32)
    bias = distance_bias(place.astype(jnp.int32), cols, pair_bias)
    cross = rows[:, :channels] * every[:, channels : 2 * channels]
    cross = cross + every[:, :channels] * rows[:, channels:]
    pair_out = (0.5 * (mine + mirror + cross) + bias).astype(jnp.bfloat16)[None]
    return (seq_out, pair_out)


def solution(mesh):
    names = SEQ + ("pair",)
    fine = Mesh(mesh.devices.reshape([SIZES[name] for name in names]), names)
    placed = (
        P(SEQ),
        P(),
        P(SEQ, "pair"),
        P(None, "pair"),
        P(None, "pair"),
        P(None, "pair"),
        P("pair", None),
        P(None, None, "pair"),
        P(None, "pair"),
        P(SEQ, None, "pair"),
    )
    return jax.shard_map(
        on_device,
        mesh=fine,
        in_specs=placed,
        out_specs=(P(SEQ, "pair"), P(SEQ, None, "pair")),
        check_vma=False,
    )
```

```python
import math

import jax
import jax.numpy as jnp
from jax import lax
from jax.experimental import pallas as pl
from jax.experimental.pallas import tpu as pltpu
from jax.sharding import Mesh
from jax.sharding import PartitionSpec as P

HQK = 128
HV = 192
KS_STEM = 15
KS_CONV = 5
STEM_POOL = 64
PAIR_POOL = 16
EDGES = (1, 2, 3, 4, 6, 8, 12, 16, 24, 32, 48, 64, 96, 128, 192, 256, 384)

SIZES = {"zl": 2, "yh": 2, "yl": 4, "xh": 2, "xl": 2, "core": 2, "pair": 4}
SEQ = ("zl", "yh", "yl", "xh", "xl", "core")
HALF = ("zl", "yl", "xh", "xl", "core")
SHARE = ("zl", "xl", "core")
SPREAD = ("xh", "xl", "core")
LINE = ("zl", "yh", "yl")
N_SEQ = math.prod(SIZES[name] for name in SEQ)
N_SHARE = math.prod(SIZES[name] for name in SHARE)
N_PAIR = SIZES["pair"]
N_SPREAD = math.prod(SIZES[name] for name in SPREAD)
N_LINE = math.prod(SIZES[name] for name in LINE)

SIDE = 256
ROWS = 32
EXT = ROWS + 4
EXT_PAD = 40
VMEM = 48 * 1024 * 1024


def params(**kw):
    return pltpu.CompilerParams(vmem_limit_bytes=VMEM, **kw)


def whole(count):
    return [pl.BlockSpec(memory_space=pltpu.VMEM) for _ in range(count)]


def gelu(x):
    return 0.5 * x * (1.0 + jnp.tanh(math.sqrt(2.0 / math.pi) * (x + 0.044715 * (x * x * x))))


def stem_kernel(place_ref, codes_ref, weight_ref, out_ref):
    length = codes_ref.shape[1]
    codes = jnp.broadcast_to(codes_ref[...], (16, length))
    first = SIDE - 2 * STEM_POOL + KS_STEM // 2
    shifted = pltpu.roll(codes, length - first, 1, stride=1, stride_axis=0)
    shifted = shifted[:, : EXT * STEM_POOL]
    onehot = jnp.concatenate(
        [(shifted == base + 1).astype(jnp.float32) for base in range(4)], axis=0
    ).astype(jnp.bfloat16)
    weight = weight_ref[...]
    step = 6
    for at in range(0, EXT, step):
        part = onehot[:, at * STEM_POOL : (at + step) * STEM_POOL]
        hidden = lax.dot_general(
            part, weight, (((0,), (0,)), ((), ())), preferred_element_type=jnp.float32
        ).reshape(step, STEM_POOL, weight.shape[1])
        high = gelu(jnp.max(hidden, axis=1))
        low = gelu(jnp.min(hidden, axis=1))
        rows = jnp.maximum(high, low)
        index = place_ref[0] * ROWS - 2 + at + lax.broadcasted_iota(jnp.int32, rows.shape, 0)
        inside = (index >= 0) & (index < N_SEQ * ROWS)
        out_ref[at : at + step, :] = jnp.where(inside, rows, 0.0)
    out_ref[EXT:EXT_PAD, :] = jnp.zeros((EXT_PAD - EXT, weight.shape[1]), jnp.float32)


def stem(place, codes, weight):
    return pl.pallas_call(
        stem_kernel,
        out_shape=jax.ShapeDtypeStruct((EXT_PAD, weight.shape[1]), jnp.float32),
        in_specs=[pl.BlockSpec(memory_space=pltpu.SMEM)] + whole(2),
        out_specs=whole(1)[0],
        compiler_params=params(),
        cost_estimate=pl.CostEstimate(flops=2 * 2304 * 64 * 768, bytes_accessed=200000, transcendentals=0),
    )(place, codes, weight)


def pack_kernel(half_ref, near_ref, far_ref, section_ref, out_ref, wide, joined):
    taps, width = near_ref.shape
    share = width // N_SHARE
    rows = taps // 2
    pairs = []
    for ref in (near_ref, far_ref):
        even, odd = [], []
        for part in range(wide.shape[0]):
            lanes = ref[:, part * HQK : (part + 1) * HQK]
            wide[part, :taps, :] = lanes.astype(jnp.float32)
            wide[part, taps:, :] = jnp.zeros((wide.shape[1] - taps, HQK), jnp.float32)
            even.append(wide[part, pl.ds(0, rows + 1, stride=2), :])
            odd.append(wide[part, pl.ds(1, rows + 1, stride=2), :])
        pairs.append((jnp.concatenate(even, axis=1), jnp.concatenate(odd, axis=1)))
    first = half_ref[0] == 0
    lane = lax.broadcasted_iota(jnp.int32, (rows + 1, HQK), 1)
    blocks = []
    for index in range(N_SHARE):
        near, far = [
            jnp.where(
                lane < share,
                pltpu.roll(even, (width - index * share) % width, 1)[:, :HQK],
                pltpu.roll(odd, (width - index * share + share) % width, 1)[:, :HQK],
            )
            for even, odd in pairs
        ]
        joined[index, : rows + 1, :] = jnp.where(first, near, far)
        joined[index, rows : 2 * rows + 1, :] = jnp.where(first, far, near)
        blocks.append(joined[index, :taps, : 2 * share].astype(jnp.bfloat16))
    for place in range(out_ref.shape[0]):
        at, index, base = place, 0, 1
        for name in reversed(HALF):
            if name in SHARE:
                index, base = index + base * (at % SIZES[name]), base * SIZES[name]
            at = at // SIZES[name]
        out_ref[place] = blocks[index]


def pack(half, near, far, section):
    taps, width = near.shape
    count = math.prod(SIZES[name] for name in HALF)
    return pl.pallas_call(
        pack_kernel,
        out_shape=jax.ShapeDtypeStruct((count, taps, 2 * width // N_SHARE), jnp.bfloat16),
        in_specs=[pl.BlockSpec(memory_space=pltpu.SMEM)] + whole(2) + [pl.BlockSpec(memory_space=pl.ANY)],
        out_specs=whole(1)[0],
        scratch_shapes=[
            pltpu.VMEM((width // HQK, taps + 2, HQK), jnp.float32),
            pltpu.VMEM((N_SHARE, taps + 2, HQK), jnp.float32),
        ],
        compiler_params=params(),
    )(half, near, far, section)


def conv_kernel(section_ref, blocks_ref, out_ref, weights, wide, act, best):
    count, taps, _ = blocks_ref.shape
    rows = taps // 2
    line = count // SIZES["zl"]
    for source in range(count):
        block = blocks_ref[source].astype(jnp.float32)
        for index in range(2):
            at = (source // line * 2 + index) * line + source % line
            weights[at * rows : (at + 1) * rows, :] = block[index * rows : (index + 1) * rows, :]
    windows, _, channels = section_ref.shape
    half = channels // 2
    columns = out_ref.shape[2] // 8
    wide[...] = section_ref[...].astype(jnp.float32)
    even, odd = None, None
    for tap in range(KS_CONV):
        rows = wide[:, tap : tap + ROWS, :].astype(jnp.bfloat16).reshape(windows * ROWS, channels)
        weight = weights[tap * half : (tap + 1) * half, :].astype(jnp.bfloat16)
        term = jnp.dot(rows[:, :half], weight, preferred_element_type=jnp.float32)
        even = term if even is None else even + term
        term = jnp.dot(rows[:, half:], weight, preferred_element_type=jnp.float32)
        odd = term if odd is None else odd + term
    act[...] = jnp.zeros(act.shape, jnp.float32)
    act[:, :columns] = gelu(even[:, :columns] + odd[:, columns:])
    count = windows * ROWS // 2
    best[...] = jnp.maximum(act[pl.ds(0, count, stride=2), :], act[pl.ds(1, count, stride=2), :])
    flat = None
    for index in range(8):
        part = best[pl.ds(index, count // 8, stride=8), :]
        part = jnp.pad(part, ((0, 0), (0, 8 * columns - part.shape[1])))
        part = pltpu.roll(part, index * columns, 1)
        flat = part if flat is None else flat + part
    for window in range(windows):
        block = flat[2 * window : 2 * window + 2, :].astype(jnp.bfloat16)
        for index in range(N_PAIR):
            out_ref[window * N_PAIR + index] = block


def conv(section, blocks):
    windows, _, channels = section.shape
    columns = blocks.shape[2] // 2
    return pl.pallas_call(
        conv_kernel,
        out_shape=jax.ShapeDtypeStruct((windows * N_PAIR, 2, 8 * columns), jnp.bfloat16),
        in_specs=whole(2),
        out_specs=whole(1)[0],
        scratch_shapes=[
            pltpu.VMEM((blocks.shape[0] * blocks.shape[1], 2 * columns), jnp.float32),
            pltpu.VMEM((windows, EXT_PAD, channels), jnp.float32),
            pltpu.VMEM((windows * ROWS, HQK), jnp.float32),
            pltpu.VMEM((windows * ROWS // 2, HQK), jnp.float32),
        ],
        compiler_params=params(),
    )(section, blocks)


def project_kernel(trunk_ref, w_query_ref, w_key_ref, w_value_ref, query_ref, kv_ref):
    trunk = trunk_ref[...]
    query, key, value = [
        jnp.dot(trunk, ref[...], preferred_element_type=jnp.float32).astype(jnp.bfloat16)
        for ref in (w_query_ref, w_key_ref, w_value_ref)
    ]
    query_ref[...] = query
    rest = jnp.zeros((trunk.shape[0], kv_ref.shape[2] - HQK - HV), jnp.bfloat16)
    for index in range(N_LINE):
        kv_ref[index, :, :HQK] = key
        kv_ref[index, :, HQK : HQK + HV] = value
        kv_ref[index, :, HQK + HV :] = rest


def project(trunk, w_query, w_key, w_value):
    count = trunk.shape[0]
    return pl.pallas_call(
        project_kernel,
        out_shape=(
            jax.ShapeDtypeStruct((count, HQK), jnp.bfloat16),
            jax.ShapeDtypeStruct((N_LINE, count, 3 * HQK), jnp.bfloat16),
        ),
        in_specs=whole(4),
        out_specs=tuple(whole(2)),
        compiler_params=params(),
    )(trunk, w_query, w_key, w_value)


def split(x):
    parts = []
    for _ in range(3):
        part = x.astype(jnp.bfloat16).astype(jnp.float32)
        parts.append(part)
        x = x - part
    return parts


def attention_kernel(place_ref, query_ref, kv_ref, out_ref):
    scale = 1.0 / math.sqrt(HQK)
    scores = (
        lax.dot_general(
            query_ref[...],
            kv_ref[:, :HQK],
            (((1,), (1,)), ((), ())),
            preferred_element_type=jnp.float32,
        )
        * scale
    )
    top = jnp.max(scores, axis=1, keepdims=True)
    expo = jnp.exp(scores - top)
    total = jnp.sum(expo, axis=1, keepdims=True)
    mixed = jnp.dot(expo.astype(jnp.bfloat16), kv_ref[:, HQK:], preferred_element_type=jnp.float32)
    lane = lax.broadcasted_iota(jnp.int32, mixed.shape, 1)
    for index, column in enumerate(split(top) + split(total)):
        mixed = jnp.where(lane == HV + index, column, mixed)
    mixed = mixed.astype(jnp.bfloat16)
    groups, count, _ = out_ref.shape
    for index in range(groups):
        out_ref[place_ref[0] ^ index] = mixed[index * count : (index + 1) * count, :]


def attention(place, query, kv):
    groups = N_SPREAD
    count, width = query.shape[0] // groups, kv.shape[1] - HQK
    return pl.pallas_call(
        attention_kernel,
        out_shape=jax.ShapeDtypeStruct((groups, count, width), jnp.bfloat16),
        in_specs=[pl.BlockSpec(memory_space=pltpu.SMEM)] + whole(2),
        out_specs=whole(1)[0],
        compiler_params=params(),
    )(place, query, kv)


def combine_kernel(parts_ref, w_out_ref, out_ref):
    parts = parts_ref[...].astype(jnp.float32)
    top = jnp.sum(parts[:, :, HV : HV + 3], axis=2, keepdims=True)
    gain = jnp.exp(top - jnp.max(top, axis=0, keepdims=True))
    total = jnp.sum(gain * jnp.sum(parts[:, :, HV + 3 : HV + 6], axis=2, keepdims=True), axis=0)
    mixed = (jnp.sum(gain * parts, axis=0) / total)[:, :HV].astype(jnp.bfloat16)
    term = jnp.dot(mixed, w_out_ref[...], preferred_element_type=jnp.float32)
    mean = jnp.sum(term, axis=0, keepdims=True) * (1.0 / PAIR_POOL)
    width = term.shape[1] // N_PAIR
    count = term.shape[0]
    tail = jnp.concatenate(
        [mean[:, c * width : (c + 1) * width] for c in range(N_PAIR)]
        + [jnp.zeros((8 - N_PAIR, width), jnp.float32)],
        axis=0,
    )
    for c in range(N_PAIR):
        out_ref[c, :count, :] = term[:, c * width : (c + 1) * width]
        out_ref[c, count:, :] = tail


def combine(parts, w_out):
    count = parts.shape[1]
    width = w_out.shape[1] // N_PAIR
    return pl.pallas_call(
        combine_kernel,
        out_shape=jax.ShapeDtypeStruct((N_PAIR, count + 8, width), jnp.float32),
        in_specs=whole(2),
        out_specs=whole(1)[0],
        compiler_params=params(),
    )(parts, w_out)


def close_kernel(terms_ref, own_ref, trunk_ref, w_pair_ref, pair_ref, seq_ref, rows_ref, every_ref):
    count, width = own_ref.shape
    total = jnp.sum(terms_ref[...], axis=0)
    seq_ref[...] = (own_ref[...].astype(jnp.float32) + total[:count, :]).astype(jnp.bfloat16)
    trunk_mean = jnp.sum(trunk_ref[...].astype(jnp.float32), axis=0, keepdims=True) * (1.0 / PAIR_POOL)
    rows = None
    for c in range(N_PAIR):
        pooled = trunk_mean[:, c * width : (c + 1) * width] + total[count + c : count + c + 1, :]
        term = jnp.dot(
            jnp.broadcast_to(pooled, (8, width)).astype(jnp.bfloat16),
            w_pair_ref[c * width : (c + 1) * width, :],
            preferred_element_type=jnp.float32,
        )
        rows = term if rows is None else rows + term
    rows_ref[...] = rows
    mine = pair_ref[0].astype(jnp.float32)
    factors = jnp.broadcast_to(rows[:1], (mine.shape[0], rows.shape[1]))
    every_ref[...] = jnp.concatenate([factors, mine], axis=1)


def close(terms, own, trunk, w_pair, pair_in):
    return pl.pallas_call(
        close_kernel,
        out_shape=(
            jax.ShapeDtypeStruct(own.shape, jnp.bfloat16),
            jax.ShapeDtypeStruct((8, w_pair.shape[1]), jnp.float32),
            jax.ShapeDtypeStruct((pair_in.shape[1], w_pair.shape[1] + pair_in.shape[2]), jnp.float32),
        ),
        in_specs=whole(5),
        out_specs=tuple(whole(3)),
        compiler_params=params(),
    )(terms, own, trunk, w_pair, pair_in)


def distance_bias(row, cols, pair_bias):
    delta = jnp.abs(row - cols)
    bins = jnp.zeros(delta.shape, jnp.int32)
    for edge in EDGES:
        bins = bins + (delta >= edge).astype(jnp.int32)
    labels = jnp.arange(pair_bias.shape[0], dtype=jnp.int32)
    onehot = (bins[:, None] == labels[None, :]).astype(jnp.bfloat16)
    return jnp.dot(onehot, pair_bias, preferred_element_type=jnp.float32)


def exchange(blocks, axes):
    return lax.all_to_all(blocks, axes, split_axis=0, concat_axis=0, tiled=True)


def on_device(tokens, w_stem, w_conv, w_query, w_key, w_value, w_out, w_pair, pair_bias, pair_in):
    place = lax.axis_index(SEQ)
    pair_place = lax.axis_index("pair")

    taps, width = w_conv.shape
    share = width // N_SHARE
    swapped = lax.ppermute(w_conv, "yh", [(0, 1), (1, 0)])

    codes = tokens + 1
    ends = N_SEQ - 1
    left = lax.ppermute(codes[-SIDE:], SEQ, [(i, i + 1) for i in range(ends)])
    right = lax.ppermute(codes[:SIDE], SEQ, [(i + 1, i) for i in range(ends)])
    codes = jnp.concatenate([left, codes, right])[None, :]
    source = jnp.arange(w_stem.shape[1]).reshape(2, -1)
    source = (2 * (source % source.shape[1]) + jnp.arange(2)[:, None]).reshape(-1)
    order = (jnp.arange(w_stem.shape[1])[:, None] == source[None, :]).astype(jnp.bfloat16)
    stem_weight = jnp.dot(w_stem, order, preferred_element_type=jnp.float32).astype(jnp.bfloat16)
    stem_weight = stem_weight.reshape(KS_STEM, 4, -1)[::-1].transpose(1, 0, 2)
    stem_weight = jnp.pad(stem_weight, ((0, 0), (0, 1), (0, 0))).reshape(64, -1)
    section = stem(place.astype(jnp.int32)[None], codes, stem_weight).astype(jnp.bfloat16)

    half = lax.axis_index("yh").astype(jnp.int32)[None]
    blocks = exchange(pack(half, w_conv, swapped, section), HALF)
    sections = lax.all_gather(section, SHARE, axis=0, tiled=False)

    parts = exchange(conv(sections, blocks), SHARE + ("pair",))
    count = ROWS // 2
    trunk = parts.reshape(N_SHARE, N_PAIR, count, share).transpose(2, 1, 0, 3)
    trunk = trunk.reshape(count, N_PAIR * width)

    query, kv = project(trunk, w_query, w_key, w_value)
    for name in reversed(SPREAD):
        other = lax.ppermute(query, name, [(0, 1), (1, 0)])
        query = jnp.concatenate([query, other], axis=0)
    kv = exchange(kv, LINE).reshape(N_LINE * count, kv.shape[2])
    spread = lax.axis_index(SPREAD).astype(jnp.int32)[None]
    parts = exchange(attention(spread, query, kv), SPREAD)
    terms = exchange(combine(parts, w_out), ("pair",))

    own = lax.dynamic_slice_in_dim(trunk, pair_place * width, width, 1)
    factors = jnp.concatenate([w_pair[0], w_pair[1]], axis=1)
    seq_out, rows, every = close(terms, own, trunk, factors, pair_in)
    channels = pair_in.shape[2]
    mine = pair_in[0].astype(jnp.float32)
    rows = rows[:1]
    every = exchange(every[:, None], SEQ)[:, 0]
    mirror = every[:, 2 * channels :]

    cols = jnp.arange(N_SEQ, dtype=jnp.int32)
    bias = distance_bias(place.astype(jnp.int32), cols, pair_bias)
    cross = rows[:, :channels] * every[:, channels : 2 * channels]
    cross = cross + every[:, :channels] * rows[:, channels:]
    pair_out = (0.5 * (mine + mirror + cross) + bias).astype(jnp.bfloat16)[None]
    return (seq_out, pair_out)


def solution(mesh):
    names = SEQ + ("pair",)
    fine = Mesh(mesh.devices.reshape([SIZES[name] for name in names]), names)
    placed = (
        P(SEQ),
        P(),
        P(SEQ, "pair"),
        P(None, "pair"),
        P(None, "pair"),
        P(None, "pair"),
        P("pair", None),
        P(None, None, "pair"),
        P(None, "pair"),
        P(SEQ, None, "pair"),
    )
    return jax.shard_map(
        on_device,
        mesh=fine,
        in_specs=placed,
        out_specs=(P(SEQ, "pair"), P(SEQ, None, "pair")),
        check_vma=False,
    )
```

```python
import math

import jax
import jax.numpy as jnp
from jax import lax
from jax.experimental import pallas as pl
from jax.experimental.pallas import tpu as pltpu
from jax.sharding import Mesh
from jax.sharding import PartitionSpec as P

HQK = 128
HV = 192
KS_STEM = 15
KS_CONV = 5
STEM_POOL = 64
PAIR_POOL = 16
EDGES = (1, 2, 3, 4, 6, 8, 12, 16, 24, 32, 48, 64, 96, 128, 192, 256, 384)

SIZES = {"zl": 2, "y": 8, "xh": 2, "xl": 2, "core": 2, "pair": 4}
SEQ = ("zl", "y", "xh", "xl", "core")
SHARE = ("zl", "xl", "core")
SPREAD = ("xh", "xl", "core")
LINE = ("zl", "y")
N_SEQ = math.prod(SIZES[name] for name in SEQ)
N_SHARE = math.prod(SIZES[name] for name in SHARE)
N_PAIR = SIZES["pair"]
N_SPREAD = math.prod(SIZES[name] for name in SPREAD)
N_LINE = math.prod(SIZES[name] for name in LINE)

ROWS = 32
EXT_PAD = 40
EDGE = 4
RUN = 4
VMEM = 48 * 1024 * 1024


def params(**kw):
    return pltpu.CompilerParams(vmem_limit_bytes=VMEM, **kw)


def whole(count):
    return [pl.BlockSpec(memory_space=pltpu.VMEM) for _ in range(count)]


def gelu(x):
    return 0.5 * x * (1.0 + jnp.tanh(math.sqrt(2.0 / math.pi) * (x + 0.044715 * (x * x * x))))


def onehot_rows(codes, first, count):
    length = codes.shape[1]
    start = (length - first - KS_STEM // 2) % length
    shifted = pltpu.roll(jnp.broadcast_to(codes, (16, length)), start, 1, stride=1, stride_axis=0)
    shifted = shifted[:, :count]
    return jnp.concatenate(
        [(shifted == base + 1).astype(jnp.float32) for base in range(4)], axis=0
    ).astype(jnp.bfloat16)


def pooled_rows(onehot, weight):
    hidden = lax.dot_general(
        onehot, weight, (((0,), (0,)), ((), ())), preferred_element_type=jnp.float32
    ).reshape(onehot.shape[1] // STEM_POOL, STEM_POOL, weight.shape[1])
    high = gelu(jnp.max(hidden, axis=1))
    low = gelu(jnp.min(hidden, axis=1))
    return jnp.maximum(high, low)


def stem_kernel(tokens_ref, weight_ref, out_ref):
    onehot = onehot_rows(tokens_ref[...] + 1, 0, tokens_ref.shape[1])
    weight = weight_ref[...]
    step = 8
    for at in range(0, ROWS, step):
        part = onehot[:, at * STEM_POOL : (at + step) * STEM_POOL]
        out_ref[at : at + step, :] = pooled_rows(part, weight)


def stem(tokens, weight):
    return pl.pallas_call(
        stem_kernel,
        out_shape=jax.ShapeDtypeStruct((ROWS, weight.shape[1]), jnp.float32),
        in_specs=whole(2),
        out_specs=whole(1)[0],
        compiler_params=params(),
        cost_estimate=pl.CostEstimate(flops=2 * 2048 * 64 * 768, bytes_accessed=200000, transcendentals=0),
    )(tokens, weight)


def pack_kernel(weight_ref, tokens_ref, out_ref, wide):
    taps, width = weight_ref.shape
    share = width // N_SHARE
    half = taps // 2
    even, odd = [], []
    for part in range(wide.shape[0]):
        lanes = weight_ref[:, part * HQK : (part + 1) * HQK]
        wide[part, :taps, :] = lanes.astype(jnp.float32)
        wide[part, taps:, :] = jnp.zeros((wide.shape[1] - taps, HQK), jnp.float32)
        even.append(wide[part, pl.ds(0, half + 1, stride=2), :])
        odd.append(wide[part, pl.ds(1, half + 1, stride=2), :])
    even, odd = jnp.concatenate(even, axis=1), jnp.concatenate(odd, axis=1)
    lane = lax.broadcasted_iota(jnp.int32, (half + 1, HQK), 1)
    row = lax.broadcasted_iota(jnp.int32, (half + 1, HQK), 0)
    codes = (tokens_ref[...] + 1).astype(jnp.float32)
    last = codes.shape[0] - 1
    line = [jnp.broadcast_to(codes[at : at + 1, :], lane.shape) for at in (0, 1, last - 1, last)]
    outer = jnp.where(lane >= HQK - 7, line[2], pltpu.roll(line[1], 96, 1))
    for index in range(4):
        outer = jnp.where(row == index, pltpu.roll(line[3], (96 - 32 * index) % HQK, 1), outer)
    blocks = []
    for index in range(N_SHARE):
        low = pltpu.roll(even, (width - index * share) % width, 1)[:, :HQK]
        high = pltpu.roll(odd, (width - index * share + share) % width, 1)[:, :HQK]
        block = jnp.where(lane < share, low, jnp.where(lane < 2 * share, high, outer))
        blocks.append(jnp.where(row == half, line[0], block).astype(jnp.bfloat16))
    for place in range(N_SEQ):
        at, index, base = place, 0, 1
        for name in reversed(SEQ):
            if name in SHARE:
                index, base = index + base * (at % SIZES[name]), base * SIZES[name]
            at = at // SIZES[name]
        out_ref[place] = blocks[index]


def pack(weight, tokens):
    taps, width = weight.shape
    return pl.pallas_call(
        pack_kernel,
        out_shape=jax.ShapeDtypeStruct((N_SEQ, taps // 2 + 1, HQK), jnp.bfloat16),
        in_specs=whole(2),
        out_specs=whole(1)[0],
        scratch_shapes=[pltpu.VMEM((width // HQK, taps + 2, HQK), jnp.float32)],
        compiler_params=params(),
    )(weight, tokens)


def border_codes(held_ref, right):
    before = held_ref[jnp.maximum(right - 1, 0)].astype(jnp.float32)
    after = held_ref[jnp.minimum(right, N_SEQ - 1)].astype(jnp.float32)
    before = jnp.where(right > 0, before, 0.0)
    after = jnp.where(right < N_SEQ, after, 0.0)
    lane = lax.broadcasted_iota(jnp.int32, (1, HQK), 1)
    tail = jnp.zeros((1, HQK), jnp.float32)
    for index in range(4):
        part = pltpu.roll(before, (32 * index + 32) % HQK, 1)[index : index + 1, :]
        tail = jnp.where(lane // 32 == index, part, tail)
    return jnp.concatenate(
        [before[4:5, :], tail, after[15:16, :], pltpu.roll(after, 32, 1)[4:5, :]], axis=1
    )


def conv_kernel(place_ref, section_ref, held_ref, stem_ref, out_ref, weights, edges, wide, act, best):
    count, rows, _ = held_ref.shape
    for source in range(count):
        block = held_ref[source].astype(jnp.float32)
        weights[source * (rows - 1) : (source + 1) * (rows - 1), :] = block[: rows - 1, :]
    first = ((place_ref[0] & (N_SEQ // 2 - 1)) // RUN) * RUN
    borders = [run * (N_SEQ // 2) + first + index for run in range(2) for index in range(RUN + 1)]
    for at in range(0, len(borders), 2):
        onehot = jnp.concatenate(
            [
                onehot_rows(border_codes(held_ref, right), 128, EDGE * STEM_POOL)
                for right in borders[at : at + 2]
            ],
            axis=1,
        )
        made = pooled_rows(onehot, stem_ref[...])
        place = lax.broadcasted_iota(jnp.int32, made.shape, 0)
        right = jnp.where(place < EDGE, borders[at], borders[at + 1])
        place = right * ROWS - EDGE // 2 + place % EDGE
        inside = (place >= 0) & (place < count * ROWS)
        edges[at * EDGE : (at + 2) * EDGE, :] = jnp.where(inside, made, 0.0)
    windows, _, channels = section_ref.shape
    half = channels // 2
    columns = out_ref.shape[2] // 8
    for window in range(windows):
        at = (window // RUN * (RUN + 1) + window % RUN) * EDGE
        wide[window, 3 : ROWS + 1, :] = section_ref[window].astype(jnp.float32)[1 : ROWS - 1, :]
        wide[window, 0:3, :] = edges[at : at + 3, :]
        wide[window, ROWS + 1 : ROWS + 4, :] = edges[at + EDGE + 1 : at + EDGE + 4, :]
    even, odd = None, None
    for tap in range(KS_CONV):
        rows = wide[:, tap : tap + ROWS, :].astype(jnp.bfloat16).reshape(windows * ROWS, channels)
        weight = weights[tap * half : (tap + 1) * half, :].astype(jnp.bfloat16)
        term = jnp.dot(rows[:, :half], weight, preferred_element_type=jnp.float32)
        even = term if even is None else even + term
        term = jnp.dot(rows[:, half:], weight, preferred_element_type=jnp.float32)
        odd = term if odd is None else odd + term
    act[...] = jnp.zeros(act.shape, jnp.float32)
    act[:, :columns] = gelu(even[:, :columns] + odd[:, columns : 2 * columns])
    count = windows * ROWS // 2
    best[...] = jnp.maximum(act[pl.ds(0, count, stride=2), :], act[pl.ds(1, count, stride=2), :])
    flat = None
    for index in range(8):
        part = best[pl.ds(index, count // 8, stride=8), :]
        part = jnp.pad(part, ((0, 0), (0, 8 * columns - part.shape[1])))
        part = pltpu.roll(part, index * columns, 1)
        flat = part if flat is None else flat + part
    for window in range(windows):
        block = flat[2 * window : 2 * window + 2, :].astype(jnp.bfloat16)
        for index in range(N_PAIR):
            out_ref[window * N_PAIR + index] = block


def conv(place, section, held, stem_weight, columns):
    windows, _, channels = section.shape
    borders = windows // RUN * (RUN + 1)
    return pl.pallas_call(
        conv_kernel,
        out_shape=jax.ShapeDtypeStruct((windows * N_PAIR, 2, 8 * columns), jnp.bfloat16),
        in_specs=[pl.BlockSpec(memory_space=pltpu.SMEM)] + whole(3),
        out_specs=whole(1)[0],
        scratch_shapes=[
            pltpu.VMEM((held.shape[0] * (held.shape[1] - 1), HQK), jnp.float32),
            pltpu.VMEM((borders * EDGE, channels), jnp.float32),
            pltpu.VMEM((windows, EXT_PAD, channels), jnp.float32),
            pltpu.VMEM((windows * ROWS, HQK), jnp.float32),
            pltpu.VMEM((windows * ROWS // 2, HQK), jnp.float32),
        ],
        compiler_params=params(),
    )(place, section, held, stem_weight)


def project_kernel(trunk_ref, w_query_ref, w_key_ref, w_value_ref, query_ref, kv_ref):
    trunk = trunk_ref[...]
    query, key, value = [
        jnp.dot(trunk, ref[...], preferred_element_type=jnp.float32).astype(jnp.bfloat16)
        for ref in (w_query_ref, w_key_ref, w_value_ref)
    ]
    query_ref[...] = query
    rest = jnp.zeros((trunk.shape[0], kv_ref.shape[2] - HQK - HV), jnp.bfloat16)
    for index in range(N_LINE):
        kv_ref[index, :, :HQK] = key
        kv_ref[index, :, HQK : HQK + HV] = value
        kv_ref[index, :, HQK + HV :] = rest


def project(trunk, w_query, w_key, w_value):
    count = trunk.shape[0]
    return pl.pallas_call(
        project_kernel,
        out_shape=(
            jax.ShapeDtypeStruct((count, HQK), jnp.bfloat16),
            jax.ShapeDtypeStruct((N_LINE, count, 3 * HQK), jnp.bfloat16),
        ),
        in_specs=whole(4),
        out_specs=tuple(whole(2)),
        compiler_params=params(),
    )(trunk, w_query, w_key, w_value)


def split(x):
    parts = []
    for _ in range(3):
        part = x.astype(jnp.bfloat16).astype(jnp.float32)
        parts.append(part)
        x = x - part
    return parts


def attention_kernel(place_ref, query_ref, kv_ref, out_ref):
    scale = 1.0 / math.sqrt(HQK)
    scores = (
        lax.dot_general(
            query_ref[...],
            kv_ref[:, :HQK],
            (((1,), (1,)), ((), ())),
            preferred_element_type=jnp.float32,
        )
        * scale
    )
    top = jnp.max(scores, axis=1, keepdims=True)
    expo = jnp.exp(scores - top)
    total = jnp.sum(expo, axis=1, keepdims=True)
    mixed = jnp.dot(expo.astype(jnp.bfloat16), kv_ref[:, HQK:], preferred_element_type=jnp.float32)
    lane = lax.broadcasted_iota(jnp.int32, mixed.shape, 1)
    for index, column in enumerate(split(top) + split(total)):
        mixed = jnp.where(lane == HV + index, column, mixed)
    mixed = mixed.astype(jnp.bfloat16)
    groups, count, _ = out_ref.shape
    for index in range(groups):
        out_ref[place_ref[0] ^ index] = mixed[index * count : (index + 1) * count, :]


def attention(place, query, kv):
    groups = N_SPREAD
    count, width = query.shape[0] // groups, kv.shape[1] - HQK
    return pl.pallas_call(
        attention_kernel,
        out_shape=jax.ShapeDtypeStruct((groups, count, width), jnp.bfloat16),
        in_specs=[pl.BlockSpec(memory_space=pltpu.SMEM)] + whole(2),
        out_specs=whole(1)[0],
        compiler_params=params(),
    )(place, query, kv)


def combine_kernel(parts_ref, w_out_ref, out_ref):
    parts = parts_ref[...].astype(jnp.float32)
    top = jnp.sum(parts[:, :, HV : HV + 3], axis=2, keepdims=True)
    gain = jnp.exp(top - jnp.max(top, axis=0, keepdims=True))
    total = jnp.sum(gain * jnp.sum(parts[:, :, HV + 3 : HV + 6], axis=2, keepdims=True), axis=0)
    mixed = (jnp.sum(gain * parts, axis=0) / total)[:, :HV].astype(jnp.bfloat16)
    term = jnp.dot(mixed, w_out_ref[...], preferred_element_type=jnp.float32)
    mean = jnp.sum(term, axis=0, keepdims=True) * (1.0 / PAIR_POOL)
    width = term.shape[1] // N_PAIR
    count = term.shape[0]
    tail = jnp.concatenate(
        [mean[:, c * width : (c + 1) * width] for c in range(N_PAIR)]
        + [jnp.zeros((8 - N_PAIR, width), jnp.float32)],
        axis=0,
    )
    for c in range(N_PAIR):
        out_ref[c, :count, :] = term[:, c * width : (c + 1) * width]
        out_ref[c, count:, :] = tail


def combine(parts, w_out):
    count = parts.shape[1]
    width = w_out.shape[1] // N_PAIR
    return pl.pallas_call(
        combine_kernel,
        out_shape=jax.ShapeDtypeStruct((N_PAIR, count + 8, width), jnp.float32),
        in_specs=whole(2),
        out_specs=whole(1)[0],
        compiler_params=params(),
    )(parts, w_out)


def close_kernel(terms_ref, own_ref, trunk_ref, w_pair_ref, pair_ref, seq_ref, rows_ref, every_ref):
    count, width = own_ref.shape
    total = jnp.sum(terms_ref[...], axis=0)
    seq_ref[...] = (own_ref[...].astype(jnp.float32) + total[:count, :]).astype(jnp.bfloat16)
    trunk_mean = jnp.sum(trunk_ref[...].astype(jnp.float32), axis=0, keepdims=True) * (1.0 / PAIR_POOL)
    rows = None
    for c in range(N_PAIR):
        pooled = trunk_mean[:, c * width : (c + 1) * width] + total[count + c : count + c + 1, :]
        term = jnp.dot(
            jnp.broadcast_to(pooled, (8, width)).astype(jnp.bfloat16),
            w_pair_ref[c * width : (c + 1) * width, :],
            preferred_element_type=jnp.float32,
        )
        rows = term if rows is None else rows + term
    rows_ref[...] = rows
    mine = pair_ref[0].astype(jnp.float32)
    factors = jnp.broadcast_to(rows[:1], (mine.shape[0], rows.shape[1]))
    every_ref[...] = jnp.concatenate([factors, mine], axis=1)


def close(terms, own, trunk, w_pair, pair_in):
    return pl.pallas_call(
        close_kernel,
        out_shape=(
            jax.ShapeDtypeStruct(own.shape, jnp.bfloat16),
            jax.ShapeDtypeStruct((8, w_pair.shape[1]), jnp.float32),
            jax.ShapeDtypeStruct((pair_in.shape[1], w_pair.shape[1] + pair_in.shape[2]), jnp.float32),
        ),
        in_specs=whole(5),
        out_specs=tuple(whole(3)),
        compiler_params=params(),
    )(terms, own, trunk, w_pair, pair_in)


def distance_bias(row, cols, pair_bias):
    delta = jnp.abs(row - cols)
    bins = jnp.zeros(delta.shape, jnp.int32)
    for edge in EDGES:
        bins = bins + (delta >= edge).astype(jnp.int32)
    labels = jnp.arange(pair_bias.shape[0], dtype=jnp.int32)
    onehot = (bins[:, None] == labels[None, :]).astype(jnp.bfloat16)
    return jnp.dot(onehot, pair_bias, preferred_element_type=jnp.float32)


def exchange(blocks, axes):
    return lax.all_to_all(blocks, axes, split_axis=0, concat_axis=0, tiled=True)


def on_device(tokens, w_stem, w_conv, w_query, w_key, w_value, w_out, w_pair, pair_bias, pair_in):
    place = lax.axis_index(SEQ)
    pair_place = lax.axis_index("pair")

    taps, width = w_conv.shape
    share = width // N_SHARE
    held = exchange(pack(w_conv, tokens.reshape(-1, HQK)), SEQ)

    source = jnp.arange(w_stem.shape[1]).reshape(2, -1)
    source = (2 * (source % source.shape[1]) + jnp.arange(2)[:, None]).reshape(-1)
    order = (jnp.arange(w_stem.shape[1])[:, None] == source[None, :]).astype(jnp.bfloat16)
    stem_weight = jnp.dot(w_stem, order, preferred_element_type=jnp.float32).astype(jnp.bfloat16)
    stem_weight = stem_weight.reshape(KS_STEM, 4, -1)[::-1].transpose(1, 0, 2)
    stem_weight = jnp.pad(stem_weight, ((0, 0), (0, 1), (0, 0))).reshape(64, -1)
    section = stem(tokens.reshape(1, -1), stem_weight).astype(jnp.bfloat16)
    sections = lax.all_gather(section, SHARE, axis=0, tiled=False)

    parts = exchange(conv(place.astype(jnp.int32)[None], sections, held, stem_weight, share), SHARE + ("pair",))
    count = ROWS // 2
    trunk = parts.reshape(N_SHARE, N_PAIR, count, share).transpose(2, 1, 0, 3)
    trunk = trunk.reshape(count, N_PAIR * width)

    query, kv = project(trunk, w_query, w_key, w_value)
    for name in reversed(SPREAD):
        other = lax.ppermute(query, name, [(0, 1), (1, 0)])
        query = jnp.concatenate([query, other], axis=0)
    kv = exchange(kv, LINE).reshape(N_LINE * count, kv.shape[2])
    spread = lax.axis_index(SPREAD).astype(jnp.int32)[None]
    parts = exchange(attention(spread, query, kv), SPREAD)
    terms = exchange(combine(parts, w_out), ("pair",))

    own = lax.dynamic_slice_in_dim(trunk, pair_place * width, width, 1)
    factors = jnp.concatenate([w_pair[0], w_pair[1]], axis=1)
    seq_out, rows, every = close(terms, own, trunk, factors, pair_in)
    channels = pair_in.shape[2]
    mine = pair_in[0].astype(jnp.float32)
    rows = rows[:1]
    every = exchange(every[:, None], SEQ)[:, 0]
    mirror = every[:, 2 * channels :]

    cols = jnp.arange(N_SEQ, dtype=jnp.int32)
    bias = distance_bias(place.astype(jnp.int32), cols, pair_bias)
    cross = rows[:, :channels] * every[:, channels : 2 * channels]
    cross = cross + every[:, :channels] * rows[:, channels:]
    pair_out = (0.5 * (mine + mirror + cross) + bias).astype(jnp.bfloat16)[None]
    return (seq_out, pair_out)


def solution(mesh):
    names = SEQ + ("pair",)
    fine = Mesh(mesh.devices.reshape([SIZES[name] for name in names]), names)
    placed = (
        P(SEQ),
        P(),
        P(SEQ, "pair"),
        P(None, "pair"),
        P(None, "pair"),
        P(None, "pair"),
        P("pair", None),
        P(None, None, "pair"),
        P(None, "pair"),
        P(SEQ, None, "pair"),
    )
    return jax.shard_map(
        on_device,
        mesh=fine,
        in_specs=placed,
        out_specs=(P(SEQ, "pair"), P(SEQ, None, "pair")),
        check_vma=False,
    )
```

```python
import math

import jax
import jax.numpy as jnp
from jax import lax
from jax.experimental import pallas as pl
from jax.experimental.pallas import tpu as pltpu
from jax.sharding import Mesh
from jax.sharding import PartitionSpec as P

HQK = 128
HV = 192
KS_STEM = 15
KS_CONV = 5
STEM_POOL = 64
PAIR_POOL = 16
EDGES = (1, 2, 3, 4, 6, 8, 12, 16, 24, 32, 48, 64, 96, 128, 192, 256, 384)

SIZES = {"zl": 2, "y": 8, "xh": 2, "xl": 2, "core": 2, "pair": 4}
SEQ = ("zl", "y", "xh", "xl", "core")
SHARE = ("zl", "xl", "core")
SPREAD = ("xh", "xl", "core")
LINE = ("zl", "y")
N_SEQ = math.prod(SIZES[name] for name in SEQ)
N_SHARE = math.prod(SIZES[name] for name in SHARE)
N_PAIR = SIZES["pair"]
N_SPREAD = math.prod(SIZES[name] for name in SPREAD)
N_LINE = math.prod(SIZES[name] for name in LINE)

ROWS = 32
EXT_PAD = 40
EDGE = 4
RUN = 4
VMEM = 48 * 1024 * 1024


def params(**kw):
    return pltpu.CompilerParams(vmem_limit_bytes=VMEM, **kw)


def whole(count):
    return [pl.BlockSpec(memory_space=pltpu.VMEM) for _ in range(count)]


def gelu(x):
    return 0.5 * x * (1.0 + jnp.tanh(math.sqrt(2.0 / math.pi) * (x + 0.044715 * (x * x * x))))


def onehot_rows(codes, first, count):
    length = codes.shape[1]
    start = (length - first - KS_STEM // 2) % length
    shifted = pltpu.roll(jnp.broadcast_to(codes, (16, length)), start, 1, stride=1, stride_axis=0)
    shifted = shifted[:, :count]
    return jnp.concatenate(
        [(shifted == base + 1).astype(jnp.float32) for base in range(4)], axis=0
    ).astype(jnp.bfloat16)


def pooled_rows(onehot, weight):
    hidden = lax.dot_general(
        onehot, weight, (((0,), (0,)), ((), ())), preferred_element_type=jnp.float32
    ).reshape(onehot.shape[1] // STEM_POOL, STEM_POOL, weight.shape[1])
    high = gelu(jnp.max(hidden, axis=1))
    low = gelu(jnp.min(hidden, axis=1))
    return jnp.maximum(high, low)


def stem_kernel(tokens_ref, weight_ref, out_ref):
    onehot = onehot_rows(tokens_ref[...] + 1, 0, tokens_ref.shape[1])
    weight = weight_ref[...]
    step = 8
    for at in range(0, ROWS, step):
        part = onehot[:, at * STEM_POOL : (at + step) * STEM_POOL]
        out_ref[at : at + step, :] = pooled_rows(part, weight)


def stem(tokens, weight):
    return pl.pallas_call(
        stem_kernel,
        out_shape=jax.ShapeDtypeStruct((ROWS, weight.shape[1]), jnp.float32),
        in_specs=whole(2),
        out_specs=whole(1)[0],
        compiler_params=params(),
        cost_estimate=pl.CostEstimate(flops=2 * 2048 * 64 * 768, bytes_accessed=200000, transcendentals=0),
    )(tokens, weight)


def start_kernel(weight_ref, stem_ref, tokens_hbm, out_ref, made_ref, wide, tokens_ref, arrived):
    copy = pltpu.make_async_copy(tokens_hbm, tokens_ref, arrived)
    copy.start()
    rows, channels = stem_ref.shape
    row = lax.broadcasted_iota(jnp.int32, (64, rows), 0)
    column = lax.broadcasted_iota(jnp.int32, (64, rows), 1)
    picked = (column == (KS_STEM - 1 - row % 16) * 4 + row // 16) & (row % 16 < KS_STEM)
    picked = picked.astype(jnp.float32).astype(jnp.bfloat16)
    made = jnp.dot(picked, stem_ref[...], preferred_element_type=jnp.float32).astype(jnp.bfloat16)
    half = channels // 2
    row = lax.broadcasted_iota(jnp.int32, (channels, half), 0)
    column = lax.broadcasted_iota(jnp.int32, (channels, half), 1)
    for odd in range(2):
        order = (row == 2 * column + odd).astype(jnp.float32).astype(jnp.bfloat16)
        part = jnp.dot(made, order, preferred_element_type=jnp.float32)
        made_ref[:, odd * half : (odd + 1) * half] = part.astype(jnp.bfloat16)
    taps, width = weight_ref.shape
    share = width // N_SHARE
    half = taps // 2
    even, odd = [], []
    for part in range(wide.shape[0]):
        lanes = weight_ref[:, part * HQK : (part + 1) * HQK]
        wide[part, :taps, :] = lanes.astype(jnp.float32)
        wide[part, taps:, :] = jnp.zeros((wide.shape[1] - taps, HQK), jnp.float32)
        even.append(wide[part, pl.ds(0, half + 1, stride=2), :])
        odd.append(wide[part, pl.ds(1, half + 1, stride=2), :])
    even, odd = jnp.concatenate(even, axis=1), jnp.concatenate(odd, axis=1)
    lane = lax.broadcasted_iota(jnp.int32, (half + 1, HQK), 1)
    row = lax.broadcasted_iota(jnp.int32, (half + 1, HQK), 0)
    copy.wait()
    codes = (tokens_ref[...] + 1).astype(jnp.float32)
    last = codes.shape[0] - 1
    line = [jnp.broadcast_to(codes[at : at + 1, :], lane.shape) for at in (0, 1, last - 1, last)]
    outer = jnp.where(lane >= HQK - 7, line[2], pltpu.roll(line[1], 96, 1))
    for index in range(4):
        outer = jnp.where(row == index, pltpu.roll(line[3], (96 - 32 * index) % HQK, 1), outer)
    blocks = []
    for index in range(N_SHARE):
        low = pltpu.roll(even, (width - index * share) % width, 1)[:, :HQK]
        high = pltpu.roll(odd, (width - index * share + share) % width, 1)[:, :HQK]
        block = jnp.where(lane < share, low, jnp.where(lane < 2 * share, high, outer))
        blocks.append(jnp.where(row == half, line[0], block).astype(jnp.bfloat16))
    for place in range(N_SEQ):
        at, index, base = place, 0, 1
        for name in reversed(SEQ):
            if name in SHARE:
                index, base = index + base * (at % SIZES[name]), base * SIZES[name]
            at = at // SIZES[name]
        out_ref[place] = blocks[index]


def start(weight, stem_weight, tokens):
    taps, width = weight.shape
    return pl.pallas_call(
        start_kernel,
        out_shape=(
            jax.ShapeDtypeStruct((N_SEQ, taps // 2 + 1, HQK), jnp.bfloat16),
            jax.ShapeDtypeStruct((64, stem_weight.shape[1]), jnp.bfloat16),
        ),
        in_specs=whole(2) + [pl.BlockSpec(memory_space=pl.ANY)],
        out_specs=tuple(whole(2)),
        scratch_shapes=[
            pltpu.VMEM((width // HQK, taps + 2, HQK), jnp.float32),
            pltpu.VMEM(tokens.shape, jnp.int32),
            pltpu.SemaphoreType.DMA,
        ],
        compiler_params=params(),
    )(weight, stem_weight, tokens)


def border_codes(held_ref, right):
    before = held_ref[jnp.maximum(right - 1, 0)].astype(jnp.float32)
    after = held_ref[jnp.minimum(right, N_SEQ - 1)].astype(jnp.float32)
    before = jnp.where(right > 0, before, 0.0)
    after = jnp.where(right < N_SEQ, after, 0.0)
    lane = lax.broadcasted_iota(jnp.int32, (1, HQK), 1)
    tail = jnp.zeros((1, HQK), jnp.float32)
    for index in range(4):
        part = pltpu.roll(before, (32 * index + 32) % HQK, 1)[index : index + 1, :]
        tail = jnp.where(lane // 32 == index, part, tail)
    return jnp.concatenate(
        [before[4:5, :], tail, after[15:16, :], pltpu.roll(after, 32, 1)[4:5, :]], axis=1
    )


def conv_kernel(place_ref, section_ref, held_ref, stem_ref, out_ref, weights, edges, wide, act, best):
    count, rows, _ = held_ref.shape
    for source in range(count):
        block = held_ref[source].astype(jnp.float32)
        weights[source * (rows - 1) : (source + 1) * (rows - 1), :] = block[: rows - 1, :]
    first = ((place_ref[0] & (N_SEQ // 2 - 1)) // RUN) * RUN
    borders = [run * (N_SEQ // 2) + first + index for run in range(2) for index in range(RUN + 1)]
    for at in range(0, len(borders), 2):
        onehot = jnp.concatenate(
            [
                onehot_rows(border_codes(held_ref, right), 128, EDGE * STEM_POOL)
                for right in borders[at : at + 2]
            ],
            axis=1,
        )
        made = pooled_rows(onehot, stem_ref[...])
        place = lax.broadcasted_iota(jnp.int32, made.shape, 0)
        right = jnp.where(place < EDGE, borders[at], borders[at + 1])
        place = right * ROWS - EDGE // 2 + place % EDGE
        inside = (place >= 0) & (place < count * ROWS)
        edges[at * EDGE : (at + 2) * EDGE, :] = jnp.where(inside, made, 0.0)
    windows, _, channels = section_ref.shape
    half = channels // 2
    columns = out_ref.shape[2] // 8
    for window in range(windows):
        at = (window // RUN * (RUN + 1) + window % RUN) * EDGE
        wide[window, 3 : ROWS + 1, :] = section_ref[window].astype(jnp.float32)[1 : ROWS - 1, :]
        wide[window, 0:3, :] = edges[at : at + 3, :]
        wide[window, ROWS + 1 : ROWS + 4, :] = edges[at + EDGE + 1 : at + EDGE + 4, :]
    even, odd = None, None
    for tap in range(KS_CONV):
        rows = wide[:, tap : tap + ROWS, :].astype(jnp.bfloat16).reshape(windows * ROWS, channels)
        weight = weights[tap * half : (tap + 1) * half, :].astype(jnp.bfloat16)
        term = jnp.dot(rows[:, :half], weight, preferred_element_type=jnp.float32)
        even = term if even is None else even + term
        term = jnp.dot(rows[:, half:], weight, preferred_element_type=jnp.float32)
        odd = term if odd is None else odd + term
    act[...] = jnp.zeros(act.shape, jnp.float32)
    act[:, :columns] = gelu(even[:, :columns] + odd[:, columns : 2 * columns])
    count = windows * ROWS // 2
    best[...] = jnp.maximum(act[pl.ds(0, count, stride=2), :], act[pl.ds(1, count, stride=2), :])
    flat = None
    for index in range(8):
        part = best[pl.ds(index, count // 8, stride=8), :]
        part = jnp.pad(part, ((0, 0), (0, 8 * columns - part.shape[1])))
        part = pltpu.roll(part, index * columns, 1)
        flat = part if flat is None else flat + part
    for window in range(windows):
        block = flat[window // 2 * 4 : window // 2 * 4 + 4, :].astype(jnp.bfloat16)
        for index in range(N_PAIR):
            out_ref[window * N_PAIR + index] = block


def conv(place, section, held, stem_weight, columns):
    windows, _, channels = section.shape
    borders = windows // RUN * (RUN + 1)
    return pl.pallas_call(
        conv_kernel,
        out_shape=jax.ShapeDtypeStruct((windows * N_PAIR, 4, 8 * columns), jnp.bfloat16),
        in_specs=[pl.BlockSpec(memory_space=pltpu.SMEM)] + whole(3),
        out_specs=whole(1)[0],
        scratch_shapes=[
            pltpu.VMEM((held.shape[0] * (held.shape[1] - 1), HQK), jnp.float32),
            pltpu.VMEM((borders * EDGE, channels), jnp.float32),
            pltpu.VMEM((windows, EXT_PAD, channels), jnp.float32),
            pltpu.VMEM((windows * ROWS, HQK), jnp.float32),
            pltpu.VMEM((windows * ROWS // 2, HQK), jnp.float32),
        ],
        compiler_params=params(),
    )(place, section, held, stem_weight)


def project_kernel(core_ref, trunk_ref, w_query_ref, w_key_ref, w_value_ref, query_ref, kv_ref, own_ref):
    trunk = trunk_ref[...]
    first = core_ref[0] == 0
    count = own_ref.shape[0]
    query_ref[...] = jnp.dot(trunk, w_query_ref[...], preferred_element_type=jnp.float32).astype(jnp.bfloat16)
    wide = trunk.astype(jnp.float32)
    own = jnp.where(first, wide[:count], wide[count:]).astype(jnp.bfloat16)
    own_ref[...] = own
    key, value = [
        jnp.dot(own, ref[...], preferred_element_type=jnp.float32).astype(jnp.bfloat16)
        for ref in (w_key_ref, w_value_ref)
    ]
    rest = jnp.zeros((count, kv_ref.shape[2] - HQK - HV), jnp.bfloat16)
    for index in range(N_LINE):
        kv_ref[index, :, :HQK] = key
        kv_ref[index, :, HQK : HQK + HV] = value
        kv_ref[index, :, HQK + HV :] = rest


def project(core, trunk, w_query, w_key, w_value):
    count = trunk.shape[0] // 2
    return pl.pallas_call(
        project_kernel,
        out_shape=(
            jax.ShapeDtypeStruct((2 * count, HQK), jnp.bfloat16),
            jax.ShapeDtypeStruct((N_LINE, count, 3 * HQK), jnp.bfloat16),
            jax.ShapeDtypeStruct((count, trunk.shape[1]), jnp.bfloat16),
        ),
        in_specs=[pl.BlockSpec(memory_space=pltpu.SMEM)] + whole(4),
        out_specs=tuple(whole(3)),
        compiler_params=params(),
    )(core, trunk, w_query, w_key, w_value)


def split(x):
    parts = []
    for _ in range(3):
        part = x.astype(jnp.bfloat16).astype(jnp.float32)
        parts.append(part)
        x = x - part
    return parts


def attention_kernel(place_ref, query_ref, kv_ref, out_ref):
    scale = 1.0 / math.sqrt(HQK)
    scores = (
        lax.dot_general(
            query_ref[...],
            kv_ref[:, :HQK],
            (((1,), (1,)), ((), ())),
            preferred_element_type=jnp.float32,
        )
        * scale
    )
    top = jnp.max(scores, axis=1, keepdims=True)
    expo = jnp.exp(scores - top)
    total = jnp.sum(expo, axis=1, keepdims=True)
    mixed = jnp.dot(expo.astype(jnp.bfloat16), kv_ref[:, HQK:], preferred_element_type=jnp.float32)
    lane = lax.broadcasted_iota(jnp.int32, mixed.shape, 1)
    for index, column in enumerate(split(top) + split(total)):
        mixed = jnp.where(lane == HV + index, column, mixed)
    mixed = mixed.astype(jnp.bfloat16)
    groups, count, _ = out_ref.shape
    for index in range(groups):
        place = ((place_ref[0] >> 1) ^ (index // 2)) * 2 + index % 2
        out_ref[place] = mixed[index * count : (index + 1) * count, :]


def attention(place, query, kv):
    groups = N_SPREAD
    count, width = query.shape[0] // groups, kv.shape[1] - HQK
    return pl.pallas_call(
        attention_kernel,
        out_shape=jax.ShapeDtypeStruct((groups, count, width), jnp.bfloat16),
        in_specs=[pl.BlockSpec(memory_space=pltpu.SMEM)] + whole(2),
        out_specs=whole(1)[0],
        compiler_params=params(),
    )(place, query, kv)


def combine_kernel(parts_ref, w_out_ref, out_ref):
    parts = parts_ref[...].astype(jnp.float32)
    top = jnp.sum(parts[:, :, HV : HV + 3], axis=2, keepdims=True)
    gain = jnp.exp(top - jnp.max(top, axis=0, keepdims=True))
    total = jnp.sum(gain * jnp.sum(parts[:, :, HV + 3 : HV + 6], axis=2, keepdims=True), axis=0)
    mixed = (jnp.sum(gain * parts, axis=0) / total)[:, :HV].astype(jnp.bfloat16)
    term = jnp.dot(mixed, w_out_ref[...], preferred_element_type=jnp.float32)
    mean = jnp.sum(term, axis=0, keepdims=True) * (1.0 / PAIR_POOL)
    width = term.shape[1] // N_PAIR
    count = term.shape[0]
    tail = jnp.concatenate(
        [mean[:, c * width : (c + 1) * width] for c in range(N_PAIR)]
        + [jnp.zeros((8 - N_PAIR, width), jnp.float32)],
        axis=0,
    )
    for c in range(N_PAIR):
        out_ref[c, :count, :] = term[:, c * width : (c + 1) * width]
        out_ref[c, count:, :] = tail


def combine(parts, w_out):
    count = parts.shape[1]
    width = w_out.shape[1] // N_PAIR
    return pl.pallas_call(
        combine_kernel,
        out_shape=jax.ShapeDtypeStruct((N_PAIR, count + 8, width), jnp.float32),
        in_specs=whole(2),
        out_specs=whole(1)[0],
        compiler_params=params(),
    )(parts, w_out)


def close_kernel(terms_ref, own_ref, trunk_ref, w_pair_ref, pair_ref, seq_ref, rows_ref, every_ref):
    count, width = own_ref.shape
    total = jnp.sum(terms_ref[...], axis=0)
    seq_ref[...] = (own_ref[...].astype(jnp.float32) + total[:count, :]).astype(jnp.bfloat16)
    trunk_mean = jnp.sum(trunk_ref[...].astype(jnp.float32), axis=0, keepdims=True) * (1.0 / PAIR_POOL)
    rows = None
    for c in range(N_PAIR):
        pooled = trunk_mean[:, c * width : (c + 1) * width] + total[count + c : count + c + 1, :]
        term = jnp.dot(
            jnp.broadcast_to(pooled, (8, width)).astype(jnp.bfloat16),
            w_pair_ref[c * width : (c + 1) * width, :],
            preferred_element_type=jnp.float32,
        )
        rows = term if rows is None else rows + term
    rows_ref[...] = rows
    mine = pair_ref[0].astype(jnp.float32)
    factors = jnp.broadcast_to(rows[:1], (mine.shape[0], rows.shape[1]))
    every_ref[...] = jnp.concatenate([factors, mine], axis=1)


def close(terms, own, trunk, w_pair, pair_in):
    return pl.pallas_call(
        close_kernel,
        out_shape=(
            jax.ShapeDtypeStruct(own.shape, jnp.bfloat16),
            jax.ShapeDtypeStruct((8, w_pair.shape[1]), jnp.float32),
            jax.ShapeDtypeStruct((pair_in.shape[1], w_pair.shape[1] + pair_in.shape[2]), jnp.float32),
        ),
        in_specs=whole(5),
        out_specs=tuple(whole(3)),
        compiler_params=params(),
    )(terms, own, trunk, w_pair, pair_in)


def distance_bias(row, cols, pair_bias):
    delta = jnp.abs(row - cols)
    bins = jnp.zeros(delta.shape, jnp.int32)
    for edge in EDGES:
        bins = bins + (delta >= edge).astype(jnp.int32)
    labels = jnp.arange(pair_bias.shape[0], dtype=jnp.int32)
    onehot = (bins[:, None] == labels[None, :]).astype(jnp.bfloat16)
    return jnp.dot(onehot, pair_bias, preferred_element_type=jnp.float32)


def exchange(blocks, axes):
    return lax.all_to_all(blocks, axes, split_axis=0, concat_axis=0, tiled=True)


def on_device(tokens, w_stem, w_conv, w_query, w_key, w_value, w_out, w_pair, pair_bias, pair_in):
    place = lax.axis_index(SEQ)
    pair_place = lax.axis_index("pair")

    taps, width = w_conv.shape
    share = width // N_SHARE
    blocks, stem_weight = start(w_conv, w_stem, tokens.reshape(-1, HQK))
    held = exchange(blocks, SEQ)

    section = stem(tokens.reshape(1, -1), stem_weight).astype(jnp.bfloat16)
    sections = lax.all_gather(section, SHARE, axis=0, tiled=False)

    parts = exchange(conv(place.astype(jnp.int32)[None], sections, held, stem_weight, share), SHARE + ("pair",))
    count = ROWS // 2
    trunk = parts.reshape(N_SHARE, N_PAIR, 2 * count, share).transpose(2, 1, 0, 3)
    trunk = trunk.reshape(2 * count, N_PAIR * width)

    core = lax.axis_index("core").astype(jnp.int32)[None]
    query, kv, trunk = project(core, trunk, w_query, w_key, w_value)
    chips = SPREAD[:-1]
    others = [
        lax.ppermute(query, chips, [(i, i ^ bits) for i in range(N_SPREAD // 2)])
        for bits in range(1, N_SPREAD // 2)
    ]
    query = jnp.concatenate([query] + others, axis=0)
    kv = exchange(kv, LINE).reshape(N_LINE * count, kv.shape[2])
    spread = lax.axis_index(SPREAD).astype(jnp.int32)[None]
    parts = exchange(attention(spread, query, kv), SPREAD)
    terms = exchange(combine(parts, w_out), ("pair",))

    own = lax.dynamic_slice_in_dim(trunk, pair_place * width, width, 1)
    factors = jnp.concatenate([w_pair[0], w_pair[1]], axis=1)
    seq_out, rows, every = close(terms, own, trunk, factors, pair_in)
    channels = pair_in.shape[2]
    mine = pair_in[0].astype(jnp.float32)
    rows = rows[:1]
    every = exchange(every[:, None], SEQ)[:, 0]
    mirror = every[:, 2 * channels :]

    cols = jnp.arange(N_SEQ, dtype=jnp.int32)
    bias = lax.optimization_barrier(distance_bias(place.astype(jnp.int32), cols, pair_bias))
    cross = rows[:, :channels] * every[:, channels : 2 * channels]
    cross = cross + every[:, :channels] * rows[:, channels:]
    pair_out = (0.5 * (mine + mirror + cross) + bias).astype(jnp.bfloat16)[None]
    return (seq_out, pair_out)


def solution(mesh):
    names = SEQ + ("pair",)
    fine = Mesh(mesh.devices.reshape([SIZES[name] for name in names]), names)
    placed = (
        P(SEQ),
        P(),
        P(SEQ, "pair"),
        P(None, "pair"),
        P(None, "pair"),
        P(None, "pair"),
        P("pair", None),
        P(None, None, "pair"),
        P(None, "pair"),
        P(SEQ, None, "pair"),
    )
    return jax.shard_map(
        on_device,
        mesh=fine,
        in_specs=placed,
        out_specs=(P(SEQ, "pair"), P(SEQ, None, "pair")),
        check_vma=False,
    )
```

```python
import math

import jax
import jax.numpy as jnp
from jax import lax
from jax.experimental import pallas as pl
from jax.experimental.pallas import tpu as pltpu
from jax.sharding import Mesh
from jax.sharding import PartitionSpec as P

HQK = 128
HV = 192
KS_STEM = 15
KS_CONV = 5
STEM_POOL = 64
PAIR_POOL = 16
EDGES = (1, 2, 3, 4, 6, 8, 12, 16, 24, 32, 48, 64, 96, 128, 192, 256, 384)

SIZES = {"zl": 2, "y": 8, "xh": 2, "xl": 2, "core": 2, "pair": 4}
SEQ = ("zl", "y", "xh", "xl", "core")
SHARE = ("zl", "xl", "core")
SPREAD = ("xh", "xl", "core")
LINE = ("zl", "y")
N_SEQ = math.prod(SIZES[name] for name in SEQ)
N_SHARE = math.prod(SIZES[name] for name in SHARE)
N_PAIR = SIZES["pair"]
N_SPREAD = math.prod(SIZES[name] for name in SPREAD)
N_LINE = math.prod(SIZES[name] for name in LINE)

ROWS = 32
EXT_PAD = 40
RUN = 4
EDGES_RUN = 14
VMEM = 48 * 1024 * 1024
WHOLE = 60 * 1000 * 1000


def params(limit=VMEM):
    return pltpu.CompilerParams(vmem_limit_bytes=limit)


def whole(count):
    return [pl.BlockSpec(memory_space=pltpu.VMEM) for _ in range(count)]


def gelu(x):
    return 0.5 * x * (1.0 + jnp.tanh(math.sqrt(2.0 / math.pi) * (x + 0.044715 * (x * x * x))))


def onehot_rows(codes, first, count):
    length = codes.shape[1]
    start = (length - first - KS_STEM // 2) % length
    codes = jnp.broadcast_to(codes, (16, length))
    shifted = pltpu.roll(codes, start, 1, stride=1, stride_axis=0)
    shifted = shifted[:, :count]
    return jnp.concatenate(
        [(shifted == base + 1).astype(jnp.float32) for base in range(4)], axis=0
    ).astype(jnp.bfloat16)


def pooled_rows(onehot, weight):
    hidden = lax.dot_general(
        onehot, weight, (((0,), (0,)), ((), ())), preferred_element_type=jnp.float32
    ).reshape(onehot.shape[1] // STEM_POOL, STEM_POOL, weight.shape[1])
    high = gelu(jnp.max(hidden, axis=1))
    low = gelu(jnp.min(hidden, axis=1))
    return jnp.maximum(high, low)


def stem_kernel(made_ref, out_ref):
    onehot = onehot_rows(made_ref[64:, :].astype(jnp.float32), 0, made_ref.shape[1])
    weight = made_ref[:64, : out_ref.shape[1]]
    step = 8
    for at in range(0, ROWS, step):
        part = onehot[:, at * STEM_POOL : (at + step) * STEM_POOL]
        out_ref[at : at + step, :] = pooled_rows(part, weight)


def stem(made, channels):
    return pl.pallas_call(
        stem_kernel,
        out_shape=jax.ShapeDtypeStruct((ROWS, channels), jnp.float32),
        in_specs=whole(1),
        out_specs=whole(1)[0],
        compiler_params=params(),
        cost_estimate=pl.CostEstimate(flops=2 * 2048 * 64 * 768, bytes_accessed=200000, transcendentals=0),
    )(made)


def start_kernel(weight_ref, stem_ref, tokens_hbm, line_hbm, out_ref, made_ref, wide, tokens_ref, line_ref, arrived):
    copies = [
        pltpu.make_async_copy(tokens_hbm, tokens_ref, arrived.at[0]),
        pltpu.make_async_copy(line_hbm, line_ref, arrived.at[1]),
    ]
    for copy in copies:
        copy.start()
    rows, channels = stem_ref.shape
    row = lax.broadcasted_iota(jnp.int32, (64, rows), 0)
    column = lax.broadcasted_iota(jnp.int32, (64, rows), 1)
    picked = (column == (KS_STEM - 1 - row % 16) * 4 + row // 16) & (row % 16 < KS_STEM)
    picked = picked.astype(jnp.float32).astype(jnp.bfloat16)
    made = jnp.dot(picked, stem_ref[...], preferred_element_type=jnp.float32).astype(jnp.bfloat16)
    half = channels // 2
    row = lax.broadcasted_iota(jnp.int32, (channels, half), 0)
    column = lax.broadcasted_iota(jnp.int32, (channels, half), 1)
    for odd in range(2):
        order = (row == 2 * column + odd).astype(jnp.float32).astype(jnp.bfloat16)
        part = jnp.dot(made, order, preferred_element_type=jnp.float32)
        made_ref[:64, odd * half : (odd + 1) * half] = part.astype(jnp.bfloat16)
    taps, width = weight_ref.shape
    share = width // N_SHARE
    half = taps // 2
    even, odd = [], []
    for part in range(wide.shape[0]):
        lanes = weight_ref[:, part * HQK : (part + 1) * HQK]
        wide[part, :taps, :] = lanes.astype(jnp.float32)
        wide[part, taps:, :] = jnp.zeros((wide.shape[1] - taps, HQK), jnp.float32)
        even.append(wide[part, pl.ds(0, half + 1, stride=2), :])
        odd.append(wide[part, pl.ds(1, half + 1, stride=2), :])
    even, odd = jnp.concatenate(even, axis=1), jnp.concatenate(odd, axis=1)
    lane = lax.broadcasted_iota(jnp.int32, (half + 1, HQK), 1)
    row = lax.broadcasted_iota(jnp.int32, (half + 1, HQK), 0)
    for copy in copies:
        copy.wait()
    line = (line_ref[...] + 1).astype(jnp.float32).astype(jnp.bfloat16)
    made_ref[64:, :] = jnp.broadcast_to(line, (16, line.shape[1]))
    made_ref[:64, channels:] = jnp.zeros((64, line.shape[1] - channels), jnp.bfloat16)
    codes = (tokens_ref[...] + 1).astype(jnp.float32)
    last = codes.shape[0] - 1
    line = [jnp.broadcast_to(codes[at : at + 1, :], lane.shape) for at in (0, 1, last - 1, last)]
    outer = jnp.where(lane >= HQK - 7, line[2], pltpu.roll(line[1], 96, 1))
    for index in range(4):
        outer = jnp.where(row == index, pltpu.roll(line[3], (96 - 32 * index) % HQK, 1), outer)
    blocks = []
    for index in range(N_SHARE):
        low = pltpu.roll(even, (width - index * share) % width, 1)[:, :HQK]
        high = pltpu.roll(odd, (width - index * share + share) % width, 1)[:, :HQK]
        block = jnp.where(lane < share, low, jnp.where(lane < 2 * share, high, outer))
        blocks.append(jnp.where(row == half, line[0], block).astype(jnp.bfloat16))
    for place in range(N_SEQ):
        at, index, base = place, 0, 1
        for name in reversed(SEQ):
            if name in SHARE:
                index, base = index + base * (at % SIZES[name]), base * SIZES[name]
            at = at // SIZES[name]
        out_ref[place] = blocks[index]


def start(weight, stem_weight, tokens):
    taps, width = weight.shape
    tokens, line = tokens.reshape(-1, HQK), tokens.reshape(1, -1)
    return pl.pallas_call(
        start_kernel,
        out_shape=(
            jax.ShapeDtypeStruct((N_SEQ, taps // 2 + 1, HQK), jnp.bfloat16),
            jax.ShapeDtypeStruct((80, line.shape[1]), jnp.bfloat16),
        ),
        in_specs=whole(2) + [pl.BlockSpec(memory_space=pltpu.HBM)] * 2,
        out_specs=tuple(whole(2)),
        scratch_shapes=[
            pltpu.VMEM((width // HQK, taps + 2, HQK), jnp.float32),
            pltpu.VMEM(tokens.shape, jnp.int32),
            pltpu.VMEM(line.shape, jnp.int32),
            pltpu.SemaphoreType.DMA((2,)),
        ],
        compiler_params=params(WHOLE),
    )(weight, stem_weight, tokens, line)


def border_codes(held_ref, right):
    before = held_ref[jnp.maximum(right - 1, 0)].astype(jnp.float32)
    after = held_ref[jnp.minimum(right, N_SEQ - 1)].astype(jnp.float32)
    before = jnp.where(right > 0, before, 0.0)
    after = jnp.where(right < N_SEQ, after, 0.0)
    lane = lax.broadcasted_iota(jnp.int32, (1, HQK), 1)
    tail = jnp.zeros((1, HQK), jnp.float32)
    for index in range(4):
        part = pltpu.roll(before, (32 * index + 32) % HQK, 1)[index : index + 1, :]
        tail = jnp.where(lane // 32 == index, part, tail)
    return jnp.concatenate(
        [before[4:5, :], tail, after[15:16, :], pltpu.roll(after, 32, 1)[4:5, :]], axis=1
    )


def conv_kernel(place_ref, section_ref, held_ref, stem_ref, out_ref, weights, edges, wide, act, best):
    count, rows, _ = held_ref.shape
    for source in range(count):
        block = held_ref[source].astype(jnp.float32)
        weights[source * (rows - 1) : (source + 1) * (rows - 1), :] = block[: rows - 1, :]
    first = ((place_ref[0] & (N_SEQ // 2 - 1)) // RUN) * RUN
    for run in range(2):
        right = run * (N_SEQ // 2) + first
        onehot = jnp.concatenate(
            [
                onehot_rows(border_codes(held_ref, right + index), 192 if inner else 128, 128 if inner else 256)
                for index in range(RUN + 1)
                for inner in [0 < index < RUN]
            ],
            axis=1,
        )
        made = pooled_rows(onehot, stem_ref[:64, : section_ref.shape[2]])
        place = lax.broadcasted_iota(jnp.int32, made.shape, 0)
        outside = ((place < 2) & (right == 0)) | ((place >= EDGES_RUN - 2) & (right + RUN == count))
        edges[run * 16 : run * 16 + EDGES_RUN, :] = jnp.where(outside, 0.0, made)
    windows, _, channels = section_ref.shape
    half = channels // 2
    columns = out_ref.shape[2] // 8
    for window in range(windows):
        run, index = window // RUN, window % RUN
        rows = section_ref[window].astype(jnp.float32)
        wide[window, 3 : ROWS + 1, :] = rows[1 : ROWS - 1, :]
        at = run * 16 + 2 + 2 * index
        if index == 0:
            wide[window, 0:3, :] = edges[run * 16 : run * 16 + 3, :]
        else:
            wide[window, 1:3, :] = edges[at : at + 2, :]
            wide[window - 1, ROWS + 3 : ROWS + 4, :] = rows[1:2, :]
        at = at + 2
        if index == RUN - 1:
            wide[window, ROWS + 1 : ROWS + 4, :] = edges[at + 1 : at + 4, :]
        else:
            wide[window, ROWS + 1 : ROWS + 3, :] = edges[at : at + 2, :]
            wide[window + 1, 0:1, :] = rows[ROWS - 2 : ROWS - 1, :]
    even, odd = None, None
    for tap in range(KS_CONV):
        rows = wide[:, tap : tap + ROWS, :].astype(jnp.bfloat16).reshape(windows * ROWS, channels)
        weight = weights[tap * half : (tap + 1) * half, :].astype(jnp.bfloat16)
        term = jnp.dot(rows[:, :half], weight, preferred_element_type=jnp.float32)
        even = term if even is None else even + term
        term = jnp.dot(rows[:, half:], weight, preferred_element_type=jnp.float32)
        odd = term if odd is None else odd + term
    act[...] = jnp.zeros(act.shape, jnp.float32)
    act[:, :columns] = gelu(even[:, :columns] + odd[:, columns : 2 * columns])
    count = windows * ROWS // 2
    best[...] = jnp.maximum(act[pl.ds(0, count, stride=2), :], act[pl.ds(1, count, stride=2), :])
    flat = None
    for index in range(8):
        part = best[pl.ds(index, count // 8, stride=8), :]
        part = jnp.pad(part, ((0, 0), (0, 8 * columns - part.shape[1])))
        part = pltpu.roll(part, index * columns, 1)
        flat = part if flat is None else flat + part
    for window in range(windows):
        block = flat[2 * window : 2 * window + 2, :].astype(jnp.bfloat16)
        for index in range(N_PAIR):
            out_ref[window * N_PAIR + index] = block


def conv(place, section, held, stem_weight, columns):
    windows, _, channels = section.shape
    return pl.pallas_call(
        conv_kernel,
        out_shape=jax.ShapeDtypeStruct((windows * N_PAIR, 2, 8 * columns), jnp.bfloat16),
        in_specs=[pl.BlockSpec(memory_space=pltpu.SMEM)] + whole(3),
        out_specs=whole(1)[0],
        scratch_shapes=[
            pltpu.VMEM((held.shape[0] * (held.shape[1] - 1), HQK), jnp.float32),
            pltpu.VMEM((32, channels), jnp.float32),
            pltpu.VMEM((windows, EXT_PAD, channels), jnp.float32),
            pltpu.VMEM((windows * ROWS, HQK), jnp.float32),
            pltpu.VMEM((windows * ROWS // 2, HQK), jnp.float32),
        ],
        compiler_params=params(),
    )(place, section, held, stem_weight)


def project_kernel(trunk_ref, w_query_ref, w_key_ref, w_value_ref, query_ref, kv_ref):
    trunk = trunk_ref[...]
    query, key, value = [
        jnp.dot(trunk, ref[...], preferred_element_type=jnp.float32).astype(jnp.bfloat16)
        for ref in (w_query_ref, w_key_ref, w_value_ref)
    ]
    query_ref[...] = query
    rest = jnp.zeros((trunk.shape[0], kv_ref.shape[2] - HQK - HV), jnp.bfloat16)
    for index in range(N_LINE):
        kv_ref[index, :, :HQK] = key
        kv_ref[index, :, HQK : HQK + HV] = value
        kv_ref[index, :, HQK + HV :] = rest


def project(trunk, w_query, w_key, w_value):
    count = trunk.shape[0]
    return pl.pallas_call(
        project_kernel,
        out_shape=(
            jax.ShapeDtypeStruct((count, HQK), jnp.bfloat16),
            jax.ShapeDtypeStruct((N_LINE, count, 3 * HQK), jnp.bfloat16),
        ),
        in_specs=whole(4),
        out_specs=tuple(whole(2)),
        compiler_params=params(),
    )(trunk, w_query, w_key, w_value)


def split(x):
    parts = []
    for _ in range(3):
        part = x.astype(jnp.bfloat16).astype(jnp.float32)
        parts.append(part)
        x = x - part
    return parts


def attention_kernel(place_ref, query_ref, kv_ref, out_ref):
    scale = 1.0 / math.sqrt(HQK)
    scores = (
        lax.dot_general(
            query_ref[...],
            kv_ref[:, :HQK],
            (((1,), (1,)), ((), ())),
            preferred_element_type=jnp.float32,
        )
        * scale
    )
    top = jnp.max(scores, axis=1, keepdims=True)
    expo = jnp.exp(scores - top)
    total = jnp.sum(expo, axis=1, keepdims=True)
    mixed = jnp.dot(expo.astype(jnp.bfloat16), kv_ref[:, HQK:], preferred_element_type=jnp.float32)
    lane = lax.broadcasted_iota(jnp.int32, mixed.shape, 1)
    for index, column in enumerate(split(top) + split(total)):
        mixed = jnp.where(lane == HV + index, column, mixed)
    mixed = mixed.astype(jnp.bfloat16)
    groups, count, _ = out_ref.shape
    for index in range(groups):
        out_ref[place_ref[0] ^ index] = mixed[index * count : (index + 1) * count, :]


def attention(place, query, kv):
    groups = N_SPREAD
    count, width = query.shape[0] // groups, kv.shape[1] - HQK
    return pl.pallas_call(
        attention_kernel,
        out_shape=jax.ShapeDtypeStruct((groups, count, width), jnp.bfloat16),
        in_specs=[pl.BlockSpec(memory_space=pltpu.SMEM)] + whole(2),
        out_specs=whole(1)[0],
        compiler_params=params(),
    )(place, query, kv)


def combine_kernel(parts_ref, w_out_ref, out_ref):
    parts = parts_ref[...].astype(jnp.float32)
    top = jnp.sum(parts[:, :, HV : HV + 3], axis=2, keepdims=True)
    gain = jnp.exp(top - jnp.max(top, axis=0, keepdims=True))
    total = jnp.sum(gain * jnp.sum(parts[:, :, HV + 3 : HV + 6], axis=2, keepdims=True), axis=0)
    mixed = (jnp.sum(gain * parts, axis=0) / total)[:, :HV].astype(jnp.bfloat16)
    term = jnp.dot(mixed, w_out_ref[...], preferred_element_type=jnp.float32)
    mean = jnp.sum(term, axis=0, keepdims=True) * (1.0 / PAIR_POOL)
    width = term.shape[1] // N_PAIR
    count = term.shape[0]
    tail = jnp.concatenate(
        [mean[:, c * width : (c + 1) * width] for c in range(N_PAIR)]
        + [jnp.zeros((8 - N_PAIR, width), jnp.float32)],
        axis=0,
    )
    for c in range(N_PAIR):
        out_ref[c, :count, :] = term[:, c * width : (c + 1) * width]
        out_ref[c, count:, :] = tail


def combine(parts, w_out):
    count = parts.shape[1]
    width = w_out.shape[1] // N_PAIR
    return pl.pallas_call(
        combine_kernel,
        out_shape=jax.ShapeDtypeStruct((N_PAIR, count + 8, width), jnp.float32),
        in_specs=whole(2),
        out_specs=whole(1)[0],
        compiler_params=params(),
    )(parts, w_out)


def close_kernel(terms_ref, own_ref, trunk_ref, w_pair_ref, pair_ref, seq_ref, rows_ref, every_ref):
    count, width = own_ref.shape
    total = jnp.sum(terms_ref[...], axis=0)
    seq_ref[...] = (own_ref[...].astype(jnp.float32) + total[:count, :]).astype(jnp.bfloat16)
    trunk_mean = jnp.sum(trunk_ref[...].astype(jnp.float32), axis=0, keepdims=True) * (1.0 / PAIR_POOL)
    rows = None
    for c in range(N_PAIR):
        pooled = trunk_mean[:, c * width : (c + 1) * width] + total[count + c : count + c + 1, :]
        term = jnp.dot(
            jnp.broadcast_to(pooled, (8, width)).astype(jnp.bfloat16),
            w_pair_ref[c * width : (c + 1) * width, :],
            preferred_element_type=jnp.float32,
        )
        rows = term if rows is None else rows + term
    rows_ref[...] = rows
    mine = pair_ref[0].astype(jnp.float32)
    factors = jnp.broadcast_to(rows[:1], (mine.shape[0], rows.shape[1]))
    every_ref[...] = jnp.concatenate([factors, mine], axis=1)


def close(terms, own, trunk, w_pair, pair_in):
    return pl.pallas_call(
        close_kernel,
        out_shape=(
            jax.ShapeDtypeStruct(own.shape, jnp.bfloat16),
            jax.ShapeDtypeStruct((8, w_pair.shape[1]), jnp.float32),
            jax.ShapeDtypeStruct((pair_in.shape[1], w_pair.shape[1] + pair_in.shape[2]), jnp.float32),
        ),
        in_specs=whole(5),
        out_specs=tuple(whole(3)),
        compiler_params=params(),
    )(terms, own, trunk, w_pair, pair_in)


def distance_bias(row, cols, pair_bias):
    delta = jnp.abs(row - cols)
    bins = jnp.zeros(delta.shape, jnp.int32)
    for edge in EDGES:
        bins = bins + (delta >= edge).astype(jnp.int32)
    labels = jnp.arange(pair_bias.shape[0], dtype=jnp.int32)
    onehot = (bins[:, None] == labels[None, :]).astype(jnp.bfloat16)
    return jnp.dot(onehot, pair_bias, preferred_element_type=jnp.float32)


def exchange(blocks, axes):
    return lax.all_to_all(blocks, axes, split_axis=0, concat_axis=0, tiled=True)


def on_device(tokens, w_stem, w_conv, w_query, w_key, w_value, w_out, w_pair, pair_bias, pair_in):
    place = lax.axis_index(SEQ)
    pair_place = lax.axis_index("pair")

    taps, width = w_conv.shape
    share = width // N_SHARE
    blocks, made = start(w_conv, w_stem, tokens)
    held = exchange(blocks, SEQ)

    section = stem(made, w_stem.shape[1]).astype(jnp.bfloat16)
    sections = lax.all_gather(section, SHARE, axis=0, tiled=False)

    parts = exchange(conv(place.astype(jnp.int32)[None], sections, held, made, share), SHARE + ("pair",))
    count = ROWS // 2
    trunk = parts.reshape(N_SHARE, N_PAIR, count, share).transpose(2, 1, 0, 3)
    trunk = trunk.reshape(count, N_PAIR * width)

    query, kv = project(trunk, w_query, w_key, w_value)
    for name in reversed(SPREAD):
        other = lax.ppermute(query, name, [(0, 1), (1, 0)])
        query = jnp.concatenate([query, other], axis=0)
    kv = exchange(kv, LINE).reshape(N_LINE * count, kv.shape[2])
    spread = lax.axis_index(SPREAD).astype(jnp.int32)[None]
    parts = exchange(attention(spread, query, kv), SPREAD)
    terms = exchange(combine(parts, w_out), ("pair",))

    own = lax.dynamic_slice_in_dim(trunk, pair_place * width, width, 1)
    factors = jnp.concatenate([w_pair[0], w_pair[1]], axis=1)
    seq_out, rows, every = close(terms, own, trunk, factors, pair_in)
    channels = pair_in.shape[2]
    mine = pair_in[0].astype(jnp.float32)
    rows = rows[:1]
    every = exchange(every[:, None], SEQ)[:, 0]
    mirror = every[:, 2 * channels :]

    cols = jnp.arange(N_SEQ, dtype=jnp.int32)
    bias = distance_bias(place.astype(jnp.int32), cols, pair_bias)
    cross = rows[:, :channels] * every[:, channels : 2 * channels]
    cross = cross + every[:, :channels] * rows[:, channels:]
    pair_out = (0.5 * (mine + mirror + cross) + bias).astype(jnp.bfloat16)[None]
    return (seq_out, pair_out)


def solution(mesh):
    names = SEQ + ("pair",)
    fine = Mesh(mesh.devices.reshape([SIZES[name] for name in names]), names)
    placed = (
        P(SEQ),
        P(),
        P(SEQ, "pair"),
        P(None, "pair"),
        P(None, "pair"),
        P(None, "pair"),
        P("pair", None),
        P(None, None, "pair"),
        P(None, "pair"),
        P(SEQ, None, "pair"),
    )
    return jax.shard_map(
        on_device,
        mesh=fine,
        in_specs=placed,
        out_specs=(P(SEQ, "pair"), P(SEQ, None, "pair")),
        check_vma=False,
    )
```

```python
import math

import jax
import jax.numpy as jnp
from jax import lax
from jax.experimental import pallas as pl
from jax.experimental.pallas import tpu as pltpu
from jax.sharding import Mesh
from jax.sharding import PartitionSpec as P

HQK = 128
HV = 192
KS_STEM = 15
KS_CONV = 5
STEM_POOL = 64
PAIR_POOL = 16
EDGES = (1, 2, 3, 4, 6, 8, 12, 16, 24, 32, 48, 64, 96, 128, 192, 256, 384)

SIZES = {"zl": 2, "y": 8, "xh": 2, "xl": 2, "core": 2, "pair": 4}
SEQ = ("zl", "y", "xh", "xl", "core")
SHARE = ("zl", "xl", "core")
SPREAD = ("xh", "xl", "core")
LINE = ("zl", "y")
N_SEQ = math.prod(SIZES[name] for name in SEQ)
N_SHARE = math.prod(SIZES[name] for name in SHARE)
N_PAIR = SIZES["pair"]
N_SPREAD = math.prod(SIZES[name] for name in SPREAD)
N_LINE = math.prod(SIZES[name] for name in LINE)

ROWS = 32
EXT_PAD = 40
RUN = 4
EDGES_RUN = 14
VMEM = 48 * 1024 * 1024
WHOLE = 60 * 1000 * 1000


def params(limit=VMEM):
    return pltpu.CompilerParams(vmem_limit_bytes=limit)


def whole(count):
    return [pl.BlockSpec(memory_space=pltpu.VMEM) for _ in range(count)]


def gelu(x):
    return 0.5 * x * (1.0 + jnp.tanh(math.sqrt(2.0 / math.pi) * (x + 0.044715 * (x * x * x))))


def onehot_rows(codes, first, count):
    length = codes.shape[1]
    start = (length - first - KS_STEM // 2) % length
    codes = jnp.broadcast_to(codes, (16, length))
    shifted = pltpu.roll(codes, start, 1, stride=1, stride_axis=0)
    shifted = shifted[:, :count]
    return jnp.concatenate(
        [(shifted == base + 1).astype(jnp.float32) for base in range(4)], axis=0
    ).astype(jnp.bfloat16)


def pooled_rows(onehot, weight):
    hidden = lax.dot_general(
        onehot, weight, (((0,), (0,)), ((), ())), preferred_element_type=jnp.float32
    ).reshape(onehot.shape[1] // STEM_POOL, STEM_POOL, weight.shape[1])
    high = gelu(jnp.max(hidden, axis=1))
    low = gelu(jnp.min(hidden, axis=1))
    return jnp.maximum(high, low)


def stem_kernel(made_ref, out_ref):
    onehot = onehot_rows(made_ref[64:, :].astype(jnp.float32), 0, made_ref.shape[1])
    weight = made_ref[:64, : out_ref.shape[1]]
    step = 8
    for at in range(0, ROWS, step):
        part = onehot[:, at * STEM_POOL : (at + step) * STEM_POOL]
        out_ref[at : at + step, :] = pooled_rows(part, weight)


def stem(made, channels):
    return pl.pallas_call(
        stem_kernel,
        out_shape=jax.ShapeDtypeStruct((ROWS, channels), jnp.float32),
        in_specs=whole(1),
        out_specs=whole(1)[0],
        compiler_params=params(),
        cost_estimate=pl.CostEstimate(flops=2 * 2048 * 64 * 768, bytes_accessed=200000, transcendentals=0),
    )(made)


def start_kernel(weight_ref, stem_ref, tokens_hbm, line_hbm, out_ref, made_ref, wide, tokens_ref, line_ref, arrived):
    copies = [
        pltpu.make_async_copy(tokens_hbm, tokens_ref, arrived.at[0]),
        pltpu.make_async_copy(line_hbm, line_ref, arrived.at[1]),
    ]
    for copy in copies:
        copy.start()
    rows, channels = stem_ref.shape
    row = lax.broadcasted_iota(jnp.int32, (64, rows), 0)
    column = lax.broadcasted_iota(jnp.int32, (64, rows), 1)
    picked = (column == (KS_STEM - 1 - row % 16) * 4 + row // 16) & (row % 16 < KS_STEM)
    picked = picked.astype(jnp.float32).astype(jnp.bfloat16)
    made = jnp.dot(picked, stem_ref[...], preferred_element_type=jnp.float32).astype(jnp.bfloat16)
    half = channels // 2
    row = lax.broadcasted_iota(jnp.int32, (channels, half), 0)
    column = lax.broadcasted_iota(jnp.int32, (channels, half), 1)
    for odd in range(2):
        order = (row == 2 * column + odd).astype(jnp.float32).astype(jnp.bfloat16)
        part = jnp.dot(made, order, preferred_element_type=jnp.float32)
        made_ref[:64, odd * half : (odd + 1) * half] = part.astype(jnp.bfloat16)
    taps, width = weight_ref.shape
    share = width // N_SHARE
    half = taps // 2
    even, odd = [], []
    for part in range(wide.shape[0]):
        lanes = weight_ref[:, part * HQK : (part + 1) * HQK]
        wide[part, :taps, :] = lanes.astype(jnp.float32)
        wide[part, taps:, :] = jnp.zeros((wide.shape[1] - taps, HQK), jnp.float32)
        even.append(wide[part, pl.ds(0, half + 1, stride=2), :])
        odd.append(wide[part, pl.ds(1, half + 1, stride=2), :])
    even, odd = jnp.concatenate(even, axis=1), jnp.concatenate(odd, axis=1)
    lane = lax.broadcasted_iota(jnp.int32, (half + 1, HQK), 1)
    row = lax.broadcasted_iota(jnp.int32, (half + 1, HQK), 0)
    for copy in copies:
        copy.wait()
    line = (line_ref[...] + 1).astype(jnp.float32).astype(jnp.bfloat16)
    made_ref[64:, :] = jnp.broadcast_to(line, (16, line.shape[1]))
    made_ref[:64, channels:] = jnp.zeros((64, line.shape[1] - channels), jnp.bfloat16)
    codes = (tokens_ref[...] + 1).astype(jnp.float32)
    last = codes.shape[0] - 1
    line = [jnp.broadcast_to(codes[at : at + 1, :], lane.shape) for at in (0, 1, last - 1, last)]
    outer = jnp.where(lane >= HQK - 7, line[2], pltpu.roll(line[1], 96, 1))
    for index in range(4):
        outer = jnp.where(row == index, pltpu.roll(line[3], (96 - 32 * index) % HQK, 1), outer)
    blocks = []
    for index in range(N_SHARE):
        low = pltpu.roll(even, (width - index * share) % width, 1)[:, :HQK]
        high = pltpu.roll(odd, (width - index * share + share) % width, 1)[:, :HQK]
        block = jnp.where(lane < share, low, jnp.where(lane < 2 * share, high, outer))
        blocks.append(jnp.where(row == half, line[0], block).astype(jnp.bfloat16))
    for place in range(N_SEQ):
        at, index, base = place, 0, 1
        for name in reversed(SEQ):
            if name in SHARE:
                index, base = index + base * (at % SIZES[name]), base * SIZES[name]
            at = at // SIZES[name]
        out_ref[place] = blocks[index]


def start(weight, stem_weight, tokens):
    taps, width = weight.shape
    tokens, line = tokens.reshape(-1, HQK), tokens.reshape(1, -1)
    return pl.pallas_call(
        start_kernel,
        out_shape=(
            jax.ShapeDtypeStruct((N_SEQ, taps // 2 + 1, HQK), jnp.bfloat16),
            jax.ShapeDtypeStruct((80, line.shape[1]), jnp.bfloat16),
        ),
        in_specs=whole(2) + [pl.BlockSpec(memory_space=pltpu.HBM)] * 2,
        out_specs=tuple(whole(2)),
        scratch_shapes=[
            pltpu.VMEM((width // HQK, taps + 2, HQK), jnp.float32),
            pltpu.VMEM(tokens.shape, jnp.int32),
            pltpu.VMEM(line.shape, jnp.int32),
            pltpu.SemaphoreType.DMA((2,)),
        ],
        compiler_params=params(WHOLE),
    )(weight, stem_weight, tokens, line)


def border_codes(held_ref, right):
    before = held_ref[jnp.maximum(right - 1, 0)].astype(jnp.float32)
    after = held_ref[jnp.minimum(right, N_SEQ - 1)].astype(jnp.float32)
    before = jnp.where(right > 0, before, 0.0)
    after = jnp.where(right < N_SEQ, after, 0.0)
    lane = lax.broadcasted_iota(jnp.int32, (1, HQK), 1)
    tail = jnp.zeros((1, HQK), jnp.float32)
    for index in range(4):
        part = pltpu.roll(before, (32 * index + 32) % HQK, 1)[index : index + 1, :]
        tail = jnp.where(lane // 32 == index, part, tail)
    return jnp.concatenate(
        [before[4:5, :], tail, after[15:16, :], pltpu.roll(after, 32, 1)[4:5, :]], axis=1
    )


def conv_kernel(place_ref, section_ref, held_ref, stem_ref, out_ref, weights, edges, wide, act, best):
    count, rows, _ = held_ref.shape
    for source in range(count):
        block = held_ref[source].astype(jnp.float32)
        weights[source * (rows - 1) : (source + 1) * (rows - 1), :] = block[: rows - 1, :]
    first = ((place_ref[0] & (N_SEQ // 2 - 1)) // RUN) * RUN
    for run in range(2):
        right = run * (N_SEQ // 2) + first
        onehot = jnp.concatenate(
            [
                onehot_rows(border_codes(held_ref, right + index), 192 if inner else 128, 128 if inner else 256)
                for index in range(RUN + 1)
                for inner in [0 < index < RUN]
            ],
            axis=1,
        )
        made = pooled_rows(onehot, stem_ref[:64, : section_ref.shape[2]])
        place = lax.broadcasted_iota(jnp.int32, made.shape, 0)
        outside = ((place < 2) & (right == 0)) | ((place >= EDGES_RUN - 2) & (right + RUN == count))
        edges[run * 16 : run * 16 + EDGES_RUN, :] = jnp.where(outside, 0.0, made)
    windows, _, channels = section_ref.shape
    half = channels // 2
    columns = out_ref.shape[2] // 8
    for window in range(windows):
        run, index = window // RUN, window % RUN
        rows = section_ref[window].astype(jnp.float32)
        wide[window, 3 : ROWS + 1, :] = rows[1 : ROWS - 1, :]
        at = run * 16 + 2 + 2 * index
        if index == 0:
            wide[window, 0:3, :] = edges[run * 16 : run * 16 + 3, :]
        else:
            wide[window, 1:3, :] = edges[at : at + 2, :]
            wide[window - 1, ROWS + 3 : ROWS + 4, :] = rows[1:2, :]
        at = at + 2
        if index == RUN - 1:
            wide[window, ROWS + 1 : ROWS + 4, :] = edges[at + 1 : at + 4, :]
        else:
            wide[window, ROWS + 1 : ROWS + 3, :] = edges[at : at + 2, :]
            wide[window + 1, 0:1, :] = rows[ROWS - 2 : ROWS - 1, :]
    even, odd = None, None
    for tap in range(KS_CONV):
        rows = wide[:, tap : tap + ROWS, :].astype(jnp.bfloat16).reshape(windows * ROWS, channels)
        weight = weights[tap * half : (tap + 1) * half, :].astype(jnp.bfloat16)
        term = jnp.dot(rows[:, :half], weight, preferred_element_type=jnp.float32)
        even = term if even is None else even + term
        term = jnp.dot(rows[:, half:], weight, preferred_element_type=jnp.float32)
        odd = term if odd is None else odd + term
    act[...] = jnp.zeros(act.shape, jnp.float32)
    act[:, :columns] = gelu(even[:, :columns] + odd[:, columns : 2 * columns])
    count = windows * ROWS // 2
    best[...] = jnp.maximum(act[pl.ds(0, count, stride=2), :], act[pl.ds(1, count, stride=2), :])
    flat = None
    for index in range(8):
        part = best[pl.ds(index, count // 8, stride=8), :]
        part = jnp.pad(part, ((0, 0), (0, 8 * columns - part.shape[1])))
        part = pltpu.roll(part, index * columns, 1)
        flat = part if flat is None else flat + part
    for window in range(windows):
        block = flat[window // 2 * 4 : window // 2 * 4 + 4, :].astype(jnp.bfloat16)
        for index in range(N_PAIR):
            out_ref[window * N_PAIR + index] = block


def conv(place, section, held, stem_weight, columns):
    windows, _, channels = section.shape
    return pl.pallas_call(
        conv_kernel,
        out_shape=jax.ShapeDtypeStruct((windows * N_PAIR, 4, 8 * columns), jnp.bfloat16),
        in_specs=[pl.BlockSpec(memory_space=pltpu.SMEM)] + whole(3),
        out_specs=whole(1)[0],
        scratch_shapes=[
            pltpu.VMEM((held.shape[0] * (held.shape[1] - 1), HQK), jnp.float32),
            pltpu.VMEM((32, channels), jnp.float32),
            pltpu.VMEM((windows, EXT_PAD, channels), jnp.float32),
            pltpu.VMEM((windows * ROWS, HQK), jnp.float32),
            pltpu.VMEM((windows * ROWS // 2, HQK), jnp.float32),
        ],
        compiler_params=params(),
    )(place, section, held, stem_weight)


def project_kernel(core_ref, trunk_ref, w_query_ref, w_key_ref, w_value_ref, query_ref, kv_ref, own_ref):
    trunk = trunk_ref[...]
    first = core_ref[0] == 0
    count = own_ref.shape[0]
    half = count // 2
    query_ref[...] = jnp.dot(trunk, w_query_ref[...], preferred_element_type=jnp.float32).astype(jnp.bfloat16)
    wide = trunk.astype(jnp.float32)
    own = jnp.where(first, wide[:count], wide[count:]).astype(jnp.bfloat16)
    own_ref[...] = own
    key = jnp.dot(own, w_key_ref[...], preferred_element_type=jnp.float32).astype(jnp.bfloat16)
    value = jnp.dot(own, w_value_ref[...], preferred_element_type=jnp.float32)
    rest = jnp.pad(value[:, HQK:], ((0, 0), (0, 2 * HQK - HV)))
    rest = (rest[:half] + pltpu.roll(rest[half:], HV - HQK, 1)).astype(jnp.bfloat16)
    value = value[:, :HQK].astype(jnp.bfloat16)
    for index in range(N_LINE):
        kv_ref[index, :count, :] = key
        kv_ref[index, count : 2 * count, :] = value
        kv_ref[index, 2 * count :, :] = rest


def project(core, trunk, w_query, w_key, w_value):
    count = trunk.shape[0] // 2
    return pl.pallas_call(
        project_kernel,
        out_shape=(
            jax.ShapeDtypeStruct((2 * count, HQK), jnp.bfloat16),
            jax.ShapeDtypeStruct((N_LINE, 2 * count + count // 2, HQK), jnp.bfloat16),
            jax.ShapeDtypeStruct((count, trunk.shape[1]), jnp.bfloat16),
        ),
        in_specs=[pl.BlockSpec(memory_space=pltpu.SMEM)] + whole(4),
        out_specs=tuple(whole(3)),
        compiler_params=params(),
    )(core, trunk, w_query, w_key, w_value)


def split(x):
    parts = []
    for _ in range(3):
        part = x.astype(jnp.bfloat16).astype(jnp.float32)
        parts.append(part)
        x = x - part
    return parts


def attention_kernel(place_ref, query_ref, kv_ref, out_ref):
    scale = 1.0 / math.sqrt(HQK)
    line, rows, _ = kv_ref.shape
    count = out_ref.shape[1]
    keys = kv_ref[:, :count, :].reshape(line * count, HQK)
    values = kv_ref[:, count : 2 * count, :].reshape(line * count, HQK)
    rest = kv_ref[:, 2 * count :, :].astype(jnp.float32)
    rest = jnp.stack([rest, pltpu.roll(rest, HQK - (HV - HQK), 2)], axis=1)
    rest = rest.reshape(line * count, HQK).astype(jnp.bfloat16)
    scores = (
        lax.dot_general(
            query_ref[...], keys, (((1,), (1,)), ((), ())), preferred_element_type=jnp.float32
        )
        * scale
    )
    top = jnp.max(scores, axis=1, keepdims=True)
    expo = jnp.exp(scores - top)
    total = jnp.sum(expo, axis=1, keepdims=True)
    expo = expo.astype(jnp.bfloat16)
    mixed = jnp.concatenate(
        [jnp.dot(expo, part, preferred_element_type=jnp.float32) for part in (values, rest)], axis=1
    )
    lane = lax.broadcasted_iota(jnp.int32, mixed.shape, 1)
    for index, column in enumerate(split(top) + split(total)):
        mixed = jnp.where(lane == HV + index, column, mixed)
    mixed = mixed.astype(jnp.bfloat16)
    groups, count, _ = out_ref.shape
    for index in range(groups):
        place = ((place_ref[0] >> 1) ^ (index // 2)) * 2 + index % 2
        out_ref[place] = mixed[index * count : (index + 1) * count, :]


def attention(place, query, kv):
    groups = N_SPREAD
    count, width = query.shape[0] // groups, 2 * HQK
    return pl.pallas_call(
        attention_kernel,
        out_shape=jax.ShapeDtypeStruct((groups, count, width), jnp.bfloat16),
        in_specs=[pl.BlockSpec(memory_space=pltpu.SMEM)] + whole(2),
        out_specs=whole(1)[0],
        compiler_params=params(),
    )(place, query, kv)


def combine_kernel(parts_ref, w_out_ref, out_ref):
    parts = parts_ref[...].astype(jnp.float32)
    top = jnp.sum(parts[:, :, HV : HV + 3], axis=2, keepdims=True)
    gain = jnp.exp(top - jnp.max(top, axis=0, keepdims=True))
    total = jnp.sum(gain * jnp.sum(parts[:, :, HV + 3 : HV + 6], axis=2, keepdims=True), axis=0)
    mixed = (jnp.sum(gain * parts, axis=0) / total)[:, :HV].astype(jnp.bfloat16)
    term = jnp.dot(mixed, w_out_ref[...], preferred_element_type=jnp.float32)
    mean = jnp.sum(term, axis=0, keepdims=True) * (1.0 / PAIR_POOL)
    width = term.shape[1] // N_PAIR
    count = term.shape[0]
    tail = jnp.concatenate(
        [mean[:, c * width : (c + 1) * width] for c in range(N_PAIR)]
        + [jnp.zeros((8 - N_PAIR, width), jnp.float32)],
        axis=0,
    )
    for c in range(N_PAIR):
        out_ref[c, :count, :] = term[:, c * width : (c + 1) * width]
        out_ref[c, count:, :] = tail


def combine(parts, w_out):
    count = parts.shape[1]
    width = w_out.shape[1] // N_PAIR
    return pl.pallas_call(
        combine_kernel,
        out_shape=jax.ShapeDtypeStruct((N_PAIR, count + 8, width), jnp.float32),
        in_specs=whole(2),
        out_specs=whole(1)[0],
        compiler_params=params(),
    )(parts, w_out)


def close_kernel(terms_ref, own_ref, trunk_ref, w_pair_ref, pair_ref, seq_ref, rows_ref, every_ref):
    count, width = own_ref.shape
    total = jnp.sum(terms_ref[...], axis=0)
    seq_ref[...] = (own_ref[...].astype(jnp.float32) + total[:count, :]).astype(jnp.bfloat16)
    trunk_mean = jnp.sum(trunk_ref[...].astype(jnp.float32), axis=0, keepdims=True) * (1.0 / PAIR_POOL)
    rows = None
    for c in range(N_PAIR):
        pooled = trunk_mean[:, c * width : (c + 1) * width] + total[count + c : count + c + 1, :]
        term = jnp.dot(
            jnp.broadcast_to(pooled, (8, width)).astype(jnp.bfloat16),
            w_pair_ref[c * width : (c + 1) * width, :],
            preferred_element_type=jnp.float32,
        )
        rows = term if rows is None else rows + term
    rows_ref[...] = rows
    mine = pair_ref[0].astype(jnp.float32)
    factors = jnp.broadcast_to(rows[:1], (mine.shape[0], rows.shape[1]))
    every_ref[...] = jnp.concatenate([factors, mine], axis=1)


def close(terms, own, trunk, w_pair, pair_in):
    return pl.pallas_call(
        close_kernel,
        out_shape=(
            jax.ShapeDtypeStruct(own.shape, jnp.bfloat16),
            jax.ShapeDtypeStruct((8, w_pair.shape[1]), jnp.float32),
            jax.ShapeDtypeStruct((pair_in.shape[1], w_pair.shape[1] + pair_in.shape[2]), jnp.float32),
        ),
        in_specs=whole(5),
        out_specs=tuple(whole(3)),
        compiler_params=params(),
    )(terms, own, trunk, w_pair, pair_in)


def distance_bias(row, cols, pair_bias):
    delta = jnp.abs(row - cols)
    bins = jnp.zeros(delta.shape, jnp.int32)
    for edge in EDGES:
        bins = bins + (delta >= edge).astype(jnp.int32)
    labels = jnp.arange(pair_bias.shape[0], dtype=jnp.int32)
    onehot = (bins[:, None] == labels[None, :]).astype(jnp.bfloat16)
    return jnp.dot(onehot, pair_bias, preferred_element_type=jnp.float32)


def exchange(blocks, axes):
    return lax.all_to_all(blocks, axes, split_axis=0, concat_axis=0, tiled=True)


def on_device(tokens, w_stem, w_conv, w_query, w_key, w_value, w_out, w_pair, pair_bias, pair_in):
    place = lax.axis_index(SEQ)
    pair_place = lax.axis_index("pair")

    taps, width = w_conv.shape
    share = width // N_SHARE
    blocks, made = start(w_conv, w_stem, tokens)
    held = exchange(blocks, SEQ)

    section = stem(made, w_stem.shape[1]).astype(jnp.bfloat16)
    sections = lax.all_gather(section, SHARE, axis=0, tiled=False)

    parts = exchange(conv(place.astype(jnp.int32)[None], sections, held, made, share), SHARE + ("pair",))
    count = ROWS // 2
    trunk = parts.reshape(N_SHARE, N_PAIR, 2 * count, share).transpose(2, 1, 0, 3)
    trunk = trunk.reshape(2 * count, N_PAIR * width)

    core = lax.axis_index("core").astype(jnp.int32)[None]
    query, kv, trunk = project(core, trunk, w_query, w_key, w_value)
    for name in reversed(SPREAD[:-1]):
        other = lax.ppermute(query, name, [(0, 1), (1, 0)])
        query = jnp.concatenate([query, other], axis=0)
    kv = exchange(kv, LINE)
    spread = lax.axis_index(SPREAD).astype(jnp.int32)[None]
    parts = exchange(attention(spread, query, kv), SPREAD)
    terms = exchange(combine(parts, w_out), ("pair",))

    own = lax.dynamic_slice_in_dim(trunk, pair_place * width, width, 1)
    factors = jnp.concatenate([w_pair[0], w_pair[1]], axis=1)
    seq_out, rows, every = close(terms, own, trunk, factors, pair_in)
    channels = pair_in.shape[2]
    mine = pair_in[0].astype(jnp.float32)
    rows = rows[:1]
    every = exchange(every[:, None], SEQ)[:, 0]
    mirror = every[:, 2 * channels :]

    cols = jnp.arange(N_SEQ, dtype=jnp.int32)
    bias = distance_bias(place.astype(jnp.int32), cols, pair_bias)
    cross = rows[:, :channels] * every[:, channels : 2 * channels]
    cross = cross + every[:, :channels] * rows[:, channels:]
    pair_out = (0.5 * (mine + mirror + cross) + bias).astype(jnp.bfloat16)[None]
    return (seq_out, pair_out)


def solution(mesh):
    names = SEQ + ("pair",)
    fine = Mesh(mesh.devices.reshape([SIZES[name] for name in names]), names)
    placed = (
        P(SEQ),
        P(),
        P(SEQ, "pair"),
        P(None, "pair"),
        P(None, "pair"),
        P(None, "pair"),
        P("pair", None),
        P(None, None, "pair"),
        P(None, "pair"),
        P(SEQ, None, "pair"),
    )
    return jax.shard_map(
        on_device,
        mesh=fine,
        in_specs=placed,
        out_specs=(P(SEQ, "pair"), P(SEQ, None, "pair")),
        check_vma=False,
    )
```

```python
import math

import jax
import jax.numpy as jnp
from jax import lax
from jax.experimental import pallas as pl
from jax.experimental.pallas import tpu as pltpu
from jax.sharding import Mesh
from jax.sharding import PartitionSpec as P

HQK = 128
HV = 192
KS_STEM = 15
KS_CONV = 5
STEM_POOL = 64
PAIR_POOL = 16
EDGES = (1, 2, 3, 4, 6, 8, 12, 16, 24, 32, 48, 64, 96, 128, 192, 256, 384)

SIZES = {"zl": 2, "y": 8, "xh": 2, "xl": 2, "core": 2, "pair": 4}
SEQ = ("zl", "y", "xh", "xl", "core")
SHARE = ("zl", "xl", "core")
SPREAD = ("xh", "xl", "core")
LINE = ("zl", "y")
MIDDLE_SEQ = 32
MIDDLE_LINE = 4
MIDDLE_SPREAD = 2
MIDDLE_PAIR = 1
N_SEQ = math.prod(SIZES[name] for name in SEQ)
N_SHARE = math.prod(SIZES[name] for name in SHARE)
N_PAIR = SIZES["pair"]
N_SPREAD = math.prod(SIZES[name] for name in SPREAD)
N_LINE = math.prod(SIZES[name] for name in LINE)

ROWS = 32
EXT_PAD = 40
RUN = 4
EDGES_RUN = 14
VMEM = 48 * 1024 * 1024
WHOLE = 60 * 1000 * 1000


def params(limit=VMEM):
    return pltpu.CompilerParams(vmem_limit_bytes=limit)


def whole(count):
    return [pl.BlockSpec(memory_space=pltpu.VMEM) for _ in range(count)]


def gelu(x):
    return 0.5 * x * (1.0 + jnp.tanh(math.sqrt(2.0 / math.pi) * (x + 0.044715 * (x * x * x))))


def onehot_rows(codes, first, count):
    length = codes.shape[1]
    start = (length - first - KS_STEM // 2) % length
    codes = jnp.broadcast_to(codes, (16, length))
    shifted = pltpu.roll(codes, start, 1, stride=1, stride_axis=0)
    shifted = shifted[:, :count]
    return jnp.concatenate(
        [(shifted == base + 1).astype(jnp.float32) for base in range(4)], axis=0
    ).astype(jnp.bfloat16)


def pooled_rows(onehot, weight):
    hidden = lax.dot_general(
        onehot, weight, (((0,), (0,)), ((), ())), preferred_element_type=jnp.float32
    ).reshape(onehot.shape[1] // STEM_POOL, STEM_POOL, weight.shape[1])
    high = gelu(jnp.max(hidden, axis=1))
    low = gelu(jnp.min(hidden, axis=1))
    return jnp.maximum(high, low)


def stem_kernel(made_ref, out_ref):
    onehot = onehot_rows(made_ref[64:, :].astype(jnp.float32), 0, made_ref.shape[1])
    weight = made_ref[:64, : out_ref.shape[1]]
    step = 8
    for at in range(0, ROWS, step):
        part = onehot[:, at * STEM_POOL : (at + step) * STEM_POOL]
        out_ref[at : at + step, :] = pooled_rows(part, weight)


def stem(made, channels):
    return pl.pallas_call(
        stem_kernel,
        out_shape=jax.ShapeDtypeStruct((ROWS, channels), jnp.float32),
        in_specs=whole(1),
        out_specs=whole(1)[0],
        compiler_params=params(),
        cost_estimate=pl.CostEstimate(flops=2 * 2048 * 64 * 768, bytes_accessed=200000, transcendentals=0),
    )(made)


def start_kernel(weight_ref, stem_ref, tokens_hbm, line_hbm, out_ref, made_ref, wide, tokens_ref, line_ref, arrived):
    copies = [
        pltpu.make_async_copy(tokens_hbm, tokens_ref, arrived.at[0]),
        pltpu.make_async_copy(line_hbm, line_ref, arrived.at[1]),
    ]
    for copy in copies:
        copy.start()
    rows, channels = stem_ref.shape
    row = lax.broadcasted_iota(jnp.int32, (64, rows), 0)
    column = lax.broadcasted_iota(jnp.int32, (64, rows), 1)
    picked = (column == (KS_STEM - 1 - row % 16) * 4 + row // 16) & (row % 16 < KS_STEM)
    picked = picked.astype(jnp.float32).astype(jnp.bfloat16)
    made = jnp.dot(picked, stem_ref[...], preferred_element_type=jnp.float32).astype(jnp.bfloat16)
    half = channels // 2
    row = lax.broadcasted_iota(jnp.int32, (channels, half), 0)
    column = lax.broadcasted_iota(jnp.int32, (channels, half), 1)
    for odd in range(2):
        order = (row == 2 * column + odd).astype(jnp.float32).astype(jnp.bfloat16)
        part = jnp.dot(made, order, preferred_element_type=jnp.float32)
        made_ref[:64, odd * half : (odd + 1) * half] = part.astype(jnp.bfloat16)
    taps, width = weight_ref.shape
    share = width // N_SHARE
    half = taps // 2
    even, odd = [], []
    for part in range(wide.shape[0]):
        lanes = weight_ref[:, part * HQK : (part + 1) * HQK]
        wide[part, :taps, :] = lanes.astype(jnp.float32)
        wide[part, taps:, :] = jnp.zeros((wide.shape[1] - taps, HQK), jnp.float32)
        even.append(wide[part, pl.ds(0, half + 1, stride=2), :])
        odd.append(wide[part, pl.ds(1, half + 1, stride=2), :])
    even, odd = jnp.concatenate(even, axis=1), jnp.concatenate(odd, axis=1)
    lane = lax.broadcasted_iota(jnp.int32, (half + 1, HQK), 1)
    row = lax.broadcasted_iota(jnp.int32, (half + 1, HQK), 0)
    for copy in copies:
        copy.wait()
    line = (line_ref[...] + 1).astype(jnp.float32).astype(jnp.bfloat16)
    made_ref[64:, :] = jnp.broadcast_to(line, (16, line.shape[1]))
    made_ref[:64, channels:] = jnp.zeros((64, line.shape[1] - channels), jnp.bfloat16)
    codes = (tokens_ref[...] + 1).astype(jnp.float32)
    last = codes.shape[0] - 1
    line = [jnp.broadcast_to(codes[at : at + 1, :], lane.shape) for at in (0, 1, last - 1, last)]
    outer = jnp.where(lane >= HQK - 7, line[2], pltpu.roll(line[1], 96, 1))
    for index in range(4):
        outer = jnp.where(row == index, pltpu.roll(line[3], (96 - 32 * index) % HQK, 1), outer)
    blocks = []
    for index in range(N_SHARE):
        low = pltpu.roll(even, (width - index * share) % width, 1)[:, :HQK]
        high = pltpu.roll(odd, (width - index * share + share) % width, 1)[:, :HQK]
        block = jnp.where(lane < share, low, jnp.where(lane < 2 * share, high, outer))
        blocks.append(jnp.where(row == half, line[0], block).astype(jnp.bfloat16))
    for place in range(N_SEQ):
        at, index, base = place, 0, 1
        for name in reversed(SEQ):
            if name in SHARE:
                index, base = index + base * (at % SIZES[name]), base * SIZES[name]
            at = at // SIZES[name]
        out_ref[place] = blocks[index]


def start(weight, stem_weight, tokens):
    taps, width = weight.shape
    tokens, line = tokens.reshape(-1, HQK), tokens.reshape(1, -1)
    return pl.pallas_call(
        start_kernel,
        out_shape=(
            jax.ShapeDtypeStruct((N_SEQ, taps // 2 + 1, HQK), jnp.bfloat16),
            jax.ShapeDtypeStruct((80, line.shape[1]), jnp.bfloat16),
        ),
        in_specs=whole(2) + [pl.BlockSpec(memory_space=pltpu.HBM)] * 2,
        out_specs=tuple(whole(2)),
        scratch_shapes=[
            pltpu.VMEM((width // HQK, taps + 2, HQK), jnp.float32),
            pltpu.VMEM(tokens.shape, jnp.int32),
            pltpu.VMEM(line.shape, jnp.int32),
            pltpu.SemaphoreType.DMA((2,)),
        ],
        compiler_params=params(WHOLE),
    )(weight, stem_weight, tokens, line)


def border_codes(held_ref, right):
    before = held_ref[jnp.maximum(right - 1, 0) ^ MIDDLE_SEQ].astype(jnp.float32)
    after = held_ref[jnp.minimum(right, N_SEQ - 1) ^ MIDDLE_SEQ].astype(jnp.float32)
    before = jnp.where(right > 0, before, 0.0)
    after = jnp.where(right < N_SEQ, after, 0.0)
    lane = lax.broadcasted_iota(jnp.int32, (1, HQK), 1)
    tail = jnp.zeros((1, HQK), jnp.float32)
    for index in range(4):
        part = pltpu.roll(before, (32 * index + 32) % HQK, 1)[index : index + 1, :]
        tail = jnp.where(lane // 32 == index, part, tail)
    return jnp.concatenate(
        [before[4:5, :], tail, after[15:16, :], pltpu.roll(after, 32, 1)[4:5, :]], axis=1
    )


def conv_kernel(place_ref, section_ref, held_ref, stem_ref, out_ref, weights, edges, wide, act, best):
    count, rows, _ = held_ref.shape
    for source in range(count):
        block = held_ref[source ^ MIDDLE_SEQ].astype(jnp.float32)
        weights[source * (rows - 1) : (source + 1) * (rows - 1), :] = block[: rows - 1, :]
    first = ((place_ref[0] & (N_SEQ // 2 - 1)) // RUN) * RUN
    for run in range(2):
        right = run * (N_SEQ // 2) + first
        onehot = jnp.concatenate(
            [
                onehot_rows(border_codes(held_ref, right + index), 192 if inner else 128, 128 if inner else 256)
                for index in range(RUN + 1)
                for inner in [0 < index < RUN]
            ],
            axis=1,
        )
        made = pooled_rows(onehot, stem_ref[:64, : section_ref.shape[2]])
        place = lax.broadcasted_iota(jnp.int32, made.shape, 0)
        outside = ((place < 2) & (right == 0)) | ((place >= EDGES_RUN - 2) & (right + RUN == count))
        edges[run * 16 : run * 16 + EDGES_RUN, :] = jnp.where(outside, 0.0, made)
    windows, _, channels = section_ref.shape
    half = channels // 2
    columns = out_ref.shape[2] // 8
    for window in range(windows):
        run, index = window // RUN, window % RUN
        rows = section_ref[window].astype(jnp.float32)
        wide[window, 3 : ROWS + 1, :] = rows[1 : ROWS - 1, :]
        at = run * 16 + 2 + 2 * index
        if index == 0:
            wide[window, 0:3, :] = edges[run * 16 : run * 16 + 3, :]
        else:
            wide[window, 1:3, :] = edges[at : at + 2, :]
            wide[window - 1, ROWS + 3 : ROWS + 4, :] = rows[1:2, :]
        at = at + 2
        if index == RUN - 1:
            wide[window, ROWS + 1 : ROWS + 4, :] = edges[at + 1 : at + 4, :]
        else:
            wide[window, ROWS + 1 : ROWS + 3, :] = edges[at : at + 2, :]
            wide[window + 1, 0:1, :] = rows[ROWS - 2 : ROWS - 1, :]
    even, odd = None, None
    for tap in range(KS_CONV):
        rows = wide[:, tap : tap + ROWS, :].astype(jnp.bfloat16).reshape(windows * ROWS, channels)
        weight = weights[tap * half : (tap + 1) * half, :].astype(jnp.bfloat16)
        term = jnp.dot(rows[:, :half], weight, preferred_element_type=jnp.float32)
        even = term if even is None else even + term
        term = jnp.dot(rows[:, half:], weight, preferred_element_type=jnp.float32)
        odd = term if odd is None else odd + term
    act[...] = jnp.zeros(act.shape, jnp.float32)
    act[:, :columns] = gelu(even[:, :columns] + odd[:, columns : 2 * columns])
    count = windows * ROWS // 2
    best[...] = jnp.maximum(act[pl.ds(0, count, stride=2), :], act[pl.ds(1, count, stride=2), :])
    flat = None
    for index in range(8):
        part = best[pl.ds(index, count // 8, stride=8), :]
        part = jnp.pad(part, ((0, 0), (0, 8 * columns - part.shape[1])))
        part = pltpu.roll(part, index * columns, 1)
        flat = part if flat is None else flat + part
    for window in range(windows):
        block = flat[window // 2 * 4 : window // 2 * 4 + 4, :].astype(jnp.bfloat16)
        for index in range(N_PAIR):
            out_ref[window * N_PAIR + index] = block


def conv(place, section, held, stem_weight, columns):
    windows, _, channels = section.shape
    return pl.pallas_call(
        conv_kernel,
        out_shape=jax.ShapeDtypeStruct((windows * N_PAIR, 4, 8 * columns), jnp.bfloat16),
        in_specs=[pl.BlockSpec(memory_space=pltpu.SMEM)] + whole(3),
        out_specs=whole(1)[0],
        scratch_shapes=[
            pltpu.VMEM((held.shape[0] * (held.shape[1] - 1), HQK), jnp.float32),
            pltpu.VMEM((32, channels), jnp.float32),
            pltpu.VMEM((windows, EXT_PAD, channels), jnp.float32),
            pltpu.VMEM((windows * ROWS, HQK), jnp.float32),
            pltpu.VMEM((windows * ROWS // 2, HQK), jnp.float32),
        ],
        compiler_params=params(),
    )(place, section, held, stem_weight)


def project_kernel(core_ref, trunk_ref, w_query_ref, w_key_ref, w_value_ref, query_ref, kv_ref, own_ref):
    trunk = trunk_ref[...]
    first = core_ref[0] == 0
    count = own_ref.shape[0]
    half = count // 2
    query_ref[...] = jnp.dot(trunk, w_query_ref[...], preferred_element_type=jnp.float32).astype(jnp.bfloat16)
    wide = trunk.astype(jnp.float32)
    own = jnp.where(first, wide[:count], wide[count:]).astype(jnp.bfloat16)
    own_ref[...] = own
    key = jnp.dot(own, w_key_ref[...], preferred_element_type=jnp.float32).astype(jnp.bfloat16)
    value = jnp.dot(own, w_value_ref[...], preferred_element_type=jnp.float32)
    rest = jnp.pad(value[:, HQK:], ((0, 0), (0, 2 * HQK - HV)))
    rest = (rest[:half] + pltpu.roll(rest[half:], HV - HQK, 1)).astype(jnp.bfloat16)
    value = value[:, :HQK].astype(jnp.bfloat16)
    for index in range(N_LINE):
        kv_ref[index, :count, :] = key
        kv_ref[index, count : 2 * count, :] = value
        kv_ref[index, 2 * count :, :] = rest


def project(core, trunk, w_query, w_key, w_value):
    count = trunk.shape[0] // 2
    return pl.pallas_call(
        project_kernel,
        out_shape=(
            jax.ShapeDtypeStruct((2 * count, HQK), jnp.bfloat16),
            jax.ShapeDtypeStruct((N_LINE, 2 * count + count // 2, HQK), jnp.bfloat16),
            jax.ShapeDtypeStruct((count, trunk.shape[1]), jnp.bfloat16),
        ),
        in_specs=[pl.BlockSpec(memory_space=pltpu.SMEM)] + whole(4),
        out_specs=tuple(whole(3)),
        compiler_params=params(),
    )(core, trunk, w_query, w_key, w_value)


def split(x):
    parts = []
    for _ in range(3):
        part = x.astype(jnp.bfloat16).astype(jnp.float32)
        parts.append(part)
        x = x - part
    return parts


def attention_kernel(place_ref, query_ref, kv_ref, out_ref):
    scale = 1.0 / math.sqrt(HQK)
    line, rows, _ = kv_ref.shape
    count = out_ref.shape[1]
    keys = kv_ref[:, :count, :].reshape(line * count, HQK)
    values = kv_ref[:, count : 2 * count, :].reshape(line * count, HQK)
    rest = kv_ref[:, 2 * count :, :].astype(jnp.float32)
    rest = jnp.stack([rest, pltpu.roll(rest, HQK - (HV - HQK), 2)], axis=1)
    rest = rest.reshape(line * count, HQK).astype(jnp.bfloat16)
    scores = (
        lax.dot_general(
            query_ref[...], keys, (((1,), (1,)), ((), ())), preferred_element_type=jnp.float32
        )
        * scale
    )
    top = jnp.max(scores, axis=1, keepdims=True)
    expo = jnp.exp(scores - top)
    total = jnp.sum(expo, axis=1, keepdims=True)
    expo = expo.astype(jnp.bfloat16)
    mixed = jnp.concatenate(
        [jnp.dot(expo, part, preferred_element_type=jnp.float32) for part in (values, rest)], axis=1
    )
    lane = lax.broadcasted_iota(jnp.int32, mixed.shape, 1)
    for index, column in enumerate(split(top) + split(total)):
        mixed = jnp.where(lane == HV + index, column, mixed)
    mixed = mixed.astype(jnp.bfloat16)
    groups, count, _ = out_ref.shape
    for index in range(groups):
        place = ((place_ref[0] >> 1) ^ (index // 2)) * 2 + index % 2
        out_ref[place ^ MIDDLE_SPREAD] = mixed[index * count : (index + 1) * count, :]


def attention(place, query, kv):
    groups = N_SPREAD
    count, width = query.shape[0] // groups, 2 * HQK
    return pl.pallas_call(
        attention_kernel,
        out_shape=jax.ShapeDtypeStruct((groups, count, width), jnp.bfloat16),
        in_specs=[pl.BlockSpec(memory_space=pltpu.SMEM)] + whole(2),
        out_specs=whole(1)[0],
        compiler_params=params(),
    )(place, query, kv)


def combine_kernel(parts_ref, w_out_ref, out_ref):
    parts = parts_ref[...].astype(jnp.float32)
    top = jnp.sum(parts[:, :, HV : HV + 3], axis=2, keepdims=True)
    gain = jnp.exp(top - jnp.max(top, axis=0, keepdims=True))
    total = jnp.sum(gain * jnp.sum(parts[:, :, HV + 3 : HV + 6], axis=2, keepdims=True), axis=0)
    mixed = (jnp.sum(gain * parts, axis=0) / total)[:, :HV].astype(jnp.bfloat16)
    term = jnp.dot(mixed, w_out_ref[...], preferred_element_type=jnp.float32)
    mean = jnp.sum(term, axis=0, keepdims=True) * (1.0 / PAIR_POOL)
    width = term.shape[1] // N_PAIR
    count = term.shape[0]
    tail = jnp.concatenate(
        [mean[:, c * width : (c + 1) * width] for c in range(N_PAIR)]
        + [jnp.zeros((8 - N_PAIR, width), jnp.float32)],
        axis=0,
    )
    for c in range(N_PAIR):
        out_ref[c ^ MIDDLE_PAIR, :count, :] = term[:, c * width : (c + 1) * width]
        out_ref[c ^ MIDDLE_PAIR, count:, :] = tail


def combine(parts, w_out):
    count = parts.shape[1]
    width = w_out.shape[1] // N_PAIR
    return pl.pallas_call(
        combine_kernel,
        out_shape=jax.ShapeDtypeStruct((N_PAIR, count + 8, width), jnp.float32),
        in_specs=whole(2),
        out_specs=whole(1)[0],
        compiler_params=params(),
    )(parts, w_out)


def close_kernel(terms_ref, own_ref, trunk_ref, w_pair_ref, pair_ref, seq_ref, rows_ref, every_ref):
    count, width = own_ref.shape
    total = jnp.sum(terms_ref[...], axis=0)
    seq_ref[...] = (own_ref[...].astype(jnp.float32) + total[:count, :]).astype(jnp.bfloat16)
    trunk_mean = jnp.sum(trunk_ref[...].astype(jnp.float32), axis=0, keepdims=True) * (1.0 / PAIR_POOL)
    rows = None
    for c in range(N_PAIR):
        pooled = trunk_mean[:, c * width : (c + 1) * width] + total[count + c : count + c + 1, :]
        term = jnp.dot(
            jnp.broadcast_to(pooled, (8, width)).astype(jnp.bfloat16),
            w_pair_ref[c * width : (c + 1) * width, :],
            preferred_element_type=jnp.float32,
        )
        rows = term if rows is None else rows + term
    rows_ref[...] = rows
    mine = pair_ref[0].astype(jnp.float32)
    factors = jnp.broadcast_to(rows[:1], (mine.shape[0], rows.shape[1]))
    every = jnp.concatenate([factors, mine], axis=1)
    for at in range(0, every.shape[0], MIDDLE_SEQ):
        to = at ^ MIDDLE_SEQ
        every_ref[to : to + MIDDLE_SEQ, :] = every[at : at + MIDDLE_SEQ, :]


def close(terms, own, trunk, w_pair, pair_in):
    return pl.pallas_call(
        close_kernel,
        out_shape=(
            jax.ShapeDtypeStruct(own.shape, jnp.bfloat16),
            jax.ShapeDtypeStruct((8, w_pair.shape[1]), jnp.float32),
            jax.ShapeDtypeStruct((pair_in.shape[1], w_pair.shape[1] + pair_in.shape[2]), jnp.float32),
        ),
        in_specs=whole(5),
        out_specs=tuple(whole(3)),
        compiler_params=params(),
    )(terms, own, trunk, w_pair, pair_in)


def distance_bias(row, cols, pair_bias):
    delta = jnp.abs(row - cols)
    bins = jnp.zeros(delta.shape, jnp.int32)
    for edge in EDGES:
        bins = bins + (delta >= edge).astype(jnp.int32)
    labels = jnp.arange(pair_bias.shape[0], dtype=jnp.int32)
    onehot = (bins[:, None] == labels[None, :]).astype(jnp.bfloat16)
    return jnp.dot(onehot, pair_bias, preferred_element_type=jnp.float32)


def exchange(blocks, axes, middle=0):
    order = [index ^ middle for index in range(blocks.shape[0])]
    return lax.all_to_all(
        blocks, axes, split_axis=0, concat_axis=0, tiled=True, axis_index_groups=[order] if middle else None
    )


def on_device(tokens, w_stem, w_conv, w_query, w_key, w_value, w_out, w_pair, pair_bias, pair_in):
    place = lax.axis_index(SEQ)
    pair_place = lax.axis_index("pair")

    taps, width = w_conv.shape
    share = width // N_SHARE
    blocks, made = start(w_conv, w_stem, tokens)
    held = exchange(blocks, SEQ, MIDDLE_SEQ)

    section = stem(made, w_stem.shape[1]).astype(jnp.bfloat16)
    sections = lax.all_gather(section, SHARE, axis=0, tiled=False)

    parts = exchange(conv(place.astype(jnp.int32)[None], sections, held, made, share), SHARE + ("pair",))
    count = ROWS // 2
    trunk = parts.reshape(N_SHARE, N_PAIR, 2 * count, share).transpose(2, 1, 0, 3)
    trunk = trunk.reshape(2 * count, N_PAIR * width)

    core = lax.axis_index("core").astype(jnp.int32)[None]
    query, kv, trunk = project(core, trunk, w_query, w_key, w_value)
    for name in reversed(SPREAD[:-1]):
        other = lax.ppermute(query, name, [(0, 1), (1, 0)])
        query = jnp.concatenate([query, other], axis=0)
    kv = exchange(kv, LINE, MIDDLE_LINE)
    spread = lax.axis_index(SPREAD).astype(jnp.int32)[None]
    parts = exchange(attention(spread, query, kv), SPREAD, MIDDLE_SPREAD)
    terms = exchange(combine(parts, w_out), ("pair",), MIDDLE_PAIR)

    own = lax.dynamic_slice_in_dim(trunk, pair_place * width, width, 1)
    factors = jnp.concatenate([w_pair[0], w_pair[1]], axis=1)
    seq_out, rows, every = close(terms, own, trunk, factors, pair_in)
    channels = pair_in.shape[2]
    mine = pair_in[0].astype(jnp.float32)
    rows = rows[:1]
    every = exchange(every[:, None], SEQ, MIDDLE_SEQ)[:, 0]
    every = every.reshape(-1, 2, MIDDLE_SEQ, every.shape[1])[:, ::-1].reshape(every.shape)
    mirror = every[:, 2 * channels :]

    cols = jnp.arange(N_SEQ, dtype=jnp.int32)
    bias = distance_bias(place.astype(jnp.int32), cols, pair_bias)
    cross = rows[:, :channels] * every[:, channels : 2 * channels]
    cross = cross + every[:, :channels] * rows[:, channels:]
    pair_out = (0.5 * (mine + mirror + cross) + bias).astype(jnp.bfloat16)[None]
    return (seq_out, pair_out)


def solution(mesh):
    names = SEQ + ("pair",)
    fine = Mesh(mesh.devices.reshape([SIZES[name] for name in names]), names)
    placed = (
        P(SEQ),
        P(),
        P(SEQ, "pair"),
        P(None, "pair"),
        P(None, "pair"),
        P(None, "pair"),
        P("pair", None),
        P(None, None, "pair"),
        P(None, "pair"),
        P(SEQ, None, "pair"),
    )
    return jax.shard_map(
        on_device,
        mesh=fine,
        in_specs=placed,
        out_specs=(P(SEQ, "pair"), P(SEQ, None, "pair")),
        check_vma=False,
    )
```

```python
import math

import jax
import jax.numpy as jnp
from jax import lax
from jax.experimental import pallas as pl
from jax.experimental.pallas import tpu as pltpu
from jax.sharding import Mesh
from jax.sharding import PartitionSpec as P

HQK = 128
HV = 192
KS_STEM = 15
KS_CONV = 5
STEM_POOL = 64
PAIR_POOL = 16
EDGES = (1, 2, 3, 4, 6, 8, 12, 16, 24, 32, 48, 64, 96, 128, 192, 256, 384)

SIZES = {"zl": 2, "y": 8, "xh": 2, "xl": 2, "core": 2, "pair": 4}
SEQ = ("zl", "y", "xh", "xl", "core")
SHARE = ("zl", "xl", "core")
SPREAD = ("xh", "xl", "core")
LINE = ("zl", "y")
MIDDLE_SEQ = 32 + 2
MIDDLE_SHARE = 16 + 1
MIDDLE_LINE = 4
MIDDLE_SPREAD = 2
MIDDLE_PAIR = 1
N_SEQ = math.prod(SIZES[name] for name in SEQ)
N_SHARE = math.prod(SIZES[name] for name in SHARE)
N_PAIR = SIZES["pair"]
N_SPREAD = math.prod(SIZES[name] for name in SPREAD)
N_LINE = math.prod(SIZES[name] for name in LINE)

ROWS = 32
EXT_PAD = 40
RUN = 4
EDGES_RUN = 14
VMEM = 48 * 1024 * 1024
WHOLE = 60 * 1000 * 1000


def params(limit=VMEM):
    return pltpu.CompilerParams(vmem_limit_bytes=limit)


def whole(count):
    return [pl.BlockSpec(memory_space=pltpu.VMEM) for _ in range(count)]


def gelu(x):
    return 0.5 * x * (1.0 + jnp.tanh(math.sqrt(2.0 / math.pi) * (x + 0.044715 * (x * x * x))))


def onehot_rows(codes, first, count):
    length = codes.shape[1]
    start = (length - first - KS_STEM // 2) % length
    codes = jnp.broadcast_to(codes, (16, length))
    shifted = pltpu.roll(codes, start, 1, stride=1, stride_axis=0)
    shifted = shifted[:, :count]
    return jnp.concatenate(
        [(shifted == base + 1).astype(jnp.float32) for base in range(4)], axis=0
    ).astype(jnp.bfloat16)


def pooled_rows(onehot, weight):
    hidden = lax.dot_general(
        onehot, weight, (((0,), (0,)), ((), ())), preferred_element_type=jnp.float32
    ).reshape(onehot.shape[1] // STEM_POOL, STEM_POOL, weight.shape[1])
    high = gelu(jnp.max(hidden, axis=1))
    low = gelu(jnp.min(hidden, axis=1))
    return jnp.maximum(high, low)


def stem_kernel(made_ref, out_ref):
    onehot = onehot_rows(made_ref[64:, :].astype(jnp.float32), 0, made_ref.shape[1])
    weight = made_ref[:64, : out_ref.shape[1]]
    step = 8
    for at in range(0, ROWS, step):
        part = onehot[:, at * STEM_POOL : (at + step) * STEM_POOL]
        out_ref[at : at + step, :] = pooled_rows(part, weight)


def stem(made, channels):
    return pl.pallas_call(
        stem_kernel,
        out_shape=jax.ShapeDtypeStruct((ROWS, channels), jnp.float32),
        in_specs=whole(1),
        out_specs=whole(1)[0],
        compiler_params=params(),
        cost_estimate=pl.CostEstimate(flops=2 * 2048 * 64 * 768, bytes_accessed=200000, transcendentals=0),
    )(made)


def start_kernel(weight_ref, stem_ref, tokens_hbm, line_hbm, out_ref, made_ref, wide, tokens_ref, line_ref, arrived):
    copies = [
        pltpu.make_async_copy(tokens_hbm, tokens_ref, arrived.at[0]),
        pltpu.make_async_copy(line_hbm, line_ref, arrived.at[1]),
    ]
    for copy in copies:
        copy.start()
    rows, channels = stem_ref.shape
    row = lax.broadcasted_iota(jnp.int32, (64, rows), 0)
    column = lax.broadcasted_iota(jnp.int32, (64, rows), 1)
    picked = (column == (KS_STEM - 1 - row % 16) * 4 + row // 16) & (row % 16 < KS_STEM)
    picked = picked.astype(jnp.float32).astype(jnp.bfloat16)
    made = jnp.dot(picked, stem_ref[...], preferred_element_type=jnp.float32).astype(jnp.bfloat16)
    half = channels // 2
    row = lax.broadcasted_iota(jnp.int32, (channels, half), 0)
    column = lax.broadcasted_iota(jnp.int32, (channels, half), 1)
    for odd in range(2):
        order = (row == 2 * column + odd).astype(jnp.float32).astype(jnp.bfloat16)
        part = jnp.dot(made, order, preferred_element_type=jnp.float32)
        made_ref[:64, odd * half : (odd + 1) * half] = part.astype(jnp.bfloat16)
    taps, width = weight_ref.shape
    share = width // N_SHARE
    half = taps // 2
    even, odd = [], []
    for part in range(wide.shape[0]):
        lanes = weight_ref[:, part * HQK : (part + 1) * HQK]
        wide[part, :taps, :] = lanes.astype(jnp.float32)
        wide[part, taps:, :] = jnp.zeros((wide.shape[1] - taps, HQK), jnp.float32)
        even.append(wide[part, pl.ds(0, half + 1, stride=2), :])
        odd.append(wide[part, pl.ds(1, half + 1, stride=2), :])
    even, odd = jnp.concatenate(even, axis=1), jnp.concatenate(odd, axis=1)
    lane = lax.broadcasted_iota(jnp.int32, (half + 1, HQK), 1)
    row = lax.broadcasted_iota(jnp.int32, (half + 1, HQK), 0)
    for copy in copies:
        copy.wait()
    line = (line_ref[...] + 1).astype(jnp.float32).astype(jnp.bfloat16)
    made_ref[64:, :] = jnp.broadcast_to(line, (16, line.shape[1]))
    made_ref[:64, channels:] = jnp.zeros((64, line.shape[1] - channels), jnp.bfloat16)
    codes = (tokens_ref[...] + 1).astype(jnp.float32)
    last = codes.shape[0] - 1
    line = [jnp.broadcast_to(codes[at : at + 1, :], lane.shape) for at in (0, 1, last - 1, last)]
    outer = jnp.where(lane >= HQK - 7, line[2], pltpu.roll(line[1], 96, 1))
    for index in range(4):
        outer = jnp.where(row == index, pltpu.roll(line[3], (96 - 32 * index) % HQK, 1), outer)
    blocks = []
    for index in range(N_SHARE):
        low = pltpu.roll(even, (width - index * share) % width, 1)[:, :HQK]
        high = pltpu.roll(odd, (width - index * share + share) % width, 1)[:, :HQK]
        block = jnp.where(lane < share, low, jnp.where(lane < 2 * share, high, outer))
        blocks.append(jnp.where(row == half, line[0], block).astype(jnp.bfloat16))
    for place in range(N_SEQ):
        at, index, base = place, 0, 1
        for name in reversed(SEQ):
            if name in SHARE:
                index, base = index + base * (at % SIZES[name]), base * SIZES[name]
            at = at // SIZES[name]
        out_ref[place ^ MIDDLE_SEQ] = blocks[index]


def start(weight, stem_weight, tokens):
    taps, width = weight.shape
    tokens, line = tokens.reshape(-1, HQK), tokens.reshape(1, -1)
    return pl.pallas_call(
        start_kernel,
        out_shape=(
            jax.ShapeDtypeStruct((N_SEQ, taps // 2 + 1, HQK), jnp.bfloat16),
            jax.ShapeDtypeStruct((80, line.shape[1]), jnp.bfloat16),
        ),
        in_specs=whole(2) + [pl.BlockSpec(memory_space=pltpu.HBM)] * 2,
        out_specs=tuple(whole(2)),
        scratch_shapes=[
            pltpu.VMEM((width // HQK, taps + 2, HQK), jnp.float32),
            pltpu.VMEM(tokens.shape, jnp.int32),
            pltpu.VMEM(line.shape, jnp.int32),
            pltpu.SemaphoreType.DMA((2,)),
        ],
        compiler_params=params(WHOLE),
    )(weight, stem_weight, tokens, line)


def border_codes(held_ref, right):
    before = held_ref[jnp.maximum(right - 1, 0) ^ MIDDLE_SEQ].astype(jnp.float32)
    after = held_ref[jnp.minimum(right, N_SEQ - 1) ^ MIDDLE_SEQ].astype(jnp.float32)
    before = jnp.where(right > 0, before, 0.0)
    after = jnp.where(right < N_SEQ, after, 0.0)
    lane = lax.broadcasted_iota(jnp.int32, (1, HQK), 1)
    tail = jnp.zeros((1, HQK), jnp.float32)
    for index in range(4):
        part = pltpu.roll(before, (32 * index + 32) % HQK, 1)[index : index + 1, :]
        tail = jnp.where(lane // 32 == index, part, tail)
    return jnp.concatenate(
        [before[4:5, :], tail, after[15:16, :], pltpu.roll(after, 32, 1)[4:5, :]], axis=1
    )


def conv_kernel(place_ref, section_ref, held_ref, stem_ref, out_ref, weights, edges, wide, act, best):
    count, rows, _ = held_ref.shape
    for source in range(count):
        block = held_ref[source ^ MIDDLE_SEQ].astype(jnp.float32)
        weights[source * (rows - 1) : (source + 1) * (rows - 1), :] = block[: rows - 1, :]
    first = ((place_ref[0] & (N_SEQ // 2 - 1)) // RUN) * RUN
    for run in range(2):
        right = run * (N_SEQ // 2) + first
        onehot = jnp.concatenate(
            [
                onehot_rows(border_codes(held_ref, right + index), 192 if inner else 128, 128 if inner else 256)
                for index in range(RUN + 1)
                for inner in [0 < index < RUN]
            ],
            axis=1,
        )
        made = pooled_rows(onehot, stem_ref[:64, : section_ref.shape[2]])
        place = lax.broadcasted_iota(jnp.int32, made.shape, 0)
        outside = ((place < 2) & (right == 0)) | ((place >= EDGES_RUN - 2) & (right + RUN == count))
        edges[run * 16 : run * 16 + EDGES_RUN, :] = jnp.where(outside, 0.0, made)
    windows, _, channels = section_ref.shape
    half = channels // 2
    columns = out_ref.shape[2] // 8
    for window in range(windows):
        run, index = window // RUN, window % RUN
        rows = section_ref[window].astype(jnp.float32)
        wide[window, 3 : ROWS + 1, :] = rows[1 : ROWS - 1, :]
        at = run * 16 + 2 + 2 * index
        if index == 0:
            wide[window, 0:3, :] = edges[run * 16 : run * 16 + 3, :]
        else:
            wide[window, 1:3, :] = edges[at : at + 2, :]
            wide[window - 1, ROWS + 3 : ROWS + 4, :] = rows[1:2, :]
        at = at + 2
        if index == RUN - 1:
            wide[window, ROWS + 1 : ROWS + 4, :] = edges[at + 1 : at + 4, :]
        else:
            wide[window, ROWS + 1 : ROWS + 3, :] = edges[at : at + 2, :]
            wide[window + 1, 0:1, :] = rows[ROWS - 2 : ROWS - 1, :]
    even, odd = None, None
    for tap in range(KS_CONV):
        rows = wide[:, tap : tap + ROWS, :].astype(jnp.bfloat16).reshape(windows * ROWS, channels)
        weight = weights[tap * half : (tap + 1) * half, :].astype(jnp.bfloat16)
        term = jnp.dot(rows[:, :half], weight, preferred_element_type=jnp.float32)
        even = term if even is None else even + term
        term = jnp.dot(rows[:, half:], weight, preferred_element_type=jnp.float32)
        odd = term if odd is None else odd + term
    act[...] = jnp.zeros(act.shape, jnp.float32)
    act[:, :columns] = gelu(even[:, :columns] + odd[:, columns : 2 * columns])
    count = windows * ROWS // 2
    best[...] = jnp.maximum(act[pl.ds(0, count, stride=2), :], act[pl.ds(1, count, stride=2), :])
    flat = None
    for index in range(8):
        part = best[pl.ds(index, count // 8, stride=8), :]
        part = jnp.pad(part, ((0, 0), (0, 8 * columns - part.shape[1])))
        part = pltpu.roll(part, index * columns, 1)
        flat = part if flat is None else flat + part
    for window in range(windows):
        block = flat[window // 2 * 4 : window // 2 * 4 + 4, :].astype(jnp.bfloat16)
        for index in range(N_PAIR):
            out_ref[(window * N_PAIR + index) ^ MIDDLE_SHARE] = block


def conv(place, section, held, stem_weight, columns):
    windows, _, channels = section.shape
    return pl.pallas_call(
        conv_kernel,
        out_shape=jax.ShapeDtypeStruct((windows * N_PAIR, 4, 8 * columns), jnp.bfloat16),
        in_specs=[pl.BlockSpec(memory_space=pltpu.SMEM)] + whole(3),
        out_specs=whole(1)[0],
        scratch_shapes=[
            pltpu.VMEM((held.shape[0] * (held.shape[1] - 1), HQK), jnp.float32),
            pltpu.VMEM((32, channels), jnp.float32),
            pltpu.VMEM((windows, EXT_PAD, channels), jnp.float32),
            pltpu.VMEM((windows * ROWS, HQK), jnp.float32),
            pltpu.VMEM((windows * ROWS // 2, HQK), jnp.float32),
        ],
        compiler_params=params(),
    )(place, section, held, stem_weight)


def project_kernel(core_ref, trunk_ref, w_query_ref, w_key_ref, w_value_ref, query_ref, kv_ref, own_ref):
    trunk = trunk_ref[...]
    first = core_ref[0] == 0
    count = own_ref.shape[0]
    half = count // 2
    query_ref[...] = jnp.dot(trunk, w_query_ref[...], preferred_element_type=jnp.float32).astype(jnp.bfloat16)
    wide = trunk.astype(jnp.float32)
    own = jnp.where(first, wide[:count], wide[count:]).astype(jnp.bfloat16)
    own_ref[...] = own
    key = jnp.dot(own, w_key_ref[...], preferred_element_type=jnp.float32).astype(jnp.bfloat16)
    value = jnp.dot(own, w_value_ref[...], preferred_element_type=jnp.float32)
    rest = jnp.pad(value[:, HQK:], ((0, 0), (0, 2 * HQK - HV)))
    rest = (rest[:half] + pltpu.roll(rest[half:], HV - HQK, 1)).astype(jnp.bfloat16)
    value = value[:, :HQK].astype(jnp.bfloat16)
    for index in range(N_LINE):
        kv_ref[index, :count, :] = key
        kv_ref[index, count : 2 * count, :] = value
        kv_ref[index, 2 * count :, :] = rest


def project(core, trunk, w_query, w_key, w_value):
    count = trunk.shape[0] // 2
    return pl.pallas_call(
        project_kernel,
        out_shape=(
            jax.ShapeDtypeStruct((2 * count, HQK), jnp.bfloat16),
            jax.ShapeDtypeStruct((N_LINE, 2 * count + count // 2, HQK), jnp.bfloat16),
            jax.ShapeDtypeStruct((count, trunk.shape[1]), jnp.bfloat16),
        ),
        in_specs=[pl.BlockSpec(memory_space=pltpu.SMEM)] + whole(4),
        out_specs=tuple(whole(3)),
        compiler_params=params(),
    )(core, trunk, w_query, w_key, w_value)


def split(x):
    parts = []
    for _ in range(3):
        part = x.astype(jnp.bfloat16).astype(jnp.float32)
        parts.append(part)
        x = x - part
    return parts


def attention_kernel(place_ref, query_ref, kv_ref, out_ref):
    scale = 1.0 / math.sqrt(HQK)
    line, rows, _ = kv_ref.shape
    count = out_ref.shape[1]
    keys = kv_ref[:, :count, :].reshape(line * count, HQK)
    values = kv_ref[:, count : 2 * count, :].reshape(line * count, HQK)
    rest = kv_ref[:, 2 * count :, :].astype(jnp.float32)
    rest = jnp.stack([rest, pltpu.roll(rest, HQK - (HV - HQK), 2)], axis=1)
    rest = rest.reshape(line * count, HQK).astype(jnp.bfloat16)
    scores = (
        lax.dot_general(
            query_ref[...], keys, (((1,), (1,)), ((), ())), preferred_element_type=jnp.float32
        )
        * scale
    )
    top = jnp.max(scores, axis=1, keepdims=True)
    expo = jnp.exp(scores - top)
    total = jnp.sum(expo, axis=1, keepdims=True)
    expo = expo.astype(jnp.bfloat16)
    mixed = jnp.concatenate(
        [jnp.dot(expo, part, preferred_element_type=jnp.float32) for part in (values, rest)], axis=1
    )
    lane = lax.broadcasted_iota(jnp.int32, mixed.shape, 1)
    for index, column in enumerate(split(top) + split(total)):
        mixed = jnp.where(lane == HV + index, column, mixed)
    mixed = mixed.astype(jnp.bfloat16)
    groups, count, _ = out_ref.shape
    for index in range(groups):
        place = ((place_ref[0] >> 1) ^ (index // 2)) * 2 + index % 2
        out_ref[place ^ MIDDLE_SPREAD] = mixed[index * count : (index + 1) * count, :]


def attention(place, query, kv):
    groups = N_SPREAD
    count, width = query.shape[0] // groups, 2 * HQK
    return pl.pallas_call(
        attention_kernel,
        out_shape=jax.ShapeDtypeStruct((groups, count, width), jnp.bfloat16),
        in_specs=[pl.BlockSpec(memory_space=pltpu.SMEM)] + whole(2),
        out_specs=whole(1)[0],
        compiler_params=params(),
    )(place, query, kv)


def combine_kernel(parts_ref, w_out_ref, out_ref):
    parts = parts_ref[...].astype(jnp.float32)
    top = jnp.sum(parts[:, :, HV : HV + 3], axis=2, keepdims=True)
    gain = jnp.exp(top - jnp.max(top, axis=0, keepdims=True))
    total = jnp.sum(gain * jnp.sum(parts[:, :, HV + 3 : HV + 6], axis=2, keepdims=True), axis=0)
    mixed = (jnp.sum(gain * parts, axis=0) / total)[:, :HV].astype(jnp.bfloat16)
    term = jnp.dot(mixed, w_out_ref[...], preferred_element_type=jnp.float32)
    mean = jnp.sum(term, axis=0, keepdims=True) * (1.0 / PAIR_POOL)
    width = term.shape[1] // N_PAIR
    count = term.shape[0]
    tail = jnp.concatenate(
        [mean[:, c * width : (c + 1) * width] for c in range(N_PAIR)]
        + [jnp.zeros((8 - N_PAIR, width), jnp.float32)],
        axis=0,
    )
    for c in range(N_PAIR):
        out_ref[c ^ MIDDLE_PAIR, :count, :] = term[:, c * width : (c + 1) * width]
        out_ref[c ^ MIDDLE_PAIR, count:, :] = tail


def combine(parts, w_out):
    count = parts.shape[1]
    width = w_out.shape[1] // N_PAIR
    return pl.pallas_call(
        combine_kernel,
        out_shape=jax.ShapeDtypeStruct((N_PAIR, count + 8, width), jnp.float32),
        in_specs=whole(2),
        out_specs=whole(1)[0],
        compiler_params=params(),
    )(parts, w_out)


def close_kernel(terms_ref, own_ref, trunk_ref, w_pair_ref, pair_ref, seq_ref, rows_ref, every_ref):
    count, width = own_ref.shape
    total = jnp.sum(terms_ref[...], axis=0)
    seq_ref[...] = (own_ref[...].astype(jnp.float32) + total[:count, :]).astype(jnp.bfloat16)
    trunk_mean = jnp.sum(trunk_ref[...].astype(jnp.float32), axis=0, keepdims=True) * (1.0 / PAIR_POOL)
    rows = None
    for c in range(N_PAIR):
        pooled = trunk_mean[:, c * width : (c + 1) * width] + total[count + c : count + c + 1, :]
        term = jnp.dot(
            jnp.broadcast_to(pooled, (8, width)).astype(jnp.bfloat16),
            w_pair_ref[c * width : (c + 1) * width, :],
            preferred_element_type=jnp.float32,
        )
        rows = term if rows is None else rows + term
    rows_ref[...] = rows
    mine = pair_ref[0].astype(jnp.float32)
    factors = jnp.broadcast_to(rows[:1], (mine.shape[0], rows.shape[1]))
    every_ref[...] = jnp.concatenate([factors, mine], axis=1)


def close(terms, own, trunk, w_pair, pair_in):
    return pl.pallas_call(
        close_kernel,
        out_shape=(
            jax.ShapeDtypeStruct(own.shape, jnp.bfloat16),
            jax.ShapeDtypeStruct((8, w_pair.shape[1]), jnp.float32),
            jax.ShapeDtypeStruct((pair_in.shape[1], w_pair.shape[1] + pair_in.shape[2]), jnp.float32),
        ),
        in_specs=whole(5),
        out_specs=tuple(whole(3)),
        compiler_params=params(),
    )(terms, own, trunk, w_pair, pair_in)


def distance_bias(row, cols, pair_bias):
    delta = jnp.abs(row - cols)
    bins = jnp.zeros(delta.shape, jnp.int32)
    for edge in EDGES:
        bins = bins + (delta >= edge).astype(jnp.int32)
    labels = jnp.arange(pair_bias.shape[0], dtype=jnp.int32)
    onehot = (bins[:, None] == labels[None, :]).astype(jnp.bfloat16)
    return jnp.dot(onehot, pair_bias, preferred_element_type=jnp.float32)


def exchange(blocks, axes, middle=0):
    order = [index ^ middle for index in range(blocks.shape[0])]
    return lax.all_to_all(
        blocks, axes, split_axis=0, concat_axis=0, tiled=True, axis_index_groups=[order] if middle else None
    )


def from_middle(rows):
    return rows.reshape(2, 2, 8, 2, 2, -1)[:, ::-1, :, ::-1].reshape(rows.shape)


def on_device(tokens, w_stem, w_conv, w_query, w_key, w_value, w_out, w_pair, pair_bias, pair_in):
    place = lax.axis_index(SEQ)
    pair_place = lax.axis_index("pair")

    taps, width = w_conv.shape
    share = width // N_SHARE
    blocks, made = start(w_conv, w_stem, tokens)
    held = exchange(blocks, SEQ, MIDDLE_SEQ)

    section = stem(made, w_stem.shape[1]).astype(jnp.bfloat16)
    sections = lax.all_gather(section, SHARE, axis=0, tiled=False)

    parts = exchange(
        conv(place.astype(jnp.int32)[None], sections, held, made, share), SHARE + ("pair",), MIDDLE_SHARE
    )
    count = ROWS // 2
    parts = parts.reshape(2, N_SHARE // 2, 2, 2, 2 * count, share)[::-1, :, :, ::-1]
    trunk = parts.reshape(N_SHARE, N_PAIR, 2 * count, share).transpose(2, 1, 0, 3)
    trunk = trunk.reshape(2 * count, N_PAIR * width)

    core = lax.axis_index("core").astype(jnp.int32)[None]
    query, kv, trunk = project(core, trunk, w_query, w_key, w_value)
    for name in reversed(SPREAD[:-1]):
        other = lax.ppermute(query, name, [(0, 1), (1, 0)])
        query = jnp.concatenate([query, other], axis=0)
    kv = exchange(kv, LINE, MIDDLE_LINE)
    spread = lax.axis_index(SPREAD).astype(jnp.int32)[None]
    parts = exchange(attention(spread, query, kv), SPREAD, MIDDLE_SPREAD)
    terms = exchange(combine(parts, w_out), ("pair",), MIDDLE_PAIR)

    own = lax.dynamic_slice_in_dim(trunk, pair_place * width, width, 1)
    factors = jnp.concatenate([w_pair[0], w_pair[1]], axis=1)
    seq_out, rows, every = close(terms, own, trunk, factors, from_middle(pair_in[0])[None])
    channels = pair_in.shape[2]
    mine = pair_in[0].astype(jnp.float32)
    rows = rows[:1]
    every = exchange(every[:, None], SEQ, MIDDLE_SEQ)[:, 0]
    every = from_middle(every)
    mirror = every[:, 2 * channels :]

    cols = jnp.arange(N_SEQ, dtype=jnp.int32)
    bias = distance_bias(place.astype(jnp.int32), cols, pair_bias)
    cross = rows[:, :channels] * every[:, channels : 2 * channels]
    cross = cross + every[:, :channels] * rows[:, channels:]
    pair_out = (0.5 * (mine + mirror + cross) + bias).astype(jnp.bfloat16)[None]
    return (seq_out, pair_out)


def solution(mesh):
    names = SEQ + ("pair",)
    fine = Mesh(mesh.devices.reshape([SIZES[name] for name in names]), names)
    placed = (
        P(SEQ),
        P(),
        P(SEQ, "pair"),
        P(None, "pair"),
        P(None, "pair"),
        P(None, "pair"),
        P("pair", None),
        P(None, None, "pair"),
        P(None, "pair"),
        P(SEQ, None, "pair"),
    )
    return jax.shard_map(
        on_device,
        mesh=fine,
        in_specs=placed,
        out_specs=(P(SEQ, "pair"), P(SEQ, None, "pair")),
        check_vma=False,
    )
```

```python
import math

import jax
import jax.numpy as jnp
from jax import lax
from jax.experimental import pallas as pl
from jax.experimental.pallas import tpu as pltpu
from jax.sharding import Mesh
from jax.sharding import PartitionSpec as P

HQK = 128
HV = 192
KS_STEM = 15
KS_CONV = 5
STEM_POOL = 64
PAIR_POOL = 16
EDGES = (1, 2, 3, 4, 6, 8, 12, 16, 24, 32, 48, 64, 96, 128, 192, 256, 384)

SIZES = {"zl": 2, "y": 8, "xh": 2, "xl": 2, "core": 2, "pair": 4}
SEQ = ("zl", "y", "xh", "xl", "core")
SHARE = ("zl", "xl", "core")
SPREAD = ("xh", "xl", "core")
LINE = ("zl", "y")
MIDDLE_SEQ = 32
MIDDLE_SHARE = 16 + 1
MIDDLE_LINE = 4
MIDDLE_SPREAD = 2
MIDDLE_PAIR = 1
N_SEQ = math.prod(SIZES[name] for name in SEQ)
N_SHARE = math.prod(SIZES[name] for name in SHARE)
N_PAIR = SIZES["pair"]
N_SPREAD = math.prod(SIZES[name] for name in SPREAD)
N_LINE = math.prod(SIZES[name] for name in LINE)

ROWS = 32
EXT_PAD = 40
RUN = 4
EDGES_RUN = 14
VMEM = 48 * 1024 * 1024
WHOLE = 60 * 1000 * 1000


def params(limit=VMEM):
    return pltpu.CompilerParams(vmem_limit_bytes=limit)


def whole(count):
    return [pl.BlockSpec(memory_space=pltpu.VMEM) for _ in range(count)]


def gelu(x):
    return 0.5 * x * (1.0 + jnp.tanh(math.sqrt(2.0 / math.pi) * (x + 0.044715 * (x * x * x))))


def onehot_rows(codes, first, count):
    length = codes.shape[1]
    start = (length - first - KS_STEM // 2) % length
    codes = jnp.broadcast_to(codes, (16, length))
    shifted = pltpu.roll(codes, start, 1, stride=1, stride_axis=0)
    shifted = shifted[:, :count]
    return jnp.concatenate(
        [(shifted == base + 1).astype(jnp.float32) for base in range(4)], axis=0
    ).astype(jnp.bfloat16)


def pooled_rows(onehot, weight):
    hidden = lax.dot_general(
        onehot, weight, (((0,), (0,)), ((), ())), preferred_element_type=jnp.float32
    ).reshape(onehot.shape[1] // STEM_POOL, STEM_POOL, weight.shape[1])
    high = gelu(jnp.max(hidden, axis=1))
    low = gelu(jnp.min(hidden, axis=1))
    return jnp.maximum(high, low)


def stem_kernel(made_ref, out_ref):
    onehot = onehot_rows(made_ref[64:, :].astype(jnp.float32), 0, made_ref.shape[1])
    weight = made_ref[:64, : out_ref.shape[1]]
    step = 8
    for at in range(0, ROWS, step):
        part = onehot[:, at * STEM_POOL : (at + step) * STEM_POOL]
        out_ref[at : at + step, :] = pooled_rows(part, weight)


def stem(made, channels):
    return pl.pallas_call(
        stem_kernel,
        out_shape=jax.ShapeDtypeStruct((ROWS, channels), jnp.float32),
        in_specs=whole(1),
        out_specs=whole(1)[0],
        compiler_params=params(),
        cost_estimate=pl.CostEstimate(flops=2 * 2048 * 64 * 768, bytes_accessed=200000, transcendentals=0),
    )(made)


def start_kernel(weight_ref, stem_ref, tokens_hbm, line_hbm, out_ref, made_ref, wide, tokens_ref, line_ref, arrived):
    copies = [
        pltpu.make_async_copy(tokens_hbm, tokens_ref, arrived.at[0]),
        pltpu.make_async_copy(line_hbm, line_ref, arrived.at[1]),
    ]
    for copy in copies:
        copy.start()
    rows, channels = stem_ref.shape
    row = lax.broadcasted_iota(jnp.int32, (64, rows), 0)
    column = lax.broadcasted_iota(jnp.int32, (64, rows), 1)
    picked = (column == (KS_STEM - 1 - row % 16) * 4 + row // 16) & (row % 16 < KS_STEM)
    picked = picked.astype(jnp.float32).astype(jnp.bfloat16)
    made = jnp.dot(picked, stem_ref[...], preferred_element_type=jnp.float32).astype(jnp.bfloat16)
    half = channels // 2
    row = lax.broadcasted_iota(jnp.int32, (channels, half), 0)
    column = lax.broadcasted_iota(jnp.int32, (channels, half), 1)
    for odd in range(2):
        order = (row == 2 * column + odd).astype(jnp.float32).astype(jnp.bfloat16)
        part = jnp.dot(made, order, preferred_element_type=jnp.float32)
        made_ref[:64, odd * half : (odd + 1) * half] = part.astype(jnp.bfloat16)
    taps, width = weight_ref.shape
    share = width // N_SHARE
    half = taps // 2
    even, odd = [], []
    for part in range(wide.shape[0]):
        lanes = weight_ref[:, part * HQK : (part + 1) * HQK]
        wide[part, :taps, :] = lanes.astype(jnp.float32)
        wide[part, taps:, :] = jnp.zeros((wide.shape[1] - taps, HQK), jnp.float32)
        even.append(wide[part, pl.ds(0, half + 1, stride=2), :])
        odd.append(wide[part, pl.ds(1, half + 1, stride=2), :])
    even, odd = jnp.concatenate(even, axis=1), jnp.concatenate(odd, axis=1)
    lane = lax.broadcasted_iota(jnp.int32, (half + 1, HQK), 1)
    row = lax.broadcasted_iota(jnp.int32, (half + 1, HQK), 0)
    for copy in copies:
        copy.wait()
    line = (line_ref[...] + 1).astype(jnp.float32).astype(jnp.bfloat16)
    made_ref[64:, :] = jnp.broadcast_to(line, (16, line.shape[1]))
    made_ref[:64, channels:] = jnp.zeros((64, line.shape[1] - channels), jnp.bfloat16)
    codes = (tokens_ref[...] + 1).astype(jnp.float32)
    last = codes.shape[0] - 1
    line = [jnp.broadcast_to(codes[at : at + 1, :], lane.shape) for at in (0, 1, last - 1, last)]
    outer = jnp.where(lane >= HQK - 7, line[2], pltpu.roll(line[1], 96, 1))
    for index in range(4):
        outer = jnp.where(row == index, pltpu.roll(line[3], (96 - 32 * index) % HQK, 1), outer)
    blocks = []
    for index in range(N_SHARE):
        low = pltpu.roll(even, (width - index * share) % width, 1)[:, :HQK]
        high = pltpu.roll(odd, (width - index * share + share) % width, 1)[:, :HQK]
        block = jnp.where(lane < share, low, jnp.where(lane < 2 * share, high, outer))
        blocks.append(jnp.where(row == half, line[0], block).astype(jnp.bfloat16))
    for place in range(N_SEQ):
        at, index, base = place, 0, 1
        for name in reversed(SEQ):
            if name in SHARE:
                index, base = index + base * (at % SIZES[name]), base * SIZES[name]
            at = at // SIZES[name]
        out_ref[place] = blocks[index]


def start(weight, stem_weight, tokens):
    taps, width = weight.shape
    tokens, line = tokens.reshape(-1, HQK), tokens.reshape(1, -1)
    return pl.pallas_call(
        start_kernel,
        out_shape=(
            jax.ShapeDtypeStruct((N_SEQ, taps // 2 + 1, HQK), jnp.bfloat16),
            jax.ShapeDtypeStruct((80, line.shape[1]), jnp.bfloat16),
        ),
        in_specs=whole(2) + [pl.BlockSpec(memory_space=pltpu.HBM)] * 2,
        out_specs=tuple(whole(2)),
        scratch_shapes=[
            pltpu.VMEM((width // HQK, taps + 2, HQK), jnp.float32),
            pltpu.VMEM(tokens.shape, jnp.int32),
            pltpu.VMEM(line.shape, jnp.int32),
            pltpu.SemaphoreType.DMA((2,)),
        ],
        compiler_params=params(WHOLE),
    )(weight, stem_weight, tokens, line)


def border_codes(held_ref, right):
    before = held_ref[jnp.maximum(right - 1, 0) ^ MIDDLE_SEQ].astype(jnp.float32)
    after = held_ref[jnp.minimum(right, N_SEQ - 1) ^ MIDDLE_SEQ].astype(jnp.float32)
    before = jnp.where(right > 0, before, 0.0)
    after = jnp.where(right < N_SEQ, after, 0.0)
    lane = lax.broadcasted_iota(jnp.int32, (1, HQK), 1)
    tail = jnp.zeros((1, HQK), jnp.float32)
    for index in range(4):
        part = pltpu.roll(before, (32 * index + 32) % HQK, 1)[index : index + 1, :]
        tail = jnp.where(lane // 32 == index, part, tail)
    return jnp.concatenate(
        [before[4:5, :], tail, after[15:16, :], pltpu.roll(after, 32, 1)[4:5, :]], axis=1
    )


def conv_kernel(place_ref, section_ref, held_ref, stem_ref, out_ref, weights, edges, wide, act, best):
    count, rows, _ = held_ref.shape
    for source in range(count):
        block = held_ref[source ^ MIDDLE_SEQ].astype(jnp.float32)
        weights[source * (rows - 1) : (source + 1) * (rows - 1), :] = block[: rows - 1, :]
    first = ((place_ref[0] & (N_SEQ // 2 - 1)) // RUN) * RUN
    for run in range(2):
        right = run * (N_SEQ // 2) + first
        onehot = jnp.concatenate(
            [
                onehot_rows(border_codes(held_ref, right + index), 192 if inner else 128, 128 if inner else 256)
                for index in range(RUN + 1)
                for inner in [0 < index < RUN]
            ],
            axis=1,
        )
        made = pooled_rows(onehot, stem_ref[:64, : section_ref.shape[2]])
        place = lax.broadcasted_iota(jnp.int32, made.shape, 0)
        outside = ((place < 2) & (right == 0)) | ((place >= EDGES_RUN - 2) & (right + RUN == count))
        edges[run * 16 : run * 16 + EDGES_RUN, :] = jnp.where(outside, 0.0, made)
    windows, _, channels = section_ref.shape
    half = channels // 2
    columns = out_ref.shape[2] // 8
    for window in range(windows):
        run, index = window // RUN, window % RUN
        rows = section_ref[window].astype(jnp.float32)
        wide[window, 3 : ROWS + 1, :] = rows[1 : ROWS - 1, :]
        at = run * 16 + 2 + 2 * index
        if index == 0:
            wide[window, 0:3, :] = edges[run * 16 : run * 16 + 3, :]
        else:
            wide[window, 1:3, :] = edges[at : at + 2, :]
            wide[window - 1, ROWS + 3 : ROWS + 4, :] = rows[1:2, :]
        at = at + 2
        if index == RUN - 1:
            wide[window, ROWS + 1 : ROWS + 4, :] = edges[at + 1 : at + 4, :]
        else:
            wide[window, ROWS + 1 : ROWS + 3, :] = edges[at : at + 2, :]
            wide[window + 1, 0:1, :] = rows[ROWS - 2 : ROWS - 1, :]
    even, odd = None, None
    for tap in range(KS_CONV):
        rows = wide[:, tap : tap + ROWS, :].astype(jnp.bfloat16).reshape(windows * ROWS, channels)
        weight = weights[tap * half : (tap + 1) * half, :].astype(jnp.bfloat16)
        term = jnp.dot(rows[:, :half], weight, preferred_element_type=jnp.float32)
        even = term if even is None else even + term
        term = jnp.dot(rows[:, half:], weight, preferred_element_type=jnp.float32)
        odd = term if odd is None else odd + term
    act[...] = jnp.zeros(act.shape, jnp.float32)
    act[:, :columns] = gelu(even[:, :columns] + odd[:, columns : 2 * columns])
    count = windows * ROWS // 2
    best[...] = jnp.maximum(act[pl.ds(0, count, stride=2), :], act[pl.ds(1, count, stride=2), :])
    flat = None
    for index in range(8):
        part = best[pl.ds(index, count // 8, stride=8), :]
        part = jnp.pad(part, ((0, 0), (0, 8 * columns - part.shape[1])))
        part = pltpu.roll(part, index * columns, 1)
        flat = part if flat is None else flat + part
    for window in range(windows):
        block = flat[window // 2 * 4 : window // 2 * 4 + 4, :].astype(jnp.bfloat16)
        for index in range(N_PAIR):
            out_ref[(window * N_PAIR + index) ^ MIDDLE_SHARE] = block


def conv(place, section, held, stem_weight, columns):
    windows, _, channels = section.shape
    return pl.pallas_call(
        conv_kernel,
        out_shape=jax.ShapeDtypeStruct((windows * N_PAIR, 4, 8 * columns), jnp.bfloat16),
        in_specs=[pl.BlockSpec(memory_space=pltpu.SMEM)] + whole(3),
        out_specs=whole(1)[0],
        scratch_shapes=[
            pltpu.VMEM((held.shape[0] * (held.shape[1] - 1), HQK), jnp.float32),
            pltpu.VMEM((32, channels), jnp.float32),
            pltpu.VMEM((windows, EXT_PAD, channels), jnp.float32),
            pltpu.VMEM((windows * ROWS, HQK), jnp.float32),
            pltpu.VMEM((windows * ROWS // 2, HQK), jnp.float32),
        ],
        compiler_params=params(),
    )(place, section, held, stem_weight)


def project_kernel(core_ref, trunk_ref, w_query_ref, w_key_ref, w_value_ref, query_ref, kv_ref, own_ref):
    trunk = trunk_ref[...]
    first = core_ref[0] == 0
    count = own_ref.shape[0]
    half = count // 2
    query_ref[...] = jnp.dot(trunk, w_query_ref[...], preferred_element_type=jnp.float32).astype(jnp.bfloat16)
    wide = trunk.astype(jnp.float32)
    own = jnp.where(first, wide[:count], wide[count:]).astype(jnp.bfloat16)
    own_ref[...] = own
    key = jnp.dot(own, w_key_ref[...], preferred_element_type=jnp.float32).astype(jnp.bfloat16)
    value = jnp.dot(own, w_value_ref[...], preferred_element_type=jnp.float32)
    rest = jnp.pad(value[:, HQK:], ((0, 0), (0, 2 * HQK - HV)))
    rest = (rest[:half] + pltpu.roll(rest[half:], HV - HQK, 1)).astype(jnp.bfloat16)
    value = value[:, :HQK].astype(jnp.bfloat16)
    for index in range(N_LINE):
        kv_ref[index, :count, :] = key
        kv_ref[index, count : 2 * count, :] = value
        kv_ref[index, 2 * count :, :] = rest


def project(core, trunk, w_query, w_key, w_value):
    count = trunk.shape[0] // 2
    return pl.pallas_call(
        project_kernel,
        out_shape=(
            jax.ShapeDtypeStruct((2 * count, HQK), jnp.bfloat16),
            jax.ShapeDtypeStruct((N_LINE, 2 * count + count // 2, HQK), jnp.bfloat16),
            jax.ShapeDtypeStruct((count, trunk.shape[1]), jnp.bfloat16),
        ),
        in_specs=[pl.BlockSpec(memory_space=pltpu.SMEM)] + whole(4),
        out_specs=tuple(whole(3)),
        compiler_params=params(),
    )(core, trunk, w_query, w_key, w_value)


def split(x):
    parts = []
    for _ in range(3):
        part = x.astype(jnp.bfloat16).astype(jnp.float32)
        parts.append(part)
        x = x - part
    return parts


def attention_kernel(place_ref, query_ref, kv_ref, out_ref):
    scale = 1.0 / math.sqrt(HQK)
    line, rows, _ = kv_ref.shape
    count = out_ref.shape[1]
    keys = kv_ref[:, :count, :].reshape(line * count, HQK)
    values = kv_ref[:, count : 2 * count, :].reshape(line * count, HQK)
    rest = kv_ref[:, 2 * count :, :].astype(jnp.float32)
    rest = jnp.stack([rest, pltpu.roll(rest, HQK - (HV - HQK), 2)], axis=1)
    rest = rest.reshape(line * count, HQK).astype(jnp.bfloat16)
    scores = (
        lax.dot_general(
            query_ref[...], keys, (((1,), (1,)), ((), ())), preferred_element_type=jnp.float32
        )
        * scale
    )
    top = jnp.max(scores, axis=1, keepdims=True)
    expo = jnp.exp(scores - top)
    total = jnp.sum(expo, axis=1, keepdims=True)
    expo = expo.astype(jnp.bfloat16)
    mixed = jnp.concatenate(
        [jnp.dot(expo, part, preferred_element_type=jnp.float32) for part in (values, rest)], axis=1
    )
    lane = lax.broadcasted_iota(jnp.int32, mixed.shape, 1)
    for index, column in enumerate(split(top) + split(total)):
        mixed = jnp.where(lane == HV + index, column, mixed)
    mixed = mixed.astype(jnp.bfloat16)
    groups, count, _ = out_ref.shape
    for index in range(groups):
        place = ((place_ref[0] >> 1) ^ (index // 2)) * 2 + index % 2
        out_ref[place ^ MIDDLE_SPREAD] = mixed[index * count : (index + 1) * count, :]


def attention(place, query, kv):
    groups = N_SPREAD
    count, width = query.shape[0] // groups, 2 * HQK
    return pl.pallas_call(
        attention_kernel,
        out_shape=jax.ShapeDtypeStruct((groups, count, width), jnp.bfloat16),
        in_specs=[pl.BlockSpec(memory_space=pltpu.SMEM)] + whole(2),
        out_specs=whole(1)[0],
        compiler_params=params(),
    )(place, query, kv)


def combine_kernel(parts_ref, w_out_ref, out_ref):
    parts = parts_ref[...].astype(jnp.float32)
    top = jnp.sum(parts[:, :, HV : HV + 3], axis=2, keepdims=True)
    gain = jnp.exp(top - jnp.max(top, axis=0, keepdims=True))
    total = jnp.sum(gain * jnp.sum(parts[:, :, HV + 3 : HV + 6], axis=2, keepdims=True), axis=0)
    mixed = (jnp.sum(gain * parts, axis=0) / total)[:, :HV].astype(jnp.bfloat16)
    term = jnp.dot(mixed, w_out_ref[...], preferred_element_type=jnp.float32)
    mean = jnp.sum(term, axis=0, keepdims=True) * (1.0 / PAIR_POOL)
    width = term.shape[1] // N_PAIR
    count = term.shape[0]
    tail = jnp.concatenate(
        [mean[:, c * width : (c + 1) * width] for c in range(N_PAIR)]
        + [jnp.zeros((8 - N_PAIR, width), jnp.float32)],
        axis=0,
    )
    for c in range(N_PAIR):
        out_ref[c ^ MIDDLE_PAIR, :count, :] = term[:, c * width : (c + 1) * width]
        out_ref[c ^ MIDDLE_PAIR, count:, :] = tail


def combine(parts, w_out):
    count = parts.shape[1]
    width = w_out.shape[1] // N_PAIR
    return pl.pallas_call(
        combine_kernel,
        out_shape=jax.ShapeDtypeStruct((N_PAIR, count + 8, width), jnp.float32),
        in_specs=whole(2),
        out_specs=whole(1)[0],
        compiler_params=params(),
    )(parts, w_out)


def close_kernel(terms_ref, own_ref, trunk_ref, w_pair_ref, pair_ref, seq_ref, rows_ref, every_ref):
    count, width = own_ref.shape
    total = jnp.sum(terms_ref[...], axis=0)
    seq_ref[...] = (own_ref[...].astype(jnp.float32) + total[:count, :]).astype(jnp.bfloat16)
    trunk_mean = jnp.sum(trunk_ref[...].astype(jnp.float32), axis=0, keepdims=True) * (1.0 / PAIR_POOL)
    rows = None
    for c in range(N_PAIR):
        pooled = trunk_mean[:, c * width : (c + 1) * width] + total[count + c : count + c + 1, :]
        term = jnp.dot(
            jnp.broadcast_to(pooled, (8, width)).astype(jnp.bfloat16),
            w_pair_ref[c * width : (c + 1) * width, :],
            preferred_element_type=jnp.float32,
        )
        rows = term if rows is None else rows + term
    rows_ref[...] = rows
    mine = pair_ref[0].astype(jnp.float32)
    factors = jnp.broadcast_to(rows[:1], (mine.shape[0], rows.shape[1]))
    every = jnp.concatenate([factors, mine], axis=1)
    for at in range(0, every.shape[0], MIDDLE_SEQ):
        to = at ^ MIDDLE_SEQ
        every_ref[to : to + MIDDLE_SEQ, :] = every[at : at + MIDDLE_SEQ, :]


def close(terms, own, trunk, w_pair, pair_in):
    return pl.pallas_call(
        close_kernel,
        out_shape=(
            jax.ShapeDtypeStruct(own.shape, jnp.bfloat16),
            jax.ShapeDtypeStruct((8, w_pair.shape[1]), jnp.float32),
            jax.ShapeDtypeStruct((pair_in.shape[1], w_pair.shape[1] + pair_in.shape[2]), jnp.float32),
        ),
        in_specs=whole(5),
        out_specs=tuple(whole(3)),
        compiler_params=params(),
    )(terms, own, trunk, w_pair, pair_in)


def distance_bias(row, cols, pair_bias):
    delta = jnp.abs(row - cols)
    bins = jnp.zeros(delta.shape, jnp.int32)
    for edge in EDGES:
        bins = bins + (delta >= edge).astype(jnp.int32)
    labels = jnp.arange(pair_bias.shape[0], dtype=jnp.int32)
    onehot = (bins[:, None] == labels[None, :]).astype(jnp.bfloat16)
    return jnp.dot(onehot, pair_bias, preferred_element_type=jnp.float32)


def exchange(blocks, axes, middle=0):
    order = [index ^ middle for index in range(blocks.shape[0])]
    return lax.all_to_all(
        blocks, axes, split_axis=0, concat_axis=0, tiled=True, axis_index_groups=[order] if middle else None
    )


def on_device(tokens, w_stem, w_conv, w_query, w_key, w_value, w_out, w_pair, pair_bias, pair_in):
    place = lax.axis_index(SEQ)
    pair_place = lax.axis_index("pair")

    taps, width = w_conv.shape
    share = width // N_SHARE
    blocks, made = start(w_conv, w_stem, tokens)
    held = exchange(blocks, SEQ, MIDDLE_SEQ)

    section = stem(made, w_stem.shape[1]).astype(jnp.bfloat16)
    sections = lax.all_gather(section, SHARE, axis=0, tiled=False)

    parts = exchange(
        conv(place.astype(jnp.int32)[None], sections, held, made, share), SHARE + ("pair",), MIDDLE_SHARE
    )
    count = ROWS // 2
    parts = parts.reshape(2, N_SHARE // 2, 2, 2, 2 * count, share)[::-1, :, :, ::-1]
    trunk = parts.reshape(N_SHARE, N_PAIR, 2 * count, share).transpose(2, 1, 0, 3)
    trunk = trunk.reshape(2 * count, N_PAIR * width)

    core = lax.axis_index("core").astype(jnp.int32)[None]
    query, kv, trunk = project(core, trunk, w_query, w_key, w_value)
    for name in reversed(SPREAD[:-1]):
        other = lax.ppermute(query, name, [(0, 1), (1, 0)])
        query = jnp.concatenate([query, other], axis=0)
    kv = exchange(kv, LINE, MIDDLE_LINE)
    spread = lax.axis_index(SPREAD).astype(jnp.int32)[None]
    parts = exchange(attention(spread, query, kv), SPREAD, MIDDLE_SPREAD)
    terms = exchange(combine(parts, w_out), ("pair",), MIDDLE_PAIR)

    own = lax.dynamic_slice_in_dim(trunk, pair_place * width, width, 1)
    factors = jnp.concatenate([w_pair[0], w_pair[1]], axis=1)
    seq_out, rows, every = close(terms, own, trunk, factors, pair_in)
    channels = pair_in.shape[2]
    mine = pair_in[0].astype(jnp.float32)
    rows = rows[:1]
    every = exchange(every[:, None], SEQ, MIDDLE_SEQ)[:, 0]
    every = every.reshape(-1, 2, MIDDLE_SEQ, every.shape[1])[:, ::-1].reshape(every.shape)
    mirror = every[:, 2 * channels :]

    cols = jnp.arange(N_SEQ, dtype=jnp.int32)
    bias = distance_bias(place.astype(jnp.int32), cols, pair_bias)
    cross = rows[:, :channels] * every[:, channels : 2 * channels]
    cross = cross + every[:, :channels] * rows[:, channels:]
    pair_out = (0.5 * (mine + mirror + cross) + bias).astype(jnp.bfloat16)[None]
    return (seq_out, pair_out)


def solution(mesh):
    names = SEQ + ("pair",)
    fine = Mesh(mesh.devices.reshape([SIZES[name] for name in names]), names)
    placed = (
        P(SEQ),
        P(),
        P(SEQ, "pair"),
        P(None, "pair"),
        P(None, "pair"),
        P(None, "pair"),
        P("pair", None),
        P(None, None, "pair"),
        P(None, "pair"),
        P(SEQ, None, "pair"),
    )
    return jax.shard_map(
        on_device,
        mesh=fine,
        in_specs=placed,
        out_specs=(P(SEQ, "pair"), P(SEQ, None, "pair")),
        check_vma=False,
    )
```

```python
import math

import jax
import jax.numpy as jnp
from jax import lax
from jax.experimental import pallas as pl
from jax.experimental.pallas import tpu as pltpu
from jax.sharding import Mesh
from jax.sharding import PartitionSpec as P

HQK = 128
HV = 192
KS_STEM = 15
KS_CONV = 5
STEM_POOL = 64
PAIR_POOL = 16
EDGES = (1, 2, 3, 4, 6, 8, 12, 16, 24, 32, 48, 64, 96, 128, 192, 256, 384)

SIZES = {"zl": 2, "y": 8, "xh": 2, "xl": 2, "core": 2, "pair": 4}
SEQ = ("zl", "y", "xh", "xl", "core")
SHARE = ("zl", "xl", "core")
SPREAD = ("xh", "xl", "core")
LINE = ("zl", "y")
MIDDLE_SEQ = 32
MIDDLE_LINE = 4
MIDDLE_SPREAD = 2
MIDDLE_PAIR = 1
N_SEQ = math.prod(SIZES[name] for name in SEQ)
N_SHARE = math.prod(SIZES[name] for name in SHARE)
N_PAIR = SIZES["pair"]
N_SPREAD = math.prod(SIZES[name] for name in SPREAD)
N_LINE = math.prod(SIZES[name] for name in LINE)

ROWS = 32
EXT_PAD = 40
RUN = 4
EDGES_RUN = 14
VMEM = 48 * 1024 * 1024
WHOLE = 60 * 1000 * 1000


def params(limit=VMEM):
    return pltpu.CompilerParams(vmem_limit_bytes=limit)


def whole(count):
    return [pl.BlockSpec(memory_space=pltpu.VMEM) for _ in range(count)]


def gelu(x):
    return 0.5 * x * (1.0 + jnp.tanh(math.sqrt(2.0 / math.pi) * (x + 0.044715 * (x * x * x))))


def onehot_rows(codes, first, count):
    length = codes.shape[1]
    start = (length - first - KS_STEM // 2) % length
    codes = jnp.broadcast_to(codes, (16, length))
    shifted = pltpu.roll(codes, start, 1, stride=1, stride_axis=0)
    shifted = shifted[:, :count]
    return jnp.concatenate(
        [(shifted == base + 1).astype(jnp.float32) for base in range(4)], axis=0
    ).astype(jnp.bfloat16)


def pooled_rows(onehot, weight):
    hidden = lax.dot_general(
        onehot, weight, (((0,), (0,)), ((), ())), preferred_element_type=jnp.float32
    ).reshape(onehot.shape[1] // STEM_POOL, STEM_POOL, weight.shape[1])
    high = gelu(jnp.max(hidden, axis=1))
    low = gelu(jnp.min(hidden, axis=1))
    return jnp.maximum(high, low)


def stem_kernel(made_ref, out_ref):
    onehot = onehot_rows(made_ref[64:, :].astype(jnp.float32), 0, made_ref.shape[1])
    weight = made_ref[:64, : out_ref.shape[1]]
    step = 8
    for at in range(0, ROWS, step):
        part = onehot[:, at * STEM_POOL : (at + step) * STEM_POOL]
        out_ref[at : at + step, :] = pooled_rows(part, weight)


def stem(made, channels):
    return pl.pallas_call(
        stem_kernel,
        out_shape=jax.ShapeDtypeStruct((ROWS, channels), jnp.float32),
        in_specs=whole(1),
        out_specs=whole(1)[0],
        compiler_params=params(),
        cost_estimate=pl.CostEstimate(flops=2 * 2048 * 64 * 768, bytes_accessed=200000, transcendentals=0),
    )(made)


def start_kernel(weight_ref, stem_ref, tokens_hbm, line_hbm, out_ref, made_ref, wide, tokens_ref, line_ref, arrived):
    copies = [
        pltpu.make_async_copy(tokens_hbm, tokens_ref, arrived.at[0]),
        pltpu.make_async_copy(line_hbm, line_ref, arrived.at[1]),
    ]
    for copy in copies:
        copy.start()
    rows, channels = stem_ref.shape
    row = lax.broadcasted_iota(jnp.int32, (64, rows), 0)
    column = lax.broadcasted_iota(jnp.int32, (64, rows), 1)
    picked = (column == (KS_STEM - 1 - row % 16) * 4 + row // 16) & (row % 16 < KS_STEM)
    picked = picked.astype(jnp.float32).astype(jnp.bfloat16)
    made = jnp.dot(picked, stem_ref[...], preferred_element_type=jnp.float32).astype(jnp.bfloat16)
    half = channels // 2
    row = lax.broadcasted_iota(jnp.int32, (channels, half), 0)
    column = lax.broadcasted_iota(jnp.int32, (channels, half), 1)
    for odd in range(2):
        order = (row == 2 * column + odd).astype(jnp.float32).astype(jnp.bfloat16)
        part = jnp.dot(made, order, preferred_element_type=jnp.float32)
        made_ref[:64, odd * half : (odd + 1) * half] = part.astype(jnp.bfloat16)
    taps, width = weight_ref.shape
    share = width // N_SHARE
    half = taps // 2
    even, odd = [], []
    for part in range(wide.shape[0]):
        lanes = weight_ref[:, part * HQK : (part + 1) * HQK]
        wide[part, :taps, :] = lanes.astype(jnp.float32)
        wide[part, taps:, :] = jnp.zeros((wide.shape[1] - taps, HQK), jnp.float32)
        even.append(wide[part, pl.ds(0, half + 1, stride=2), :])
        odd.append(wide[part, pl.ds(1, half + 1, stride=2), :])
    even, odd = jnp.concatenate(even, axis=1), jnp.concatenate(odd, axis=1)
    lane = lax.broadcasted_iota(jnp.int32, (half + 1, HQK), 1)
    row = lax.broadcasted_iota(jnp.int32, (half + 1, HQK), 0)
    for copy in copies:
        copy.wait()
    line = (line_ref[...] + 1).astype(jnp.float32).astype(jnp.bfloat16)
    made_ref[64:, :] = jnp.broadcast_to(line, (16, line.shape[1]))
    made_ref[:64, channels:] = jnp.zeros((64, line.shape[1] - channels), jnp.bfloat16)
    codes = (tokens_ref[...] + 1).astype(jnp.float32)
    last = codes.shape[0] - 1
    line = [jnp.broadcast_to(codes[at : at + 1, :], lane.shape) for at in (0, 1, last - 1, last)]
    outer = jnp.where(lane >= HQK - 7, line[2], pltpu.roll(line[1], 96, 1))
    for index in range(4):
        outer = jnp.where(row == index, pltpu.roll(line[3], (96 - 32 * index) % HQK, 1), outer)
    blocks = []
    for index in range(N_SHARE):
        low = pltpu.roll(even, (width - index * share) % width, 1)[:, :HQK]
        high = pltpu.roll(odd, (width - index * share + share) % width, 1)[:, :HQK]
        block = jnp.where(lane < share, low, jnp.where(lane < 2 * share, high, outer))
        blocks.append(jnp.where(row == half, line[0], block).astype(jnp.bfloat16))
    for place in range(N_SEQ):
        at, index, base = place, 0, 1
        for name in reversed(SEQ):
            if name in SHARE:
                index, base = index + base * (at % SIZES[name]), base * SIZES[name]
            at = at // SIZES[name]
        out_ref[place] = blocks[index]


def start(weight, stem_weight, tokens):
    taps, width = weight.shape
    tokens, line = tokens.reshape(-1, HQK), tokens.reshape(1, -1)
    return pl.pallas_call(
        start_kernel,
        out_shape=(
            jax.ShapeDtypeStruct((N_SEQ, taps // 2 + 1, HQK), jnp.bfloat16),
            jax.ShapeDtypeStruct((80, line.shape[1]), jnp.bfloat16),
        ),
        in_specs=whole(2) + [pl.BlockSpec(memory_space=pltpu.HBM)] * 2,
        out_specs=tuple(whole(2)),
        scratch_shapes=[
            pltpu.VMEM((width // HQK, taps + 2, HQK), jnp.float32),
            pltpu.VMEM(tokens.shape, jnp.int32),
            pltpu.VMEM(line.shape, jnp.int32),
            pltpu.SemaphoreType.DMA((2,)),
        ],
        compiler_params=params(WHOLE),
    )(weight, stem_weight, tokens, line)


def border_codes(held_ref, right):
    before = held_ref[jnp.maximum(right - 1, 0) ^ MIDDLE_SEQ].astype(jnp.float32)
    after = held_ref[jnp.minimum(right, N_SEQ - 1) ^ MIDDLE_SEQ].astype(jnp.float32)
    before = jnp.where(right > 0, before, 0.0)
    after = jnp.where(right < N_SEQ, after, 0.0)
    lane = lax.broadcasted_iota(jnp.int32, (1, HQK), 1)
    tail = jnp.zeros((1, HQK), jnp.float32)
    for index in range(4):
        part = pltpu.roll(before, (32 * index + 32) % HQK, 1)[index : index + 1, :]
        tail = jnp.where(lane // 32 == index, part, tail)
    return jnp.concatenate(
        [before[4:5, :], tail, after[15:16, :], pltpu.roll(after, 32, 1)[4:5, :]], axis=1
    )


def conv_kernel(place_ref, section_ref, held_ref, stem_ref, out_ref, weights, edges, wide, act, best):
    count, rows, _ = held_ref.shape
    for source in range(count):
        block = held_ref[source ^ MIDDLE_SEQ].astype(jnp.float32)
        weights[source * (rows - 1) : (source + 1) * (rows - 1), :] = block[: rows - 1, :]
    first = ((place_ref[0] & (N_SEQ // 2 - 1)) // RUN) * RUN
    for run in range(2):
        right = run * (N_SEQ // 2) + first
        onehot = jnp.concatenate(
            [
                onehot_rows(border_codes(held_ref, right + index), 192 if inner else 128, 128 if inner else 256)
                for index in range(RUN + 1)
                for inner in [0 < index < RUN]
            ],
            axis=1,
        )
        made = pooled_rows(onehot, stem_ref[:64, : section_ref.shape[2]])
        place = lax.broadcasted_iota(jnp.int32, made.shape, 0)
        outside = ((place < 2) & (right == 0)) | ((place >= EDGES_RUN - 2) & (right + RUN == count))
        edges[run * 16 : run * 16 + EDGES_RUN, :] = jnp.where(outside, 0.0, made)
    windows, _, channels = section_ref.shape
    half = channels // 2
    columns = out_ref.shape[2] // 8
    for window in range(windows):
        run, index = window // RUN, window % RUN
        rows = section_ref[window].astype(jnp.float32)
        wide[window, 3 : ROWS + 1, :] = rows[1 : ROWS - 1, :]
        at = run * 16 + 2 + 2 * index
        if index == 0:
            wide[window, 0:3, :] = edges[run * 16 : run * 16 + 3, :]
        else:
            wide[window, 1:3, :] = edges[at : at + 2, :]
            wide[window - 1, ROWS + 3 : ROWS + 4, :] = rows[1:2, :]
        at = at + 2
        if index == RUN - 1:
            wide[window, ROWS + 1 : ROWS + 4, :] = edges[at + 1 : at + 4, :]
        else:
            wide[window, ROWS + 1 : ROWS + 3, :] = edges[at : at + 2, :]
            wide[window + 1, 0:1, :] = rows[ROWS - 2 : ROWS - 1, :]
    even, odd = None, None
    for tap in range(KS_CONV):
        rows = wide[:, tap : tap + ROWS, :].astype(jnp.bfloat16).reshape(windows * ROWS, channels)
        weight = weights[tap * half : (tap + 1) * half, :].astype(jnp.bfloat16)
        term = jnp.dot(rows[:, :half], weight, preferred_element_type=jnp.float32)
        even = term if even is None else even + term
        term = jnp.dot(rows[:, half:], weight, preferred_element_type=jnp.float32)
        odd = term if odd is None else odd + term
    act[...] = jnp.zeros(act.shape, jnp.float32)
    act[:, :columns] = gelu(even[:, :columns] + odd[:, columns : 2 * columns])
    count = windows * ROWS // 2
    best[...] = jnp.maximum(act[pl.ds(0, count, stride=2), :], act[pl.ds(1, count, stride=2), :])
    flat = None
    for index in range(8):
        part = best[pl.ds(index, count // 8, stride=8), :]
        part = jnp.pad(part, ((0, 0), (0, 8 * columns - part.shape[1])))
        part = pltpu.roll(part, index * columns, 1)
        flat = part if flat is None else flat + part
    for window in range(windows):
        block = flat[window // 2 * 4 : window // 2 * 4 + 4, :].astype(jnp.bfloat16)
        for index in range(N_PAIR):
            out_ref[window * N_PAIR + index] = block


def conv(place, section, held, stem_weight, columns):
    windows, _, channels = section.shape
    return pl.pallas_call(
        conv_kernel,
        out_shape=jax.ShapeDtypeStruct((windows * N_PAIR, 4, 8 * columns), jnp.bfloat16),
        in_specs=[pl.BlockSpec(memory_space=pltpu.SMEM)] + whole(3),
        out_specs=whole(1)[0],
        scratch_shapes=[
            pltpu.VMEM((held.shape[0] * (held.shape[1] - 1), HQK), jnp.float32),
            pltpu.VMEM((32, channels), jnp.float32),
            pltpu.VMEM((windows, EXT_PAD, channels), jnp.float32),
            pltpu.VMEM((windows * ROWS, HQK), jnp.float32),
            pltpu.VMEM((windows * ROWS // 2, HQK), jnp.float32),
        ],
        compiler_params=params(),
    )(place, section, held, stem_weight)


def project_kernel(core_ref, trunk_ref, w_query_ref, w_key_ref, w_value_ref, query_ref, kv_ref, own_ref):
    trunk = trunk_ref[...]
    first = core_ref[0] == 0
    count = own_ref.shape[0]
    half = count // 2
    query_ref[...] = jnp.dot(trunk, w_query_ref[...], preferred_element_type=jnp.float32).astype(jnp.bfloat16)
    wide = trunk.astype(jnp.float32)
    own = jnp.where(first, wide[:count], wide[count:]).astype(jnp.bfloat16)
    own_ref[...] = own
    key = jnp.dot(own, w_key_ref[...], preferred_element_type=jnp.float32).astype(jnp.bfloat16)
    value = jnp.dot(own, w_value_ref[...], preferred_element_type=jnp.float32)
    rest = jnp.pad(value[:, HQK:], ((0, 0), (0, 2 * HQK - HV)))
    rest = (rest[:half] + pltpu.roll(rest[half:], HV - HQK, 1)).astype(jnp.bfloat16)
    value = value[:, :HQK].astype(jnp.bfloat16)
    for index in range(N_LINE):
        kv_ref[index, :count, :] = key
        kv_ref[index, count : 2 * count, :] = value
        kv_ref[index, 2 * count :, :] = rest


def project(core, trunk, w_query, w_key, w_value):
    count = trunk.shape[0] // 2
    return pl.pallas_call(
        project_kernel,
        out_shape=(
            jax.ShapeDtypeStruct((2 * count, HQK), jnp.bfloat16),
            jax.ShapeDtypeStruct((N_LINE, 2 * count + count // 2, HQK), jnp.bfloat16),
            jax.ShapeDtypeStruct((count, trunk.shape[1]), jnp.bfloat16),
        ),
        in_specs=[pl.BlockSpec(memory_space=pltpu.SMEM)] + whole(4),
        out_specs=tuple(whole(3)),
        compiler_params=params(),
    )(core, trunk, w_query, w_key, w_value)


def split(x):
    parts = []
    for _ in range(3):
        part = x.astype(jnp.bfloat16).astype(jnp.float32)
        parts.append(part)
        x = x - part
    return parts


def attention_kernel(place_ref, query_ref, kv_ref, out_ref):
    scale = 1.0 / math.sqrt(HQK)
    line, rows, _ = kv_ref.shape
    count = out_ref.shape[1]
    keys = kv_ref[:, :count, :].reshape(line * count, HQK)
    values = kv_ref[:, count : 2 * count, :].reshape(line * count, HQK)
    rest = kv_ref[:, 2 * count :, :].astype(jnp.float32)
    rest = jnp.stack([rest, pltpu.roll(rest, HQK - (HV - HQK), 2)], axis=1)
    rest = rest.reshape(line * count, HQK).astype(jnp.bfloat16)
    scores = (
        lax.dot_general(
            query_ref[...], keys, (((1,), (1,)), ((), ())), preferred_element_type=jnp.float32
        )
        * scale
    )
    top = jnp.max(scores, axis=1, keepdims=True)
    expo = jnp.exp(scores - top)
    total = jnp.sum(expo, axis=1, keepdims=True)
    expo = expo.astype(jnp.bfloat16)
    mixed = jnp.concatenate(
        [jnp.dot(expo, part, preferred_element_type=jnp.float32) for part in (values, rest)], axis=1
    )
    lane = lax.broadcasted_iota(jnp.int32, mixed.shape, 1)
    for index, column in enumerate(split(top) + split(total)):
        mixed = jnp.where(lane == HV + index, column, mixed)
    mixed = mixed.astype(jnp.bfloat16)
    flips = (0, 2, 1, 3)
    groups, count, _ = out_ref.shape
    for index in range(groups):
        place = ((place_ref[0] >> 1) ^ flips[index // 2]) * 2 + index % 2
        out_ref[place ^ MIDDLE_SPREAD] = mixed[index * count : (index + 1) * count, :]


def attention(place, query, kv):
    groups = N_SPREAD
    count, width = query.shape[0] // groups, 2 * HQK
    return pl.pallas_call(
        attention_kernel,
        out_shape=jax.ShapeDtypeStruct((groups, count, width), jnp.bfloat16),
        in_specs=[pl.BlockSpec(memory_space=pltpu.SMEM)] + whole(2),
        out_specs=whole(1)[0],
        compiler_params=params(),
    )(place, query, kv)


def combine_kernel(parts_ref, w_out_ref, out_ref):
    parts = parts_ref[...].astype(jnp.float32)
    top = jnp.sum(parts[:, :, HV : HV + 3], axis=2, keepdims=True)
    gain = jnp.exp(top - jnp.max(top, axis=0, keepdims=True))
    total = jnp.sum(gain * jnp.sum(parts[:, :, HV + 3 : HV + 6], axis=2, keepdims=True), axis=0)
    mixed = (jnp.sum(gain * parts, axis=0) / total)[:, :HV].astype(jnp.bfloat16)
    term = jnp.dot(mixed, w_out_ref[...], preferred_element_type=jnp.float32)
    mean = jnp.sum(term, axis=0, keepdims=True) * (1.0 / PAIR_POOL)
    width = term.shape[1] // N_PAIR
    count = term.shape[0]
    tail = jnp.concatenate(
        [mean[:, c * width : (c + 1) * width] for c in range(N_PAIR)]
        + [jnp.zeros((8 - N_PAIR, width), jnp.float32)],
        axis=0,
    )
    for c in range(N_PAIR):
        out_ref[c ^ MIDDLE_PAIR, :count, :] = term[:, c * width : (c + 1) * width]
        out_ref[c ^ MIDDLE_PAIR, count:, :] = tail


def combine(parts, w_out):
    count = parts.shape[1]
    width = w_out.shape[1] // N_PAIR
    return pl.pallas_call(
        combine_kernel,
        out_shape=jax.ShapeDtypeStruct((N_PAIR, count + 8, width), jnp.float32),
        in_specs=whole(2),
        out_specs=whole(1)[0],
        compiler_params=params(),
    )(parts, w_out)


def close_kernel(terms_ref, own_ref, trunk_ref, w_pair_ref, pair_ref, seq_ref, rows_ref, every_ref):
    count, width = own_ref.shape
    total = jnp.sum(terms_ref[...], axis=0)
    seq_ref[...] = (own_ref[...].astype(jnp.float32) + total[:count, :]).astype(jnp.bfloat16)
    trunk_mean = jnp.sum(trunk_ref[...].astype(jnp.float32), axis=0, keepdims=True) * (1.0 / PAIR_POOL)
    rows = None
    for c in range(N_PAIR):
        pooled = trunk_mean[:, c * width : (c + 1) * width] + total[count + c : count + c + 1, :]
        term = jnp.dot(
            jnp.broadcast_to(pooled, (8, width)).astype(jnp.bfloat16),
            w_pair_ref[c * width : (c + 1) * width, :],
            preferred_element_type=jnp.float32,
        )
        rows = term if rows is None else rows + term
    rows_ref[...] = rows
    mine = pair_ref[0].astype(jnp.float32)
    factors = jnp.broadcast_to(rows[:1], (mine.shape[0], rows.shape[1]))
    every = jnp.concatenate([factors, mine], axis=1)
    for at in range(0, every.shape[0], MIDDLE_SEQ):
        to = at ^ MIDDLE_SEQ
        every_ref[to : to + MIDDLE_SEQ, :] = every[at : at + MIDDLE_SEQ, :]


def close(terms, own, trunk, w_pair, pair_in):
    return pl.pallas_call(
        close_kernel,
        out_shape=(
            jax.ShapeDtypeStruct(own.shape, jnp.bfloat16),
            jax.ShapeDtypeStruct((8, w_pair.shape[1]), jnp.float32),
            jax.ShapeDtypeStruct((pair_in.shape[1], w_pair.shape[1] + pair_in.shape[2]), jnp.float32),
        ),
        in_specs=whole(5),
        out_specs=tuple(whole(3)),
        compiler_params=params(),
    )(terms, own, trunk, w_pair, pair_in)


def distance_bias(row, cols, pair_bias):
    delta = jnp.abs(row - cols)
    bins = jnp.zeros(delta.shape, jnp.int32)
    for edge in EDGES:
        bins = bins + (delta >= edge).astype(jnp.int32)
    labels = jnp.arange(pair_bias.shape[0], dtype=jnp.int32)
    onehot = (bins[:, None] == labels[None, :]).astype(jnp.bfloat16)
    return jnp.dot(onehot, pair_bias, preferred_element_type=jnp.float32)


def exchange(blocks, axes, middle=0):
    order = [index ^ middle for index in range(blocks.shape[0])]
    return lax.all_to_all(
        blocks, axes, split_axis=0, concat_axis=0, tiled=True, axis_index_groups=[order] if middle else None
    )


def on_device(tokens, w_stem, w_conv, w_query, w_key, w_value, w_out, w_pair, pair_bias, pair_in):
    place = lax.axis_index(SEQ)
    pair_place = lax.axis_index("pair")

    taps, width = w_conv.shape
    share = width // N_SHARE
    blocks, made = start(w_conv, w_stem, tokens)
    held = exchange(blocks, SEQ, MIDDLE_SEQ)

    section = stem(made, w_stem.shape[1]).astype(jnp.bfloat16)
    sections = lax.all_gather(section, SHARE, axis=0, tiled=False)

    parts = exchange(conv(place.astype(jnp.int32)[None], sections, held, made, share), SHARE + ("pair",))
    count = ROWS // 2
    trunk = parts.reshape(N_SHARE, N_PAIR, 2 * count, share).transpose(2, 1, 0, 3)
    trunk = trunk.reshape(2 * count, N_PAIR * width)

    core = lax.axis_index("core").astype(jnp.int32)[None]
    query, kv, trunk = project(core, trunk, w_query, w_key, w_value)
    for name in SPREAD[:-1]:
        other = lax.ppermute(query, name, [(0, 1), (1, 0)])
        query = jnp.concatenate([query, other], axis=0)
    kv = exchange(kv, LINE, MIDDLE_LINE)
    spread = lax.axis_index(SPREAD).astype(jnp.int32)[None]
    parts = exchange(attention(spread, query, kv), SPREAD, MIDDLE_SPREAD)
    terms = exchange(combine(parts, w_out), ("pair",), MIDDLE_PAIR)

    own = lax.dynamic_slice_in_dim(trunk, pair_place * width, width, 1)
    factors = jnp.concatenate([w_pair[0], w_pair[1]], axis=1)
    seq_out, rows, every = close(terms, own, trunk, factors, pair_in)
    channels = pair_in.shape[2]
    mine = pair_in[0].astype(jnp.float32)
    rows = rows[:1]
    every = exchange(every[:, None], SEQ, MIDDLE_SEQ)[:, 0]
    every = every.reshape(-1, 2, MIDDLE_SEQ, every.shape[1])[:, ::-1].reshape(every.shape)
    mirror = every[:, 2 * channels :]

    cols = jnp.arange(N_SEQ, dtype=jnp.int32)
    bias = lax.optimization_barrier(distance_bias(place.astype(jnp.int32), cols, pair_bias))
    cross = rows[:, :channels] * every[:, channels : 2 * channels]
    cross = cross + every[:, :channels] * rows[:, channels:]
    pair_out = (0.5 * (mine + mirror + cross) + bias).astype(jnp.bfloat16)[None]
    return (seq_out, pair_out)


def solution(mesh):
    names = SEQ + ("pair",)
    fine = Mesh(mesh.devices.reshape([SIZES[name] for name in names]), names)
    placed = (
        P(SEQ),
        P(),
        P(SEQ, "pair"),
        P(None, "pair"),
        P(None, "pair"),
        P(None, "pair"),
        P("pair", None),
        P(None, None, "pair"),
        P(None, "pair"),
        P(SEQ, None, "pair"),
    )
    return jax.shard_map(
        on_device,
        mesh=fine,
        in_specs=placed,
        out_specs=(P(SEQ, "pair"), P(SEQ, None, "pair")),
        check_vma=False,
    )
```

```python
import math

import jax
import jax.numpy as jnp
from jax import lax
from jax.experimental import pallas as pl
from jax.experimental.pallas import tpu as pltpu
from jax.sharding import Mesh
from jax.sharding import PartitionSpec as P

HQK = 128
HV = 192
KS_STEM = 15
KS_CONV = 5
STEM_POOL = 64
PAIR_POOL = 16
EDGES = (1, 2, 3, 4, 6, 8, 12, 16, 24, 32, 48, 64, 96, 128, 192, 256, 384)

SIZES = {"zl": 2, "y": 8, "xh": 2, "xl": 2, "core": 2, "pair": 4}
SEQ = ("zl", "y", "xh", "xl", "core")
SHARE = ("zl", "xl", "core")
SPREAD = ("xh", "xl", "core")
LINE = ("zl", "y")
MIDDLE_SEQ = 32
MIDDLE_LINE = 4
MIDDLE_SPREAD = 2
MIDDLE_PAIR = 1
N_SEQ = math.prod(SIZES[name] for name in SEQ)
N_SHARE = math.prod(SIZES[name] for name in SHARE)
N_PAIR = SIZES["pair"]
N_SPREAD = math.prod(SIZES[name] for name in SPREAD)
N_LINE = math.prod(SIZES[name] for name in LINE)

ROWS = 32
EXT_PAD = 40
RUN = 4
EDGES_RUN = 14
VMEM = 48 * 1024 * 1024
WHOLE = 60 * 1000 * 1000


def params(limit=VMEM):
    return pltpu.CompilerParams(vmem_limit_bytes=limit)


def whole(count):
    return [pl.BlockSpec(memory_space=pltpu.VMEM) for _ in range(count)]


def gelu(x):
    return 0.5 * x * (1.0 + jnp.tanh(math.sqrt(2.0 / math.pi) * (x + 0.044715 * (x * x * x))))


def onehot_rows(codes, first, count):
    length = codes.shape[1]
    start = (length - first - KS_STEM // 2) % length
    codes = jnp.broadcast_to(codes, (16, length))
    shifted = pltpu.roll(codes, start, 1, stride=1, stride_axis=0)
    shifted = shifted[:, :count]
    return jnp.concatenate(
        [(shifted == base + 1).astype(jnp.float32) for base in range(4)], axis=0
    ).astype(jnp.bfloat16)


def pooled_rows(onehot, weight):
    hidden = lax.dot_general(
        onehot, weight, (((0,), (0,)), ((), ())), preferred_element_type=jnp.float32
    ).reshape(onehot.shape[1] // STEM_POOL, STEM_POOL, weight.shape[1])
    high = gelu(jnp.max(hidden, axis=1))
    low = gelu(jnp.min(hidden, axis=1))
    return jnp.maximum(high, low)


def stem_kernel(made_ref, out_ref):
    onehot = onehot_rows(made_ref[64:, :].astype(jnp.float32), 0, made_ref.shape[1])
    weight = made_ref[:64, : out_ref.shape[1]]
    step = 8
    for at in range(0, ROWS, step):
        part = onehot[:, at * STEM_POOL : (at + step) * STEM_POOL]
        out_ref[at : at + step, :] = pooled_rows(part, weight)


def stem(made, channels):
    return pl.pallas_call(
        stem_kernel,
        out_shape=jax.ShapeDtypeStruct((ROWS, channels), jnp.float32),
        in_specs=whole(1),
        out_specs=whole(1)[0],
        compiler_params=params(),
        cost_estimate=pl.CostEstimate(flops=2 * 2048 * 64 * 768, bytes_accessed=200000, transcendentals=0),
    )(made)


def start_kernel(weight_ref, stem_ref, tokens_hbm, line_hbm, out_ref, made_ref, wide, tokens_ref, line_ref, arrived):
    copies = [
        pltpu.make_async_copy(tokens_hbm, tokens_ref, arrived.at[0]),
        pltpu.make_async_copy(line_hbm, line_ref, arrived.at[1]),
    ]
    for copy in copies:
        copy.start()
    rows, channels = stem_ref.shape
    row = lax.broadcasted_iota(jnp.int32, (64, rows), 0)
    column = lax.broadcasted_iota(jnp.int32, (64, rows), 1)
    picked = (column == (KS_STEM - 1 - row % 16) * 4 + row // 16) & (row % 16 < KS_STEM)
    picked = picked.astype(jnp.float32).astype(jnp.bfloat16)
    made = jnp.dot(picked, stem_ref[...], preferred_element_type=jnp.float32).astype(jnp.bfloat16)
    half = channels // 2
    row = lax.broadcasted_iota(jnp.int32, (channels, half), 0)
    column = lax.broadcasted_iota(jnp.int32, (channels, half), 1)
    for odd in range(2):
        order = (row == 2 * column + odd).astype(jnp.float32).astype(jnp.bfloat16)
        part = jnp.dot(made, order, preferred_element_type=jnp.float32)
        made_ref[:64, odd * half : (odd + 1) * half] = part.astype(jnp.bfloat16)
    taps, width = weight_ref.shape
    share = width // N_SHARE
    half = taps // 2
    even, odd = [], []
    for part in range(wide.shape[0]):
        lanes = weight_ref[:, part * HQK : (part + 1) * HQK]
        wide[part, :taps, :] = lanes.astype(jnp.float32)
        wide[part, taps:, :] = jnp.zeros((wide.shape[1] - taps, HQK), jnp.float32)
        even.append(wide[part, pl.ds(0, half + 1, stride=2), :])
        odd.append(wide[part, pl.ds(1, half + 1, stride=2), :])
    even, odd = jnp.concatenate(even, axis=1), jnp.concatenate(odd, axis=1)
    lane = lax.broadcasted_iota(jnp.int32, (half + 1, HQK), 1)
    row = lax.broadcasted_iota(jnp.int32, (half + 1, HQK), 0)
    for copy in copies:
        copy.wait()
    line = (line_ref[...] + 1).astype(jnp.float32).astype(jnp.bfloat16)
    made_ref[64:, :] = jnp.broadcast_to(line, (16, line.shape[1]))
    made_ref[:64, channels:] = jnp.zeros((64, line.shape[1] - channels), jnp.bfloat16)
    codes = (tokens_ref[...] + 1).astype(jnp.float32)
    last = codes.shape[0] - 1
    line = [jnp.broadcast_to(codes[at : at + 1, :], lane.shape) for at in (0, 1, last - 1, last)]
    outer = jnp.where(lane >= HQK - 7, line[2], pltpu.roll(line[1], 96, 1))
    for index in range(4):
        outer = jnp.where(row == index, pltpu.roll(line[3], (96 - 32 * index) % HQK, 1), outer)
    blocks = []
    for index in range(N_SHARE):
        low = pltpu.roll(even, (width - index * share) % width, 1)[:, :HQK]
        high = pltpu.roll(odd, (width - index * share + share) % width, 1)[:, :HQK]
        block = jnp.where(lane < share, low, jnp.where(lane < 2 * share, high, outer))
        blocks.append(jnp.where(row == half, line[0], block).astype(jnp.bfloat16))
    for place in range(N_SEQ):
        at, index, base = place, 0, 1
        for name in reversed(SEQ):
            if name in SHARE:
                index, base = index + base * (at % SIZES[name]), base * SIZES[name]
            at = at // SIZES[name]
        out_ref[place] = blocks[index]


def start(weight, stem_weight, tokens):
    taps, width = weight.shape
    tokens, line = tokens.reshape(-1, HQK), tokens.reshape(1, -1)
    return pl.pallas_call(
        start_kernel,
        out_shape=(
            jax.ShapeDtypeStruct((N_SEQ, taps // 2 + 1, HQK), jnp.bfloat16),
            jax.ShapeDtypeStruct((80, line.shape[1]), jnp.bfloat16),
        ),
        in_specs=whole(2) + [pl.BlockSpec(memory_space=pltpu.HBM)] * 2,
        out_specs=tuple(whole(2)),
        scratch_shapes=[
            pltpu.VMEM((width // HQK, taps + 2, HQK), jnp.float32),
            pltpu.VMEM(tokens.shape, jnp.int32),
            pltpu.VMEM(line.shape, jnp.int32),
            pltpu.SemaphoreType.DMA((2,)),
        ],
        compiler_params=params(WHOLE),
    )(weight, stem_weight, tokens, line)


def border_codes(held_ref, right):
    before = held_ref[jnp.maximum(right - 1, 0) ^ MIDDLE_SEQ].astype(jnp.float32)
    after = held_ref[jnp.minimum(right, N_SEQ - 1) ^ MIDDLE_SEQ].astype(jnp.float32)
    before = jnp.where(right > 0, before, 0.0)
    after = jnp.where(right < N_SEQ, after, 0.0)
    lane = lax.broadcasted_iota(jnp.int32, (1, HQK), 1)
    tail = jnp.zeros((1, HQK), jnp.float32)
    for index in range(4):
        part = pltpu.roll(before, (32 * index + 32) % HQK, 1)[index : index + 1, :]
        tail = jnp.where(lane // 32 == index, part, tail)
    return jnp.concatenate(
        [before[4:5, :], tail, after[15:16, :], pltpu.roll(after, 32, 1)[4:5, :]], axis=1
    )


def conv_kernel(place_ref, section_ref, held_ref, stem_ref, out_ref, weights, edges, wide, act, best):
    count, rows, _ = held_ref.shape
    for source in range(count):
        block = held_ref[source ^ MIDDLE_SEQ].astype(jnp.float32)
        weights[source * (rows - 1) : (source + 1) * (rows - 1), :] = block[: rows - 1, :]
    first = ((place_ref[0] & (N_SEQ // 2 - 1)) // RUN) * RUN
    for run in range(2):
        right = run * (N_SEQ // 2) + first
        onehot = jnp.concatenate(
            [
                onehot_rows(border_codes(held_ref, right + index), 192 if inner else 128, 128 if inner else 256)
                for index in range(RUN + 1)
                for inner in [0 < index < RUN]
            ],
            axis=1,
        )
        made = pooled_rows(onehot, stem_ref[:64, : section_ref.shape[2]])
        place = lax.broadcasted_iota(jnp.int32, made.shape, 0)
        outside = ((place < 2) & (right == 0)) | ((place >= EDGES_RUN - 2) & (right + RUN == count))
        edges[run * 16 : run * 16 + EDGES_RUN, :] = jnp.where(outside, 0.0, made)
    windows, _, channels = section_ref.shape
    half = channels // 2
    columns = out_ref.shape[2] // 8
    for window in range(windows):
        run, index = window // RUN, window % RUN
        rows = section_ref[window].astype(jnp.float32)
        wide[window, 3 : ROWS + 1, :] = rows[1 : ROWS - 1, :]
        at = run * 16 + 2 + 2 * index
        if index == 0:
            wide[window, 0:3, :] = edges[run * 16 : run * 16 + 3, :]
        else:
            wide[window, 1:3, :] = edges[at : at + 2, :]
            wide[window - 1, ROWS + 3 : ROWS + 4, :] = rows[1:2, :]
        at = at + 2
        if index == RUN - 1:
            wide[window, ROWS + 1 : ROWS + 4, :] = edges[at + 1 : at + 4, :]
        else:
            wide[window, ROWS + 1 : ROWS + 3, :] = edges[at : at + 2, :]
            wide[window + 1, 0:1, :] = rows[ROWS - 2 : ROWS - 1, :]
    even, odd = None, None
    for tap in range(KS_CONV):
        rows = wide[:, tap : tap + ROWS, :].astype(jnp.bfloat16).reshape(windows * ROWS, channels)
        weight = weights[tap * half : (tap + 1) * half, :].astype(jnp.bfloat16)
        term = jnp.dot(rows[:, :half], weight, preferred_element_type=jnp.float32)
        even = term if even is None else even + term
        term = jnp.dot(rows[:, half:], weight, preferred_element_type=jnp.float32)
        odd = term if odd is None else odd + term
    act[...] = jnp.zeros(act.shape, jnp.float32)
    act[:, :columns] = gelu(even[:, :columns] + odd[:, columns : 2 * columns])
    count = windows * ROWS // 2
    best[...] = jnp.maximum(act[pl.ds(0, count, stride=2), :], act[pl.ds(1, count, stride=2), :])
    flat = None
    for index in range(8):
        part = best[pl.ds(index, count // 8, stride=8), :]
        part = jnp.pad(part, ((0, 0), (0, 8 * columns - part.shape[1])))
        part = pltpu.roll(part, index * columns, 1)
        flat = part if flat is None else flat + part
    for window in range(windows):
        block = flat[window // 2 * 4 : window // 2 * 4 + 4, :].astype(jnp.bfloat16)
        for index in range(N_PAIR):
            out_ref[window * N_PAIR + index] = block


def conv(place, section, held, stem_weight, columns):
    windows, _, channels = section.shape
    return pl.pallas_call(
        conv_kernel,
        out_shape=jax.ShapeDtypeStruct((windows * N_PAIR, 4, 8 * columns), jnp.bfloat16),
        in_specs=[pl.BlockSpec(memory_space=pltpu.SMEM)] + whole(3),
        out_specs=whole(1)[0],
        scratch_shapes=[
            pltpu.VMEM((held.shape[0] * (held.shape[1] - 1), HQK), jnp.float32),
            pltpu.VMEM((32, channels), jnp.float32),
            pltpu.VMEM((windows, EXT_PAD, channels), jnp.float32),
            pltpu.VMEM((windows * ROWS, HQK), jnp.float32),
            pltpu.VMEM((windows * ROWS // 2, HQK), jnp.float32),
        ],
        compiler_params=params(),
    )(place, section, held, stem_weight)


def project_kernel(core_ref, trunk_ref, weight_ref, query_ref, kv_ref, own_ref):
    trunk = trunk_ref[...]
    first = core_ref[0] == 0
    count = own_ref.shape[0]
    half = count // 2
    query = jnp.dot(trunk, weight_ref[:, :HQK], preferred_element_type=jnp.float32)
    query_ref[...] = query.astype(jnp.bfloat16)
    wide = trunk.astype(jnp.float32)
    own = jnp.where(first, wide[:count], wide[count:]).astype(jnp.bfloat16)
    own_ref[...] = own
    key = jnp.dot(own, weight_ref[:, HQK : 2 * HQK], preferred_element_type=jnp.float32)
    key = key.astype(jnp.bfloat16)
    value = jnp.dot(own, weight_ref[:, 2 * HQK :], preferred_element_type=jnp.float32)
    rest = jnp.pad(value[:, HQK:], ((0, 0), (0, 2 * HQK - HV)))
    rest = (rest[:half] + pltpu.roll(rest[half:], HV - HQK, 1)).astype(jnp.bfloat16)
    value = value[:, :HQK].astype(jnp.bfloat16)
    for index in range(N_LINE):
        kv_ref[index, :count, :] = key
        kv_ref[index, count : 2 * count, :] = value
        kv_ref[index, 2 * count :, :] = rest


def project(core, trunk, weight):
    count = trunk.shape[0] // 2
    return pl.pallas_call(
        project_kernel,
        out_shape=(
            jax.ShapeDtypeStruct((2 * count, HQK), jnp.bfloat16),
            jax.ShapeDtypeStruct((N_LINE, 2 * count + count // 2, HQK), jnp.bfloat16),
            jax.ShapeDtypeStruct((count, trunk.shape[1]), jnp.bfloat16),
        ),
        in_specs=[pl.BlockSpec(memory_space=pltpu.SMEM)] + whole(2),
        out_specs=tuple(whole(3)),
        compiler_params=params(),
    )(core, trunk, weight)


def split(x):
    parts = []
    for _ in range(3):
        part = x.astype(jnp.bfloat16).astype(jnp.float32)
        parts.append(part)
        x = x - part
    return parts


def attention_kernel(place_ref, query_ref, kv_ref, out_ref):
    scale = 1.0 / math.sqrt(HQK)
    line, rows, _ = kv_ref.shape
    count = out_ref.shape[1]
    keys = kv_ref[:, :count, :].reshape(line * count, HQK)
    values = kv_ref[:, count : 2 * count, :].reshape(line * count, HQK)
    rest = kv_ref[:, 2 * count :, :].astype(jnp.float32)
    rest = jnp.stack([rest, pltpu.roll(rest, HQK - (HV - HQK), 2)], axis=1)
    rest = rest.reshape(line * count, HQK).astype(jnp.bfloat16)
    scores = (
        lax.dot_general(
            query_ref[...], keys, (((1,), (1,)), ((), ())), preferred_element_type=jnp.float32
        )
        * scale
    )
    top = jnp.max(scores, axis=1, keepdims=True)
    expo = jnp.exp(scores - top)
    total = jnp.sum(expo, axis=1, keepdims=True)
    expo = expo.astype(jnp.bfloat16)
    mixed = jnp.concatenate(
        [jnp.dot(expo, part, preferred_element_type=jnp.float32) for part in (values, rest)], axis=1
    )
    lane = lax.broadcasted_iota(jnp.int32, mixed.shape, 1)
    for index, column in enumerate(split(top) + split(total)):
        mixed = jnp.where(lane == HV + index, column, mixed)
    mixed = mixed.astype(jnp.bfloat16)
    flips = (0, 2, 1, 3)
    groups, count, _ = out_ref.shape
    for index in range(groups):
        place = ((place_ref[0] >> 1) ^ flips[index // 2]) * 2 + index % 2
        out_ref[place ^ MIDDLE_SPREAD] = mixed[index * count : (index + 1) * count, :]


def attention(place, query, kv):
    groups = N_SPREAD
    count, width = query.shape[0] // groups, 2 * HQK
    return pl.pallas_call(
        attention_kernel,
        out_shape=jax.ShapeDtypeStruct((groups, count, width), jnp.bfloat16),
        in_specs=[pl.BlockSpec(memory_space=pltpu.SMEM)] + whole(2),
        out_specs=whole(1)[0],
        compiler_params=params(),
    )(place, query, kv)


def combine_kernel(parts_ref, w_out_ref, out_ref):
    parts = parts_ref[...].astype(jnp.float32)
    top = jnp.sum(parts[:, :, HV : HV + 3], axis=2, keepdims=True)
    gain = jnp.exp(top - jnp.max(top, axis=0, keepdims=True))
    total = jnp.sum(gain * jnp.sum(parts[:, :, HV + 3 : HV + 6], axis=2, keepdims=True), axis=0)
    mixed = (jnp.sum(gain * parts, axis=0) / total)[:, :HV].astype(jnp.bfloat16)
    term = jnp.dot(mixed, w_out_ref[...], preferred_element_type=jnp.float32)
    mean = jnp.sum(term, axis=0, keepdims=True) * (1.0 / PAIR_POOL)
    width = term.shape[1] // N_PAIR
    count = term.shape[0]
    tail = jnp.concatenate(
        [mean[:, c * width : (c + 1) * width] for c in range(N_PAIR)]
        + [jnp.zeros((8 - N_PAIR, width), jnp.float32)],
        axis=0,
    )
    for c in range(N_PAIR):
        out_ref[c ^ MIDDLE_PAIR, :count, :] = term[:, c * width : (c + 1) * width]
        out_ref[c ^ MIDDLE_PAIR, count:, :] = tail


def combine(parts, w_out):
    count = parts.shape[1]
    width = w_out.shape[1] // N_PAIR
    return pl.pallas_call(
        combine_kernel,
        out_shape=jax.ShapeDtypeStruct((N_PAIR, count + 8, width), jnp.float32),
        in_specs=whole(2),
        out_specs=whole(1)[0],
        compiler_params=params(),
    )(parts, w_out)


def close_kernel(terms_ref, own_ref, trunk_ref, w_pair_ref, pair_ref, seq_ref, rows_ref, every_ref):
    count, width = own_ref.shape
    total = jnp.sum(terms_ref[...], axis=0)
    seq_ref[...] = (own_ref[...].astype(jnp.float32) + total[:count, :]).astype(jnp.bfloat16)
    trunk_mean = jnp.sum(trunk_ref[...].astype(jnp.float32), axis=0, keepdims=True) * (1.0 / PAIR_POOL)
    rows = None
    for c in range(N_PAIR):
        pooled = trunk_mean[:, c * width : (c + 1) * width] + total[count + c : count + c + 1, :]
        term = jnp.dot(
            jnp.broadcast_to(pooled, (8, width)).astype(jnp.bfloat16),
            w_pair_ref[c * width : (c + 1) * width, :],
            preferred_element_type=jnp.float32,
        )
        rows = term if rows is None else rows + term
    rows_ref[...] = rows
    mine = pair_ref[0].astype(jnp.float32)
    factors = jnp.broadcast_to(rows[:1], (mine.shape[0], rows.shape[1]))
    every = jnp.concatenate([factors, mine], axis=1)
    for at in range(0, every.shape[0], MIDDLE_SEQ):
        to = at ^ MIDDLE_SEQ
        every_ref[to : to + MIDDLE_SEQ, :] = every[at : at + MIDDLE_SEQ, :]


def close(terms, own, trunk, w_pair, pair_in):
    return pl.pallas_call(
        close_kernel,
        out_shape=(
            jax.ShapeDtypeStruct(own.shape, jnp.bfloat16),
            jax.ShapeDtypeStruct((8, w_pair.shape[1]), jnp.float32),
            jax.ShapeDtypeStruct((pair_in.shape[1], w_pair.shape[1] + pair_in.shape[2]), jnp.float32),
        ),
        in_specs=whole(5),
        out_specs=tuple(whole(3)),
        compiler_params=params(),
    )(terms, own, trunk, w_pair, pair_in)


def distance_bias(row, cols, pair_bias):
    delta = jnp.abs(row - cols)
    bins = jnp.zeros(delta.shape, jnp.int32)
    for edge in EDGES:
        bins = bins + (delta >= edge).astype(jnp.int32)
    labels = jnp.arange(pair_bias.shape[0], dtype=jnp.int32)
    onehot = (bins[:, None] == labels[None, :]).astype(jnp.bfloat16)
    return jnp.dot(onehot, pair_bias, preferred_element_type=jnp.float32)


def exchange(blocks, axes, middle=0):
    order = [index ^ middle for index in range(blocks.shape[0])]
    return lax.all_to_all(
        blocks, axes, split_axis=0, concat_axis=0, tiled=True, axis_index_groups=[order] if middle else None
    )


def on_device(tokens, w_stem, w_conv, w_query, w_key, w_value, w_out, w_pair, pair_bias, pair_in):
    place = lax.axis_index(SEQ)
    pair_place = lax.axis_index("pair")

    taps, width = w_conv.shape
    share = width // N_SHARE
    blocks, made = start(w_conv, w_stem, tokens)
    held = exchange(blocks, SEQ, MIDDLE_SEQ)

    section = stem(made, w_stem.shape[1]).astype(jnp.bfloat16)
    sections = lax.all_gather(section, SHARE, axis=0, tiled=False)

    parts = exchange(conv(place.astype(jnp.int32)[None], sections, held, made, share), SHARE + ("pair",))
    count = ROWS // 2
    trunk = parts.reshape(N_SHARE, N_PAIR, 2 * count, share).transpose(2, 1, 0, 3)
    trunk = trunk.reshape(2 * count, N_PAIR * width)

    core = lax.axis_index("core").astype(jnp.int32)[None]
    query, kv, trunk = project(core, trunk, jnp.concatenate([w_query, w_key, w_value], axis=1))
    for name in SPREAD[:-1]:
        other = lax.ppermute(query, name, [(0, 1), (1, 0)])
        query = jnp.concatenate([query, other], axis=0)
    kv = exchange(kv, LINE, MIDDLE_LINE)
    spread = lax.axis_index(SPREAD).astype(jnp.int32)[None]
    parts = exchange(attention(spread, query, kv), SPREAD, MIDDLE_SPREAD)
    terms = exchange(combine(parts, w_out), ("pair",), MIDDLE_PAIR)

    own = lax.dynamic_slice_in_dim(trunk, pair_place * width, width, 1)
    factors = jnp.concatenate([w_pair[0], w_pair[1]], axis=1)
    seq_out, rows, every = close(terms, own, trunk, factors, pair_in)
    channels = pair_in.shape[2]
    mine = pair_in[0].astype(jnp.float32)
    rows = rows[:1]
    every = exchange(every[:, None], SEQ, MIDDLE_SEQ)[:, 0]
    every = every.reshape(-1, 2, MIDDLE_SEQ, every.shape[1])[:, ::-1].reshape(every.shape)
    mirror = every[:, 2 * channels :]

    cols = jnp.arange(N_SEQ, dtype=jnp.int32)
    bias = lax.optimization_barrier(distance_bias(place.astype(jnp.int32), cols, pair_bias))
    cross = rows[:, :channels] * every[:, channels : 2 * channels]
    cross = cross + every[:, :channels] * rows[:, channels:]
    pair_out = (0.5 * (mine + mirror + cross) + bias).astype(jnp.bfloat16)[None]
    return (seq_out, pair_out)


def solution(mesh):
    names = SEQ + ("pair",)
    fine = Mesh(mesh.devices.reshape([SIZES[name] for name in names]), names)
    placed = (
        P(SEQ),
        P(),
        P(SEQ, "pair"),
        P(None, "pair"),
        P(None, "pair"),
        P(None, "pair"),
        P("pair", None),
        P(None, None, "pair"),
        P(None, "pair"),
        P(SEQ, None, "pair"),
    )
    return jax.shard_map(
        on_device,
        mesh=fine,
        in_specs=placed,
        out_specs=(P(SEQ, "pair"), P(SEQ, None, "pair")),
        check_vma=False,
    )
```

```python
import math

import jax
import jax.numpy as jnp
from jax import lax
from jax.experimental import pallas as pl
from jax.experimental.pallas import tpu as pltpu
from jax.sharding import Mesh
from jax.sharding import PartitionSpec as P

HQK = 128
HV = 192
KS_STEM = 15
KS_CONV = 5
STEM_POOL = 64
PAIR_POOL = 16
EDGES = (1, 2, 3, 4, 6, 8, 12, 16, 24, 32, 48, 64, 96, 128, 192, 256, 384)

SIZES = {"zl": 2, "y": 8, "xh": 2, "xl": 2, "core": 2, "pair": 4}
SEQ = ("zl", "y", "xh", "xl", "core")
SHARE = ("zl", "xl", "core")
SPREAD = ("xh", "xl", "core")
LINE = ("zl", "y")
MIDDLE_SEQ = 32
LATE_SHARE = 3
MIDDLE_LINE = 4
MIDDLE_SPREAD = 2
MIDDLE_PAIR = 1
N_SEQ = math.prod(SIZES[name] for name in SEQ)
N_SHARE = math.prod(SIZES[name] for name in SHARE)
N_PAIR = SIZES["pair"]
N_SPREAD = math.prod(SIZES[name] for name in SPREAD)
N_LINE = math.prod(SIZES[name] for name in LINE)

ROWS = 32
EXT_PAD = 40
RUN = 4
EDGES_RUN = 14
VMEM = 48 * 1024 * 1024
WHOLE = 60 * 1000 * 1000


def params(limit=VMEM):
    return pltpu.CompilerParams(vmem_limit_bytes=limit)


def whole(count):
    return [pl.BlockSpec(memory_space=pltpu.VMEM) for _ in range(count)]


def gelu(x):
    return 0.5 * x * (1.0 + jnp.tanh(math.sqrt(2.0 / math.pi) * (x + 0.044715 * (x * x * x))))


def onehot_rows(codes, first, count):
    length = codes.shape[1]
    start = (length - first - KS_STEM // 2) % length
    codes = jnp.broadcast_to(codes, (16, length))
    shifted = pltpu.roll(codes, start, 1, stride=1, stride_axis=0)
    shifted = shifted[:, :count]
    return jnp.concatenate(
        [(shifted == base + 1).astype(jnp.float32) for base in range(4)], axis=0
    ).astype(jnp.bfloat16)


def pooled_rows(onehot, weight):
    hidden = lax.dot_general(
        onehot, weight, (((0,), (0,)), ((), ())), preferred_element_type=jnp.float32
    ).reshape(onehot.shape[1] // STEM_POOL, STEM_POOL, weight.shape[1])
    high = gelu(jnp.max(hidden, axis=1))
    low = gelu(jnp.min(hidden, axis=1))
    return jnp.maximum(high, low)


def stem_kernel(made_ref, out_ref):
    onehot = onehot_rows(made_ref[64:, :].astype(jnp.float32), 0, made_ref.shape[1])
    weight = made_ref[:64, : out_ref.shape[1]]
    step = 8
    for at in range(0, ROWS, step):
        part = onehot[:, at * STEM_POOL : (at + step) * STEM_POOL]
        out_ref[at : at + step, :] = pooled_rows(part, weight)


def stem(made, channels):
    return pl.pallas_call(
        stem_kernel,
        out_shape=jax.ShapeDtypeStruct((ROWS, channels), jnp.float32),
        in_specs=whole(1),
        out_specs=whole(1)[0],
        compiler_params=params(),
        cost_estimate=pl.CostEstimate(flops=2 * 2048 * 64 * 768, bytes_accessed=200000, transcendentals=0),
    )(made)


def start_kernel(weight_ref, stem_ref, tokens_hbm, line_hbm, out_ref, made_ref, wide, tokens_ref, line_ref, arrived):
    copies = [
        pltpu.make_async_copy(tokens_hbm, tokens_ref, arrived.at[0]),
        pltpu.make_async_copy(line_hbm, line_ref, arrived.at[1]),
    ]
    for copy in copies:
        copy.start()
    rows, channels = stem_ref.shape
    row = lax.broadcasted_iota(jnp.int32, (64, rows), 0)
    column = lax.broadcasted_iota(jnp.int32, (64, rows), 1)
    picked = (column == (KS_STEM - 1 - row % 16) * 4 + row // 16) & (row % 16 < KS_STEM)
    picked = picked.astype(jnp.float32).astype(jnp.bfloat16)
    made = jnp.dot(picked, stem_ref[...], preferred_element_type=jnp.float32).astype(jnp.bfloat16)
    half = channels // 2
    row = lax.broadcasted_iota(jnp.int32, (channels, half), 0)
    column = lax.broadcasted_iota(jnp.int32, (channels, half), 1)
    for odd in range(2):
        order = (row == 2 * column + odd).astype(jnp.float32).astype(jnp.bfloat16)
        part = jnp.dot(made, order, preferred_element_type=jnp.float32)
        made_ref[:64, odd * half : (odd + 1) * half] = part.astype(jnp.bfloat16)
    taps, width = weight_ref.shape
    share = width // N_SHARE
    half = taps // 2
    even, odd = [], []
    for part in range(wide.shape[0]):
        lanes = weight_ref[:, part * HQK : (part + 1) * HQK]
        wide[part, :taps, :] = lanes.astype(jnp.float32)
        wide[part, taps:, :] = jnp.zeros((wide.shape[1] - taps, HQK), jnp.float32)
        even.append(wide[part, pl.ds(0, half + 1, stride=2), :])
        odd.append(wide[part, pl.ds(1, half + 1, stride=2), :])
    even, odd = jnp.concatenate(even, axis=1), jnp.concatenate(odd, axis=1)
    lane = lax.broadcasted_iota(jnp.int32, (half + 1, HQK), 1)
    row = lax.broadcasted_iota(jnp.int32, (half + 1, HQK), 0)
    for copy in copies:
        copy.wait()
    line = (line_ref[...] + 1).astype(jnp.float32).astype(jnp.bfloat16)
    made_ref[64:, :] = jnp.broadcast_to(line, (16, line.shape[1]))
    made_ref[:64, channels:] = jnp.zeros((64, line.shape[1] - channels), jnp.bfloat16)
    codes = (tokens_ref[...] + 1).astype(jnp.float32)
    last = codes.shape[0] - 1
    line = [jnp.broadcast_to(codes[at : at + 1, :], lane.shape) for at in (0, 1, last - 1, last)]
    outer = jnp.where(lane >= HQK - 7, line[2], pltpu.roll(line[1], 96, 1))
    for index in range(4):
        outer = jnp.where(row == index, pltpu.roll(line[3], (96 - 32 * index) % HQK, 1), outer)
    blocks = []
    for index in range(N_SHARE):
        low = pltpu.roll(even, (width - index * share) % width, 1)[:, :HQK]
        high = pltpu.roll(odd, (width - index * share + share) % width, 1)[:, :HQK]
        block = jnp.where(lane < share, low, jnp.where(lane < 2 * share, high, outer))
        blocks.append(jnp.where(row == half, line[0], block).astype(jnp.bfloat16))
    for place in range(N_SEQ):
        at, index, base = place, 0, 1
        for name in reversed(SEQ):
            if name in SHARE:
                index, base = index + base * (at % SIZES[name]), base * SIZES[name]
            at = at // SIZES[name]
        out_ref[place] = blocks[index]


def start(weight, stem_weight, tokens):
    taps, width = weight.shape
    tokens, line = tokens.reshape(-1, HQK), tokens.reshape(1, -1)
    return pl.pallas_call(
        start_kernel,
        out_shape=(
            jax.ShapeDtypeStruct((N_SEQ, taps // 2 + 1, HQK), jnp.bfloat16),
            jax.ShapeDtypeStruct((80, line.shape[1]), jnp.bfloat16),
        ),
        in_specs=whole(2) + [pl.BlockSpec(memory_space=pltpu.HBM)] * 2,
        out_specs=tuple(whole(2)),
        scratch_shapes=[
            pltpu.VMEM((width // HQK, taps + 2, HQK), jnp.float32),
            pltpu.VMEM(tokens.shape, jnp.int32),
            pltpu.VMEM(line.shape, jnp.int32),
            pltpu.SemaphoreType.DMA((2,)),
        ],
        compiler_params=params(WHOLE),
    )(weight, stem_weight, tokens, line)


def border_codes(held_ref, right):
    before = held_ref[jnp.maximum(right - 1, 0) ^ MIDDLE_SEQ].astype(jnp.float32)
    after = held_ref[jnp.minimum(right, N_SEQ - 1) ^ MIDDLE_SEQ].astype(jnp.float32)
    before = jnp.where(right > 0, before, 0.0)
    after = jnp.where(right < N_SEQ, after, 0.0)
    lane = lax.broadcasted_iota(jnp.int32, (1, HQK), 1)
    tail = jnp.zeros((1, HQK), jnp.float32)
    for index in range(4):
        part = pltpu.roll(before, (32 * index + 32) % HQK, 1)[index : index + 1, :]
        tail = jnp.where(lane // 32 == index, part, tail)
    return jnp.concatenate(
        [before[4:5, :], tail, after[15:16, :], pltpu.roll(after, 32, 1)[4:5, :]], axis=1
    )


def conv_kernel(place_ref, section_ref, held_ref, stem_ref, out_ref, weights, edges, wide, act, best):
    count, rows, _ = held_ref.shape
    for source in range(count):
        block = held_ref[source ^ MIDDLE_SEQ].astype(jnp.float32)
        weights[source * (rows - 1) : (source + 1) * (rows - 1), :] = block[: rows - 1, :]
    first = ((place_ref[0] & (N_SEQ // 2 - 1)) // RUN) * RUN
    for run in range(2):
        right = run * (N_SEQ // 2) + first
        onehot = jnp.concatenate(
            [
                onehot_rows(border_codes(held_ref, right + index), 192 if inner else 128, 128 if inner else 256)
                for index in range(RUN + 1)
                for inner in [0 < index < RUN]
            ],
            axis=1,
        )
        made = pooled_rows(onehot, stem_ref[:64, : section_ref.shape[2]])
        place = lax.broadcasted_iota(jnp.int32, made.shape, 0)
        outside = ((place < 2) & (right == 0)) | ((place >= EDGES_RUN - 2) & (right + RUN == count))
        edges[run * 16 : run * 16 + EDGES_RUN, :] = jnp.where(outside, 0.0, made)
    windows, _, channels = section_ref.shape
    half = channels // 2
    columns = out_ref.shape[2] // 8
    for window in range(windows):
        run, index = window // RUN, window % RUN
        rows = section_ref[window].astype(jnp.float32)
        wide[window, 3 : ROWS + 1, :] = rows[1 : ROWS - 1, :]
        at = run * 16 + 2 + 2 * index
        if index == 0:
            wide[window, 0:3, :] = edges[run * 16 : run * 16 + 3, :]
        else:
            wide[window, 1:3, :] = edges[at : at + 2, :]
            wide[window - 1, ROWS + 3 : ROWS + 4, :] = rows[1:2, :]
        at = at + 2
        if index == RUN - 1:
            wide[window, ROWS + 1 : ROWS + 4, :] = edges[at + 1 : at + 4, :]
        else:
            wide[window, ROWS + 1 : ROWS + 3, :] = edges[at : at + 2, :]
            wide[window + 1, 0:1, :] = rows[ROWS - 2 : ROWS - 1, :]
    even, odd = None, None
    for tap in range(KS_CONV):
        rows = wide[:, tap : tap + ROWS, :].astype(jnp.bfloat16).reshape(windows * ROWS, channels)
        weight = weights[tap * half : (tap + 1) * half, :].astype(jnp.bfloat16)
        term = jnp.dot(rows[:, :half], weight, preferred_element_type=jnp.float32)
        even = term if even is None else even + term
        term = jnp.dot(rows[:, half:], weight, preferred_element_type=jnp.float32)
        odd = term if odd is None else odd + term
    act[...] = jnp.zeros(act.shape, jnp.float32)
    act[:, :columns] = gelu(even[:, :columns] + odd[:, columns : 2 * columns])
    count = windows * ROWS // 2
    best[...] = jnp.maximum(act[pl.ds(0, count, stride=2), :], act[pl.ds(1, count, stride=2), :])
    flat = None
    for index in range(8):
        part = best[pl.ds(index, count // 8, stride=8), :]
        part = jnp.pad(part, ((0, 0), (0, 8 * columns - part.shape[1])))
        part = pltpu.roll(part, index * columns, 1)
        flat = part if flat is None else flat + part
    for window in range(windows):
        block = flat[window // 2 * 4 : window // 2 * 4 + 4, :].astype(jnp.bfloat16)
        for index in range(N_PAIR):
            out_ref[(window * N_PAIR + index) ^ LATE_SHARE] = block


def conv(place, section, held, stem_weight, columns):
    windows, _, channels = section.shape
    return pl.pallas_call(
        conv_kernel,
        out_shape=jax.ShapeDtypeStruct((windows * N_PAIR, 4, 8 * columns), jnp.bfloat16),
        in_specs=[pl.BlockSpec(memory_space=pltpu.SMEM)] + whole(3),
        out_specs=whole(1)[0],
        scratch_shapes=[
            pltpu.VMEM((held.shape[0] * (held.shape[1] - 1), HQK), jnp.float32),
            pltpu.VMEM((32, channels), jnp.float32),
            pltpu.VMEM((windows, EXT_PAD, channels), jnp.float32),
            pltpu.VMEM((windows * ROWS, HQK), jnp.float32),
            pltpu.VMEM((windows * ROWS // 2, HQK), jnp.float32),
        ],
        compiler_params=params(),
    )(place, section, held, stem_weight)


def project_kernel(core_ref, trunk_ref, w_query_ref, w_key_ref, w_value_ref, query_ref, kv_ref, own_ref):
    trunk = trunk_ref[...]
    first = core_ref[0] == 0
    count = own_ref.shape[0]
    half = count // 2
    query_ref[...] = jnp.dot(trunk, w_query_ref[...], preferred_element_type=jnp.float32).astype(jnp.bfloat16)
    wide = trunk.astype(jnp.float32)
    own = jnp.where(first, wide[:count], wide[count:]).astype(jnp.bfloat16)
    own_ref[...] = own
    key = jnp.dot(own, w_key_ref[...], preferred_element_type=jnp.float32).astype(jnp.bfloat16)
    value = jnp.dot(own, w_value_ref[...], preferred_element_type=jnp.float32)
    rest = jnp.pad(value[:, HQK:], ((0, 0), (0, 2 * HQK - HV)))
    rest = (rest[:half] + pltpu.roll(rest[half:], HV - HQK, 1)).astype(jnp.bfloat16)
    value = value[:, :HQK].astype(jnp.bfloat16)
    for index in range(N_LINE):
        kv_ref[index, :count, :] = key
        kv_ref[index, count : 2 * count, :] = value
        kv_ref[index, 2 * count :, :] = rest


def project(core, trunk, w_query, w_key, w_value):
    count = trunk.shape[0] // 2
    return pl.pallas_call(
        project_kernel,
        out_shape=(
            jax.ShapeDtypeStruct((2 * count, HQK), jnp.bfloat16),
            jax.ShapeDtypeStruct((N_LINE, 2 * count + count // 2, HQK), jnp.bfloat16),
            jax.ShapeDtypeStruct((count, trunk.shape[1]), jnp.bfloat16),
        ),
        in_specs=[pl.BlockSpec(memory_space=pltpu.SMEM)] + whole(4),
        out_specs=tuple(whole(3)),
        compiler_params=params(),
    )(core, trunk, w_query, w_key, w_value)


def split(x):
    parts = []
    for _ in range(3):
        part = x.astype(jnp.bfloat16).astype(jnp.float32)
        parts.append(part)
        x = x - part
    return parts


def attention_kernel(place_ref, query_ref, kv_ref, out_ref):
    scale = 1.0 / math.sqrt(HQK)
    line, rows, _ = kv_ref.shape
    count = out_ref.shape[1]
    keys = kv_ref[:, :count, :].reshape(line * count, HQK)
    values = kv_ref[:, count : 2 * count, :].reshape(line * count, HQK)
    rest = kv_ref[:, 2 * count :, :].astype(jnp.float32)
    rest = jnp.stack([rest, pltpu.roll(rest, HQK - (HV - HQK), 2)], axis=1)
    rest = rest.reshape(line * count, HQK).astype(jnp.bfloat16)
    scores = (
        lax.dot_general(
            query_ref[...], keys, (((1,), (1,)), ((), ())), preferred_element_type=jnp.float32
        )
        * scale
    )
    top = jnp.max(scores, axis=1, keepdims=True)
    expo = jnp.exp(scores - top)
    total = jnp.sum(expo, axis=1, keepdims=True)
    expo = expo.astype(jnp.bfloat16)
    mixed = jnp.concatenate(
        [jnp.dot(expo, part, preferred_element_type=jnp.float32) for part in (values, rest)], axis=1
    )
    lane = lax.broadcasted_iota(jnp.int32, mixed.shape, 1)
    for index, column in enumerate(split(top) + split(total)):
        mixed = jnp.where(lane == HV + index, column, mixed)
    mixed = mixed.astype(jnp.bfloat16)
    flips = (0, 2, 1, 3)
    groups, count, _ = out_ref.shape
    for index in range(groups):
        place = ((place_ref[0] >> 1) ^ flips[index // 2]) * 2 + index % 2
        out_ref[place ^ MIDDLE_SPREAD] = mixed[index * count : (index + 1) * count, :]


def attention(place, query, kv):
    groups = N_SPREAD
    count, width = query.shape[0] // groups, 2 * HQK
    return pl.pallas_call(
        attention_kernel,
        out_shape=jax.ShapeDtypeStruct((groups, count, width), jnp.bfloat16),
        in_specs=[pl.BlockSpec(memory_space=pltpu.SMEM)] + whole(2),
        out_specs=whole(1)[0],
        compiler_params=params(),
    )(place, query, kv)


def combine_kernel(parts_ref, w_out_ref, out_ref):
    parts = parts_ref[...].astype(jnp.float32)
    top = jnp.sum(parts[:, :, HV : HV + 3], axis=2, keepdims=True)
    gain = jnp.exp(top - jnp.max(top, axis=0, keepdims=True))
    total = jnp.sum(gain * jnp.sum(parts[:, :, HV + 3 : HV + 6], axis=2, keepdims=True), axis=0)
    mixed = (jnp.sum(gain * parts, axis=0) / total)[:, :HV].astype(jnp.bfloat16)
    term = jnp.dot(mixed, w_out_ref[...], preferred_element_type=jnp.float32)
    mean = jnp.sum(term, axis=0, keepdims=True) * (1.0 / PAIR_POOL)
    width = term.shape[1] // N_PAIR
    count = term.shape[0]
    tail = jnp.concatenate(
        [mean[:, c * width : (c + 1) * width] for c in range(N_PAIR)]
        + [jnp.zeros((8 - N_PAIR, width), jnp.float32)],
        axis=0,
    )
    for c in range(N_PAIR):
        out_ref[c ^ MIDDLE_PAIR, :count, :] = term[:, c * width : (c + 1) * width]
        out_ref[c ^ MIDDLE_PAIR, count:, :] = tail


def combine(parts, w_out):
    count = parts.shape[1]
    width = w_out.shape[1] // N_PAIR
    return pl.pallas_call(
        combine_kernel,
        out_shape=jax.ShapeDtypeStruct((N_PAIR, count + 8, width), jnp.float32),
        in_specs=whole(2),
        out_specs=whole(1)[0],
        compiler_params=params(),
    )(parts, w_out)


def close_kernel(terms_ref, own_ref, trunk_ref, w_pair_ref, pair_ref, seq_ref, rows_ref, every_ref):
    count, width = own_ref.shape
    total = jnp.sum(terms_ref[...], axis=0)
    seq_ref[...] = (own_ref[...].astype(jnp.float32) + total[:count, :]).astype(jnp.bfloat16)
    trunk_mean = jnp.sum(trunk_ref[...].astype(jnp.float32), axis=0, keepdims=True) * (1.0 / PAIR_POOL)
    rows = None
    for c in range(N_PAIR):
        pooled = trunk_mean[:, c * width : (c + 1) * width] + total[count + c : count + c + 1, :]
        term = jnp.dot(
            jnp.broadcast_to(pooled, (8, width)).astype(jnp.bfloat16),
            w_pair_ref[c * width : (c + 1) * width, :],
            preferred_element_type=jnp.float32,
        )
        rows = term if rows is None else rows + term
    rows_ref[...] = rows
    mine = pair_ref[0].astype(jnp.float32)
    factors = jnp.broadcast_to(rows[:1], (mine.shape[0], rows.shape[1]))
    every = jnp.concatenate([factors, mine], axis=1)
    for at in range(0, every.shape[0], MIDDLE_SEQ):
        to = at ^ MIDDLE_SEQ
        every_ref[to : to + MIDDLE_SEQ, :] = every[at : at + MIDDLE_SEQ, :]


def close(terms, own, trunk, w_pair, pair_in):
    return pl.pallas_call(
        close_kernel,
        out_shape=(
            jax.ShapeDtypeStruct(own.shape, jnp.bfloat16),
            jax.ShapeDtypeStruct((8, w_pair.shape[1]), jnp.float32),
            jax.ShapeDtypeStruct((pair_in.shape[1], w_pair.shape[1] + pair_in.shape[2]), jnp.float32),
        ),
        in_specs=whole(5),
        out_specs=tuple(whole(3)),
        compiler_params=params(),
    )(terms, own, trunk, w_pair, pair_in)


def distance_bias(row, cols, pair_bias):
    delta = jnp.abs(row - cols)
    bins = jnp.zeros(delta.shape, jnp.int32)
    for edge in EDGES:
        bins = bins + (delta >= edge).astype(jnp.int32)
    labels = jnp.arange(pair_bias.shape[0], dtype=jnp.int32)
    onehot = (bins[:, None] == labels[None, :]).astype(jnp.bfloat16)
    return jnp.dot(onehot, pair_bias, preferred_element_type=jnp.float32)


def exchange(blocks, axes, middle=0):
    order = [index ^ middle for index in range(blocks.shape[0])]
    return lax.all_to_all(
        blocks, axes, split_axis=0, concat_axis=0, tiled=True, axis_index_groups=[order] if middle else None
    )


def on_device(tokens, w_stem, w_conv, w_query, w_key, w_value, w_out, w_pair, pair_bias, pair_in):
    place = lax.axis_index(SEQ)
    pair_place = lax.axis_index("pair")

    taps, width = w_conv.shape
    share = width // N_SHARE
    blocks, made = start(w_conv, w_stem, tokens)
    held = exchange(blocks, SEQ, MIDDLE_SEQ)

    section = stem(made, w_stem.shape[1]).astype(jnp.bfloat16)
    sections = lax.all_gather(section, SHARE, axis=0, tiled=False)

    parts = exchange(
        conv(place.astype(jnp.int32)[None], sections, held, made, share), SHARE + ("pair",), LATE_SHARE
    )
    count = ROWS // 2
    parts = parts.reshape(N_SHARE, N_PAIR, 2 * count, share)[:, ::-1]
    trunk = parts.transpose(2, 1, 0, 3)
    trunk = trunk.reshape(2 * count, N_PAIR * width)

    core = lax.axis_index("core").astype(jnp.int32)[None]
    query, kv, trunk = project(core, trunk, w_query, w_key, w_value)
    for name in SPREAD[:-1]:
        other = lax.ppermute(query, name, [(0, 1), (1, 0)])
        query = jnp.concatenate([query, other], axis=0)
    kv = exchange(kv, LINE, MIDDLE_LINE)
    spread = lax.axis_index(SPREAD).astype(jnp.int32)[None]
    parts = exchange(attention(spread, query, kv), SPREAD, MIDDLE_SPREAD)
    terms = exchange(combine(parts, w_out), ("pair",), MIDDLE_PAIR)

    own = lax.dynamic_slice_in_dim(trunk, pair_place * width, width, 1)
    factors = jnp.concatenate([w_pair[0], w_pair[1]], axis=1)
    seq_out, rows, every = close(terms, own, trunk, factors, pair_in)
    channels = pair_in.shape[2]
    mine = pair_in[0].astype(jnp.float32)
    rows = rows[:1]
    every = exchange(every[:, None], SEQ, MIDDLE_SEQ)[:, 0]
    every = every.reshape(-1, 2, MIDDLE_SEQ, every.shape[1])[:, ::-1].reshape(every.shape)
    mirror = every[:, 2 * channels :]

    cols = jnp.arange(N_SEQ, dtype=jnp.int32)
    bias = lax.optimization_barrier(distance_bias(place.astype(jnp.int32), cols, pair_bias))
    cross = rows[:, :channels] * every[:, channels : 2 * channels]
    cross = cross + every[:, :channels] * rows[:, channels:]
    pair_out = (0.5 * (mine + mirror + cross) + bias).astype(jnp.bfloat16)[None]
    return (seq_out, pair_out)


def solution(mesh):
    names = SEQ + ("pair",)
    fine = Mesh(mesh.devices.reshape([SIZES[name] for name in names]), names)
    placed = (
        P(SEQ),
        P(),
        P(SEQ, "pair"),
        P(None, "pair"),
        P(None, "pair"),
        P(None, "pair"),
        P("pair", None),
        P(None, None, "pair"),
        P(None, "pair"),
        P(SEQ, None, "pair"),
    )
    return jax.shard_map(
        on_device,
        mesh=fine,
        in_specs=placed,
        out_specs=(P(SEQ, "pair"), P(SEQ, None, "pair")),
        check_vma=False,
    )
```

```python
import math

import jax
import jax.numpy as jnp
from jax import lax
from jax.experimental import pallas as pl
from jax.experimental.pallas import tpu as pltpu
from jax.sharding import Mesh
from jax.sharding import PartitionSpec as P

HQK = 128
HV = 192
KS_STEM = 15
KS_CONV = 5
STEM_POOL = 64
PAIR_POOL = 16
EDGES = (1, 2, 3, 4, 6, 8, 12, 16, 24, 32, 48, 64, 96, 128, 192, 256, 384)

SIZES = {"zl": 2, "y": 8, "xh": 2, "xl": 2, "core": 2, "pair": 4}
SEQ = ("zl", "y", "xh", "xl", "core")
SHARE = ("zl", "xl", "core")
SPREAD = ("xh", "xl", "core")
LINE = ("zl", "y")
MIDDLE_SEQ = 32
MIDDLE_LINE = 4
MIDDLE_SPREAD = 2
MIDDLE_PAIR = 2
N_SEQ = math.prod(SIZES[name] for name in SEQ)
N_SHARE = math.prod(SIZES[name] for name in SHARE)
N_PAIR = SIZES["pair"]
N_SPREAD = math.prod(SIZES[name] for name in SPREAD)
N_LINE = math.prod(SIZES[name] for name in LINE)

ROWS = 32
EXT_PAD = 40
RUN = 4
EDGES_RUN = 14
VMEM = 48 * 1024 * 1024
WHOLE = 60 * 1000 * 1000


def params(limit=VMEM):
    return pltpu.CompilerParams(vmem_limit_bytes=limit)


def whole(count):
    return [pl.BlockSpec(memory_space=pltpu.VMEM) for _ in range(count)]


def gelu(x):
    return 0.5 * x * (1.0 + jnp.tanh(math.sqrt(2.0 / math.pi) * (x + 0.044715 * (x * x * x))))


def onehot_rows(codes, first, count):
    length = codes.shape[1]
    start = (length - first - KS_STEM // 2) % length
    codes = jnp.broadcast_to(codes, (16, length))
    shifted = pltpu.roll(codes, start, 1, stride=1, stride_axis=0)
    shifted = shifted[:, :count]
    return jnp.concatenate(
        [(shifted == base + 1).astype(jnp.float32) for base in range(4)], axis=0
    ).astype(jnp.bfloat16)


def pooled_rows(onehot, weight):
    hidden = lax.dot_general(
        onehot, weight, (((0,), (0,)), ((), ())), preferred_element_type=jnp.float32
    ).reshape(onehot.shape[1] // STEM_POOL, STEM_POOL, weight.shape[1])
    high = gelu(jnp.max(hidden, axis=1))
    low = gelu(jnp.min(hidden, axis=1))
    return jnp.maximum(high, low)


def stem_kernel(made_ref, out_ref):
    onehot = onehot_rows(made_ref[64:, :].astype(jnp.float32), 0, made_ref.shape[1])
    weight = made_ref[:64, : out_ref.shape[1]]
    step = 8
    for at in range(0, ROWS, step):
        part = onehot[:, at * STEM_POOL : (at + step) * STEM_POOL]
        out_ref[at : at + step, :] = pooled_rows(part, weight)


def stem(made, channels):
    return pl.pallas_call(
        stem_kernel,
        out_shape=jax.ShapeDtypeStruct((ROWS, channels), jnp.float32),
        in_specs=whole(1),
        out_specs=whole(1)[0],
        compiler_params=params(),
        cost_estimate=pl.CostEstimate(flops=2 * 2048 * 64 * 768, bytes_accessed=200000, transcendentals=0),
    )(made)


def start_kernel(weight_ref, stem_ref, tokens_hbm, line_hbm, out_ref, made_ref, wide, tokens_ref, line_ref, arrived):
    copies = [
        pltpu.make_async_copy(tokens_hbm, tokens_ref, arrived.at[0]),
        pltpu.make_async_copy(line_hbm, line_ref, arrived.at[1]),
    ]
    for copy in copies:
        copy.start()
    rows, channels = stem_ref.shape
    row = lax.broadcasted_iota(jnp.int32, (64, rows), 0)
    column = lax.broadcasted_iota(jnp.int32, (64, rows), 1)
    picked = (column == (KS_STEM - 1 - row % 16) * 4 + row // 16) & (row % 16 < KS_STEM)
    picked = picked.astype(jnp.float32).astype(jnp.bfloat16)
    made = jnp.dot(picked, stem_ref[...], preferred_element_type=jnp.float32).astype(jnp.bfloat16)
    half = channels // 2
    row = lax.broadcasted_iota(jnp.int32, (channels, half), 0)
    column = lax.broadcasted_iota(jnp.int32, (channels, half), 1)
    for odd in range(2):
        order = (row == 2 * column + odd).astype(jnp.float32).astype(jnp.bfloat16)
        part = jnp.dot(made, order, preferred_element_type=jnp.float32)
        made_ref[:64, odd * half : (odd + 1) * half] = part.astype(jnp.bfloat16)
    taps, width = weight_ref.shape
    share = width // N_SHARE
    half = taps // 2
    even, odd = [], []
    for part in range(wide.shape[0]):
        lanes = weight_ref[:, part * HQK : (part + 1) * HQK]
        wide[part, :taps, :] = lanes.astype(jnp.float32)
        wide[part, taps:, :] = jnp.zeros((wide.shape[1] - taps, HQK), jnp.float32)
        even.append(wide[part, pl.ds(0, half + 1, stride=2), :])
        odd.append(wide[part, pl.ds(1, half + 1, stride=2), :])
    even, odd = jnp.concatenate(even, axis=1), jnp.concatenate(odd, axis=1)
    lane = lax.broadcasted_iota(jnp.int32, (half + 1, HQK), 1)
    row = lax.broadcasted_iota(jnp.int32, (half + 1, HQK), 0)
    for copy in copies:
        copy.wait()
    line = (line_ref[...] + 1).astype(jnp.float32).astype(jnp.bfloat16)
    made_ref[64:, :] = jnp.broadcast_to(line, (16, line.shape[1]))
    made_ref[:64, channels:] = jnp.zeros((64, line.shape[1] - channels), jnp.bfloat16)
    codes = (tokens_ref[...] + 1).astype(jnp.float32)
    last = codes.shape[0] - 1
    line = [jnp.broadcast_to(codes[at : at + 1, :], lane.shape) for at in (0, 1, last - 1, last)]
    outer = jnp.where(lane >= HQK - 7, line[2], pltpu.roll(line[1], 96, 1))
    for index in range(4):
        outer = jnp.where(row == index, pltpu.roll(line[3], (96 - 32 * index) % HQK, 1), outer)
    blocks = []
    for index in range(N_SHARE):
        low = pltpu.roll(even, (width - index * share) % width, 1)[:, :HQK]
        high = pltpu.roll(odd, (width - index * share + share) % width, 1)[:, :HQK]
        block = jnp.where(lane < share, low, jnp.where(lane < 2 * share, high, outer))
        blocks.append(jnp.where(row == half, line[0], block).astype(jnp.bfloat16))
    for place in range(N_SEQ):
        at, index, base = place, 0, 1
        for name in reversed(SEQ):
            if name in SHARE:
                index, base = index + base * (at % SIZES[name]), base * SIZES[name]
            at = at // SIZES[name]
        out_ref[place] = blocks[index]


def start(weight, stem_weight, tokens):
    taps, width = weight.shape
    tokens, line = tokens.reshape(-1, HQK), tokens.reshape(1, -1)
    return pl.pallas_call(
        start_kernel,
        out_shape=(
            jax.ShapeDtypeStruct((N_SEQ, taps // 2 + 1, HQK), jnp.bfloat16),
            jax.ShapeDtypeStruct((80, line.shape[1]), jnp.bfloat16),
        ),
        in_specs=whole(2) + [pl.BlockSpec(memory_space=pltpu.HBM)] * 2,
        out_specs=tuple(whole(2)),
        scratch_shapes=[
            pltpu.VMEM((width // HQK, taps + 2, HQK), jnp.float32),
            pltpu.VMEM(tokens.shape, jnp.int32),
            pltpu.VMEM(line.shape, jnp.int32),
            pltpu.SemaphoreType.DMA((2,)),
        ],
        compiler_params=params(WHOLE),
    )(weight, stem_weight, tokens, line)


def border_codes(held_ref, right):
    before = held_ref[jnp.maximum(right - 1, 0) ^ MIDDLE_SEQ].astype(jnp.float32)
    after = held_ref[jnp.minimum(right, N_SEQ - 1) ^ MIDDLE_SEQ].astype(jnp.float32)
    before = jnp.where(right > 0, before, 0.0)
    after = jnp.where(right < N_SEQ, after, 0.0)
    lane = lax.broadcasted_iota(jnp.int32, (1, HQK), 1)
    tail = jnp.zeros((1, HQK), jnp.float32)
    for index in range(4):
        part = pltpu.roll(before, (32 * index + 32) % HQK, 1)[index : index + 1, :]
        tail = jnp.where(lane // 32 == index, part, tail)
    return jnp.concatenate(
        [before[4:5, :], tail, after[15:16, :], pltpu.roll(after, 32, 1)[4:5, :]], axis=1
    )


def conv_kernel(place_ref, section_ref, held_ref, stem_ref, out_ref, weights, edges, wide, act, best):
    count, rows, _ = held_ref.shape
    for source in range(count):
        block = held_ref[source ^ MIDDLE_SEQ].astype(jnp.float32)
        weights[source * (rows - 1) : (source + 1) * (rows - 1), :] = block[: rows - 1, :]
    first = ((place_ref[0] & (N_SEQ // 2 - 1)) // RUN) * RUN
    for run in range(2):
        right = run * (N_SEQ // 2) + first
        onehot = jnp.concatenate(
            [
                onehot_rows(border_codes(held_ref, right + index), 192 if inner else 128, 128 if inner else 256)
                for index in range(RUN + 1)
                for inner in [0 < index < RUN]
            ],
            axis=1,
        )
        made = pooled_rows(onehot, stem_ref[:64, : section_ref.shape[2]])
        place = lax.broadcasted_iota(jnp.int32, made.shape, 0)
        outside = ((place < 2) & (right == 0)) | ((place >= EDGES_RUN - 2) & (right + RUN == count))
        edges[run * 16 : run * 16 + EDGES_RUN, :] = jnp.where(outside, 0.0, made)
    windows, _, channels = section_ref.shape
    half = channels // 2
    columns = out_ref.shape[2] // 8
    for window in range(windows):
        run, index = window // RUN, window % RUN
        rows = section_ref[window].astype(jnp.float32)
        wide[window, 3 : ROWS + 1, :] = rows[1 : ROWS - 1, :]
        at = run * 16 + 2 + 2 * index
        if index == 0:
            wide[window, 0:3, :] = edges[run * 16 : run * 16 + 3, :]
        else:
            wide[window, 1:3, :] = edges[at : at + 2, :]
            wide[window - 1, ROWS + 3 : ROWS + 4, :] = rows[1:2, :]
        at = at + 2
        if index == RUN - 1:
            wide[window, ROWS + 1 : ROWS + 4, :] = edges[at + 1 : at + 4, :]
        else:
            wide[window, ROWS + 1 : ROWS + 3, :] = edges[at : at + 2, :]
            wide[window + 1, 0:1, :] = rows[ROWS - 2 : ROWS - 1, :]
    even, odd = None, None
    for tap in range(KS_CONV):
        rows = wide[:, tap : tap + ROWS, :].astype(jnp.bfloat16).reshape(windows * ROWS, channels)
        weight = weights[tap * half : (tap + 1) * half, :].astype(jnp.bfloat16)
        term = jnp.dot(rows[:, :half], weight, preferred_element_type=jnp.float32)
        even = term if even is None else even + term
        term = jnp.dot(rows[:, half:], weight, preferred_element_type=jnp.float32)
        odd = term if odd is None else odd + term
    act[...] = jnp.zeros(act.shape, jnp.float32)
    act[:, :columns] = gelu(even[:, :columns] + odd[:, columns : 2 * columns])
    count = windows * ROWS // 2
    best[...] = jnp.maximum(act[pl.ds(0, count, stride=2), :], act[pl.ds(1, count, stride=2), :])
    flat = None
    for index in range(8):
        part = best[pl.ds(index, count // 8, stride=8), :]
        part = jnp.pad(part, ((0, 0), (0, 8 * columns - part.shape[1])))
        part = pltpu.roll(part, index * columns, 1)
        flat = part if flat is None else flat + part
    for window in range(windows):
        block = flat[window // 2 * 4 : window // 2 * 4 + 4, :].astype(jnp.bfloat16)
        for index in range(N_PAIR):
            out_ref[window * N_PAIR + index] = block


def conv(place, section, held, stem_weight, columns):
    windows, _, channels = section.shape
    return pl.pallas_call(
        conv_kernel,
        out_shape=jax.ShapeDtypeStruct((windows * N_PAIR, 4, 8 * columns), jnp.bfloat16),
        in_specs=[pl.BlockSpec(memory_space=pltpu.SMEM)] + whole(3),
        out_specs=whole(1)[0],
        scratch_shapes=[
            pltpu.VMEM((held.shape[0] * (held.shape[1] - 1), HQK), jnp.float32),
            pltpu.VMEM((32, channels), jnp.float32),
            pltpu.VMEM((windows, EXT_PAD, channels), jnp.float32),
            pltpu.VMEM((windows * ROWS, HQK), jnp.float32),
            pltpu.VMEM((windows * ROWS // 2, HQK), jnp.float32),
        ],
        compiler_params=params(),
    )(place, section, held, stem_weight)


def project_kernel(core_ref, trunk_ref, w_query_ref, w_key_ref, w_value_ref, query_ref, kv_ref, own_ref):
    trunk = trunk_ref[...]
    first = core_ref[0] == 0
    count = own_ref.shape[0]
    half = count // 2
    query_ref[...] = jnp.dot(trunk, w_query_ref[...], preferred_element_type=jnp.float32).astype(jnp.bfloat16)
    wide = trunk.astype(jnp.float32)
    own = jnp.where(first, wide[:count], wide[count:]).astype(jnp.bfloat16)
    own_ref[...] = own
    key = jnp.dot(own, w_key_ref[...], preferred_element_type=jnp.float32).astype(jnp.bfloat16)
    value = jnp.dot(own, w_value_ref[...], preferred_element_type=jnp.float32)
    rest = jnp.pad(value[:, HQK:], ((0, 0), (0, 2 * HQK - HV)))
    rest = (rest[:half] + pltpu.roll(rest[half:], HV - HQK, 1)).astype(jnp.bfloat16)
    value = value[:, :HQK].astype(jnp.bfloat16)
    for index in range(N_LINE):
        kv_ref[index, :count, :] = key
        kv_ref[index, count : 2 * count, :] = value
        kv_ref[index, 2 * count :, :] = rest


def project(core, trunk, w_query, w_key, w_value):
    count = trunk.shape[0] // 2
    return pl.pallas_call(
        project_kernel,
        out_shape=(
            jax.ShapeDtypeStruct((2 * count, HQK), jnp.bfloat16),
            jax.ShapeDtypeStruct((N_LINE, 2 * count + count // 2, HQK), jnp.bfloat16),
            jax.ShapeDtypeStruct((count, trunk.shape[1]), jnp.bfloat16),
        ),
        in_specs=[pl.BlockSpec(memory_space=pltpu.SMEM)] + whole(4),
        out_specs=tuple(whole(3)),
        compiler_params=params(),
    )(core, trunk, w_query, w_key, w_value)


def split(x):
    parts = []
    for _ in range(3):
        part = x.astype(jnp.bfloat16).astype(jnp.float32)
        parts.append(part)
        x = x - part
    return parts


def attention_kernel(place_ref, query_ref, kv_ref, out_ref):
    scale = 1.0 / math.sqrt(HQK)
    line, rows, _ = kv_ref.shape
    count = out_ref.shape[1]
    keys = kv_ref[:, :count, :].reshape(line * count, HQK)
    values = kv_ref[:, count : 2 * count, :].reshape(line * count, HQK)
    rest = kv_ref[:, 2 * count :, :].astype(jnp.float32)
    rest = jnp.stack([rest, pltpu.roll(rest, HQK - (HV - HQK), 2)], axis=1)
    rest = rest.reshape(line * count, HQK).astype(jnp.bfloat16)
    scores = (
        lax.dot_general(
            query_ref[...], keys, (((1,), (1,)), ((), ())), preferred_element_type=jnp.float32
        )
        * scale
    )
    top = jnp.max(scores, axis=1, keepdims=True)
    expo = jnp.exp(scores - top)
    total = jnp.sum(expo, axis=1, keepdims=True)
    expo = expo.astype(jnp.bfloat16)
    mixed = jnp.concatenate(
        [jnp.dot(expo, part, preferred_element_type=jnp.float32) for part in (values, rest)], axis=1
    )
    lane = lax.broadcasted_iota(jnp.int32, mixed.shape, 1)
    for index, column in enumerate(split(top) + split(total)):
        mixed = jnp.where(lane == HV + index, column, mixed)
    mixed = mixed.astype(jnp.bfloat16)
    flips = (0, 2, 1, 3)
    groups, count, _ = out_ref.shape
    for index in range(groups):
        place = ((place_ref[0] >> 1) ^ flips[index // 2]) * 2 + index % 2
        out_ref[place ^ MIDDLE_SPREAD] = mixed[index * count : (index + 1) * count, :]


def attention(place, query, kv):
    groups = N_SPREAD
    count, width = query.shape[0] // groups, 2 * HQK
    return pl.pallas_call(
        attention_kernel,
        out_shape=jax.ShapeDtypeStruct((groups, count, width), jnp.bfloat16),
        in_specs=[pl.BlockSpec(memory_space=pltpu.SMEM)] + whole(2),
        out_specs=whole(1)[0],
        compiler_params=params(),
    )(place, query, kv)


def combine_kernel(parts_ref, w_out_ref, out_ref):
    parts = parts_ref[...].astype(jnp.float32)
    top = jnp.sum(parts[:, :, HV : HV + 3], axis=2, keepdims=True)
    gain = jnp.exp(top - jnp.max(top, axis=0, keepdims=True))
    total = jnp.sum(gain * jnp.sum(parts[:, :, HV + 3 : HV + 6], axis=2, keepdims=True), axis=0)
    mixed = (jnp.sum(gain * parts, axis=0) / total)[:, :HV].astype(jnp.bfloat16)
    term = jnp.dot(mixed, w_out_ref[...], preferred_element_type=jnp.float32)
    mean = jnp.sum(term, axis=0, keepdims=True) * (1.0 / PAIR_POOL)
    width = term.shape[1] // N_PAIR
    count = term.shape[0]
    tail = jnp.concatenate(
        [mean[:, c * width : (c + 1) * width] for c in range(N_PAIR)]
        + [jnp.zeros((8 - N_PAIR, width), jnp.float32)],
        axis=0,
    )
    for c in range(N_PAIR):
        out_ref[c ^ MIDDLE_PAIR, :count, :] = term[:, c * width : (c + 1) * width]
        out_ref[c ^ MIDDLE_PAIR, count:, :] = tail


def combine(parts, w_out):
    count = parts.shape[1]
    width = w_out.shape[1] // N_PAIR
    return pl.pallas_call(
        combine_kernel,
        out_shape=jax.ShapeDtypeStruct((N_PAIR, count + 8, width), jnp.float32),
        in_specs=whole(2),
        out_specs=whole(1)[0],
        compiler_params=params(),
    )(parts, w_out)


def close_kernel(terms_ref, own_ref, trunk_ref, w_pair_ref, pair_ref, seq_ref, rows_ref, every_ref):
    count, width = own_ref.shape
    total = jnp.sum(terms_ref[...], axis=0)
    seq_ref[...] = (own_ref[...].astype(jnp.float32) + total[:count, :]).astype(jnp.bfloat16)
    trunk_mean = jnp.sum(trunk_ref[...].astype(jnp.float32), axis=0, keepdims=True) * (1.0 / PAIR_POOL)
    rows = None
    for c in range(N_PAIR):
        pooled = trunk_mean[:, c * width : (c + 1) * width] + total[count + c : count + c + 1, :]
        term = jnp.dot(
            jnp.broadcast_to(pooled, (8, width)).astype(jnp.bfloat16),
            w_pair_ref[c * width : (c + 1) * width, :],
            preferred_element_type=jnp.float32,
        )
        rows = term if rows is None else rows + term
    rows_ref[...] = rows
    mine = pair_ref[0].astype(jnp.float32)
    factors = jnp.broadcast_to(rows[:1], (mine.shape[0], rows.shape[1]))
    every = jnp.concatenate([factors, mine], axis=1)
    for at in range(0, every.shape[0], MIDDLE_SEQ):
        to = at ^ MIDDLE_SEQ
        every_ref[to : to + MIDDLE_SEQ, :] = every[at : at + MIDDLE_SEQ, :]


def close(terms, own, trunk, w_pair, pair_in):
    return pl.pallas_call(
        close_kernel,
        out_shape=(
            jax.ShapeDtypeStruct(own.shape, jnp.bfloat16),
            jax.ShapeDtypeStruct((8, w_pair.shape[1]), jnp.float32),
            jax.ShapeDtypeStruct((pair_in.shape[1], w_pair.shape[1] + pair_in.shape[2]), jnp.float32),
        ),
        in_specs=whole(5),
        out_specs=tuple(whole(3)),
        compiler_params=params(),
    )(terms, own, trunk, w_pair, pair_in)


def distance_bias(row, cols, pair_bias):
    delta = jnp.abs(row - cols)
    bins = jnp.zeros(delta.shape, jnp.int32)
    for edge in EDGES:
        bins = bins + (delta >= edge).astype(jnp.int32)
    labels = jnp.arange(pair_bias.shape[0], dtype=jnp.int32)
    onehot = (bins[:, None] == labels[None, :]).astype(jnp.bfloat16)
    return jnp.dot(onehot, pair_bias, preferred_element_type=jnp.float32)


def exchange(blocks, axes, middle=0):
    order = [index ^ middle for index in range(blocks.shape[0])]
    return lax.all_to_all(
        blocks, axes, split_axis=0, concat_axis=0, tiled=True, axis_index_groups=[order] if middle else None
    )


def on_device(tokens, w_stem, w_conv, w_query, w_key, w_value, w_out, w_pair, pair_bias, pair_in):
    place = lax.axis_index(SEQ)
    pair_place = lax.axis_index("pair")

    taps, width = w_conv.shape
    share = width // N_SHARE
    blocks, made = start(w_conv, w_stem, tokens)
    held = exchange(blocks, SEQ, MIDDLE_SEQ)

    section = stem(made, w_stem.shape[1]).astype(jnp.bfloat16)
    sections = lax.all_gather(section, SHARE, axis=0, tiled=False)

    parts = exchange(conv(place.astype(jnp.int32)[None], sections, held, made, share), SHARE + ("pair",))
    count = ROWS // 2
    trunk = parts.reshape(N_SHARE, N_PAIR, 2 * count, share).transpose(2, 1, 0, 3)
    trunk = trunk.reshape(2 * count, N_PAIR * width)

    core = lax.axis_index("core").astype(jnp.int32)[None]
    query, kv, trunk = project(core, trunk, w_query, w_key, w_value)
    for name in SPREAD[:-1]:
        other = lax.ppermute(query, name, [(0, 1), (1, 0)])
        query = jnp.concatenate([query, other], axis=0)
    kv = exchange(kv, LINE, MIDDLE_LINE)
    spread = lax.axis_index(SPREAD).astype(jnp.int32)[None]
    parts = exchange(attention(spread, query, kv), SPREAD, MIDDLE_SPREAD)
    terms = exchange(combine(parts, w_out), ("pair",), MIDDLE_PAIR)

    own = lax.dynamic_slice_in_dim(trunk, pair_place * width, width, 1)
    factors = jnp.concatenate([w_pair[0], w_pair[1]], axis=1)
    seq_out, rows, every = close(terms, own, trunk, factors, pair_in)
    channels = pair_in.shape[2]
    mine = pair_in[0].astype(jnp.float32)
    rows = rows[:1]
    every = exchange(every[:, None], SEQ, MIDDLE_SEQ)[:, 0]
    every = every.reshape(-1, 2, MIDDLE_SEQ, every.shape[1])[:, ::-1].reshape(every.shape)
    mirror = every[:, 2 * channels :]

    cols = jnp.arange(N_SEQ, dtype=jnp.int32)
    bias = lax.optimization_barrier(distance_bias(place.astype(jnp.int32), cols, pair_bias))
    cross = rows[:, :channels] * every[:, channels : 2 * channels]
    cross = cross + every[:, :channels] * rows[:, channels:]
    pair_out = (0.5 * (mine + mirror + cross) + bias).astype(jnp.bfloat16)[None]
    return (seq_out, pair_out)


def solution(mesh):
    names = SEQ + ("pair",)
    fine = Mesh(mesh.devices.reshape([SIZES[name] for name in names]), names)
    placed = (
        P(SEQ),
        P(),
        P(SEQ, "pair"),
        P(None, "pair"),
        P(None, "pair"),
        P(None, "pair"),
        P("pair", None),
        P(None, None, "pair"),
        P(None, "pair"),
        P(SEQ, None, "pair"),
    )
    return jax.shard_map(
        on_device,
        mesh=fine,
        in_specs=placed,
        out_specs=(P(SEQ, "pair"), P(SEQ, None, "pair")),
        check_vma=False,
    )
```
